32 devices in a mesh: dp: 8 (over z, y), tensor: 4 (over x, core).
Axes of the slice: x: 2, y: 2, z: 4, core: 2. Of those that a mesh axis runs over, the one named last changes fastest.
Arguments:
- tokens: bfloat16 [4096, 768], P(('dp', 'tensor')), may hold values from -6 to 6
- crop_depth: int32 [8], P('dp'), may hold values from 4 to 8, as said below
- w_query: float32 [768, 768], P('dp', 'tensor'), may hold values from -0.21875 to 0.21875
- w_key: float32 [768, 768], P('dp', 'tensor'), may hold values from -0.21875 to 0.21875
- w_value: float32 [768, 768], P('dp', 'tensor'), may hold values from -0.21875 to 0.21875
- w_out: float32 [768, 768], P('tensor', 'dp'), may hold values from -2.5 to 2.5
- w_up: float32 [768, 3072], P('dp', 'tensor'), may hold values from -0.21875 to 0.21875
- w_down: float32 [3072, 768], P('tensor', 'dp'), may hold values from -0.109375 to 0.109375
- w_tconv: float32 [768, 1024], P('dp', 'tensor'), may hold values from -0.21875 to 0.21875
- w_conv1: float32 [128, 27, 128], P('dp', None, 'tensor'), may hold values from -0.109375 to 0.109375
- w_conv2: float32 [128, 27, 128], P('dp', None, 'tensor'), may hold values from -0.109375 to 0.109375
- ln1_gain: float32 [768], P('dp'), may hold values from 0.1 to 1.9
- ln1_bias: float32 [768], P('dp'), may hold values from -3 to 3
- ln2_gain: float32 [768], P('dp'), may hold values from 0.1 to 1.9
- ln2_bias: float32 [768], P('dp'), may hold values from -3 to 3
- cot_out: float32 [4096, 768], P(('dp', 'tensor')), may hold values from -6 to 6
- cot_dec: float32 [8, 16, 16, 16, 128], P('dp', None, None, None, 'tensor'), may hold values from -6 to 6
Outputs:
- out_rows: float32 [4096, 768], P(('dp', 'tensor'))
- dec_out: float32 [8, 16, 16, 16, 128], P('dp', None, None, None, 'tensor')
- grad_tokens: float32 [4096, 768], P(('dp', 'tensor'))
- grad_w_query: float32 [768, 768], P('dp', 'tensor')
- grad_w_key: float32 [768, 768], P('dp', 'tensor')
- grad_w_value: float32 [768, 768], P('dp', 'tensor')
- grad_w_out: float32 [768, 768], P('tensor', 'dp')
- grad_w_up: float32 [768, 3072], P('dp', 'tensor')
- grad_w_down: float32 [3072, 768], P('tensor', 'dp')
- grad_w_tconv: float32 [768, 1024], P('dp', 'tensor')
- grad_w_conv1: float32 [128, 27, 128], P('dp', None, 'tensor')
- grad_w_conv2: float32 [128, 27, 128], P('dp', None, 'tensor')
- grad_ln1_gain: float32 [768], P('dp')
- grad_ln1_bias: float32 [768], P('dp')
- grad_ln2_gain: float32 [768], P('dp')
- grad_ln2_bias: float32 [768], P('dp')
The draws below stay inside these ranges and needn't reach their ends.
Inputs may be any that keep to these rules, and one draw needn't show every extreme that they name: `crop_depth`: every crop has at least half of its depth slices live, and in every draw some crop has all 8 live.
All inputs are finite; a program needn't handle non-finite values.
Results may differ from the reference program's by a relative error of at most 0.035.
Values may be sent and summed in bfloat16 or wider, within the bound.
No kernel may reach another device: no remote copies, remote signals or barrier semaphores. Data moves between devices by JAX's collectives and lax.ppermute only.
A program may use at most 320 MiB of HBM per device.

```python
import jax
import jax.numpy as jnp
from jax import lax

D = 768
HEADS = 12
HD = 64
FF = 3072
C = 128
GRID = 8
CROPS = 8
TOKENS = 4096
VOX = 16


def draw_crop_depth(key, part):
    key = jax.random.fold_in(key, 7)
    first_key, second_key = jax.random.split(key)
    depths = jax.random.randint(first_key, (CROPS,), GRID // 2, GRID + 1)
    chosen = jax.random.randint(second_key, (), 0, CROPS)
    return jnp.where(jnp.arange(CROPS) == chosen, GRID, depths).astype(jnp.int32)


def steps_of(stream_key, shape, shards, smallest, high):
    level = 1.0
    for axis_at, shards_of in shards:
        steps = jax.random.uniform(jax.random.fold_in(jax.random.fold_in(stream_key, 6), axis_at), (shards_of,), jnp.float32, smallest / len(shards), high / len(shards))
        level = level * jnp.repeat(jnp.exp(steps), shape[axis_at] // shards_of).reshape((-1,) + (1,) * (len(shape) - 1 - axis_at))
    return level


def noise(own_key, dims, scale, bound, cuts=(), held_as=jnp.bfloat16):
    drawn = jax.random.normal(own_key, dims, jnp.float32) * scale
    if len(cuts) > 0:
        drawn = steps_of(own_key, dims, cuts, -0.22, 0.18) * drawn
    return jnp.clip(drawn, min=-bound, max=bound).astype(held_as)


def setup_inputs(seed: int = 0) -> dict:
    streams_of = jax.random.split(jax.random.key(seed), 18)
    return {
        "tokens": noise(streams_of[0], (TOKENS, D), 1.0, 6.0, ((0, 32),)),
        "crop_depth": draw_crop_depth(jax.random.fold_in(streams_of[17], 71), 0),
        "w_query": noise(streams_of[2], (D, D), D ** -0.5, 0.21875, ((0, 8), (1, 4)), jnp.float32),
        "w_key": noise(streams_of[3], (D, D), D ** -0.5, 0.21875, ((0, 8), (1, 4)), jnp.float32),
        "w_value": noise(streams_of[4], (D, D), D ** -0.5, 0.21875, ((0, 8), (1, 4)), jnp.float32),
        "w_out": noise(streams_of[5], (D, D), (D * 4 // GRID ** 3) ** -0.5, 2.5, ((0, 4), (1, 8)), jnp.float32),
        "w_up": noise(streams_of[6], (D, FF), D ** -0.5, 0.21875, ((0, 8), (1, 4)), jnp.float32),
        "w_down": noise(streams_of[7], (FF, D), FF ** -0.5, 0.109375, ((0, 4), (1, 8)), jnp.float32),
        "w_tconv": noise(streams_of[8], (D, 8 * C), D ** -0.5, 0.21875, ((0, 8), (1, 4)), jnp.float32),
        "w_conv1": noise(streams_of[9], (C, 27, C), (27 * C) ** -0.5, 0.109375, ((0, 8), (2, 4)), jnp.float32),
        "w_conv2": noise(streams_of[10], (C, 27, C), (27 * C) ** -0.5, 0.109375, ((0, 8), (2, 4)), jnp.float32),
        "ln1_gain": jnp.clip(1.0 + 0.18 * jax.random.normal(streams_of[11], (D,), jnp.float32), 0.1, 1.9),
        "ln1_bias": noise(streams_of[12], (D,), 0.5, 3.0, ((0, 8),), jnp.float32),
        "ln2_gain": jnp.clip(1.0 + 0.18 * jax.random.normal(streams_of[13], (D,), jnp.float32), 0.1, 1.9),
        "ln2_bias": noise(streams_of[14], (D,), 0.5, 3.0, ((0, 8),), jnp.float32),
        "cot_out": noise(streams_of[15], (TOKENS, D), 1.0, 6.0, ((0, 32),), jnp.float32),
        "cot_dec": noise(streams_of[16], (CROPS, VOX, VOX, VOX, C), 1.0, 6.0, ((0, 8), (4, 4)), jnp.float32),
    }


@jax.custom_vjp
def low(v):
    return lax.optimization_barrier(v.astype(jnp.bfloat16)).astype(jnp.float32)

@jax.custom_vjp
def low_back(v):
    return v

def low_keep(v):
    return (low(v), None)

def low_pass(kept, grad):
    return (grad,)

def back_keep(v):
    return (v, None)

def back_low(kept, grad):
    return (low(grad),)
low.defvjp(low_keep, low_pass)
low_back.defvjp(back_keep, back_low)
HIGH = lax.Precision.HIGHEST

def matmul(left, right):
    return jnp.dot(left, right, precision=HIGH, preferred_element_type=jnp.float32)

def rounded_both(value):
    return low(low_back(value))

def layer_norm(rows):
    middle = lax.optimization_barrier(jnp.mean(rows, axis=-1, keepdims=True))
    centred = rows - middle
    spread = lax.optimization_barrier(jnp.mean(centred * centred, axis=-1, keepdims=True))
    return centred * lax.rsqrt(spread + 1e-06)

def norm_act(conv_out, vox_mask):
    live = jnp.sum(vox_mask) * conv_out.shape[1] * conv_out.shape[2]
    middle = lax.optimization_barrier(jnp.sum(conv_out * vox_mask, axis=(0, 1, 2), keepdims=True)) / live
    centred = (conv_out - middle) * vox_mask
    spread = lax.optimization_barrier(jnp.sum(centred * centred, axis=(0, 1, 2), keepdims=True)) / live
    normed = (conv_out - middle) * lax.rsqrt(spread + 1e-05)
    return jax.nn.gelu(normed, approximate=False) * vox_mask

def conv_same(field, kernel):
    chan_in = kernel.shape[0]
    chan_out = kernel.shape[2]
    taps = kernel.transpose(1, 0, 2).reshape(3, 3, 3, chan_in, chan_out)
    result = lax.conv_general_dilated(field[None], taps, (1, 1, 1), 'SAME', dimension_numbers=('NDHWC', 'DHWIO', 'NDHWC'), precision=HIGH)
    return result[0]

def crop_pass(weights, crop_rows, depth_one):
    w_query, w_key, w_value, w_out, w_up, w_down, w_tconv, w_conv1, w_conv2, gain_one, shift_one, gain_two, shift_two = weights
    patches = GRID ** 3
    vox = 2 * GRID
    key_live = jnp.arange(patches) // (GRID * GRID) < depth_one
    vox_mask = (jnp.arange(vox) < 2 * depth_one).astype(jnp.float32)[:, None, None, None]
    normed1 = low(layer_norm(crop_rows) * gain_one + shift_one)
    query = rounded_both(matmul(normed1, w_query)).reshape(patches, HEADS, HD)
    keys = rounded_both(matmul(normed1, w_key)).reshape(patches, HEADS, HD)
    values = rounded_both(matmul(normed1, w_value)).reshape(patches, HEADS, HD)
    scores = low_back(jnp.einsum('qhd,khd->hqk', query, keys, precision=HIGH) * HD ** (-0.5))
    scores = jnp.where(key_live[None, None, :], scores, -1000000000.0)
    peak = lax.optimization_barrier(jnp.max(scores, axis=-1, keepdims=True))
    expo = jnp.exp(scores - peak)
    probs = low(expo / lax.optimization_barrier(jnp.sum(expo, axis=-1, keepdims=True)))
    attended = rounded_both(jnp.einsum('hqk,khd->qhd', probs, values, precision=HIGH).reshape(patches, D))
    middle_rows = crop_rows + low_back(matmul(attended, w_out))
    normed2 = low(layer_norm(middle_rows) * gain_two + shift_two)
    upper = low_back(matmul(normed2, w_up))
    hidden = low(jax.nn.gelu(upper, approximate=False))
    after = middle_rows + low_back(matmul(hidden, w_down))
    dec_in = low(after)
    tconv = low_back(matmul(dec_in, w_tconv))
    cube = tconv.reshape(GRID, GRID, GRID, C, 2, 2, 2).transpose(0, 4, 1, 5, 2, 6, 3).reshape(vox, vox, vox, C)
    first = low(cube * vox_mask)
    act_one = low(norm_act(low_back(conv_same(first, w_conv1)), vox_mask))
    act_two = norm_act(low_back(conv_same(act_one, w_conv2)), vox_mask)
    return (after, act_two)

def reference(tokens, crop_depth, w_query, w_key, w_value, w_out, w_up, w_down, w_tconv, w_conv1, w_conv2, ln1_gain, ln1_bias, ln2_gain, ln2_bias, cot_out, cot_dec):
    masters = (w_query, w_key, w_value, w_out, w_up, w_down, w_tconv, w_conv1, w_conv2, ln1_gain, ln1_bias, ln2_gain, ln2_bias)

    def forward(rows, params):
        weights = tuple((low(param) for param in params))
        step = jax.checkpoint(lambda pair: crop_pass(weights, pair[0], pair[1]))
        rows_out, dec = lax.map(step, (rows.reshape(CROPS, GRID ** 3, D), crop_depth))
        return (rows_out.reshape(CROPS * GRID ** 3, D), dec)
    primal, pull = jax.vjp(forward, tokens.astype(jnp.float32), masters)
    grad_rows, grads = pull((cot_out, cot_dec))
    return (primal[0], primal[1], grad_rows, grads[0], grads[1], grads[2], grads[3], grads[4], grads[5], grads[6], grads[7], grads[8], grads[9], grads[10], grads[11], grads[12])
```

```python
import jax
import jax.numpy as jnp
from jax import lax
from jax.sharding import PartitionSpec as P

HD = 64
GRID = 8
LOW = jnp.bfloat16


def ring_order(size):
    if size % 2:
        return list(range(size))
    return list(range(0, size, 2)) + list(range(size - 1, 0, -2))


def layer_norm(rows):
    middle = jnp.mean(rows, axis=-1, keepdims=True)
    centred = rows - middle
    spread = jnp.mean(centred * centred, axis=-1, keepdims=True)
    scale = lax.rsqrt(spread + 1e-06)
    return centred * scale, scale


def layer_norm_back(grad_normed, normed, scale):
    mean_grad = jnp.mean(grad_normed, axis=-1, keepdims=True)
    mean_dot = jnp.mean(grad_normed * normed, axis=-1, keepdims=True)
    return scale * (grad_normed - mean_grad - normed * mean_dot)


def gelu_exact(value):
    return jax.nn.gelu(value, approximate=False)


def norm_act(conv_out, vox_mask):
    live = jnp.sum(vox_mask, axis=1, keepdims=True) * conv_out.shape[2] * conv_out.shape[3]
    middle = jnp.sum(conv_out * vox_mask, axis=(1, 2, 3), keepdims=True) / live
    centred = (conv_out - middle) * vox_mask
    spread = jnp.sum(centred * centred, axis=(1, 2, 3), keepdims=True) / live
    normed = (conv_out - middle) * lax.rsqrt(spread + 1e-05)
    return gelu_exact(normed) * vox_mask


def contract_first(left, right):
    return lax.dot_general(
        left, right, (((0,), (0,)), ((), ())), preferred_element_type=jnp.float32
    )


def contract_last(left, right):
    return lax.dot_general(
        left, right, (((1,), (1,)), ((), ())), preferred_element_type=jnp.float32
    )


def dot(left, right):
    return jnp.dot(left, right, preferred_element_type=jnp.float32)


class Ring:
    def __init__(self, size):
        self.size = size
        self.order = ring_order(size)
        self.ahead = [(self.order[i], self.order[(i + 1) % size]) for i in range(size)]
        self.behind = [(b, a) for a, b in self.ahead]
        place = [0] * size
        for at, index in enumerate(self.order):
            place[index] = at
        self.spot = jnp.array(place, jnp.int32)[lax.axis_index("dp")]

    def index_at(self, distance):
        return jnp.array(self.order, jnp.int32)[(self.spot + distance) % self.size]

    def send(self, value, forward):
        return lax.ppermute(value, "dp", self.ahead if forward else self.behind)

    def gather(self, block):
        size = self.size
        rows = block.shape[0]
        pieces = [(0, 0, block)]
        one = two = block
        for step in range(1, (size - 1) // 2 + 1):
            one = self.send(one, True)
            two = self.send(two, False)
            pieces.append((-step, 0, one))
            pieces.append((step, 0, two))
        if size % 2 == 0:
            half = rows // 2
            pieces.append((-(size // 2), 0, self.send(one[:half], True)))
            pieces.append((size // 2, half, self.send(two[half:], False)))
        full = jnp.zeros((size,) + block.shape, block.dtype)
        for distance, start, piece in pieces:
            full = lax.dynamic_update_slice(
                full, piece[None], (self.index_at(distance), start, 0)
            )
        return full

    def scatter(self, terms):
        size = self.size
        rows = terms.shape[1]
        low = terms.astype(LOW)

        def term(distance):
            return lax.dynamic_index_in_dim(low, self.index_at(distance), 0, keepdims=False)

        own = lax.dynamic_index_in_dim(terms, self.index_at(0), 0, keepdims=False)
        one = two = None
        reach = (size - 1) // 2
        if size % 2 == 0:
            half = rows // 2
            far = term(size // 2)
            one = self.send(far[:half], True)
            two = self.send(far[half:], False)
            above, below = term(reach), term(-reach)
            if reach == 0:
                return own + jnp.concatenate([one, two]).astype(jnp.float32)
            one = jnp.concatenate([above[:half] + one, above[half:]])
            two = jnp.concatenate([below[:half], below[half:] + two])
        else:
            if reach == 0:
                return own
            one, two = term(reach), term(-reach)
        for step in range(reach, 0, -1):
            one = self.send(one, True)
            two = self.send(two, False)
            if step > 1:
                one = one + term(step - 1)
                two = two + term(-(step - 1))
        return own + one.astype(jnp.float32) + two.astype(jnp.float32)


class Quad:
    def __init__(self):
        me = lax.axis_index("tensor")
        self.core = me % 2
        self.chip = me // 2

    def over_core(self, value):
        return lax.ppermute(value, "tensor", [(i, i ^ 1) for i in range(4)])

    def over_chip(self, value):
        return lax.ppermute(value, "tensor", [(i, i ^ 2) for i in range(4)])

    def gather(self, block):
        far = self.over_chip(block)
        near = self.over_core(block)
        far_near = self.over_core(far)
        first = self.core == 0
        here = jnp.stack([jnp.where(first, block, near), jnp.where(first, near, block)])
        there = jnp.stack([jnp.where(first, far, far_near), jnp.where(first, far_near, far)])
        left = self.chip == 0
        return jnp.concatenate([jnp.where(left, here, there), jnp.where(left, there, here)])

    def halves(self, value):
        blocks = value.reshape(2, 2, value.shape[0] // 4, value.shape[1])
        first = self.core == 0
        mine = jnp.where(first, blocks[:, 0], blocks[:, 1])
        other = jnp.where(first, blocks[:, 1], blocks[:, 0])
        return mine, other

    def reduce_half(self, partial):
        mine, other = self.halves(partial)
        summed = (mine + self.over_core(other.astype(LOW)).astype(jnp.float32)).astype(LOW)
        return summed.astype(jnp.float32) + self.over_chip(summed).astype(jnp.float32)

    def reduce_own(self, partial):
        mine, other = self.halves(partial)
        summed = mine + self.over_core(other.astype(LOW)).astype(jnp.float32)
        keep, give = self.pick(summed), self.pick(summed[::-1])
        return keep + self.over_chip(give.astype(LOW)).astype(jnp.float32)

    def pick(self, half):
        return jnp.where(self.chip == 0, half[0], half[1])

    def join(self, half):
        other = self.over_core(half)
        first = self.core == 0
        blocks = jnp.stack([jnp.where(first, half, other), jnp.where(first, other, half)], axis=1)
        return blocks.reshape(4 * half.shape[1], half.shape[2])


def conv_same(field, taps):
    return lax.conv_general_dilated(
        field,
        taps,
        (1, 1, 1),
        "SAME",
        dimension_numbers=("NDHWC", "DHWIO", "NDHWC"),
        preferred_element_type=jnp.float32,
    )


def conv_weight_grad(field, grad_out):
    grads = lax.conv_general_dilated(
        field,
        grad_out,
        (1, 1, 1),
        ((1, 1),) * 3,
        dimension_numbers=("CDHWN", "IDHWO", "DHWNC"),
        preferred_element_type=jnp.float32,
    )
    return grads.reshape(27, grads.shape[3], grads.shape[4]).transpose(1, 0, 2)


def shards(
    tokens,
    crop_depth,
    w_query,
    w_key,
    w_value,
    w_out,
    w_up,
    w_down,
    w_tconv,
    w_conv1,
    w_conv2,
    ln1_gain,
    ln1_bias,
    ln2_gain,
    ln2_bias,
    cot_out,
    cot_dec,
    groups,
):
    ring = Ring(groups)
    quad = Quad()
    grid = GRID
    vox = 2 * grid
    patches = grid**3
    factor = HD ** (-0.5)
    width = w_query.shape[0] * groups
    part = w_query.shape[0]
    heads_here = w_query.shape[1] // HD
    span = heads_here * HD
    chans = w_conv1.shape[0] * groups
    chans_here = w_conv1.shape[2]

    low = lambda value: value.astype(LOW)
    rows_in = low(quad.gather(tokens).reshape(patches, width)).astype(jnp.float32)

    norm_params = jnp.stack([ln1_gain, ln1_bias, ln2_gain, ln2_bias])
    params = low(jnp.pad(norm_params, ((0, 12), (0, 4 * span - part))))
    pack_a = jnp.concatenate(
        [jnp.concatenate([low(w_query), low(w_key), low(w_value), low(w_out).T], axis=1), params]
    )
    pack_b = jnp.concatenate([low(w_up), low(w_down).T, low(w_tconv)], axis=1)
    pack_c = jnp.concatenate([low(w_conv1), low(w_conv2)], axis=2)
    pack_c = pack_c.reshape(pack_c.shape[0], -1)
    full_a = ring.gather(pack_a)
    full_b = ring.gather(pack_b).reshape(width, -1)
    full_c = ring.gather(pack_c).reshape(chans, 27, 2 * chans_here)

    norm_rows = full_a[:, part : part + 4, :part].astype(jnp.float32)
    gain_one, shift_one, gain_two, shift_two = norm_rows.transpose(1, 0, 2).reshape(4, width)
    matrix_a = full_a[:, :part].reshape(width, 4 * span)
    qkv_weight = matrix_a[:, : 3 * span]
    out_weight = matrix_a[:, 3 * span :]
    hidden_here = w_up.shape[1]
    up_weight = full_b[:, :hidden_here]
    down_weight = full_b[:, hidden_here : 2 * hidden_here]
    tconv_here = full_b[:, 2 * hidden_here :]
    out_full = quad.gather(out_weight).transpose(1, 0, 2).reshape(width, -1)
    tconv_full = quad.gather(tconv_here).transpose(1, 0, 2).reshape(width, -1)
    conv_full = quad.gather(full_c.reshape(chans, -1)).reshape(4, chans, 27, 2, chans_here)
    conv_full = conv_full.transpose(3, 1, 2, 0, 4).reshape(2, chans, 27, chans)
    taps_one = conv_full[0].transpose(1, 0, 2).reshape(3, 3, 3, chans, chans)
    taps_two = conv_full[1].transpose(1, 0, 2).reshape(3, 3, 3, chans, chans)
    back_one = taps_one[::-1, ::-1, ::-1].transpose(0, 1, 2, 4, 3)
    back_two = taps_two[::-1, ::-1, ::-1].transpose(0, 1, 2, 4, 3)

    key_live = jnp.arange(patches) // (grid * grid) < crop_depth[0]
    vox_mask = (jnp.arange(vox) < 2 * crop_depth[0]).astype(jnp.float32)[
        None, :, None, None, None
    ]

    cot_rows = quad.gather(cot_out).reshape(patches, width)
    cot_field = quad.gather(low(cot_dec).reshape(vox**3, chans_here)).transpose(1, 0, 2)
    cot_field = cot_field.reshape(1, vox, vox, vox, chans).astype(jnp.float32)

    normed_one, scale_one = layer_norm(rows_in)
    h_one = low(normed_one * gain_one + shift_one)
    qkv = low(dot(h_one, qkv_weight))

    def heads_view(flat):
        return flat.reshape(patches, heads_here, HD)

    query = heads_view(qkv[:, :span])
    keys = heads_view(qkv[:, span : 2 * span])
    values = heads_view(qkv[:, 2 * span :])
    scores = jnp.einsum("qhd,khd->hqk", query, keys, preferred_element_type=jnp.float32) * factor
    scores = jnp.where(key_live[None, None, :], scores, -1000000000.0)
    peak = jnp.max(scores, axis=-1, keepdims=True)
    expo = jnp.exp(scores - peak)
    probs = expo / jnp.sum(expo, axis=-1, keepdims=True)
    attended = jnp.einsum("hqk,khd->qhd", low(probs), values, preferred_element_type=jnp.float32)
    attended = low(attended.reshape(patches, span))
    attended_full = quad.gather(attended).transpose(1, 0, 2).reshape(patches, width)
    middle_rows = rows_in + contract_last(attended_full, out_full)
    normed_two, scale_two = layer_norm(middle_rows)
    h_two = low(normed_two * gain_two + shift_two)
    upper = dot(h_two, up_weight)
    hidden = low(gelu_exact(upper))
    mlp_half = quad.reduce_half(contract_last(hidden, down_weight))
    after_half = quad.halves(middle_rows)[0] + mlp_half
    after = quad.pick(after_half)
    dec_in = quad.join(low(after_half))

    tconv = dot(dec_in, tconv_full)
    cube = tconv.reshape(1, grid, grid, grid, chans, 2, 2, 2)
    cube = cube.transpose(0, 1, 5, 2, 6, 3, 7, 4).reshape(1, vox, vox, vox, chans)
    first = low(cube * vox_mask)
    conv_one = conv_same(first, taps_one)
    act_one, act_one_back = jax.vjp(lambda value: norm_act(value, vox_mask), conv_one)
    act_one = low(act_one)
    conv_two = conv_same(act_one, taps_two)
    act_two, act_two_back = jax.vjp(lambda value: norm_act(value, vox_mask), conv_two)

    def own_chans(field):
        return lax.dynamic_slice_in_dim(
            field, lax.axis_index("tensor") * chans_here, chans_here, axis=4
        )

    dec_out = own_chans(act_two)
    grad_conv_two = low(act_two_back(cot_field)[0])
    grad_act_one = conv_same(grad_conv_two, back_two)
    grad_conv_one = low(act_one_back(grad_act_one)[0])
    grad_first = conv_same(grad_conv_one, back_one)
    cube = (grad_first * vox_mask).reshape(grid, 2, grid, 2, grid, 2, chans)
    grad_tconv = low(cube.transpose(0, 2, 4, 6, 1, 3, 5).reshape(patches, 8 * chans))
    grad_after = cot_rows + contract_last(grad_tconv, tconv_full)
    grad_mlp = low(grad_after)

    grad_hidden = dot(grad_mlp, down_weight)
    grad_upper = low(jax.vjp(gelu_exact, upper)[1](grad_hidden)[0])
    grad_h_two = contract_last(grad_upper, up_weight)
    gain_two_terms = jnp.sum(grad_h_two * normed_two, axis=0)
    shift_two_terms = jnp.sum(grad_h_two, axis=0)
    norm_half = quad.reduce_half(grad_h_two)
    normed_half = quad.halves(normed_two)[0]
    scale_half = quad.halves(scale_two)[0]
    grad_mid_half = quad.halves(grad_after)[0] + layer_norm_back(
        norm_half * gain_two, normed_half, scale_half
    )
    grad_branch = quad.join(low(grad_mid_half))

    grad_attended = low(dot(grad_branch, out_weight))
    grad_heads = heads_view(grad_attended)
    low_probs = low(probs)
    grad_values = jnp.einsum("hqk,qhd->khd", low_probs, grad_heads, preferred_element_type=jnp.float32)
    grad_probs = jnp.einsum("qhd,khd->hqk", grad_heads, values, preferred_element_type=jnp.float32)
    inner = jnp.sum(probs * grad_probs, axis=-1, keepdims=True)
    grad_scores = low(probs * (grad_probs - inner))
    grad_query = factor * jnp.einsum(
        "hqk,khd->qhd", grad_scores, keys, preferred_element_type=jnp.float32
    )
    grad_keys = factor * jnp.einsum(
        "hqk,qhd->khd", grad_scores, query, preferred_element_type=jnp.float32
    )
    grad_qkv = jnp.concatenate(
        [low(grad.reshape(patches, span)) for grad in (grad_query, grad_keys, grad_values)], axis=1
    )
    grad_h_one = contract_last(grad_qkv, qkv_weight)
    gain_one_terms = jnp.sum(grad_h_one * normed_one, axis=0)
    shift_one_terms = jnp.sum(grad_h_one, axis=0)
    norm_own = quad.reduce_own(grad_h_one)
    normed_own = quad.pick(quad.halves(normed_one)[0])
    scale_own = quad.pick(quad.halves(scale_one)[0])
    grad_tokens = quad.pick(grad_mid_half) + layer_norm_back(
        norm_own * gain_one, normed_own, scale_own
    )

    def by_group(matrix):
        return matrix.reshape(groups, -1, matrix.shape[-1])

    conv_pack = jnp.concatenate(
        [
            conv_weight_grad(first, own_chans(grad_conv_one)),
            conv_weight_grad(act_one, own_chans(grad_conv_two)),
        ],
        axis=2,
    )
    conv_grads = ring.scatter(by_group(conv_pack.reshape(chans, -1)))
    conv_grads = conv_grads.reshape(-1, 27, 2 * chans_here)
    own_tconv = lax.dynamic_slice_in_dim(
        grad_tconv, lax.axis_index("tensor") * 8 * chans_here, 8 * chans_here, axis=1
    )
    mlp_pack = jnp.concatenate(
        [
            contract_first(h_two, grad_upper),
            contract_first(grad_mlp, hidden),
            contract_first(dec_in, own_tconv),
        ],
        axis=1,
    )
    mlp_grads = ring.scatter(by_group(mlp_pack))
    norm_terms = jnp.stack([gain_one_terms, shift_one_terms, gain_two_terms, shift_two_terms])
    norm_terms = lax.psum(norm_terms, "tensor")
    norm_terms = norm_terms.reshape(4, groups, part).transpose(1, 0, 2)
    norm_terms = jnp.pad(norm_terms, ((0, 0), (0, 12), (0, 4 * span - part)))
    attention_pack = jnp.concatenate(
        [contract_first(h_one, grad_qkv), contract_first(grad_branch, attended)], axis=1
    )
    attention_pack = jnp.concatenate([by_group(attention_pack), norm_terms], axis=1)
    attention_grads = ring.scatter(attention_pack)
    norm_grads = attention_grads[part : part + 4, :part]
    return (
        after,
        dec_out,
        grad_tokens,
        attention_grads[:part, :span],
        attention_grads[:part, span : 2 * span],
        attention_grads[:part, 2 * span : 3 * span],
        attention_grads[:part, 3 * span :].T,
        mlp_grads[:, :hidden_here],
        mlp_grads[:, hidden_here : 2 * hidden_here].T,
        mlp_grads[:, 2 * hidden_here :],
        conv_grads[:, :, :chans_here],
        conv_grads[:, :, chans_here:],
        norm_grads[0],
        norm_grads[1],
        norm_grads[2],
        norm_grads[3],
    )


def solution(mesh):
    in_specs = (
        P(("dp", "tensor"), None),
        P("dp"),
        P("dp", "tensor"),
        P("dp", "tensor"),
        P("dp", "tensor"),
        P("tensor", "dp"),
        P("dp", "tensor"),
        P("tensor", "dp"),
        P("dp", "tensor"),
        P("dp", None, "tensor"),
        P("dp", None, "tensor"),
        P("dp"),
        P("dp"),
        P("dp"),
        P("dp"),
        P(("dp", "tensor"), None),
        P("dp", None, None, None, "tensor"),
    )
    out_specs = (
        P(("dp", "tensor"), None),
        P("dp", None, None, None, "tensor"),
        P(("dp", "tensor"), None),
        P("dp", "tensor"),
        P("dp", "tensor"),
        P("dp", "tensor"),
        P("tensor", "dp"),
        P("dp", "tensor"),
        P("tensor", "dp"),
        P("dp", "tensor"),
        P("dp", None, "tensor"),
        P("dp", None, "tensor"),
        P("dp"),
        P("dp"),
        P("dp"),
        P("dp"),
    )
    groups = mesh.shape["dp"]

    def run(*arrays):
        return shards(*arrays, groups)

    return jax.shard_map(run, mesh=mesh, in_specs=in_specs, out_specs=out_specs, check_vma=False)
```

```python
import functools

import jax
import jax.numpy as jnp
import numpy as np
from jax import lax
from jax.experimental import pallas as pl
from jax.experimental.pallas import tpu as pltpu
from jax.sharding import PartitionSpec as P

HD = 64
GRID = 8
LOW = jnp.bfloat16


def ring_order(size):
    if size % 2:
        return list(range(size))
    return list(range(0, size, 2)) + list(range(size - 1, 0, -2))


def layer_norm_back(grad_normed, normed, scale):
    mean_grad = jnp.mean(grad_normed, axis=-1, keepdims=True)
    mean_dot = jnp.mean(grad_normed * normed, axis=-1, keepdims=True)
    return scale * (grad_normed - mean_grad - normed * mean_dot)


def contract_first(left, right):
    return lax.dot_general(
        left, right, (((0,), (0,)), ((), ())), preferred_element_type=jnp.float32
    )


MIB = 2**20


def gelu_and_slope(x):
    bell = jnp.exp(-0.5 * x * x)
    frac = 1.0 / (1.0 + 0.3275911 * 0.7071067811865476 * jnp.abs(x))
    poly = frac * (
        0.254829592
        + frac * (-0.284496736 + frac * (1.421413741 + frac * (-1.453152027 + frac * 1.061405429)))
    )
    tail = 0.5 * poly * bell
    phi = jnp.where(x >= 0.0, 1.0 - tail, tail)
    return x * phi, phi + x * bell * 0.3989422804014327


def dot(left, right):
    return jnp.dot(left, right, preferred_element_type=jnp.float32)


def dot_last(left, right):
    return lax.dot_general(
        left, right, (((1,), (1,)), ((), ())), preferred_element_type=jnp.float32
    )


BATCH = 4


def decoder_kernel(
    depth_ref,
    core_ref,
    own_ref,
    near_ref,
    tconv_ref,
    select_ref,
    spread_ref,
    conv_hbm,
    back_hbm,
    cot_hbm,
    dec_ref,
    rows_ref,
    grad_tconv_ref,
    grad_half_ref,
    grad_low_ref,
    pack_ref,
    grad_rows_ref,
    wgrad_ref,
    wide_ref,
    first_even,
    first_odd,
    act_even,
    act_odd,
    grad_even,
    grad_odd,
    conv_ref,
    normed_ref,
    slope_ref,
    held_ref,
    carry_ref,
    low_grad_ref,
    columns_ref,
    conv_w,
    back_w,
    cot_ref,
    sems,
):
    grid = 8
    vox = 16
    chans = 128
    depth = depth_ref[0]
    count = (depth * (2 * vox * vox)).astype(jnp.float32)

    copies = [
        pltpu.make_async_copy(conv_hbm.at[0], conv_w.at[0], sems.at[0]),
        pltpu.make_async_copy(conv_hbm.at[1], conv_w.at[1], sems.at[1]),
        pltpu.make_async_copy(cot_hbm, cot_ref, sems.at[2]),
        pltpu.make_async_copy(back_hbm.at[1], back_w.at[1], sems.at[3]),
        pltpu.make_async_copy(back_hbm.at[0], back_w.at[0], sems.at[4]),
    ]
    for copy in copies:
        copy.start()

    for even in (first_even, act_even, grad_even):
        even[:, 0] = jnp.zeros((grid, vox, 4 * chans), LOW)
        even[:, vox + 1] = jnp.zeros((grid, vox, 4 * chans), LOW)
    for odd in (first_odd, act_odd, grad_odd):
        odd[:, 0] = jnp.zeros((grid + 1, vox, 4 * chans), LOW)
        odd[:, vox + 1] = jnp.zeros((grid + 1, vox, 4 * chans), LOW)
    wgrad_ref[:, 864:] = jnp.zeros((2, 32, chans), jnp.float32)
    low_grad_ref[:, 0] = jnp.zeros((grid, vox, 2 * chans), LOW)
    low_grad_ref[:, vox + 1] = jnp.zeros((grid, vox, 2 * chans), LOW)

    spot = lax.broadcasted_iota(jnp.int32, (1, 1, 8, 1), 2)

    def put_field(even, odd, at, value):
        left = value[..., :chans]
        right = value[..., chans:]
        flat = (2 * vox, 8, chans)
        before = pltpu.roll(right.reshape(flat), 1, 1).reshape(right.shape)
        after = pltpu.roll(left.reshape(flat), 7, 1).reshape(left.shape)
        before = jnp.where(spot == 0, 0.0, before)
        after = jnp.where(spot == 7, 0.0, after)
        window = jnp.concatenate([before, value, after], axis=3)
        even[at, 1 : vox + 1] = window.reshape(vox, 16, 4 * chans).astype(LOW)
        early = jnp.concatenate([carry_ref[...][:, None], window[:, :1]], axis=1)
        odd[at, 1 : vox + 1] = early.reshape(vox, 16, 4 * chans).astype(LOW)
        carry_ref[...] = window[:, 1]

    def open_field():
        carry_ref[...] = jnp.zeros(carry_ref.shape, jnp.float32)

    def close_field(odd):
        late = jnp.concatenate([carry_ref[...], jnp.zeros(carry_ref.shape, jnp.float32)], axis=1)
        odd[grid, 1 : vox + 1] = late.astype(LOW)

    def live_at(at):
        return (at < depth).astype(jnp.float32)

    def convolve(even, odd, weights, target, turned):
        def step(block, total):
            at = block * BATCH
            summed = None
            for deep in range(3):
                field = even if deep == 1 else odd
                start = at + 1 if deep == 2 else at
                for tall in range(3):
                    left = field[pl.ds(start, BATCH), tall : tall + vox]
                    left = left.reshape(BATCH * vox * 16, 4 * chans)
                    right = weights[deep * 3 + tall]
                    term = dot_last(left, right) if turned else dot(left, right)
                    summed = term if summed is None else summed + term
            target[pl.ds(at, BATCH)] = summed.reshape(BATCH, vox, 16, 2 * chans)
            return total

        lax.fori_loop(0, grid // BATCH, step, 0)

    def both(total):
        row = jnp.sum(total, axis=0, keepdims=True)
        half = (row[:, :chans] + row[:, chans:]) / count
        return jnp.concatenate([half, half], axis=1)

    def zero():
        return jnp.zeros((8, 2 * chans), jnp.float32)

    def fold(value):
        return jnp.sum(value.reshape(2 * vox, 8, 2 * chans), axis=0)

    def statistics(source):
        def first(at, total):
            return total + live_at(at) * fold(source[at])

        middle = both(lax.fori_loop(0, grid, first, zero()))

        def second(at, total):
            away = source[at] - middle
            return total + live_at(at) * fold(away * away)

        spread = both(lax.fori_loop(0, grid, second, zero()))
        return middle, lax.rsqrt(spread + 1e-05)

    core = core_ref[0]
    for block in range(2):
        rows_ref[pl.ds(pl.multiple_of(block * 256 + core * 128, 128), 128)] = own_ref[block]
        rows_ref[pl.ds(pl.multiple_of(block * 256 + (1 - core) * 128, 128), 128)] = near_ref[block]
    wide_ref[...] = dot(rows_ref[...], tconv_ref[...])
    open_field()

    def place_first(at, state):
        tokens = wide_ref[pl.ds(at * 64, 64)] * live_at(at)
        offsets = [
            [tokens[:, (2 * a + b) * 256 : (2 * a + b + 1) * 256].reshape(8, 1, 1, 8, 256) for a in range(2)]
            for b in range(2)
        ]
        value = jnp.concatenate(
            [jnp.concatenate(offsets[b], axis=2) for b in range(2)], axis=1
        ).reshape(vox, 2, 8, 256)
        put_field(first_even, first_odd, at, value)
        return state

    lax.fori_loop(0, grid, place_first, 0)
    close_field(first_odd)

    copies[0].wait()
    convolve(first_even, first_odd, conv_w.at[0], normed_ref, False)
    middle, scale_one = statistics(normed_ref)
    open_field()

    def act_first(at, state):
        normed = (normed_ref[at] - middle) * scale_one
        normed_ref[at] = normed
        value, slope = gelu_and_slope(normed)
        live = live_at(at)
        slope_ref[at] = slope * live
        put_field(act_even, act_odd, at, (value * live).reshape(vox, 2, 8, 2 * chans))
        return state

    lax.fori_loop(0, grid, act_first, 0)
    close_field(act_odd)

    copies[1].wait()
    convolve(act_even, act_odd, conv_w.at[1], conv_ref, False)
    middle, scale_two = statistics(conv_ref)
    copies[2].wait()

    def act_second(at, totals):
        normed = (conv_ref[at] - middle) * scale_two
        conv_ref[at] = normed
        value, slope = gelu_and_slope(normed)
        live = live_at(at)
        low_value = (value * live).astype(LOW).reshape(vox * 16, 2 * chans)
        for e in range(2):
            shown = dot_last(low_value, select_ref[e]).reshape(vox, 2, 8, 32)
            for a in range(2):
                dec_ref[2 * at + a, :, pl.ds(e, 8, stride=2), :] = shown[:, a]
        parts = [cot_ref[t, pl.ds(768 + at * vox * 8, vox * 8)] for t in range(4)]
        packed = jnp.concatenate(parts, axis=1)
        cot = jnp.concatenate(
            [dot(packed, spread_ref[a]).reshape(vox, 1, 8, 2 * chans) for a in range(2)], axis=1
        ).reshape(vox, 16, 2 * chans)
        grad = cot * slope * live
        held_ref[at] = grad
        return totals[0] + fold(grad), totals[1] + fold(grad * normed)

    totals = lax.fori_loop(0, grid, act_second, (zero(), zero()))

    def norm_back(source, normed_source, scale, sums):
        mean_grad = both(sums[0])
        mean_dot = both(sums[1])
        open_field()

        def step(at, state):
            grad = source[at] - live_at(at) * (mean_grad + normed_source[at] * mean_dot)
            grad = scale * grad
            low_grad_ref[at, 1 : vox + 1] = grad.astype(LOW)
            put_field(grad_even, grad_odd, at, grad.reshape(vox, 2, 8, 2 * chans))
            return state

        lax.fori_loop(0, grid, step, 0)
        close_field(grad_odd)

    def weight_grad(even, odd, which):
        own = select_ref[...].reshape(64, 2 * chans)
        for at in range(grid):
            shifts = [
                dot_last(own, low_grad_ref[at, 2 - tall : 18 - tall].reshape(vox * 16, 2 * chans))
                for tall in range(3)
            ]
            columns_ref[:, at * 256 : (at + 1) * 256] = jnp.concatenate(shifts, axis=0).astype(LOW)
        for deep in range(3):
            field = even if deep == 1 else odd
            start = 1 if deep == 2 else 0
            right = field[start : start + grid, 1 : vox + 1].reshape(grid * vox * 16, 4 * chans)
            sums = dot(columns_ref[...], right)
            for tall in range(3):
                for wide in range(3):
                    top = sums[tall * 64 : tall * 64 + 32, wide * chans : (wide + 1) * chans]
                    low = sums[tall * 64 + 32 : tall * 64 + 64, (wide + 1) * chans : (wide + 2) * chans]
                    tap = deep * 9 + tall * 3 + wide
                    wgrad_ref[which, tap * 32 : (tap + 1) * 32] = top + low

    norm_back(held_ref, conv_ref, scale_two, totals)
    weight_grad(act_even, act_odd, 1)
    copies[3].wait()
    convolve(grad_even, grad_odd, back_w.at[1], conv_ref, True)

    def slope_first(at, totals):
        grad = conv_ref[at] * slope_ref[at]
        conv_ref[at] = grad
        return totals[0] + fold(grad), totals[1] + fold(grad * normed_ref[at])

    totals = lax.fori_loop(0, grid, slope_first, (zero(), zero()))
    norm_back(conv_ref, normed_ref, scale_one, totals)
    weight_grad(first_even, first_odd, 0)
    copies[4].wait()
    convolve(grad_even, grad_odd, back_w.at[0], conv_ref, True)

    def rows_back(at, state):
        grad = (conv_ref[at] * live_at(at)).reshape(8, 2, 2, 8, 2 * chans)
        for a in range(2):
            for b in range(2):
                block = grad[:, b, a].reshape(64, 2 * chans).astype(LOW)
                column = (2 * a + b) * 256
                grad_tconv_ref[pl.ds(at * 64, 64), column : column + 256] = block
        return state

    lax.fori_loop(0, grid, rows_back, 0)
    for t in range(4):
        at = slice(t * 128, (t + 1) * 128)
        tiles = [cot_ref[t, block * 128 : (block + 1) * 128] for block in range(6)]
        cot_rows = jnp.concatenate(tiles, axis=1).astype(jnp.float32)
        grad_rows_ref[at] = cot_rows + dot_last(grad_tconv_ref[at], tconv_ref[...])
    grad_low_ref[...] = grad_rows_ref[...].astype(LOW)
    for block in range(2):
        own = pl.ds(pl.multiple_of(block * 256 + core * 128, 128), 128)
        grad_half_ref[block] = grad_rows_ref[own]
    for which in range(2):
        for block in range(7):
            lanes = slice((7 * which + block) * 128, (7 * which + block + 1) * 128)
            pack_ref[:, lanes] = wgrad_ref[which, block * 128 : (block + 1) * 128].T.astype(LOW)


def decoder(depth, core, own, near, tconv, select, spread, conv, back, cot):
    f32 = jnp.float32
    vmem = pl.BlockSpec(memory_space=pltpu.VMEM)
    hbm = pl.BlockSpec(memory_space=pl.ANY)
    window = lambda planes: pltpu.VMEM((planes, 18, 16, 512), LOW)
    field = lambda kind: pltpu.VMEM((8, 16, 16, 256), kind)
    return pl.pallas_call(
        decoder_kernel,
        out_shape=(
            jax.ShapeDtypeStruct((16, 16, 16, 32), f32),
            jax.ShapeDtypeStruct((512, 768), LOW),
            jax.ShapeDtypeStruct((512, 1024), LOW),
            jax.ShapeDtypeStruct((2, 128, 768), f32),
            jax.ShapeDtypeStruct((512, 768), LOW),
            jax.ShapeDtypeStruct((128, 2 * 896), LOW),
        ),
        in_specs=[pl.BlockSpec(memory_space=pltpu.SMEM)] * 2 + [vmem] * 5 + [hbm] * 3,
        out_specs=[vmem] * 6,
        scratch_shapes=[
            pltpu.VMEM((512, 768), f32),
            pltpu.VMEM((2, 896, 128), f32),
            pltpu.VMEM((512, 1024), f32),
            window(8),
            window(9),
            window(8),
            window(9),
            window(8),
            window(9),
            field(f32),
            field(f32),
            field(f32),
            field(f32),
            pltpu.VMEM((16, 8, 512), f32),
            pltpu.VMEM((8, 18, 16, 256), LOW),
            pltpu.VMEM((192, 2048), LOW),
            pltpu.VMEM((2, 9, 512, 256), LOW),
            pltpu.VMEM((2, 9, 256, 512), LOW),
            pltpu.VMEM((4, 1792, 128), LOW),
            pltpu.SemaphoreType.DMA((5,)),
        ],
        compiler_params=pltpu.CompilerParams(vmem_limit_bytes=60 * MIB),
        cost_estimate=pl.CostEstimate(
            flops=2 * 10**10, bytes_accessed=20 * MIB, transcendentals=10**6
        ),
    )(depth, core, own, near, tconv, select, spread, conv, back, cot)


def full_spec(count, space=pltpu.VMEM):
    return [pl.BlockSpec(memory_space=space)] * count


def assemble_kernel(starts, index_ref, *refs):
    pieces, full_ref = refs[:-1], refs[-1]
    for at, (piece, start) in enumerate(zip(pieces, starts)):
        full_ref[index_ref[at], start : start + piece.shape[0]] = piece[...]


def assemble(indices, starts, pieces, shape):
    if any(piece.shape[0] % 16 for piece in pieces):
        full = jnp.zeros(shape, pieces[0].dtype)
        for at, (start, piece) in enumerate(zip(starts, pieces)):
            full = lax.dynamic_update_slice(full, piece[None], (indices[at], start, 0))
        return full
    return pl.pallas_call(
        functools.partial(assemble_kernel, tuple(starts)),
        out_shape=jax.ShapeDtypeStruct(shape, pieces[0].dtype),
        in_specs=full_spec(1, pltpu.SMEM) + full_spec(len(pieces)),
        out_specs=pl.BlockSpec(memory_space=pltpu.VMEM),
        compiler_params=pltpu.CompilerParams(vmem_limit_bytes=40 * MIB),
        cost_estimate=pl.CostEstimate(flops=0, bytes_accessed=6 * MIB, transcendentals=0),
    )(indices, *pieces)


def taps_kernel(tconv_in, conv_in, place_ref, tconv_ref, conv_ref, back_ref):
    chans = 128
    rows = tconv_in.shape[1]
    for block in range(2):
        lanes = slice(block * chans, (block + 1) * chans)
        wide = jnp.concatenate([tconv_in[t, :, lanes] for t in range(4)], axis=1)
        tconv_ref[:, block * 512 : (block + 1) * 512] = dot(wide, place_ref[...]).astype(LOW)
    none = jnp.zeros((chans, chans), LOW)
    for which in range(2):
        for plane in range(9):
            conv_ref[which, plane, 3 * chans :, :chans] = none
            conv_ref[which, plane, :chans, chans:] = none
            back_ref[which, plane, :chans, 3 * chans :] = none
            back_ref[which, plane, chans:, :chans] = none
    for block in range(14):
        lanes = slice(block % 2 * chans, (block % 2 + 1) * chans)
        wide = jnp.concatenate([conv_in[t, block // 2, :, lanes] for t in range(4)], axis=1)
        made = dot(wide, place_ref[...]).astype(LOW)
        for second in range(2):
            tap = 2 * block + second
            if tap == 27:
                continue
            plane, deep = tap // 3, tap % 3
            turned = 2 - deep
            for which in range(2):
                at = (2 * second + which) * chans
                taps = made[:, at : at + chans]
                conv_ref[which, plane, deep * chans : (deep + 1) * chans, :chans] = taps
                conv_ref[which, plane, (deep + 1) * chans : (deep + 2) * chans, chans:] = taps
                back_ref[which, 8 - plane, :chans, turned * chans : (turned + 1) * chans] = taps
                back_ref[which, 8 - plane, chans:, (turned + 1) * chans : (turned + 2) * chans] = taps


def decoder_weights(tconv_in, conv_in, place):
    rows = tconv_in.shape[1]
    return pl.pallas_call(
        taps_kernel,
        out_shape=(
            jax.ShapeDtypeStruct((rows, 1024), LOW),
            jax.ShapeDtypeStruct((2, 9, 512, 256), LOW),
            jax.ShapeDtypeStruct((2, 9, 256, 512), LOW),
        ),
        in_specs=full_spec(3),
        out_specs=full_spec(3),
        compiler_params=pltpu.CompilerParams(vmem_limit_bytes=40 * MIB),
        cost_estimate=pl.CostEstimate(
            flops=10**9, bytes_accessed=20 * MIB, transcendentals=0
        ),
    )(tconv_in, conv_in, place)


def normalise(rows):
    middle = jnp.mean(rows, axis=-1, keepdims=True)
    centred = rows - middle
    spread = jnp.mean(centred * centred, axis=-1, keepdims=True)
    scale = lax.rsqrt(spread + 1e-06)
    return centred * scale, scale


def attention_kernel(
    depth_ref, me_ref, own_ref, near_ref, far_ref, last_ref, weight_ref, norm_ref,
    rows_ref, h_ref, qkv_ref, probs_ref, out_ref,
):
    patches = rows_ref.shape[0]
    quarter = patches // 4
    for flip, block in enumerate((own_ref, near_ref, far_ref, last_ref)):
        start = pl.multiple_of(jnp.bitwise_xor(me_ref[0], flip) * quarter, quarter)
        rows_ref[pl.ds(start, quarter)] = block[...]
    heads = probs_ref.shape[0]
    span = heads * HD
    turned = norm_ref[...]
    normed, _ = normalise(rows_ref[...].astype(jnp.float32))
    low_rows = (normed * turned[0:1] + turned[1:2]).astype(LOW)
    h_ref[...] = low_rows
    qkv_ref[...] = dot(low_rows, weight_ref[:, : 3 * span]).astype(LOW)
    key_at = lax.broadcasted_iota(jnp.int32, (1, patches), 1)
    live = key_at < depth_ref[0] * (GRID * GRID)
    outs = []
    for head in range(heads):
        query = qkv_ref[:, head * HD : (head + 1) * HD]
        keys = qkv_ref[:, span + head * HD : span + (head + 1) * HD]
        values = qkv_ref[:, 2 * span + head * HD : 2 * span + (head + 1) * HD]
        scores = jnp.where(live, dot_last(query, keys) * HD ** (-0.5), -1000000000.0)
        expo = jnp.exp(scores - jnp.max(scores, axis=-1, keepdims=True))
        probs = (expo * (1.0 / jnp.sum(expo, axis=-1, keepdims=True))).astype(LOW)
        probs_ref[head] = probs
        outs.append(dot(probs, values))
    out_ref[...] = jnp.concatenate(outs, axis=1).astype(LOW)


def attention(depth, me, blocks, weight, norms, heads):
    patches, width = 4 * blocks[0].shape[0], blocks[0].shape[1]
    return pl.pallas_call(
        attention_kernel,
        out_shape=(
            jax.ShapeDtypeStruct((patches, width), LOW),
            jax.ShapeDtypeStruct((patches, width), LOW),
            jax.ShapeDtypeStruct((patches, 3 * heads * HD), LOW),
            jax.ShapeDtypeStruct((heads, patches, patches), LOW),
            jax.ShapeDtypeStruct((patches, heads * HD), LOW),
        ),
        in_specs=full_spec(2, pltpu.SMEM) + full_spec(6),
        out_specs=full_spec(5),
        compiler_params=pltpu.CompilerParams(vmem_limit_bytes=40 * MIB),
        cost_estimate=pl.CostEstimate(flops=10**9, bytes_accessed=8 * MIB, transcendentals=10**6),
    )(depth, me, *blocks, weight, norms)


def mlp_kernel(
    core_ref, rows_ref, out0, out1, out2, out3, w0, w1, w2, w3, norm_ref, weight_ref,
    mid_ref, mid_half_ref, h_ref, hidden_ref, slope_ref, mine_ref, other_ref, partial_ref,
):
    width = rows_ref.shape[1]
    hidden_here = hidden_ref.shape[1]
    core = core_ref[0]
    norms = norm_ref[...]
    for block in range(2):
        at = slice(block * 256, (block + 1) * 256)
        mid = rows_ref[at].astype(jnp.float32)
        attended = jnp.concatenate([out[at] for out in (out0, out1, out2, out3)], axis=1)
        weights = jnp.concatenate([w[...] for w in (w0, w1, w2, w3)], axis=1)
        mid = mid + dot_last(attended, weights)
        mid_ref[at] = mid
        normed, _ = normalise(mid)
        low_rows = (normed * norms[2:3] + norms[3:4]).astype(LOW)
        h_ref[at] = low_rows
        value, slope = gelu_and_slope(dot(low_rows, weight_ref[:, :hidden_here]))
        hidden = value.astype(LOW)
        hidden_ref[at] = hidden
        slope_ref[at] = slope.astype(LOW)
        partial_ref[at] = dot_last(hidden, weight_ref[:, hidden_here : 2 * hidden_here])
        own = pl.ds(pl.multiple_of(block * 256 + core * 128, 128), 128)
        their = pl.ds(pl.multiple_of(block * 256 + (1 - core) * 128, 128), 128)
        mid_half_ref[block] = mid_ref[own]
        mine_ref[block] = partial_ref[own]
        other_ref[block] = partial_ref[their].astype(LOW)


def mlp(core, rows, outs, out_weights, norms, weight, hidden_here):
    patches, width = rows.shape
    f32 = jnp.float32
    half = (2, patches // 4, width)
    return pl.pallas_call(
        mlp_kernel,
        out_shape=(
            jax.ShapeDtypeStruct((patches, width), f32),
            jax.ShapeDtypeStruct(half, f32),
            jax.ShapeDtypeStruct((patches, width), LOW),
            jax.ShapeDtypeStruct((patches, hidden_here), LOW),
            jax.ShapeDtypeStruct((patches, hidden_here), LOW),
            jax.ShapeDtypeStruct(half, f32),
            jax.ShapeDtypeStruct(half, LOW),
        ),
        in_specs=full_spec(1, pltpu.SMEM) + full_spec(11),
        out_specs=full_spec(7),
        scratch_shapes=[pltpu.VMEM((patches, width), f32)],
        compiler_params=pltpu.CompilerParams(vmem_limit_bytes=40 * MIB),
        cost_estimate=pl.CostEstimate(
            flops=2 * 10**9, bytes_accessed=10 * MIB, transcendentals=10**6
        ),
    )(core, rows, *outs, *out_weights, norms, weight)


def mlp_back_kernel(
    core_ref, grad_ref, weight_ref, slope_ref, mid_ref, upper_ref, mine_ref, other_ref, sums_ref, partial_ref
):
    hidden_here = slope_ref.shape[1]
    core = core_ref[0]
    gain = shift = 0.0
    for block in range(2):
        at = slice(block * 256, (block + 1) * 256)
        grad = dot(grad_ref[at], weight_ref[:, hidden_here : 2 * hidden_here])
        upper = (grad * slope_ref[at].astype(jnp.float32)).astype(LOW)
        upper_ref[at] = upper
        grad_rows = dot_last(upper, weight_ref[:, :hidden_here])
        normed, _ = normalise(mid_ref[at])
        gain += jnp.sum(grad_rows * normed, axis=0, keepdims=True)
        shift += jnp.sum(grad_rows, axis=0, keepdims=True)
        partial_ref[at] = grad_rows
        own = pl.ds(pl.multiple_of(block * 256 + core * 128, 128), 128)
        their = pl.ds(pl.multiple_of(block * 256 + (1 - core) * 128, 128), 128)
        mine_ref[block] = partial_ref[own]
        other_ref[block] = partial_ref[their].astype(LOW)
    sums_ref[...] = jnp.concatenate([gain, shift], axis=0)


def mlp_back(core, grad, weight, slope, mid):
    patches, width = grad.shape
    f32 = jnp.float32
    half = (2, patches // 4, width)
    return pl.pallas_call(
        mlp_back_kernel,
        out_shape=(
            jax.ShapeDtypeStruct(slope.shape, LOW),
            jax.ShapeDtypeStruct(half, f32),
            jax.ShapeDtypeStruct(half, LOW),
            jax.ShapeDtypeStruct((2, width), f32),
        ),
        in_specs=full_spec(1, pltpu.SMEM) + full_spec(4),
        out_specs=full_spec(4),
        scratch_shapes=[pltpu.VMEM((patches, width), f32)],
        compiler_params=pltpu.CompilerParams(vmem_limit_bytes=40 * MIB),
        cost_estimate=pl.CostEstimate(flops=2 * 10**9, bytes_accessed=8 * MIB, transcendentals=0),
    )(core, grad, weight, slope, mid)


def mlp_weights_kernel(
    h_ref, upper_ref, grad_ref, hidden_ref, rows_ref, grad_tconv_ref, select_ref, pack_ref
):
    hidden_here = upper_ref.shape[1]
    pack_ref[:, :hidden_here] = contract_first(h_ref[...], upper_ref[...]).astype(LOW)
    pack_ref[:, hidden_here : 2 * hidden_here] = contract_first(
        grad_ref[...], hidden_ref[...]
    ).astype(LOW)
    own = select_ref[...].reshape(64, 256)
    blocks = [dot_last(grad_tconv_ref[:, at * 256 : (at + 1) * 256], own) for at in range(4)]
    mine = jnp.concatenate(blocks, axis=1).astype(LOW)
    pack_ref[:, 2 * hidden_here :] = contract_first(rows_ref[...], mine).astype(LOW)


def mlp_weights(h_rows, upper, grad, hidden, rows, grad_tconv, select):
    width = h_rows.shape[1]
    return pl.pallas_call(
        mlp_weights_kernel,
        out_shape=jax.ShapeDtypeStruct((width, 2 * upper.shape[1] + 256), LOW),
        in_specs=full_spec(7),
        out_specs=pl.BlockSpec(memory_space=pltpu.VMEM),
        compiler_params=pltpu.CompilerParams(vmem_limit_bytes=40 * MIB),
        cost_estimate=pl.CostEstimate(flops=3 * 10**9, bytes_accessed=8 * MIB, transcendentals=0),
    )(h_rows, upper, grad, hidden, rows, grad_tconv, select)


def norm_back_kernel(sum_ref, far_ref, grad_ref, rows_ref, norm_ref, out_ref, low_ref):
    gain = norm_ref[2:3]
    for block in range(2):
        summed = sum_ref[block].astype(jnp.float32) + far_ref[block].astype(jnp.float32)
        normed, scale = normalise(rows_ref[block])
        grad = grad_ref[block] + layer_norm_back(summed * gain, normed, scale)
        out_ref[block] = grad
        low_ref[block] = grad.astype(LOW)


def norm_back(summed, far, grad, rows, norms):
    return pl.pallas_call(
        norm_back_kernel,
        out_shape=(
            jax.ShapeDtypeStruct(grad.shape, jnp.float32),
            jax.ShapeDtypeStruct(grad.shape, LOW),
        ),
        in_specs=full_spec(5),
        out_specs=full_spec(2),
        cost_estimate=pl.CostEstimate(flops=10**7, bytes_accessed=4 * MIB, transcendentals=0),
    )(summed, far, grad, rows, norms)


def attention_back_kernel(
    core_ref, own_ref, near_ref, weight_ref, qkv_ref, probs_ref, h_ref, out_ref, rows_ref, sums_ref,
    pack_ref, mine_ref, other_ref, grad_ref, partial_ref,
):
    heads = probs_ref.shape[0]
    span = heads * HD
    core = core_ref[0]
    for block in range(2):
        grad_ref[pl.ds(pl.multiple_of(block * 256 + core * 128, 128), 128)] = own_ref[block]
        grad_ref[pl.ds(pl.multiple_of(block * 256 + (1 - core) * 128, 128), 128)] = near_ref[block]
    grad_branch = grad_ref[...]
    grad_out = dot(grad_branch, weight_ref[:, 3 * span : 4 * span]).astype(LOW)
    grad_query, grad_keys, grad_values = [], [], []
    for head in range(heads):
        query = qkv_ref[:, head * HD : (head + 1) * HD]
        keys = qkv_ref[:, span + head * HD : span + (head + 1) * HD]
        values = qkv_ref[:, 2 * span + head * HD : 2 * span + (head + 1) * HD]
        grad_head = grad_out[:, head * HD : (head + 1) * HD]
        probs = probs_ref[head]
        grad_values.append(contract_first(probs, grad_head))
        probs = probs.astype(jnp.float32)
        grad_probs = dot_last(grad_head, values)
        inner = jnp.sum(probs * grad_probs, axis=-1, keepdims=True)
        grad_scores = (probs * (grad_probs - inner)).astype(LOW)
        grad_query.append(dot(grad_scores, keys) * HD ** (-0.5))
        grad_keys.append(contract_first(grad_scores, query) * HD ** (-0.5))
    grad_qkv = jnp.concatenate(grad_query + grad_keys + grad_values, axis=1).astype(LOW)
    pack_ref[:, : 3 * span] = contract_first(h_ref[...], grad_qkv).astype(LOW)
    pack_ref[:, 3 * span : 4 * span] = contract_first(grad_branch, out_ref[...]).astype(LOW)
    partial_ref[...] = dot_last(grad_qkv, weight_ref[:, : 3 * span])
    gain = shift = 0.0
    for block in range(2):
        at = slice(block * 256, (block + 1) * 256)
        normed, _ = normalise(rows_ref[at].astype(jnp.float32))
        gain += jnp.sum(partial_ref[at] * normed, axis=0, keepdims=True)
        shift += jnp.sum(partial_ref[at], axis=0, keepdims=True)
        own = pl.ds(pl.multiple_of(block * 256 + core * 128, 128), 128)
        their = pl.ds(pl.multiple_of(block * 256 + (1 - core) * 128, 128), 128)
        mine_ref[block] = partial_ref[own]
        other_ref[block] = partial_ref[their].astype(LOW)
    none = jnp.zeros((124, gain.shape[1]), jnp.float32)
    stacked = jnp.concatenate([gain, shift, sums_ref[...], none], axis=0)
    pack_ref[:, 4 * span :] = stacked.T.astype(LOW)


def attention_back(core, own, near, weight, qkv, probs, h_rows, out, rows, sums):
    patches, width = rows.shape
    f32 = jnp.float32
    half = (2, patches // 4, width)
    return pl.pallas_call(
        attention_back_kernel,
        out_shape=(
            jax.ShapeDtypeStruct(weight.shape, LOW),
            jax.ShapeDtypeStruct(half, f32),
            jax.ShapeDtypeStruct(half, LOW),
        ),
        in_specs=full_spec(1, pltpu.SMEM) + full_spec(9),
        out_specs=full_spec(3),
        scratch_shapes=[pltpu.VMEM((patches, width), LOW), pltpu.VMEM((patches, width), f32)],
        compiler_params=pltpu.CompilerParams(vmem_limit_bytes=40 * MIB),
        cost_estimate=pl.CostEstimate(flops=3 * 10**9, bytes_accessed=9 * MIB, transcendentals=0),
    )(core, own, near, weight, qkv, probs, h_rows, out, rows, sums)


class Ring:
    def __init__(self, size):
        self.size = size
        self.order = ring_order(size)
        self.ahead = [(self.order[i], self.order[(i + 1) % size]) for i in range(size)]
        self.behind = [(b, a) for a, b in self.ahead]
        self.place = [self.order.index(me) for me in range(size)]

    def indices(self, distances):
        table = np.array(
            [
                [self.order[(self.place[me] + distance) % self.size] for distance in distances]
                for me in range(self.size)
            ],
            np.int32,
        )
        return jnp.asarray(table)[lax.axis_index("dp")]

    def index_at(self, distance):
        return self.indices([distance])[0]

    def send(self, value, forward):
        return lax.ppermute(value, "dp", self.ahead if forward else self.behind)

    def gather(self, block):
        size = self.size
        rows = block.shape[0]
        pieces = [(0, 0, block)]
        one = two = block
        for step in range(1, (size - 1) // 2 + 1):
            one = self.send(one, True)
            two = self.send(two, False)
            pieces.append((-step, 0, one))
            pieces.append((step, 0, two))
        if size % 2 == 0:
            half = rows // 2
            pieces.append((-(size // 2), 0, self.send(one[:half], True)))
            pieces.append((size // 2, half, self.send(two[half:], False)))
        return assemble(
            self.indices([distance for distance, _, _ in pieces]),
            [start for _, start, _ in pieces],
            [piece for _, _, piece in pieces],
            (size,) + block.shape,
        )

    def scatter(self, *arrays):
        size = self.size
        rows = sum(array.shape[0] for array in arrays) // size

        def term(distance):
            index = self.index_at(distance)
            blocks = [
                lax.dynamic_slice_in_dim(array, index * (array.shape[0] // size), array.shape[0] // size)
                for array in arrays
            ]
            return blocks[0] if len(blocks) == 1 else jnp.concatenate(blocks)

        own = term(0).astype(jnp.float32)
        one = two = None
        reach = (size - 1) // 2
        if size % 2 == 0:
            half = rows // 2
            far = term(size // 2)
            one = self.send(far[:half], True)
            two = self.send(far[half:], False)
            above, below = term(reach), term(-reach)
            if reach == 0:
                return own + jnp.concatenate([one, two]).astype(jnp.float32)
            one = jnp.concatenate([above[:half] + one, above[half:]])
            two = jnp.concatenate([below[:half], below[half:] + two])
        else:
            if reach == 0:
                return own
            one, two = term(reach), term(-reach)
        for step in range(reach, 0, -1):
            one = self.send(one, True)
            two = self.send(two, False)
            if step > 1:
                one = one + term(step - 1)
                two = two + term(-(step - 1))
        return own + one.astype(jnp.float32) + two.astype(jnp.float32)


class Quad:
    def __init__(self):
        me = lax.axis_index("tensor")
        self.core = me % 2
        self.chip = me // 2

    def over_core(self, value):
        return lax.ppermute(value, "tensor", [(i, i ^ 1) for i in range(4)])

    def over_chip(self, value):
        return lax.ppermute(value, "tensor", [(i, i ^ 2) for i in range(4)])

    def spread(self, block):
        far = self.over_chip(block)
        return block, self.over_core(block), far, self.over_core(far)

    def reduce_half(self, mine, other):
        summed = (mine + self.over_core(other).astype(jnp.float32)).astype(LOW)
        return summed.astype(jnp.float32) + self.over_chip(summed).astype(jnp.float32)

    def pick(self, half):
        return jnp.where(self.chip == 0, half[0], half[1])


def selections(chans, chans_here):
    me = lax.axis_index("tensor")
    pair = jnp.arange(2)
    here = jnp.arange(chans_here)
    every = jnp.arange(chans)
    own = (pair[:, None, None, None] == pair[None, None, :, None]) & (
        (here + me * chans_here)[None, :, None, None] == every[None, None, None, :]
    )
    own = own.reshape(2, chans_here, 2 * chans).astype(LOW)
    four = jnp.arange(4)
    given_a = pair[:, None, None, None, None, None, None] == pair[None, None, :, None, None, None, None]
    given_e = pair[None, None, None, :, None, None, None] == pair[None, None, None, None, None, :, None]
    given_c = (four[:, None] * chans_here + here[None, :])[None, :, None, None, :, None, None] == every
    spread = (given_a & given_e & given_c).reshape(2, 16 * chans_here, 2 * chans).astype(LOW)
    same_g = four[None, :, None, None, None, None] == four[None, None, None, :, None, None]
    same_t = four[:, None, None, None, None, None] == four[None, None, None, None, :, None]
    same_c = here[None, None, :, None, None, None] == here
    place = (same_g & same_t & same_c).reshape(16 * chans_here, 16 * chans_here).astype(LOW)
    return own, spread, place


def shards(
    tokens,
    crop_depth,
    w_query,
    w_key,
    w_value,
    w_out,
    w_up,
    w_down,
    w_tconv,
    w_conv1,
    w_conv2,
    ln1_gain,
    ln1_bias,
    ln2_gain,
    ln2_bias,
    cot_out,
    cot_dec,
    groups,
):
    ring = Ring(groups)
    quad = Quad()
    grid = GRID
    vox = 2 * grid
    patches = grid**3
    width = w_query.shape[0] * groups
    part = w_query.shape[0]
    heads_here = w_query.shape[1] // HD
    span = heads_here * HD
    chans = w_conv1.shape[0] * groups
    chans_here = w_conv1.shape[2]

    low = lambda value: value.astype(LOW)
    hidden_here = w_up.shape[1]
    norm_columns = jnp.stack([ln1_gain, ln1_bias, ln2_gain, ln2_bias], axis=1)
    norm_columns = low(jnp.pad(norm_columns, ((0, 0), (0, 124))))
    pack_a = jnp.concatenate(
        [low(w_query), low(w_key), low(w_value), low(w_out).T, norm_columns], axis=1
    )
    pack_b = jnp.concatenate([low(w_up), low(w_down).T], axis=1)
    tconv_mine = low(w_tconv).reshape(part, chans_here, 8).transpose(0, 2, 1).reshape(part, -1)
    conv_mine = jnp.stack([low(w_conv1), low(w_conv2)], axis=2).reshape(w_conv1.shape[0], -1)
    conv_mine = jnp.pad(conv_mine, ((0, 0), (0, 64))).reshape(-1, 7, 256).transpose(1, 0, 2)
    pack_c = jnp.concatenate([tconv_mine, conv_mine.reshape(-1, 256)])
    cot_mine = low(cot_dec).reshape(grid, 2, vox, grid, 2, chans_here).transpose(0, 2, 3, 1, 4, 5)
    cot_mine = cot_mine.reshape(grid * vox * grid, 4 * chans_here)
    cot_tiles = low(cot_out).reshape(patches // 4, width // 128, 128).transpose(1, 0, 2)
    cot_pack = jnp.concatenate([cot_tiles.reshape(-1, 128), cot_mine])

    full_c = lax.all_gather(pack_c, ("dp", "tensor")).reshape(groups, 4, -1, 256)
    cot_full = lax.all_gather(cot_pack, "tensor")
    full_a = ring.gather(pack_a).reshape(width, -1)
    full_b = ring.gather(pack_b).reshape(width, -1)
    token_blocks = quad.spread(tokens)

    norms = full_a[:, 4 * span : 4 * span + 8].astype(jnp.float32).T
    out_weight = full_a[:, 3 * span : 4 * span]
    select, spread, place = selections(chans, chans_here)
    tconv_parts = full_c[:, :, :part].transpose(1, 0, 2, 3).reshape(4, width, 256)
    conv_parts = full_c[:, :, part:].reshape(groups, 4, 7, -1, 256).transpose(1, 2, 0, 3, 4)
    tconv_full, conv_taps, back_taps = decoder_weights(
        tconv_parts, conv_parts.reshape(4, 7, chans, 256), place
    )
    core = quad.core[None]
    rows_low, h_one, qkv, probs, attended = attention(
        crop_depth, lax.axis_index("tensor")[None], token_blocks, full_a, norms, heads_here
    )
    mid, mid_half, h_two, hidden, slope, mine, other = mlp(
        core,
        rows_low,
        quad.spread(attended),
        quad.spread(out_weight),
        norms,
        full_b,
        hidden_here,
    )
    after_half = mid_half + quad.reduce_half(mine, other)
    after = quad.pick(after_half)
    low_half = low(after_half)
    dec_out, dec_in, grad_tconv, grad_half, grad_mlp, conv_pack = decoder(
        crop_depth,
        core,
        low_half,
        quad.over_core(low_half),
        tconv_full,
        select,
        spread,
        conv_taps,
        back_taps,
        cot_full,
    )

    grad_upper, mine, other, sums_two = mlp_back(core, grad_mlp, full_b, slope, mid)
    summed = low(mine + quad.over_core(other).astype(jnp.float32))
    far = quad.over_chip(summed)
    mlp_pack = mlp_weights(h_two, grad_upper, grad_mlp, hidden, dec_in, grad_tconv, select)
    mlp_grads = ring.scatter(mlp_pack, conv_pack)
    grad_mid_half, low_mid_half = norm_back(summed, far, grad_half, mid_half, norms)
    attention_pack, mine, other = attention_back(
        core,
        low_mid_half,
        quad.over_core(low_mid_half),
        full_a,
        qkv,
        probs,
        h_one,
        attended,
        rows_low,
        sums_two,
    )
    attention_grads = ring.scatter(attention_pack)
    norm_grads = lax.psum(attention_grads[:, 4 * span : 4 * span + 4], "tensor")
    summed = mine + quad.over_core(other).astype(jnp.float32)
    norm_own = quad.pick(summed) + quad.over_chip(low(quad.pick(summed[::-1]))).astype(jnp.float32)
    normed_own, scale_own = normalise(tokens.astype(jnp.float32))
    grad_tokens = quad.pick(grad_mid_half) + layer_norm_back(
        norm_own * norms[0:1], normed_own, scale_own
    )
    conv_grads = mlp_grads[part:].reshape(-1, 2, 896)[:, :, : 27 * chans_here]
    conv_grads = conv_grads.reshape(-1, 2, 27, chans_here)
    tconv_grad = mlp_grads[:part, 2 * hidden_here :].reshape(part, 8, chans_here)
    return (
        after,
        dec_out[None],
        grad_tokens,
        attention_grads[:, :span],
        attention_grads[:, span : 2 * span],
        attention_grads[:, 2 * span : 3 * span],
        attention_grads[:, 3 * span : 4 * span].T,
        mlp_grads[:part, :hidden_here],
        mlp_grads[:part, hidden_here : 2 * hidden_here].T,
        tconv_grad.transpose(0, 2, 1).reshape(part, -1),
        conv_grads[:, 0],
        conv_grads[:, 1],
        norm_grads[:, 0],
        norm_grads[:, 1],
        norm_grads[:, 2],
        norm_grads[:, 3],
    )


def solution(mesh):
    in_specs = (
        P(("dp", "tensor"), None),
        P("dp"),
        P("dp", "tensor"),
        P("dp", "tensor"),
        P("dp", "tensor"),
        P("tensor", "dp"),
        P("dp", "tensor"),
        P("tensor", "dp"),
        P("dp", "tensor"),
        P("dp", None, "tensor"),
        P("dp", None, "tensor"),
        P("dp"),
        P("dp"),
        P("dp"),
        P("dp"),
        P(("dp", "tensor"), None),
        P("dp", None, None, None, "tensor"),
    )
    out_specs = (
        P(("dp", "tensor"), None),
        P("dp", None, None, None, "tensor"),
        P(("dp", "tensor"), None),
        P("dp", "tensor"),
        P("dp", "tensor"),
        P("dp", "tensor"),
        P("tensor", "dp"),
        P("dp", "tensor"),
        P("tensor", "dp"),
        P("dp", "tensor"),
        P("dp", None, "tensor"),
        P("dp", None, "tensor"),
        P("dp"),
        P("dp"),
        P("dp"),
        P("dp"),
    )
    groups = mesh.shape["dp"]

    def run(*arrays):
        return shards(*arrays, groups)

    return jax.shard_map(run, mesh=mesh, in_specs=in_specs, out_specs=out_specs, check_vma=False)
```

```python
import functools

import jax
import jax.numpy as jnp
import numpy as np
from jax import lax
from jax.experimental import pallas as pl
from jax.experimental.pallas import tpu as pltpu
from jax.sharding import PartitionSpec as P

HD = 64
GRID = 8
LOW = jnp.bfloat16


def ring_order(size):
    if size % 2:
        return list(range(size))
    return list(range(0, size, 2)) + list(range(size - 1, 0, -2))


def layer_norm_back(grad_normed, normed, scale):
    mean_grad = jnp.mean(grad_normed, axis=-1, keepdims=True)
    mean_dot = jnp.mean(grad_normed * normed, axis=-1, keepdims=True)
    return scale * (grad_normed - mean_grad - normed * mean_dot)


def contract_first(left, right):
    return lax.dot_general(
        left, right, (((0,), (0,)), ((), ())), preferred_element_type=jnp.float32
    )


MIB = 2**20
VMEM_LIMIT = 60 * MIB
SMALL = pl.CostEstimate(flops=10**6, bytes_accessed=2**16, transcendentals=0)


def gelu_and_slope(x):
    bell = jnp.exp(-0.5 * x * x)
    frac = 1.0 / (1.0 + 0.3275911 * 0.7071067811865476 * jnp.abs(x))
    poly = frac * (
        0.254829592
        + frac * (-0.284496736 + frac * (1.421413741 + frac * (-1.453152027 + frac * 1.061405429)))
    )
    tail = 0.5 * poly * bell
    phi = jnp.where(x >= 0.0, 1.0 - tail, tail)
    return x * phi, phi + x * bell * 0.3989422804014327


def dot(left, right):
    return jnp.dot(left, right, preferred_element_type=jnp.float32)


def dot_last(left, right):
    return lax.dot_general(
        left, right, (((1,), (1,)), ((), ())), preferred_element_type=jnp.float32
    )


BATCH = 4


def decoder_kernel(
    blocks,
    index_ref,
    order_ref,
    depth_ref,
    me_ref,
    own_ref,
    near_ref,
    tconv_hbm,
    select_ref,
    spread_ref,
    conv_hbm,
    back_hbm,
    cot0_hbm,
    cot1_hbm,
    cot2_hbm,
    cot3_hbm,
    slope_hbm,
    mid_hbm,
    h_hbm,
    hidden_hbm,
    *refs,
):
    decoder_steps(
        blocks,
        refs[: len(blocks.pieces)],
        index_ref,
        order_ref,
        depth_ref,
        me_ref,
        own_ref,
        near_ref,
        tconv_hbm,
        select_ref,
        spread_ref,
        conv_hbm,
        back_hbm,
        (cot0_hbm, cot1_hbm, cot2_hbm, cot3_hbm),
        slope_hbm,
        mid_hbm,
        h_hbm,
        hidden_hbm,
        *refs[len(blocks.pieces) :],
    )


def decoder_steps(
    blocks,
    pieces,
    index_ref,
    order_ref,
    depth_ref,
    me_ref,
    own_ref,
    near_ref,
    tconv_hbm,
    select_ref,
    spread_ref,
    conv_hbm,
    back_hbm,
    cots_hbm,
    slope_hbm,
    mid_hbm,
    h_hbm,
    hidden_hbm,
    dec_hbm,
    grad_half_hbm,
    terms_hbm,
    mine_ref,
    other_ref,
    sums_ref,
    grad_low_ref,
    dec_ref,
    rows_ref,
    grad_tconv_ref,
    pack_ref,
    terms_ref,
    upper_ref,
    grad_rows_ref,
    wgrad_ref,
    first_even,
    first_odd,
    act_even,
    act_odd,
    grad_even,
    grad_odd,
    conv_ref,
    normed_ref,
    slope_ref,
    held_ref,
    carry_ref,
    low_grad_ref,
    columns_ref,
    tconv_ref,
    conv_w,
    back_w,
    cot_ref,
    up_ref,
    down_ref,
    gate_ref,
    mid_ref,
    h_ref,
    hidden_ref,
    sems,
    load_sems,
    out_sems,
):
    grid = 8
    vox = 16
    chans = 128
    depth = depth_ref[0]
    count = (depth * (2 * vox * vox)).astype(jnp.float32)

    loads = fetch(
        [
            (tconv_hbm, tconv_ref),
            (conv_hbm.at[0], conv_w.at[0]),
            (conv_hbm.at[1], conv_w.at[1]),
            (cots_hbm[0], cot_ref.at[me_ref[0]]),
            (cots_hbm[1], cot_ref.at[jnp.bitwise_xor(me_ref[0], 1)]),
            (cots_hbm[2], cot_ref.at[jnp.bitwise_xor(me_ref[0], 2)]),
            (cots_hbm[3], cot_ref.at[jnp.bitwise_xor(me_ref[0], 3)]),
            (back_hbm.at[1], back_w.at[1]),
            (back_hbm.at[0], back_w.at[0]),
            (slope_hbm, gate_ref),
            (mid_hbm, mid_ref),
            (h_hbm, h_ref),
            (hidden_hbm, hidden_ref),
        ],
        sems.at[pl.ds(3, 13)],
    )
    hidden = up_ref.shape[1]
    loads += blocks.load(index_ref, pieces, hidden, down_ref, load_sems)
    loads += blocks.load(index_ref, pieces, 0, up_ref, load_sems.at[pl.ds(len(pieces), len(pieces))])
    dec_copy = pltpu.make_async_copy(dec_ref, dec_hbm, sems.at[0])

    for even in (first_even, act_even, grad_even):
        even[:, 0] = jnp.zeros((grid, vox, 4 * chans), LOW)
        even[:, vox + 1] = jnp.zeros((grid, vox, 4 * chans), LOW)
    for odd in (first_odd, act_odd, grad_odd):
        odd[:, 0] = jnp.zeros((grid + 1, vox, 4 * chans), LOW)
        odd[:, vox + 1] = jnp.zeros((grid + 1, vox, 4 * chans), LOW)
    wgrad_ref[:, 864:] = jnp.zeros((2, 32, chans), jnp.float32)
    low_grad_ref[:, 0] = jnp.zeros((grid, vox, 2 * chans), LOW)
    low_grad_ref[:, vox + 1] = jnp.zeros((grid, vox, 2 * chans), LOW)

    spot = lax.broadcasted_iota(jnp.int32, (1, 1, 8, 1), 2)

    def put_field(even, odd, at, value):
        left = value[..., :chans]
        right = value[..., chans:]
        flat = (2 * vox, 8, chans)
        before = pltpu.roll(right.reshape(flat), 1, 1).reshape(right.shape)
        after = pltpu.roll(left.reshape(flat), 7, 1).reshape(left.shape)
        before = jnp.where(spot == 0, 0.0, before)
        after = jnp.where(spot == 7, 0.0, after)
        window = jnp.concatenate([before, value, after], axis=3)
        even[at, 1 : vox + 1] = window.reshape(vox, 16, 4 * chans).astype(LOW)
        early = jnp.concatenate([carry_ref[...][:, None], window[:, :1]], axis=1)
        odd[at, 1 : vox + 1] = early.reshape(vox, 16, 4 * chans).astype(LOW)
        carry_ref[...] = window[:, 1]

    def open_field():
        carry_ref[...] = jnp.zeros(carry_ref.shape, jnp.float32)

    def close_field(odd):
        late = jnp.concatenate([carry_ref[...], jnp.zeros(carry_ref.shape, jnp.float32)], axis=1)
        odd[grid, 1 : vox + 1] = late.astype(LOW)

    def live_at(at):
        return (at < depth).astype(jnp.float32)

    def convolve(even, odd, weights, target, turned):
        def step(block, total):
            at = block * BATCH
            summed = None
            for deep in range(3):
                field = even if deep == 1 else odd
                start = at + 1 if deep == 2 else at
                for tall in range(3):
                    left = field[pl.ds(start, BATCH), tall : tall + vox]
                    left = left.reshape(BATCH * vox * 16, 4 * chans)
                    right = weights[deep * 3 + tall]
                    term = dot_last(left, right) if turned else dot(left, right)
                    summed = term if summed is None else summed + term
            target[pl.ds(at, BATCH)] = summed.reshape(BATCH, vox, 16, 2 * chans)
            return total

        lax.fori_loop(0, grid // BATCH, step, 0)

    def both(total):
        row = jnp.sum(total, axis=0, keepdims=True)
        half = (row[:, :chans] + row[:, chans:]) / count
        return jnp.concatenate([half, half], axis=1)

    def zero():
        return jnp.zeros((8, 2 * chans), jnp.float32)

    def fold(value):
        return jnp.sum(value.reshape(2 * vox, 8, 2 * chans), axis=0)

    def statistics(source):
        def first(at, total):
            return total + live_at(at) * fold(source[at])

        middle = both(lax.fori_loop(0, grid, first, zero()))

        def second(at, total):
            away = source[at] - middle
            return total + live_at(at) * fold(away * away)

        spread = both(lax.fori_loop(0, grid, second, zero()))
        return middle, lax.rsqrt(spread + 1e-05)

    core = lax.rem(me_ref[0], 2)
    for block in range(2):
        rows_ref[pl.ds(pl.multiple_of(block * 256 + core * 128, 128), 128)] = own_ref[block]
        rows_ref[pl.ds(pl.multiple_of(block * 256 + (1 - core) * 128, 128), 128)] = near_ref[block]
    loads[0].wait()
    for part in range(4):
        wide = dot(rows_ref[...], tconv_ref[:, part * 256 : (part + 1) * 256])
        held_ref[:, part * 4 : (part + 1) * 4] = wide.reshape(grid, 4, 16, 2 * chans)
    open_field()

    def place_first(at, state):
        tokens = held_ref[at] * live_at(at)
        offsets = [
            [tokens[8 * a + 4 * b : 8 * a + 4 * b + 4].reshape(8, 1, 1, 8, 256) for a in range(2)]
            for b in range(2)
        ]
        value = jnp.concatenate(
            [jnp.concatenate(offsets[b], axis=2) for b in range(2)], axis=1
        ).reshape(vox, 2, 8, 256)
        put_field(first_even, first_odd, at, value)
        return state

    lax.fori_loop(0, grid, place_first, 0)
    close_field(first_odd)

    loads[1].wait()
    convolve(first_even, first_odd, conv_w.at[0], normed_ref, False)
    middle, scale_one = statistics(normed_ref)
    open_field()

    def act_first(at, state):
        normed = (normed_ref[at] - middle) * scale_one
        normed_ref[at] = normed
        value, slope = gelu_and_slope(normed)
        live = live_at(at)
        slope_ref[at] = slope * live
        put_field(act_even, act_odd, at, (value * live).reshape(vox, 2, 8, 2 * chans))
        return state

    lax.fori_loop(0, grid, act_first, 0)
    close_field(act_odd)

    loads[2].wait()
    convolve(act_even, act_odd, conv_w.at[1], conv_ref, False)
    middle, scale_two = statistics(conv_ref)
    for load in loads[3:7]:
        load.wait()

    def act_second(at, totals):
        normed = (conv_ref[at] - middle) * scale_two
        conv_ref[at] = normed
        value, slope = gelu_and_slope(normed)
        live = live_at(at)
        low_value = (value * live).astype(LOW).reshape(vox * 16, 2 * chans)
        for e in range(2):
            shown = dot_last(low_value, select_ref[me_ref[0], e]).reshape(vox, 2, 8, 32)
            for a in range(2):
                dec_ref[2 * at + a, :, pl.ds(e, 8, stride=2), :] = shown[:, a]
        parts = [cot_ref[t, pl.ds(768 + at * vox * 8, vox * 8)] for t in range(4)]
        packed = jnp.concatenate(parts, axis=1)
        cot = jnp.concatenate(
            [dot(packed, spread_ref[a]).reshape(vox, 1, 8, 2 * chans) for a in range(2)], axis=1
        ).reshape(vox, 16, 2 * chans)
        grad = cot * slope * live
        held_ref[at] = grad
        return totals[0] + fold(grad), totals[1] + fold(grad * normed)

    totals = lax.fori_loop(0, grid, act_second, (zero(), zero()))
    dec_copy.start()

    def norm_back(source, normed_source, scale, sums):
        mean_grad = both(sums[0])
        mean_dot = both(sums[1])
        open_field()

        def step(at, state):
            grad = source[at] - live_at(at) * (mean_grad + normed_source[at] * mean_dot)
            grad = scale * grad
            low_grad_ref[at, 1 : vox + 1] = grad.astype(LOW)
            put_field(grad_even, grad_odd, at, grad.reshape(vox, 2, 8, 2 * chans))
            return state

        lax.fori_loop(0, grid, step, 0)
        close_field(grad_odd)

    def weight_grad(even, odd, which):
        own = select_ref[me_ref[0]].reshape(64, 2 * chans)
        for at in range(grid):
            shifts = [
                dot_last(own, low_grad_ref[at, 2 - tall : 18 - tall].reshape(vox * 16, 2 * chans))
                for tall in range(3)
            ]
            columns_ref[:, at * 256 : (at + 1) * 256] = jnp.concatenate(shifts, axis=0).astype(LOW)
        for deep in range(3):
            field = even if deep == 1 else odd
            start = 1 if deep == 2 else 0
            right = field[start : start + grid, 1 : vox + 1].reshape(grid * vox * 16, 4 * chans)
            sums = dot(columns_ref[...], right)
            for tall in range(3):
                for wide in range(3):
                    top = sums[tall * 64 : tall * 64 + 32, wide * chans : (wide + 1) * chans]
                    low = sums[tall * 64 + 32 : tall * 64 + 64, (wide + 1) * chans : (wide + 2) * chans]
                    tap = deep * 9 + tall * 3 + wide
                    wgrad_ref[which, tap * 32 : (tap + 1) * 32] = top + low

    norm_back(held_ref, conv_ref, scale_two, totals)
    weight_grad(act_even, act_odd, 1)
    loads[7].wait()
    convolve(grad_even, grad_odd, back_w.at[1], conv_ref, True)

    def slope_first(at, totals):
        grad = conv_ref[at] * slope_ref[at]
        conv_ref[at] = grad
        return totals[0] + fold(grad), totals[1] + fold(grad * normed_ref[at])

    totals = lax.fori_loop(0, grid, slope_first, (zero(), zero()))
    norm_back(conv_ref, normed_ref, scale_one, totals)
    weight_grad(first_even, first_odd, 0)
    loads[8].wait()
    convolve(grad_even, grad_odd, back_w.at[0], conv_ref, True)

    def rows_back(at, state):
        grad = (conv_ref[at] * live_at(at)).reshape(8, 2, 2, 8, 2 * chans)
        for a in range(2):
            for b in range(2):
                block = grad[:, b, a].reshape(64, 2 * chans).astype(LOW)
                column = (2 * a + b) * 256
                grad_tconv_ref[pl.ds(at * 64, 64), column : column + 256] = block
        return state

    lax.fori_loop(0, grid, rows_back, 0)
    for which in range(2):
        for block in range(7):
            at = (7 * which + block) * 128
            pack_ref[:, at : at + 128] = wgrad_ref[which, block * 128 : (block + 1) * 128].T.astype(LOW)
    own = select_ref[me_ref[0]].reshape(64, 2 * chans)
    spans = [dot_last(grad_tconv_ref[:, at * 256 : (at + 1) * 256], own) for at in range(4)]
    mine = jnp.concatenate(spans, axis=1).astype(LOW)
    terms_ref[:, 2 * hidden :] = contract_first(rows_ref[...], mine).astype(LOW)
    for t in range(4):
        at = slice(t * 128, (t + 1) * 128)
        tiles = [cot_ref[t, block * 128 : (block + 1) * 128] for block in range(6)]
        cot_rows = jnp.concatenate(tiles, axis=1).astype(jnp.float32)
        grad_rows_ref[at] = cot_rows + dot_last(grad_tconv_ref[at], tconv_ref[...])
    grad_low_ref[...] = grad_rows_ref[...].astype(LOW)
    halves = []
    for block in range(2):
        own = pl.ds(pl.multiple_of(block * 256 + core * 128, 128), 128)
        halves.append((grad_rows_ref.at[own], grad_half_hbm.at[block]))
    half_copies = fetch(halves, sems.at[pl.ds(1, 2)])
    for load in loads[9:]:
        load.wait()
    for copy in half_copies:
        copy.wait()
    gain = shift = 0.0
    for block in range(2):
        at = slice(block * 256, (block + 1) * 256)
        grad = dot(grad_low_ref[at], down_ref[...])
        upper = (grad * gate_ref[at].astype(jnp.float32)).astype(LOW)
        upper_ref[at] = upper
        grad_normed = dot_last(upper, up_ref[...])
        normed, _ = normalise(mid_ref[at])
        gain += jnp.sum(grad_normed * normed, axis=0, keepdims=True)
        shift += jnp.sum(grad_normed, axis=0, keepdims=True)
        grad_rows_ref[at] = grad_normed
        own = pl.ds(pl.multiple_of(block * 256 + core * 128, 128), 128)
        their = pl.ds(pl.multiple_of(block * 256 + (1 - core) * 128, 128), 128)
        mine_ref[block] = grad_rows_ref[own]
        other_ref[block] = grad_rows_ref[their].astype(LOW)
    sums_ref[...] = jnp.concatenate([gain, shift], axis=0)
    terms_ref[:, :hidden] = contract_first(h_ref[...], upper_ref[...]).astype(LOW)
    terms_ref[:, hidden : 2 * hidden] = contract_first(grad_low_ref[...], hidden_ref[...]).astype(LOW)
    for copy in put_chunks(order_ref, (terms_ref, pack_ref), terms_hbm, out_sems):
        copy.wait()
    dec_copy.wait()


def decoder(
    order, depth, me, own, near, tconv, select, spread, conv, back, cots, slope, mid, h_rows, hidden, blocks
):
    f32 = jnp.float32
    vmem = pl.BlockSpec(memory_space=pltpu.VMEM)
    hbm = pl.BlockSpec(memory_space=pltpu.HBM)
    here = slope.shape[1]
    columns = 2 * here + 256
    window = lambda planes: pltpu.VMEM((planes, 18, 16, 512), LOW)
    field = lambda kind: pltpu.VMEM((8, 16, 16, 256), kind)
    kept = []

    def call(order, groups):
        dec, half, terms, mine, other, sums = pl.pallas_call(
            functools.partial(decoder_kernel, blocks),
            out_shape=(
                jax.ShapeDtypeStruct((16, 16, 16, 32), f32),
                jax.ShapeDtypeStruct((2, 128, 768), f32),
                jax.ShapeDtypeStruct((groups, 896 // groups, columns), LOW),
                jax.ShapeDtypeStruct((2, 128, 768), f32),
                jax.ShapeDtypeStruct((2, 128, 768), LOW),
                jax.ShapeDtypeStruct((2, 768), f32),
            ),
            in_specs=[pl.BlockSpec(memory_space=pltpu.SMEM)] * 4
            + [vmem] * 2
            + [hbm]
            + [vmem] * 2
            + [hbm] * 10
            + blocks.specs(),
            out_specs=[hbm] * 3 + [vmem] * 3,
            scratch_shapes=[
                pltpu.VMEM((512, 768), LOW),
                pltpu.VMEM((16, 16, 16, 32), f32),
                pltpu.VMEM((512, 768), LOW),
                pltpu.VMEM((512, 1024), LOW),
                pltpu.VMEM((128, columns), LOW),
                pltpu.VMEM((768, columns), LOW),
                pltpu.VMEM(slope.shape, LOW),
                pltpu.VMEM((512, 768), f32),
                pltpu.VMEM((2, 896, 128), f32),
                window(8),
                window(9),
                window(8),
                window(9),
                window(8),
                window(9),
                field(f32),
                field(f32),
                field(f32),
                field(f32),
                pltpu.VMEM((16, 8, 512), f32),
                pltpu.VMEM((8, 18, 16, 256), LOW),
                pltpu.VMEM((192, 2048), LOW),
                pltpu.VMEM((768, 1024), LOW),
                pltpu.VMEM((2, 9, 512, 256), LOW),
                pltpu.VMEM((2, 9, 256, 512), LOW),
                pltpu.VMEM((4, 1792, 128), LOW),
                pltpu.VMEM((768, here), LOW),
                pltpu.VMEM((768, here), LOW),
                pltpu.VMEM(slope.shape, LOW),
                pltpu.VMEM(mid.shape, f32),
                pltpu.VMEM(h_rows.shape, LOW),
                pltpu.VMEM(hidden.shape, LOW),
                pltpu.SemaphoreType.DMA((16,)),
                pltpu.SemaphoreType.DMA((2 * len(blocks.pieces),)),
                pltpu.SemaphoreType.DMA((2 * groups,)),
            ],
            compiler_params=pltpu.CompilerParams(vmem_limit_bytes=VMEM_LIMIT),
            cost_estimate=SMALL,
        )(
            blocks.indices,
            order,
            depth,
            me,
            own,
            near,
            tconv,
            select,
            spread,
            conv,
            back,
            *cots,
            slope,
            mid,
            h_rows,
            hidden,
            *blocks.pieces,
        )
        kept.extend((dec, half, mine, other, sums))
        return terms

    terms = in_ring_order(call, order, (768, 128))
    dec, half, mine, other, sums = kept
    return dec, half, terms, mine, other, sums


def full_spec(count, space=pltpu.VMEM):
    return [pl.BlockSpec(memory_space=space)] * count


def fetch(pairs, sems):
    copies = [
        pltpu.make_async_copy(source, target, sems.at[at]) for at, (source, target) in enumerate(pairs)
    ]
    for copy in copies:
        copy.start()
    return copies


class Blocks:
    def __init__(self, indices, starts, pieces, size):
        block, columns = pieces[0].shape
        if any(piece.shape[0] % 16 for piece in pieces):
            full = jnp.zeros((size * block, columns), pieces[0].dtype)
            for at, (start, piece) in enumerate(zip(starts, pieces)):
                full = lax.dynamic_update_slice(full, piece, (indices[at] * block + start, 0))
            pieces, starts, indices = [full], [0], jnp.zeros((1,), jnp.int32)
            block, size = size * block, 1
        self.indices = indices
        self.starts = tuple(starts)
        self.pieces = tuple(pieces)
        self.block = block
        self.rows = size * block

    def specs(self):
        return full_spec(len(self.pieces), pl.ANY)

    def load(self, index_ref, refs, column, target, sems):
        pairs = []
        for at, (piece, start) in enumerate(zip(refs, self.starts)):
            row = pl.multiple_of(index_ref[at] * self.block + start, 16)
            rows = pl.ds(row, piece.shape[0])
            pairs.append((piece.at[:, pl.ds(column, target.shape[1])], target.at[rows]))
        return fetch(pairs, sems)


def pack_kernel(query_ref, key_ref, value_ref, out_ref, up_ref, down_ref, norm_ref, first_ref, second_ref):
    groups = (
        (first_ref, (query_ref[...], key_ref[...], value_ref[...], out_ref[...].T, norm_ref[...].T)),
        (second_ref, (up_ref[...], down_ref[...])),
    )
    for pack_ref, values in groups:
        at = 0
        for value in values:
            pack_ref[:, at : at + value.shape[1]] = value.astype(LOW)
            at += value.shape[1]


def pack_weights(query, key, value, out, up, down, norms):
    part = query.shape[0]
    if part % 16:
        groups = ((query, key, value, out.T, norms.T), (up, down))
        return [jnp.concatenate([array.astype(LOW) for array in parts], axis=1) for parts in groups]
    columns = (4 * query.shape[1] + norms.shape[0], 2 * up.shape[1])
    return pl.pallas_call(
        pack_kernel,
        out_shape=tuple(jax.ShapeDtypeStruct((part, count), LOW) for count in columns),
        in_specs=full_spec(7),
        out_specs=full_spec(2),
        cost_estimate=SMALL,
    )(query, key, value, out, up, down, norms)


def out_norm_kernel(blocks, norm_at, index_ref, *refs):
    count = len(blocks.pieces)
    pieces = refs[:count]
    out_ref, norm_ref, wide_ref, columns_ref, sems = refs[count:]
    span = out_ref.shape[1]
    copies = blocks.load(index_ref, pieces, 4 * span - 256, wide_ref, sems)
    copies += blocks.load(index_ref, pieces, norm_at, columns_ref, sems.at[pl.ds(count, count)])
    for copy in copies:
        copy.wait()
    out_ref[...] = wide_ref[:, 256 - span :]
    norm_ref[...] = columns_ref[...].astype(jnp.float32).T[:8]


def out_and_norms(blocks, span, norm_at):
    count = len(blocks.pieces)
    return pl.pallas_call(
        functools.partial(out_norm_kernel, blocks, norm_at),
        out_shape=(
            jax.ShapeDtypeStruct((blocks.rows, span), LOW),
            jax.ShapeDtypeStruct((8, blocks.rows), jnp.float32),
        ),
        in_specs=full_spec(1, pltpu.SMEM) + blocks.specs(),
        out_specs=full_spec(2),
        scratch_shapes=[
            pltpu.VMEM((blocks.rows, 256), LOW),
            pltpu.VMEM((blocks.rows, 128), LOW),
            pltpu.SemaphoreType.DMA((2 * count,)),
        ],
        compiler_params=pltpu.CompilerParams(vmem_limit_bytes=VMEM_LIMIT),
        cost_estimate=SMALL,
    )(blocks.indices, *blocks.pieces)


def join_kernel(blocks, index_ref, *refs):
    count = len(blocks.pieces)
    full_ref, sems = refs[count:]
    for copy in blocks.load(index_ref, refs[:count], 0, full_ref, sems):
        copy.wait()


def join_blocks(blocks):
    if len(blocks.pieces) == 1:
        return blocks.pieces[0]
    count = len(blocks.pieces)
    return pl.pallas_call(
        functools.partial(join_kernel, blocks),
        out_shape=jax.ShapeDtypeStruct((blocks.rows, blocks.pieces[0].shape[1]), LOW),
        in_specs=full_spec(1, pltpu.SMEM) + blocks.specs(),
        out_specs=pl.BlockSpec(memory_space=pltpu.VMEM),
        scratch_shapes=[pltpu.SemaphoreType.DMA((count,))],
        compiler_params=pltpu.CompilerParams(vmem_limit_bytes=VMEM_LIMIT),
        cost_estimate=SMALL,
    )(blocks.indices, *blocks.pieces)


def taps_kernel(
    part, me_ref, own_hbm, near_hbm, place_ref, tconv_hbm, conv_hbm, back_hbm,
    packed_ref, tconv_ref, conv_ref, back_ref, sems,
):
    chans = 128
    groups = packed_ref.shape[1]
    conv_part = (packed_ref.shape[3] - part) // 7
    core = lax.rem(me_ref[0], 2)
    loads = fetch([(own_hbm, packed_ref.at[core]), (near_hbm, packed_ref.at[1 - core])], sems.at[pl.ds(3, 2)])

    def columns(t, start, rows, lanes):
        parts = [packed_ref[t % 2, d, t // 2, start : start + rows, lanes] for d in range(groups)]
        return parts[0] if groups == 1 else jnp.concatenate(parts, axis=0)

    none = jnp.zeros((chans, chans), LOW)
    for which in range(2):
        for plane in range(9):
            conv_ref[which, plane, 3 * chans :, :chans] = none
            conv_ref[which, plane, :chans, chans:] = none
            back_ref[which, plane, :chans, 3 * chans :] = none
            back_ref[which, plane, chans:, :chans] = none
    for load in loads:
        load.wait()
    for block in range(14):
        lanes = slice(block % 2 * chans, (block % 2 + 1) * chans)
        start = part + block // 2 * conv_part
        wide = jnp.concatenate([columns(t, start, conv_part, lanes) for t in range(4)], axis=1)
        made = dot(wide, place_ref[...]).astype(LOW)
        for second in range(2):
            tap = 2 * block + second
            if tap == 27:
                continue
            plane, deep = tap // 3, tap % 3
            turned = 2 - deep
            for which in range(2):
                at = (2 * second + which) * chans
                taps = made[:, at : at + chans]
                conv_ref[which, plane, deep * chans : (deep + 1) * chans, :chans] = taps
                conv_ref[which, plane, (deep + 1) * chans : (deep + 2) * chans, chans:] = taps
                back_ref[which, 8 - plane, :chans, turned * chans : (turned + 1) * chans] = taps
                back_ref[which, 8 - plane, chans:, (turned + 1) * chans : (turned + 2) * chans] = taps
    copies = fetch([(conv_ref, conv_hbm), (back_ref, back_hbm)], sems)
    for block in range(2):
        lanes = slice(block * chans, (block + 1) * chans)
        wide = jnp.concatenate([columns(t, 0, part, lanes) for t in range(4)], axis=1)
        tconv_ref[:, block * 512 : (block + 1) * 512] = dot(wide, place_ref[...]).astype(LOW)
    copies += fetch([(tconv_ref, tconv_hbm)], sems.at[pl.ds(2, 1)])
    for copy in copies:
        copy.wait()


def decoder_weights(me, own, near, groups, part, conv_part, place):
    width = part * groups

    def by_group(packed):
        packed = packed.reshape(groups, 2, part + 7 * conv_part, 256)
        if part % 16 == 0 and conv_part % 16 == 0:
            return packed
        tconv = packed[:, :, :part].transpose(1, 0, 2, 3).reshape(2, width, 256)
        conv = packed[:, :, part:].reshape(groups, 2, 7, conv_part, 256).transpose(1, 2, 0, 3, 4)
        return jnp.concatenate([tconv, conv.reshape(2, -1, 256)], axis=1)[None]

    own, near = by_group(own), by_group(near)
    shapes = ((width, 1024), (2, 9, 512, 256), (2, 9, 256, 512))
    return pl.pallas_call(
        functools.partial(taps_kernel, width // own.shape[0]),
        out_shape=tuple(jax.ShapeDtypeStruct(shape, LOW) for shape in shapes),
        in_specs=full_spec(1, pltpu.SMEM) + full_spec(2, pltpu.HBM) + full_spec(1),
        out_specs=full_spec(3, pltpu.HBM),
        scratch_shapes=[pltpu.VMEM((2,) + own.shape, LOW)]
        + [pltpu.VMEM(shape, LOW) for shape in shapes]
        + [pltpu.SemaphoreType.DMA((5,))],
        compiler_params=pltpu.CompilerParams(vmem_limit_bytes=VMEM_LIMIT),
        cost_estimate=SMALL,
    )(me, own, near, place)


def normalise(rows):
    middle = jnp.mean(rows, axis=-1, keepdims=True)
    centred = rows - middle
    spread = jnp.mean(centred * centred, axis=-1, keepdims=True)
    scale = lax.rsqrt(spread + 1e-06)
    return centred * scale, scale


def attention_kernel(blocks, index_ref, depth_ref, me_ref, own_ref, near_ref, far_ref, last_ref, norm_ref, *refs):
    count = len(blocks.pieces)
    pieces = refs[:count]
    (
        out_ref, rows_hbm, h_hbm, qkv_hbm, probs_hbm,
        rows_ref, h_ref, qkv_ref, probs_ref, weight_ref, sems, load_sems,
    ) = refs[count:]
    patches = rows_ref.shape[0]
    heads = probs_ref.shape[0]
    span = heads * HD
    quarter = patches // 4
    loads = blocks.load(index_ref, pieces, 0, weight_ref, load_sems)
    for flip, block in enumerate((own_ref, near_ref, far_ref, last_ref)):
        start = pl.multiple_of(jnp.bitwise_xor(me_ref[0], flip) * quarter, quarter)
        rows_ref[pl.ds(start, quarter)] = block[...]
    copies = fetch([(rows_ref, rows_hbm)], sems.at[pl.ds(1, 1)])
    norms = norm_ref[...]
    normed, _ = normalise(rows_ref[...].astype(jnp.float32))
    low_rows = (normed * norms[0:1] + norms[1:2]).astype(LOW)
    h_ref[...] = low_rows
    copies += fetch([(h_ref, h_hbm)], sems.at[pl.ds(2, 1)])
    for load in loads:
        load.wait()
    qkv_ref[...] = dot(low_rows, weight_ref[:, : 3 * span]).astype(LOW)
    copies += fetch([(qkv_ref, qkv_hbm)], sems.at[pl.ds(3, 1)])
    key_at = lax.broadcasted_iota(jnp.int32, (1, patches), 1)
    live = key_at < depth_ref[0] * (GRID * GRID)
    outs = []
    for head in range(heads):
        query = qkv_ref[:, head * HD : (head + 1) * HD]
        keys = qkv_ref[:, span + head * HD : span + (head + 1) * HD]
        values = qkv_ref[:, 2 * span + head * HD : 2 * span + (head + 1) * HD]
        scores = jnp.where(live, dot_last(query, keys) * HD ** (-0.5), -1000000000.0)
        expo = jnp.exp(scores - jnp.max(scores, axis=-1, keepdims=True))
        probs = (expo * (1.0 / jnp.sum(expo, axis=-1, keepdims=True))).astype(LOW)
        probs_ref[head] = probs
        copies += fetch([(probs_ref.at[head], probs_hbm.at[head])], sems.at[pl.ds(4 + head, 1)])
        outs.append(dot(probs, values))
    out_ref[...] = jnp.concatenate(outs, axis=1).astype(LOW)
    for copy in copies:
        copy.wait()


def attention(depth, me, rows, blocks, norms, heads):
    patches, width = 4 * rows[0].shape[0], rows[0].shape[1]
    shapes = ((patches, width), (patches, width), (patches, 3 * heads * HD), (heads, patches, patches))
    count = len(blocks.pieces)
    return pl.pallas_call(
        functools.partial(attention_kernel, blocks),
        out_shape=tuple(
            jax.ShapeDtypeStruct(shape, LOW) for shape in ((patches, heads * HD),) + shapes
        ),
        in_specs=full_spec(3, pltpu.SMEM) + full_spec(5) + blocks.specs(),
        out_specs=full_spec(1) + full_spec(4, pltpu.HBM),
        scratch_shapes=[pltpu.VMEM(shape, LOW) for shape in shapes]
        + [
            pltpu.VMEM((width, 4 * heads * HD), LOW),
            pltpu.SemaphoreType.DMA((4 + heads,)),
            pltpu.SemaphoreType.DMA((count,)),
        ],
        compiler_params=pltpu.CompilerParams(vmem_limit_bytes=VMEM_LIMIT),
        cost_estimate=SMALL,
    )(blocks.indices, depth, me, *rows, norms, *blocks.pieces)


def mlp_kernel(
    blocks, index_ref, core_ref, rows_hbm, out0, out1, out2, out3, w0, w1, w2, w3, norm_ref, *refs
):
    count = len(blocks.pieces)
    pieces = refs[:count]
    (
        mine_ref, other_ref, mid_hbm, mid_half_ref, h_hbm, hidden_hbm, slope_hbm,
        partial_ref, rows_ref, weight_ref, mid_ref, h_ref, hidden_ref, slope_ref, sems, load_sems,
    ) = refs[count:]
    hidden_here = hidden_ref.shape[1]
    core = core_ref[0]
    norms = norm_ref[...]
    loads = fetch([(rows_hbm, rows_ref)], sems)
    loads += blocks.load(index_ref, pieces, 0, weight_ref, load_sems)
    loads[0].wait()
    copies = []
    for block in range(2):
        at = slice(block * 256, (block + 1) * 256)
        mid = rows_ref[at].astype(jnp.float32)
        attended = jnp.concatenate([out[at] for out in (out0, out1, out2, out3)], axis=1)
        weights = jnp.concatenate([w[...] for w in (w0, w1, w2, w3)], axis=1)
        mid = mid + dot_last(attended, weights)
        mid_ref[at] = mid
        normed, _ = normalise(mid)
        low_rows = (normed * norms[2:3] + norms[3:4]).astype(LOW)
        h_ref[at] = low_rows
        if block == 0:
            for load in loads[1:]:
                load.wait()
        value, slope = gelu_and_slope(dot(low_rows, weight_ref[:, :hidden_here]))
        hidden = value.astype(LOW)
        hidden_ref[at] = hidden
        slope_ref[at] = slope.astype(LOW)
        partial_ref[at] = dot_last(hidden, weight_ref[:, hidden_here : 2 * hidden_here])
        own = pl.ds(pl.multiple_of(block * 256 + core * 128, 128), 128)
        their = pl.ds(pl.multiple_of(block * 256 + (1 - core) * 128, 128), 128)
        mid_half_ref[block] = mid_ref[own]
        mine_ref[block] = partial_ref[own]
        other_ref[block] = partial_ref[their].astype(LOW)
        rows = pl.ds(block * 256, 256)
        copies += fetch(
            [
                (mid_ref.at[rows], mid_hbm.at[rows]),
                (h_ref.at[rows], h_hbm.at[rows]),
                (hidden_ref.at[rows], hidden_hbm.at[rows]),
                (slope_ref.at[rows], slope_hbm.at[rows]),
            ],
            sems.at[pl.ds(2 + 4 * block, 4)],
        )
    for copy in copies:
        copy.wait()


def mlp(core, rows, outs, out_weights, norms, blocks, hidden_here):
    patches, width = rows.shape
    f32 = jnp.float32
    half = (2, patches // 4, width)
    return pl.pallas_call(
        functools.partial(mlp_kernel, blocks),
        out_shape=(
            jax.ShapeDtypeStruct(half, f32),
            jax.ShapeDtypeStruct(half, LOW),
            jax.ShapeDtypeStruct((patches, width), f32),
            jax.ShapeDtypeStruct(half, f32),
            jax.ShapeDtypeStruct((patches, width), LOW),
            jax.ShapeDtypeStruct((patches, hidden_here), LOW),
            jax.ShapeDtypeStruct((patches, hidden_here), LOW),
        ),
        in_specs=full_spec(2, pltpu.SMEM) + full_spec(1, pltpu.HBM) + full_spec(9) + blocks.specs(),
        out_specs=full_spec(2)
        + full_spec(1, pltpu.HBM)
        + full_spec(1)
        + full_spec(3, pltpu.HBM),
        scratch_shapes=[
            pltpu.VMEM((patches, width), f32),
            pltpu.VMEM((patches, width), LOW),
            pltpu.VMEM((width, 2 * hidden_here), LOW),
            pltpu.VMEM((patches, width), f32),
            pltpu.VMEM((patches, width), LOW),
            pltpu.VMEM((patches, hidden_here), LOW),
            pltpu.VMEM((patches, hidden_here), LOW),
            pltpu.SemaphoreType.DMA((10,)),
            pltpu.SemaphoreType.DMA((len(blocks.pieces),)),
        ],
        compiler_params=pltpu.CompilerParams(vmem_limit_bytes=VMEM_LIMIT),
        cost_estimate=SMALL,
    )(blocks.indices, core, rows, *outs, *out_weights, norms, *blocks.pieces)


def put_chunks(index_ref, sources, target, sems):
    groups = target.shape[0]
    pairs, start = [], 0
    for source in sources:
        rows = source.shape[0] // groups
        for at in range(groups):
            row = 0 if groups == 1 else pl.multiple_of(index_ref[at] * rows, 16)
            pairs.append((source.at[pl.ds(row, rows)], target.at[at, pl.ds(start, rows)]))
        start += rows
    return fetch(pairs, sems)


def in_ring_order(call, indices, parts):
    groups = indices.shape[0]
    if all(rows // groups % 16 == 0 for rows in parts):
        return call(indices, groups)
    flat = call(jnp.zeros((1,), jnp.int32), 1)[0]
    blocks, start = [], 0
    for rows in parts:
        blocks.append(flat[start : start + rows].reshape(groups, rows // groups, -1)[indices])
        start += rows
    return jnp.concatenate(blocks, axis=1)


def mlp_sum_kernel(ahead_ref, behind_ref, own_ref, turn_ref, up_ref, down_ref, tconv_ref, conv1_ref, conv2_ref):
    part, hidden = up_ref.shape
    total = (
        own_ref[0].astype(jnp.float32)
        + ahead_ref[...].astype(jnp.float32)
        + behind_ref[...].astype(jnp.float32)
    )
    up_ref[...] = total[:part, :hidden]
    down_ref[...] = total[:part, hidden : 2 * hidden]
    tconv_ref[...] = dot(total[:part, 2 * hidden :].astype(LOW), turn_ref[...])
    for which, conv_ref in enumerate((conv1_ref, conv2_ref)):
        for tap in range(27):
            at = which * 896 + tap * 32
            conv_ref[tap] = total[part:, at : at + 32]


def mlp_sum(ahead, behind, terms, part, hidden):
    rows, columns = ahead.shape
    conv_part = rows - part
    f32 = jnp.float32
    if part % 16 or conv_part % 16:
        total = terms[0].astype(f32) + ahead.astype(f32) + behind.astype(f32)
        tconv = total[:part, 2 * hidden :].reshape(part, 8, -1).transpose(0, 2, 1).reshape(part, -1)
        conv = total[part:].reshape(conv_part, 2, 28, 32)[:, :, :27].transpose(1, 2, 0, 3)
        return total[:part, :hidden], total[:part, hidden : 2 * hidden], tconv, conv[0], conv[1]
    turn = np.zeros((8, 32, 32, 8), np.float32)
    for group in range(8):
        for chan in range(32):
            turn[group, chan, chan, group] = 1.0
    return pl.pallas_call(
        mlp_sum_kernel,
        out_shape=(
            jax.ShapeDtypeStruct((part, hidden), f32),
            jax.ShapeDtypeStruct((part, hidden), f32),
            jax.ShapeDtypeStruct((part, 256), f32),
            jax.ShapeDtypeStruct((27, conv_part, 32), f32),
            jax.ShapeDtypeStruct((27, conv_part, 32), f32),
        ),
        in_specs=full_spec(2)
        + [pl.BlockSpec((1,) + terms.shape[1:], lambda at: (0, 0, 0))]
        + full_spec(1),
        out_specs=full_spec(5),
        grid=(1,),
        compiler_params=pltpu.CompilerParams(vmem_limit_bytes=VMEM_LIMIT),
        cost_estimate=SMALL,
    )(ahead, behind, terms, jnp.asarray(turn.reshape(256, 256).astype(LOW)))


def norm_back_kernel(
    chip_ref, sum_ref, far_ref, grad_hbm, rows_hbm, norm_ref, own_ref, low_ref, grad_ref, rows_ref, sems
):
    for copy in fetch([(grad_hbm, grad_ref), (rows_hbm, rows_ref)], sems):
        copy.wait()
    gain = norm_ref[2:3]
    for block in range(2):
        summed = sum_ref[block].astype(jnp.float32) + far_ref[block].astype(jnp.float32)
        normed, scale = normalise(rows_ref[block])
        grad = grad_ref[block] + layer_norm_back(summed * gain, normed, scale)
        grad_ref[block] = grad
        low_ref[block] = grad.astype(LOW)
    own_ref[...] = grad_ref[chip_ref[0]]


def norm_back(chip, summed, far, grad, rows, norms):
    return pl.pallas_call(
        norm_back_kernel,
        out_shape=(
            jax.ShapeDtypeStruct(grad.shape[1:], jnp.float32),
            jax.ShapeDtypeStruct(grad.shape, LOW),
        ),
        in_specs=full_spec(1, pltpu.SMEM) + full_spec(2) + full_spec(2, pltpu.HBM) + full_spec(1),
        out_specs=full_spec(2),
        scratch_shapes=[
            pltpu.VMEM(grad.shape, jnp.float32),
            pltpu.VMEM(rows.shape, jnp.float32),
            pltpu.SemaphoreType.DMA((2,)),
        ],
        compiler_params=pltpu.CompilerParams(vmem_limit_bytes=VMEM_LIMIT),
        cost_estimate=SMALL,
    )(chip, summed, far, grad, rows, norms)


def attention_back_kernel(
    blocks, index_ref, order_ref, core_ref, own_ref, near_ref, qkv_hbm, probs_hbm, h_hbm, out_hbm, rows_hbm,
    sums_ref, *refs,
):
    count = len(blocks.pieces)
    pieces = refs[:count]
    (
        pack_hbm, mine_ref, other_ref, pack_ref, grad_ref, partial_ref,
        weight_ref, qkv_ref, probs_ref, h_ref, out_ref, rows_ref, sems, out_sems, load_sems,
    ) = refs[count:]
    heads = probs_ref.shape[0]
    span = heads * HD
    loads = blocks.load(index_ref, pieces, 0, weight_ref, load_sems)
    copies = fetch(
        [
            (qkv_hbm, qkv_ref),
            (probs_hbm, probs_ref),
            (h_hbm, h_ref),
            (out_hbm, out_ref),
            (rows_hbm, rows_ref),
        ],
        sems,
    )
    core = core_ref[0]
    for block in range(2):
        grad_ref[pl.ds(pl.multiple_of(block * 256 + core * 128, 128), 128)] = own_ref[block]
        grad_ref[pl.ds(pl.multiple_of(block * 256 + (1 - core) * 128, 128), 128)] = near_ref[block]
    grad_branch = grad_ref[...]
    for load in loads:
        load.wait()
    grad_out = dot(grad_branch, weight_ref[:, 3 * span : 4 * span]).astype(LOW)
    copies[0].wait()
    copies[1].wait()
    grad_query, grad_keys, grad_values = [], [], []
    for head in range(heads):
        query = qkv_ref[:, head * HD : (head + 1) * HD]
        keys = qkv_ref[:, span + head * HD : span + (head + 1) * HD]
        values = qkv_ref[:, 2 * span + head * HD : 2 * span + (head + 1) * HD]
        grad_head = grad_out[:, head * HD : (head + 1) * HD]
        probs = probs_ref[head]
        grad_values.append(contract_first(probs, grad_head))
        probs = probs.astype(jnp.float32)
        grad_probs = dot_last(grad_head, values)
        inner = jnp.sum(probs * grad_probs, axis=-1, keepdims=True)
        grad_scores = (probs * (grad_probs - inner)).astype(LOW)
        grad_query.append(dot(grad_scores, keys) * HD ** (-0.5))
        grad_keys.append(contract_first(grad_scores, query) * HD ** (-0.5))
    grad_qkv = jnp.concatenate(grad_query + grad_keys + grad_values, axis=1).astype(LOW)
    copies[2].wait()
    copies[3].wait()
    copies[4].wait()
    pack_ref[:, : 3 * span] = contract_first(h_ref[...], grad_qkv).astype(LOW)
    pack_ref[:, 3 * span : 4 * span] = contract_first(grad_branch, out_ref[...]).astype(LOW)
    partial_ref[...] = dot_last(grad_qkv, weight_ref[:, : 3 * span])
    gain = shift = 0.0
    for block in range(2):
        at = slice(block * 256, (block + 1) * 256)
        normed, _ = normalise(rows_ref[at].astype(jnp.float32))
        gain += jnp.sum(partial_ref[at] * normed, axis=0, keepdims=True)
        shift += jnp.sum(partial_ref[at], axis=0, keepdims=True)
        own = pl.ds(pl.multiple_of(block * 256 + core * 128, 128), 128)
        their = pl.ds(pl.multiple_of(block * 256 + (1 - core) * 128, 128), 128)
        mine_ref[block] = partial_ref[own]
        other_ref[block] = partial_ref[their].astype(LOW)
    none = jnp.zeros((124, gain.shape[1]), jnp.float32)
    stacked = jnp.concatenate([gain, shift, sums_ref[...], none], axis=0)
    pack_ref[:, 4 * span :] = stacked.T.astype(LOW)
    for copy in put_chunks(order_ref, (pack_ref,), pack_hbm, out_sems):
        copy.wait()


def attention_back(indices, core, own, near, blocks, qkv, probs, h_rows, out, rows, sums):
    patches, width = rows.shape
    f32 = jnp.float32
    half = (2, patches // 4, width)
    columns = 4 * out.shape[1] + 128
    kept = []

    def call(indices, groups):
        pack, mine, other = pl.pallas_call(
            functools.partial(attention_back_kernel, blocks),
            out_shape=(
                jax.ShapeDtypeStruct((groups, width // groups, columns), LOW),
                jax.ShapeDtypeStruct(half, f32),
                jax.ShapeDtypeStruct(half, LOW),
            ),
            in_specs=full_spec(3, pltpu.SMEM)
            + full_spec(2)
            + full_spec(5, pltpu.HBM)
            + full_spec(1)
            + blocks.specs(),
            out_specs=full_spec(1, pltpu.HBM) + full_spec(2),
            scratch_shapes=[
                pltpu.VMEM((width, columns), LOW),
                pltpu.VMEM((patches, width), LOW),
                pltpu.VMEM((patches, width), f32),
                pltpu.VMEM((width, 4 * out.shape[1]), LOW),
                pltpu.VMEM(qkv.shape, LOW),
                pltpu.VMEM(probs.shape, LOW),
                pltpu.VMEM(h_rows.shape, LOW),
                pltpu.VMEM(out.shape, LOW),
                pltpu.VMEM(rows.shape, LOW),
                pltpu.SemaphoreType.DMA((5,)),
                pltpu.SemaphoreType.DMA((groups,)),
                pltpu.SemaphoreType.DMA((len(blocks.pieces),)),
            ],
            compiler_params=pltpu.CompilerParams(vmem_limit_bytes=VMEM_LIMIT),
            cost_estimate=SMALL,
        )(
            blocks.indices, indices, core, own, near, qkv, probs, h_rows, out, rows, sums, *blocks.pieces
        )
        kept.extend((mine, other))
        return pack

    pack = in_ring_order(call, indices, (width,))
    return pack, *kept


def attention_sum_kernel(ahead_ref, behind_ref, own_ref, query_ref, key_ref, value_ref, out_ref, norm_ref):
    span = query_ref.shape[1]
    total = (
        own_ref[0].astype(jnp.float32)
        + ahead_ref[...].astype(jnp.float32)
        + behind_ref[...].astype(jnp.float32)
    )
    query_ref[...] = total[:, :span]
    key_ref[...] = total[:, span : 2 * span]
    value_ref[...] = total[:, 2 * span : 3 * span]
    out_ref[...] = total[:, 3 * span : 4 * span].T
    norm_ref[...] = total[:, 4 * span :]


def attention_sum(ahead, behind, terms, span):
    part = ahead.shape[0]
    f32 = jnp.float32
    if part % 16:
        total = terms[0].astype(f32) + ahead.astype(f32) + behind.astype(f32)
        parts = [total[:, at * span : (at + 1) * span] for at in range(4)]
        return parts[0], parts[1], parts[2], parts[3].T, total[:, 4 * span :]
    return pl.pallas_call(
        attention_sum_kernel,
        out_shape=(jax.ShapeDtypeStruct((part, span), f32),) * 3
        + (jax.ShapeDtypeStruct((span, part), f32), jax.ShapeDtypeStruct((part, 128), f32)),
        in_specs=full_spec(2)
        + [pl.BlockSpec((1,) + terms.shape[1:], lambda at: (0, 0, 0))],
        out_specs=full_spec(5),
        grid=(1,),
        cost_estimate=SMALL,
    )(ahead, behind, terms)


class Ring:
    def __init__(self, size):
        self.size = size
        order = ring_order(size)
        self.ahead = [(order[i], order[(i + 1) % size]) for i in range(size)]
        self.behind = [(b, a) for a, b in self.ahead]
        reach = (size - 1) // 2
        self.distances = [0]
        for step in range(1, reach + 1):
            self.distances += [-step, step]
        if size % 2 == 0:
            self.distances.append(size // 2)
        table = np.array(
            [
                [order[(order.index(me) + distance) % size] for distance in self.distances]
                for me in range(size)
            ],
            np.int32,
        )
        self.indices = jnp.asarray(table)[lax.axis_index("dp")]

    def send(self, value, forward):
        return lax.ppermute(value, "dp", self.ahead if forward else self.behind)

    def gather(self, array):
        return Gather(self, array)

    def scatter(self, terms, after=None):
        size = self.size
        rows = terms.shape[1]
        place = {distance: at for at, distance in enumerate(self.distances)}

        def term(distance):
            return terms[place[distance]]

        reach = (size - 1) // 2
        if size % 2 == 0:
            half = rows // 2
            far = term(size // 2)
            one = self.send(far[:half], True)
            two = self.send(far[half:], False)
            if reach == 0:
                return jnp.concatenate([one, two]), jnp.zeros_like(far)
            above, below = term(reach), term(-reach)
            if after is not None:
                one, two = after(one, two)
            one = jnp.concatenate([above[:half] + one, above[half:]])
            two = jnp.concatenate([below[:half], below[half:] + two])
        else:
            if reach == 0:
                return jnp.zeros_like(terms[0]), jnp.zeros_like(terms[0])
            one, two = term(reach), term(-reach)
        for step in range(reach, 0, -1):
            one = self.send(one, True)
            two = self.send(two, False)
            if step > 1:
                one = one + term(step - 1)
                two = two + term(-(step - 1))
        return one, two


class Gather:
    def __init__(self, ring, array):
        self.ring = ring
        self.array = array
        self.one = self.two = array
        self.starts = [0]
        self.pieces = [array]
        self.done = 0

    def step(self, *after):
        size = self.ring.size
        self.done += 1
        if after:
            self.one, self.two, _ = lax.optimization_barrier((self.one, self.two, after))
        if self.done <= (size - 1) // 2:
            self.one = self.ring.send(self.one, True)
            self.two = self.ring.send(self.two, False)
            self.starts += [0, 0]
        else:
            half = self.array.shape[0] // 2
            self.one = self.ring.send(self.one[:half], True)
            self.two = self.ring.send(self.two[half:], False)
            self.starts += [0, half]
        self.pieces += [self.one, self.two]

    def steps_left(self):
        return self.ring.size // 2 - self.done

    def blocks(self):
        indices = self.ring.indices
        if self.ring.size % 2 == 0:
            indices = jnp.concatenate([indices, indices[-1:]])
        return Blocks(indices, self.starts, self.pieces, self.ring.size)


class Quad:
    def __init__(self):
        self.me = lax.axis_index("tensor")
        self.core = self.me % 2
        self.chip = self.me // 2

    def over_core(self, value):
        return lax.ppermute(value, "tensor", [(i, i ^ 1) for i in range(4)])

    def over_chip(self, value):
        return lax.ppermute(value, "tensor", [(i, i ^ 2) for i in range(4)])

    def spread(self, block):
        far = self.over_chip(block)
        return block, self.over_core(block), far, self.over_core(far)

    def spread_direct(self, block):
        last = lax.ppermute(block, "tensor", [(i, i ^ 3) for i in range(4)])
        return block, self.over_core(block), self.over_chip(block), last

    def pick(self, half):
        return jnp.where(self.chip == 0, half[0], half[1])


def selections(chans, chans_here):
    own = np.zeros((4, 2, chans_here, 2, chans), np.float32)
    spread = np.zeros((2, 4, 2, 2, chans_here, 2, chans), np.float32)
    place = np.zeros((4, 4, chans_here, 4, 4, chans_here), np.float32)
    for t in range(4):
        for c in range(chans_here):
            for e in range(2):
                own[t, e, c, e, t * chans_here + c] = 1.0
                for a in range(2):
                    spread[a, t, a, e, c, e, t * chans_here + c] = 1.0
            for group in range(4):
                place[t, group, c, group, t, c] = 1.0
    own = own.reshape(4, 2, chans_here, 2 * chans).astype(LOW)
    spread = spread.reshape(2, 16 * chans_here, 2 * chans).astype(LOW)
    place = place.reshape(16 * chans_here, 16 * chans_here).astype(LOW)
    return jnp.asarray(own), jnp.asarray(spread), jnp.asarray(place)


def shards(
    tokens,
    crop_depth,
    w_query,
    w_key,
    w_value,
    w_out,
    w_up,
    w_down,
    w_tconv,
    w_conv1,
    w_conv2,
    ln1_gain,
    ln1_bias,
    ln2_gain,
    ln2_bias,
    cot_out,
    cot_dec,
    groups,
):
    ring = Ring(groups)
    quad = Quad()
    grid = GRID
    vox = 2 * grid
    patches = grid**3
    width = w_query.shape[0] * groups
    part = w_query.shape[0]
    heads_here = w_query.shape[1] // HD
    span = heads_here * HD
    chans = w_conv1.shape[0] * groups
    chans_here = w_conv1.shape[2]

    low = lambda value: value.astype(LOW)
    hidden_here = w_up.shape[1]
    norm_rows = jnp.stack([ln1_gain, ln1_bias, ln2_gain, ln2_bias])
    norm_rows = jnp.pad(norm_rows, ((0, 124), (0, 0)))
    weights = pack_weights(w_query, w_key, w_value, w_out, w_up, w_down.T, norm_rows)

    def pack_decoder():
        conv = jnp.stack([low(w_conv1), low(w_conv2)], axis=2).reshape(w_conv1.shape[0], -1)
        conv = jnp.pad(conv, ((0, 0), (0, 64))).reshape(-1, 7, 256).transpose(1, 0, 2)
        tconv = low(w_tconv).reshape(part, chans_here, 8).transpose(0, 2, 1).reshape(part, -1)
        return jnp.concatenate([tconv, conv.reshape(-1, 256)])

    def pack_cotangents():
        field = low(cot_dec).reshape(grid, 2, vox, grid, 2, chans_here).transpose(0, 2, 3, 1, 4, 5)
        field = field.reshape(grid * vox * grid, 4 * chans_here)
        tiles = low(cot_out).reshape(patches // 4, width // 128, 128).transpose(1, 0, 2)
        return jnp.concatenate([tiles.reshape(-1, 128), field])

    first, second = [ring.gather(array) for array in weights]
    conv_part = w_conv1.shape[0]
    cot_pack = pack_cotangents()
    own_pack = pack_decoder()
    first.step()
    second.step()
    before = first.one, first.two
    own_pack, tokens_now, _ = lax.optimization_barrier((own_pack, tokens, before))
    token_blocks = quad.spread(tokens_now)
    far_pack = quad.over_chip(own_pack)
    lower = quad.chip == 0
    pair_pack = jnp.concatenate(
        [jnp.where(lower, own_pack, far_pack), jnp.where(lower, far_pack, own_pack)]
    )
    third = ring.gather(pair_pack)
    first.step()
    cot_pack, _ = lax.optimization_barrier((cot_pack, (first.one, first.two)))
    cot_blocks = quad.spread(cot_pack)
    while second.steps_left():
        second.step(before)
        before = first.one, first.two
        if first.steps_left():
            first.step()
    blocks, mlp_blocks = first.blocks(), second.blocks()
    out_weight, norms = out_and_norms(blocks, span, 4 * span)
    third.step(second.pieces[-4:-2])
    norms, _ = lax.optimization_barrier((norms, cot_blocks))
    select, spread, place = selections(chans, chans_here)
    core = quad.core[None]
    me = quad.me[None]

    attended, rows_low, h_one, qkv, probs = attention(
        crop_depth, me, token_blocks, blocks, norms, heads_here
    )
    attended_blocks = quad.spread(attended)
    if third.steps_left():
        third.step(attended)
    if third.steps_left():
        third.step()
    mine, other, mid, mid_half, h_two, hidden, slope = mlp(
        core,
        rows_low,
        attended_blocks,
        quad.spread(out_weight),
        norms,
        mlp_blocks,
        hidden_here,
    )
    summed = low(mine + quad.over_core(other).astype(jnp.float32))
    far = quad.over_chip(summed)
    while third.steps_left():
        third.step(mine)
    decoder_own = join_blocks(third.blocks())
    tconv_full, conv_taps, back_taps = decoder_weights(
        me, decoder_own, quad.over_core(decoder_own), groups, part, conv_part, place
    )
    far, tconv_full, conv_taps, back_taps = lax.optimization_barrier(
        (far, tconv_full, conv_taps, back_taps)
    )
    after_half = mid_half + (summed.astype(jnp.float32) + far.astype(jnp.float32))
    after = quad.pick(after_half)
    low_half = low(after_half)
    dec_out, grad_half, mlp_terms, mine, other, sums_two = decoder(
        ring.indices,
        crop_depth,
        me,
        low_half,
        quad.over_core(low_half),
        tconv_full,
        select,
        spread,
        conv_taps,
        back_taps,
        cot_blocks,
        slope,
        mid,
        h_two,
        hidden,
        mlp_blocks,
    )
    summed = low(mine + quad.over_core(other).astype(jnp.float32))
    far = quad.over_chip(summed)
    grad_mid_own, low_mid_half = norm_back(
        quad.chip[None], summed, far, grad_half, mid_half, norms
    )
    mlp_ahead, mlp_behind = ring.scatter(mlp_terms)
    attention_terms, mine, other = attention_back(
        ring.indices,
        core,
        low_mid_half,
        quad.over_core(low_mid_half),
        blocks,
        qkv,
        probs,
        h_one,
        attended,
        rows_low,
        sums_two,
    )
    ahead, behind = ring.scatter(attention_terms)
    grad_query, grad_key, grad_value, grad_out, norm_grads = attention_sum(
        ahead, behind, attention_terms, span
    )
    norm_grads = sum(quad.spread_direct(norm_grads))
    summed = mine + quad.over_core(other).astype(jnp.float32)
    norm_own = quad.pick(summed) + quad.over_chip(low(quad.pick(summed[::-1]))).astype(jnp.float32)
    normed_own, scale_own = normalise(tokens.astype(jnp.float32))
    grad_tokens = grad_mid_own + layer_norm_back(norm_own * norms[0:1], normed_own, scale_own)
    grad_up, grad_down, grad_tconv, grad_conv1, grad_conv2 = mlp_sum(
        mlp_ahead, mlp_behind, mlp_terms, part, hidden_here
    )
    return (
        after,
        dec_out[None],
        grad_tokens,
        grad_query,
        grad_key,
        grad_value,
        grad_out,
        grad_up,
        grad_down.T,
        grad_tconv,
        grad_conv1.transpose(1, 0, 2),
        grad_conv2.transpose(1, 0, 2),
        norm_grads[:, 0],
        norm_grads[:, 1],
        norm_grads[:, 2],
        norm_grads[:, 3],
    )


def solution(mesh):
    in_specs = (
        P(("dp", "tensor"), None),
        P("dp"),
        P("dp", "tensor"),
        P("dp", "tensor"),
        P("dp", "tensor"),
        P("tensor", "dp"),
        P("dp", "tensor"),
        P("tensor", "dp"),
        P("dp", "tensor"),
        P("dp", None, "tensor"),
        P("dp", None, "tensor"),
        P("dp"),
        P("dp"),
        P("dp"),
        P("dp"),
        P(("dp", "tensor"), None),
        P("dp", None, None, None, "tensor"),
    )
    out_specs = (
        P(("dp", "tensor"), None),
        P("dp", None, None, None, "tensor"),
        P(("dp", "tensor"), None),
        P("dp", "tensor"),
        P("dp", "tensor"),
        P("dp", "tensor"),
        P("tensor", "dp"),
        P("dp", "tensor"),
        P("tensor", "dp"),
        P("dp", "tensor"),
        P("dp", None, "tensor"),
        P("dp", None, "tensor"),
        P("dp"),
        P("dp"),
        P("dp"),
        P("dp"),
    )
    groups = mesh.shape["dp"]

    def run(*arrays):
        return shards(*arrays, groups)

    return jax.shard_map(run, mesh=mesh, in_specs=in_specs, out_specs=out_specs, check_vma=False)
```

```python
import functools

import jax
import jax.numpy as jnp
import numpy as np
from jax import lax
from jax.experimental import pallas as pl
from jax.experimental.pallas import tpu as pltpu
from jax.sharding import PartitionSpec as P

HD = 64
GRID = 8
LOW = jnp.bfloat16


def ring_order(size):
    if size % 2:
        return list(range(size))
    return list(range(0, size, 2)) + list(range(size - 1, 0, -2))


def layer_norm_back(grad_normed, normed, scale):
    mean_grad = jnp.mean(grad_normed, axis=-1, keepdims=True)
    mean_dot = jnp.mean(grad_normed * normed, axis=-1, keepdims=True)
    return scale * (grad_normed - mean_grad - normed * mean_dot)


def contract_first(left, right):
    return lax.dot_general(
        left, right, (((0,), (0,)), ((), ())), preferred_element_type=jnp.float32
    )


MIB = 2**20
VMEM_LIMIT = 60 * MIB


def cost(microseconds):
    return pl.CostEstimate(flops=0, bytes_accessed=int(microseconds * 3.5e6), transcendentals=0)


def gelu_and_slope(x):
    bell = jnp.exp(-0.5 * x * x)
    frac = 1.0 / (1.0 + 0.3275911 * 0.7071067811865476 * jnp.abs(x))
    poly = frac * (
        0.254829592
        + frac * (-0.284496736 + frac * (1.421413741 + frac * (-1.453152027 + frac * 1.061405429)))
    )
    tail = 0.5 * poly * bell
    phi = jnp.where(x >= 0.0, 1.0 - tail, tail)
    return x * phi, phi + x * bell * 0.3989422804014327


def dot(left, right):
    return jnp.dot(left, right, preferred_element_type=jnp.float32)


def dot_last(left, right):
    return lax.dot_general(
        left, right, (((1,), (1,)), ((), ())), preferred_element_type=jnp.float32
    )


BATCH = 4


DECODER_REFS = 40


def decoder_kernel(
    blocks,
    index_ref,
    order_ref,
    depth_ref,
    me_ref,
    own_ref,
    near_ref,
    joined_hbm,
    joined_near_hbm,
    select_ref,
    spread_ref,
    place_ref,
    cot0_hbm,
    cot1_hbm,
    cot2_hbm,
    cot3_hbm,
    slope_hbm,
    mid_hbm,
    h_hbm,
    hidden_hbm,
    *refs,
):
    decoder_steps(
        blocks,
        refs[: len(blocks.pieces)],
        index_ref,
        order_ref,
        depth_ref,
        me_ref,
        own_ref,
        near_ref,
        joined_hbm,
        joined_near_hbm,
        select_ref,
        spread_ref,
        place_ref,
        (cot0_hbm, cot1_hbm, cot2_hbm, cot3_hbm),
        slope_hbm,
        mid_hbm,
        h_hbm,
        hidden_hbm,
        refs[len(blocks.pieces) : -DECODER_REFS],
        *refs[-DECODER_REFS:],
    )


def decoder_steps(
    blocks,
    pieces,
    index_ref,
    order_ref,
    depth_ref,
    me_ref,
    own_ref,
    near_ref,
    joined_hbm,
    joined_near_hbm,
    select_ref,
    spread_ref,
    place_ref,
    cots_hbm,
    slope_hbm,
    mid_hbm,
    h_hbm,
    hidden_hbm,
    terms_hbm,
    dec_hbm,
    grad_half_hbm,
    mine_hbm,
    other_hbm,
    sums_ref,
    other_ref,
    grad_low_ref,
    dec_ref,
    rows_ref,
    grad_tconv_ref,
    terms_ref,
    upper_ref,
    grad_rows_ref,
    wgrad_ref,
    first_even,
    first_odd,
    act_even,
    act_odd,
    grad_even,
    grad_odd,
    conv_ref,
    normed_ref,
    slope_ref,
    held_ref,
    carry_ref,
    low_grad_ref,
    columns_ref,
    tconv_ref,
    conv_w,
    back_w,
    cot_ref,
    up_ref,
    down_ref,
    gate_ref,
    mid_ref,
    h_ref,
    hidden_ref,
    sems,
    load_sems,
    out_sems,
):
    grid = 8
    vox = 16
    chans = 128
    depth = depth_ref[0]
    count = (depth * (2 * vox * vox)).astype(jnp.float32)

    core = lax.rem(me_ref[0], 2)
    loads = fetch(
        [
            (joined_hbm, terms_ref.at[pl.ds(pl.multiple_of(core * 512, 512), 512)]),
            (joined_near_hbm, terms_ref.at[pl.ds(pl.multiple_of((1 - core) * 512, 512), 512)]),
            (cots_hbm[0].at[pl.ds(TOKEN_ROWS, FIELD_ROWS)], cot_ref.at[me_ref[0]]),
            (cots_hbm[1].at[pl.ds(TOKEN_ROWS, FIELD_ROWS)], cot_ref.at[jnp.bitwise_xor(me_ref[0], 1)]),
            (cots_hbm[2].at[pl.ds(TOKEN_ROWS, FIELD_ROWS)], cot_ref.at[jnp.bitwise_xor(me_ref[0], 2)]),
            (cots_hbm[3].at[pl.ds(TOKEN_ROWS, FIELD_ROWS)], cot_ref.at[jnp.bitwise_xor(me_ref[0], 3)]),
            (slope_hbm, gate_ref),
            (mid_hbm, mid_ref),
            (h_hbm, h_ref),
            (hidden_hbm, hidden_ref),
        ],
        sems.at[pl.ds(3, 10)],
    )
    hidden = up_ref.shape[1]
    loads += blocks.load(index_ref, pieces, 0, hidden, down_ref, load_sems)
    loads += blocks.load(index_ref, pieces, 0, 0, up_ref, load_sems.at[pl.ds(len(pieces), len(pieces))])
    dec_copy = pltpu.make_async_copy(dec_ref, dec_hbm, sems.at[0])

    for even in (first_even, act_even, grad_even):
        even[:, 0] = jnp.zeros((grid, vox, 4 * chans), LOW)
        even[:, vox + 1] = jnp.zeros((grid, vox, 4 * chans), LOW)
    for odd in (first_odd, act_odd, grad_odd):
        odd[:, 0] = jnp.zeros((grid + 1, vox, 4 * chans), LOW)
        odd[:, vox + 1] = jnp.zeros((grid + 1, vox, 4 * chans), LOW)
    wgrad_ref[:, 864:] = jnp.zeros((2, 32, chans), jnp.float32)
    low_grad_ref[:, 0] = jnp.zeros((grid, vox, 2 * chans), LOW)
    low_grad_ref[:, vox + 1] = jnp.zeros((grid, vox, 2 * chans), LOW)

    spot = lax.broadcasted_iota(jnp.int32, (1, 1, 8, 1), 2)

    def put_field(even, odd, at, value):
        left = value[..., :chans]
        right = value[..., chans:]
        flat = (2 * vox, 8, chans)
        before = pltpu.roll(right.reshape(flat), 1, 1).reshape(right.shape)
        after = pltpu.roll(left.reshape(flat), 7, 1).reshape(left.shape)
        before = jnp.where(spot == 0, 0.0, before)
        after = jnp.where(spot == 7, 0.0, after)
        window = jnp.concatenate([before, value, after], axis=3)
        even[at, 1 : vox + 1] = window.reshape(vox, 16, 4 * chans).astype(LOW)
        early = jnp.concatenate([carry_ref[...][:, None], window[:, :1]], axis=1)
        odd[at, 1 : vox + 1] = early.reshape(vox, 16, 4 * chans).astype(LOW)
        carry_ref[...] = window[:, 1]

    def open_field():
        carry_ref[...] = jnp.zeros(carry_ref.shape, jnp.float32)

    def close_field(odd):
        late = jnp.concatenate([carry_ref[...], jnp.zeros(carry_ref.shape, jnp.float32)], axis=1)
        odd[grid, 1 : vox + 1] = late.astype(LOW)

    def live_at(at):
        return (at < depth).astype(jnp.float32)

    def convolve(even, odd, weights, target, turned):
        def step(block, total):
            at = block * BATCH
            summed = None
            for deep in range(3):
                field = even if deep == 1 else odd
                start = at + 1 if deep == 2 else at
                for tall in range(3):
                    left = field[pl.ds(start, BATCH), tall : tall + vox]
                    left = left.reshape(BATCH * vox * 16, 4 * chans)
                    right = weights[deep * 3 + tall]
                    term = dot_last(left, right) if turned else dot(left, right)
                    summed = term if summed is None else summed + term
            target[pl.ds(at, BATCH)] = summed.reshape(BATCH, vox, 16, 2 * chans)
            return total

        lax.fori_loop(0, grid // BATCH, step, 0)

    def both(total):
        row = jnp.sum(total, axis=0, keepdims=True)
        half = (row[:, :chans] + row[:, chans:]) / count
        return jnp.concatenate([half, half], axis=1)

    def zero():
        return jnp.zeros((8, 2 * chans), jnp.float32)

    def fold(value):
        return jnp.sum(value.reshape(2 * vox, 8, 2 * chans), axis=0)

    def statistics(source):
        def first(at, total):
            return total + live_at(at) * fold(source[at])

        middle = both(lax.fori_loop(0, grid, first, zero()))

        def second(at, total):
            away = source[at] - middle
            return total + live_at(at) * fold(away * away)

        spread = both(lax.fori_loop(0, grid, second, zero()))
        return middle, lax.rsqrt(spread + 1e-05)

    for block in range(2):
        rows_ref[pl.ds(pl.multiple_of(block * 256 + core * 128, 128), 128)] = own_ref[block]
        rows_ref[pl.ds(pl.multiple_of(block * 256 + (1 - core) * 128, 128), 128)] = near_ref[block]
    loads[0].wait()
    loads[1].wait()
    make_tconv(terms_ref, place_ref[...], tconv_ref)
    for part in range(4):
        wide = dot(rows_ref[...], tconv_ref[:, part * 256 : (part + 1) * 256])
        held_ref[:, part * 4 : (part + 1) * 4] = wide.reshape(grid, 4, 16, 2 * chans)
    open_field()

    def place_first(at, state):
        tokens = held_ref[at] * live_at(at)
        offsets = [
            [tokens[8 * a + 4 * b : 8 * a + 4 * b + 4].reshape(8, 1, 1, 8, 256) for a in range(2)]
            for b in range(2)
        ]
        value = jnp.concatenate(
            [jnp.concatenate(offsets[b], axis=2) for b in range(2)], axis=1
        ).reshape(vox, 2, 8, 256)
        put_field(first_even, first_odd, at, value)
        return state

    lax.fori_loop(0, grid, place_first, 0)
    close_field(first_odd)

    for which in range(2):
        make_taps(terms_ref, place_ref[...], which, conv_w.at[which], back_w.at[which])
    convolve(first_even, first_odd, conv_w.at[0], normed_ref, False)
    middle, scale_one = statistics(normed_ref)
    open_field()

    def act_first(at, state):
        normed = (normed_ref[at] - middle) * scale_one
        normed_ref[at] = normed
        value, slope = gelu_and_slope(normed)
        live = live_at(at)
        slope_ref[at] = slope * live
        put_field(act_even, act_odd, at, (value * live).reshape(vox, 2, 8, 2 * chans))
        return state

    lax.fori_loop(0, grid, act_first, 0)
    close_field(act_odd)

    convolve(act_even, act_odd, conv_w.at[1], conv_ref, False)
    middle, scale_two = statistics(conv_ref)
    for load in loads[2:6]:
        load.wait()

    def act_second(at, totals):
        normed = (conv_ref[at] - middle) * scale_two
        conv_ref[at] = normed
        value, slope = gelu_and_slope(normed)
        live = live_at(at)
        low_value = (value * live).astype(LOW).reshape(vox * 16, 2 * chans)
        for e in range(2):
            shown = dot_last(low_value, select_ref[me_ref[0], e]).reshape(vox, 2, 8, 32)
            for a in range(2):
                dec_ref[2 * at + a, :, pl.ds(e, 8, stride=2), :] = shown[:, a]
        parts = [cot_ref[t, pl.ds(768 + at * vox * 8, vox * 8)] for t in range(4)]
        packed = jnp.concatenate(parts, axis=1)
        cot = jnp.concatenate(
            [dot(packed, spread_ref[a]).reshape(vox, 1, 8, 2 * chans) for a in range(2)], axis=1
        ).reshape(vox, 16, 2 * chans)
        grad = cot * slope * live
        held_ref[at] = grad
        return totals[0] + fold(grad), totals[1] + fold(grad * normed)

    totals = lax.fori_loop(0, grid, act_second, (zero(), zero()))
    dec_copy.start()

    def norm_back(source, normed_source, scale, sums):
        mean_grad = both(sums[0])
        mean_dot = both(sums[1])
        open_field()

        def step(at, state):
            grad = source[at] - live_at(at) * (mean_grad + normed_source[at] * mean_dot)
            grad = scale * grad
            low_grad_ref[at, 1 : vox + 1] = grad.astype(LOW)
            put_field(grad_even, grad_odd, at, grad.reshape(vox, 2, 8, 2 * chans))
            return state

        lax.fori_loop(0, grid, step, 0)
        close_field(grad_odd)

    def weight_grad(even, odd, which):
        own = select_ref[me_ref[0]].reshape(64, 2 * chans)
        for at in range(grid):
            shifts = [
                dot_last(own, low_grad_ref[at, 2 - tall : 18 - tall].reshape(vox * 16, 2 * chans))
                for tall in range(3)
            ]
            columns_ref[:, at * 256 : (at + 1) * 256] = jnp.concatenate(shifts, axis=0).astype(LOW)
        for deep in range(3):
            field = even if deep == 1 else odd
            start = 1 if deep == 2 else 0
            right = field[start : start + grid, 1 : vox + 1].reshape(grid * vox * 16, 4 * chans)
            sums = dot(columns_ref[...], right)
            for tall in range(3):
                for wide in range(3):
                    top = sums[tall * 64 : tall * 64 + 32, wide * chans : (wide + 1) * chans]
                    low = sums[tall * 64 + 32 : tall * 64 + 64, (wide + 1) * chans : (wide + 2) * chans]
                    tap = deep * 9 + tall * 3 + wide
                    wgrad_ref[which, tap * 32 : (tap + 1) * 32] = top + low

    norm_back(held_ref, conv_ref, scale_two, totals)
    weight_grad(act_even, act_odd, 1)
    convolve(grad_even, grad_odd, back_w.at[1], conv_ref, True)

    def slope_first(at, totals):
        grad = conv_ref[at] * slope_ref[at]
        conv_ref[at] = grad
        return totals[0] + fold(grad), totals[1] + fold(grad * normed_ref[at])

    totals = lax.fori_loop(0, grid, slope_first, (zero(), zero()))
    norm_back(conv_ref, normed_ref, scale_one, totals)
    weight_grad(first_even, first_odd, 0)
    convolve(grad_even, grad_odd, back_w.at[0], conv_ref, True)

    def rows_back(at, state):
        grad = (conv_ref[at] * live_at(at)).reshape(8, 2, 2, 8, 2 * chans)
        for a in range(2):
            for b in range(2):
                block = grad[:, b, a].reshape(64, 2 * chans).astype(LOW)
                column = (2 * a + b) * 256
                grad_tconv_ref[pl.ds(at * 64, 64), column : column + 256] = block
        return state

    lax.fori_loop(0, grid, rows_back, 0)
    for which in range(2):
        for block in range(7):
            at = (7 * which + block) * 128
            taps = wgrad_ref[which, block * 128 : (block + 1) * 128].T.astype(LOW)
            terms_ref[768:896, at : at + 128] = taps
    own = select_ref[me_ref[0]].reshape(64, 2 * chans)
    spans = [dot_last(grad_tconv_ref[:, at * 256 : (at + 1) * 256], own) for at in range(4)]
    mine = jnp.concatenate(spans, axis=1).astype(LOW)
    terms_ref[:768, 2 * hidden :] = contract_first(rows_ref[...], mine).astype(LOW)
    for t in range(4):
        at = slice(t * 128, (t + 1) * 128)
        tiles = [cot_ref[t, block * 128 : (block + 1) * 128] for block in range(6)]
        cot_rows = jnp.concatenate(tiles, axis=1).astype(jnp.float32)
        grad_rows_ref[at] = cot_rows + dot_last(grad_tconv_ref[at], tconv_ref[...])
    grad_low_ref[...] = grad_rows_ref[...].astype(LOW)
    halves = []
    for block in range(2):
        own = pl.ds(pl.multiple_of(block * 256 + core * 128, 128), 128)
        halves.append((grad_rows_ref.at[own], grad_half_hbm.at[block]))
    half_copies = fetch(halves, sems.at[pl.ds(1, 2)])
    for load in loads[6:]:
        load.wait()
    for copy in half_copies:
        copy.wait()
    sent = []
    gain = shift = 0.0
    for block in range(2):
        at = slice(block * 256, (block + 1) * 256)
        grad = dot(grad_low_ref[at], down_ref[...])
        upper = (grad * gate_ref[at].astype(jnp.float32)).astype(LOW)
        upper_ref[at] = upper
        grad_normed = dot_last(upper, up_ref[...])
        normed, _ = normalise(mid_ref[at])
        gain += jnp.sum(grad_normed * normed, axis=0, keepdims=True)
        shift += jnp.sum(grad_normed, axis=0, keepdims=True)
        grad_rows_ref[at] = grad_normed
        own = pl.ds(pl.multiple_of(block * 256 + core * 128, 128), 128)
        their = pl.ds(pl.multiple_of(block * 256 + (1 - core) * 128, 128), 128)
        other_ref[block] = grad_rows_ref[their].astype(LOW)
        sent += fetch(
            [(grad_rows_ref.at[own], mine_hbm.at[block]), (other_ref.at[block], other_hbm.at[block])],
            sems.at[pl.ds(3 + 2 * block, 2)],
        )
    sums_ref[...] = jnp.concatenate([gain, shift], axis=0)
    terms_ref[:768, :hidden] = contract_first(h_ref[...], upper_ref[...]).astype(LOW)
    terms_ref[:768, hidden : 2 * hidden] = contract_first(grad_low_ref[...], hidden_ref[...]).astype(LOW)
    for copy in sent + put_chunks(order_ref, terms_ref, (768, 128), terms_hbm, out_sems):
        copy.wait()
    dec_copy.wait()


def decoder(
    order, depth, me, own, near, joined, joined_near, select, spread, place, cots, slope, mid, h_rows, hidden, blocks
):
    f32 = jnp.float32
    vmem = pl.BlockSpec(memory_space=pltpu.VMEM)
    hbm = pl.BlockSpec(memory_space=pltpu.HBM)
    here = slope.shape[1]
    columns = 2 * here + 256
    window = lambda planes: pltpu.VMEM((planes, 18, 16, 512), LOW)
    field = lambda kind: pltpu.VMEM((8, 16, 16, 256), kind)
    kept = []

    def call(order, groups):
        shapes = chunk_shapes(groups, 896 // groups, columns)
        outs = pl.pallas_call(
            functools.partial(decoder_kernel, blocks),
            out_shape=(
                *shapes,
                jax.ShapeDtypeStruct((16, 16, 16, 32), f32),
                jax.ShapeDtypeStruct((2, 128, 768), f32),
                jax.ShapeDtypeStruct((2, 128, 768), f32),
                jax.ShapeDtypeStruct((2, 128, 768), LOW),
                jax.ShapeDtypeStruct((2, 768), f32),
            ),
            in_specs=[pl.BlockSpec(memory_space=pltpu.SMEM)] * 4
            + [vmem] * 2
            + [hbm] * 2
            + [vmem] * 3
            + [hbm] * 8
            + blocks.specs(),
            out_specs=[hbm] * (len(shapes) + 4) + [vmem],
            scratch_shapes=[
                pltpu.VMEM((2, 128, 768), LOW),
                pltpu.VMEM((512, 768), LOW),
                pltpu.VMEM((16, 16, 16, 32), f32),
                pltpu.VMEM((512, 768), LOW),
                pltpu.VMEM((512, 1024), LOW),
                pltpu.VMEM((1024, columns), LOW),
                pltpu.VMEM(slope.shape, LOW),
                pltpu.VMEM((512, 768), f32),
                pltpu.VMEM((2, 896, 128), f32),
                window(8),
                window(9),
                window(8),
                window(9),
                window(8),
                window(9),
                field(f32),
                field(f32),
                field(f32),
                field(f32),
                pltpu.VMEM((16, 8, 512), f32),
                pltpu.VMEM((8, 18, 16, 256), LOW),
                pltpu.VMEM((192, 2048), LOW),
                pltpu.VMEM((768, 1024), LOW),
                pltpu.VMEM((2, 9, 512, 256), LOW),
                pltpu.VMEM((2, 9, 256, 512), LOW),
                pltpu.VMEM((4, 1792, 128), LOW),
                pltpu.VMEM((768, here), LOW),
                pltpu.VMEM((768, here), LOW),
                pltpu.VMEM(slope.shape, LOW),
                pltpu.VMEM(mid.shape, f32),
                pltpu.VMEM(h_rows.shape, LOW),
                pltpu.VMEM(hidden.shape, LOW),
                pltpu.SemaphoreType.DMA((13,)),
                pltpu.SemaphoreType.DMA((2 * len(blocks.pieces),)),
                pltpu.SemaphoreType.DMA((2 * groups + 4,)),
            ],
            compiler_params=pltpu.CompilerParams(vmem_limit_bytes=VMEM_LIMIT),
            cost_estimate=cost(52),
        )(
            blocks.indices,
            order,
            depth,
            me,
            own,
            near,
            joined,
            joined_near,
            select,
            spread,
            place,
            *cots,
            slope,
            mid,
            h_rows,
            hidden,
            *blocks.pieces,
        )
        kept.extend(outs[len(shapes) :])
        return outs[: len(shapes)]

    terms = in_ring_order(call, order, (768, 128))
    dec, half, mine, other, sums = kept
    return dec, half, terms, mine, other, sums


def full_spec(count, space=pltpu.VMEM):
    return [pl.BlockSpec(memory_space=space)] * count


def fetch(pairs, sems):
    copies = [
        pltpu.make_async_copy(source, target, sems.at[at]) for at, (source, target) in enumerate(pairs)
    ]
    for copy in copies:
        copy.start()
    return copies


class Blocks:
    def __init__(self, indices, starts, pieces, size, sections, base=0):
        self.base = base
        block, columns = pieces[0].shape
        edges = [end for section in sections for end in section]
        if any(edge % 16 for edge in edges + list(starts)):
            full = jnp.zeros((size * block, columns), pieces[0].dtype)
            for at, (start, piece) in enumerate(zip(starts, pieces)):
                full = lax.dynamic_update_slice(full, piece, (indices[at] * block + start, 0))
            full = full.reshape(size, block, columns)
            parts = [full[:, low:high].reshape(-1, columns) for low, high in sections]
            pieces, starts, indices = [jnp.concatenate(parts)], [0], jnp.zeros((1,), jnp.int32)
            sections = [(size * low, size * high) for low, high in sections]
            size = 1
        self.indices = indices
        self.starts = tuple(starts)
        self.pieces = tuple(pieces)
        self.size = size
        self.sections = tuple(sections)

    def specs(self):
        return full_spec(len(self.pieces), pl.ANY)

    def rows(self, section):
        low, high = self.sections[section]
        return self.size * (high - low)

    def load(self, index_ref, refs, section, column, target, sems):
        low, high = self.sections[section]
        copies = []
        for at, (piece, start) in enumerate(zip(refs, self.starts)):
            first, last = max(low, start), min(high, start + piece.shape[0])
            if first >= last:
                continue
            row = index_ref[at] * (high - low) + first - low
            if len(self.pieces) > 1:
                row = pl.multiple_of(row, 16)
            columns = pl.ds(self.base + column, target.shape[1])
            source = piece.at[pl.ds(first - start, last - first), columns]
            copies += fetch([(source, target.at[pl.ds(row, last - first)])], sems.at[pl.ds(at, 1)])
        return copies


def pack_kernel(query_ref, key_ref, value_ref, out_ref, norm_ref, up_ref, down_ref, pack_ref):
    at = 0
    for value in (
        query_ref[...], key_ref[...], value_ref[...], out_ref[...].T, norm_ref[...].T, up_ref[...], down_ref[...],
    ):
        pack_ref[:, at : at + value.shape[1]] = value.astype(LOW)
        at += value.shape[1]


def pack_encoder(query, key, value, out, norms, up, down):
    part = query.shape[0]
    if part % 16:
        parts = (query, key, value, out.T, norms.T, up, down)
        return jnp.concatenate([array.astype(LOW) for array in parts], axis=1)
    return pl.pallas_call(
        pack_kernel,
        out_shape=jax.ShapeDtypeStruct((part, 4 * query.shape[1] + norms.shape[0] + 2 * up.shape[1]), LOW),
        in_specs=full_spec(7),
        out_specs=pl.BlockSpec(memory_space=pltpu.VMEM),
        cost_estimate=cost(2),
    )(query, key, value, out, norms, up, down)


def pack_own_kernel(tconv_ref, conv1_ref, conv2_ref, turn_ref, after_ref, pack_ref):
    part = tconv_ref.shape[0]
    conv_part = conv1_ref.shape[1]
    pack_ref[:part] = dot(tconv_ref[...].astype(LOW), turn_ref[...]).astype(LOW)
    taps = []
    for conv_ref in (conv1_ref, conv2_ref):
        taps += [conv_ref[tap] for tap in range(27)] + [jnp.zeros(conv_ref.shape[1:], jnp.float32)]
    for tile in range(14):
        made = jnp.concatenate(taps[4 * tile : 4 * tile + 4], axis=1).astype(LOW)
        at = part + tile // 2 * conv_part
        pack_ref[at : at + conv_part, tile % 2 * 128 : (tile % 2 + 1) * 128] = made


def turn_matrix():
    turn = np.zeros((32, 8, 8, 32), np.float32)
    for group in range(8):
        for chan in range(32):
            turn[chan, group, group, chan] = 1.0
    return turn.reshape(256, 256).astype(LOW)


def pack_own(tconv, conv1, conv2, after):
    part, conv_part = tconv.shape[0], conv1.shape[0]
    if part % 16 or conv_part % 16:
        conv = jnp.stack([conv1.astype(LOW), conv2.astype(LOW)], axis=1)
        conv = jnp.pad(conv, ((0, 0), (0, 0), (0, 1), (0, 0)))
        conv = conv.reshape(conv_part, 7, 256).transpose(1, 0, 2)
        turned = tconv.astype(LOW).reshape(part, 32, 8).transpose(0, 2, 1).reshape(part, -1)
        return jnp.concatenate([turned, conv.reshape(-1, 256)])
    return pl.pallas_call(
        pack_own_kernel,
        out_shape=jax.ShapeDtypeStruct((part + 7 * conv_part, 256), LOW),
        in_specs=full_spec(4) + full_spec(1, pl.ANY),
        out_specs=pl.BlockSpec(memory_space=pltpu.VMEM),
        cost_estimate=cost(2),
    )(tconv, conv1.transpose(1, 0, 2), conv2.transpose(1, 0, 2), jnp.asarray(turn_matrix()), after)


def fold_tconv(rows, columns):
    count = rows.shape[0]
    if count % 16:
        flat = rows.reshape(-1)
        flat = jnp.pad(flat, (0, -flat.shape[0] % columns))
        return flat.reshape(-1, columns)
    folded = rows.reshape(count // 16, 16, 256).transpose(1, 0, 2).reshape(16, -1)
    return jnp.pad(folded, ((0, 0), (0, columns - folded.shape[1])))


TOKEN_ROWS = 768
FIELD_ROWS = 1792
PACK_AT = TOKEN_ROWS + FIELD_ROWS


def pack_local_kernel(tokens_ref, cot_ref, field_ref, own_ref, pack_ref):
    for block in range(6):
        lanes = slice(block * 128, (block + 1) * 128)
        pack_ref[block * 128 : (block + 1) * 128] = tokens_ref[:, lanes]
        at = TOKEN_ROWS + block * 128
        pack_ref[at : at + 128] = cot_ref[:, lanes].astype(LOW)
    for pair in range(8):
        parts = [
            field_ref[2 * pair + a, :, pl.ds(e, 8, stride=2), :].reshape(128, 32)
            for a in range(2)
            for e in range(2)
        ]
        at = 2 * TOKEN_ROWS + pair * 128
        pack_ref[at : at + 128] = jnp.concatenate(parts, axis=1).astype(LOW)
    count = own_ref.shape[0]
    if count % 16 == 0:
        for half in range(2):
            at = PACK_AT + half * count
            pack_ref[at : at + count] = own_ref[:, half * 128 : (half + 1) * 128]


def pack_local(tokens, cot, field, own):
    aligned = own.shape[0] % 16 == 0
    total = PACK_AT + (2 * own.shape[0] if aligned else 0)
    pack = pl.pallas_call(
        pack_local_kernel,
        out_shape=jax.ShapeDtypeStruct((total, 128), LOW),
        in_specs=full_spec(4),
        out_specs=pl.BlockSpec(memory_space=pltpu.VMEM),
        compiler_params=pltpu.CompilerParams(vmem_limit_bytes=VMEM_LIMIT),
        cost_estimate=cost(3),
    )(tokens, cot, field, own)
    if aligned:
        return pack
    halves = own.reshape(-1, 2, 128).transpose(1, 0, 2).reshape(-1, 128)
    return jnp.concatenate([pack, halves])


def pack_pair_kernel(part, conv_part, chip_ref, own_hbm, far_hbm, after_ref, pack_ref, held_ref, sems):
    columns = pack_ref.shape[1]
    count = part + 7 * conv_part
    source = pl.ds(PACK_AT, 2 * count)
    for copy in fetch(
        [
            (own_hbm.at[source], held_ref.at[chip_ref[0]]),
            (far_hbm.at[source], held_ref.at[1 - chip_ref[0]]),
        ],
        sems,
    ):
        copy.wait()
    for which in range(2):
        for half in range(2):
            first = half * count
            at = which * conv_part
            for block in range(7):
                start = first + part + block * conv_part
                lanes = slice(block * 256 + half * 128, block * 256 + (half + 1) * 128)
                pack_ref[at : at + conv_part, lanes] = held_ref[which, start : start + conv_part]
            at = 2 * conv_part + which * 16
            for block in range(part // 16):
                start = first + block * 16
                lanes = slice(block * 256 + half * 128, block * 256 + (half + 1) * 128)
                pack_ref[at : at + 16, lanes] = held_ref[which, start : start + 16]
        at = 2 * conv_part + which * 16
        pack_ref[at : at + 16, part * 16 :] = jnp.zeros((16, columns - part * 16), LOW)


def pack_pair(chip, own, far, part, conv_part, after):
    columns = 7 * 256
    count = part + 7 * conv_part
    if part % 16 or conv_part % 16:
        own, far = [
            packed[PACK_AT:].reshape(2, count, 128).transpose(1, 0, 2).reshape(count, 256)
            for packed in (own, far)
        ]
        first = jnp.where(chip[0] > 0, far, own)
        second = jnp.where(chip[0] > 0, own, far)
        convs = [
            packed[part:].reshape(7, conv_part, 256).transpose(1, 0, 2).reshape(conv_part, columns)
            for packed in (first, second)
        ]
        pack = jnp.concatenate(convs + [fold_tconv(packed[:part], columns) for packed in (first, second)])
    else:
        pack = pl.pallas_call(
            functools.partial(pack_pair_kernel, part, conv_part),
            out_shape=jax.ShapeDtypeStruct((2 * conv_part + 32, columns), LOW),
            in_specs=full_spec(1, pltpu.SMEM) + full_spec(3, pl.ANY),
            out_specs=pl.BlockSpec(memory_space=pltpu.VMEM),
            scratch_shapes=[pltpu.VMEM((2, 2 * count, 128), LOW), pltpu.SemaphoreType.DMA((2,))],
            cost_estimate=cost(1.7),
        )(chip, own, far, after)
    fold = (pack.shape[0] - 2 * conv_part) // 2
    edges = [0, conv_part, 2 * conv_part, 2 * conv_part + fold, pack.shape[0]]
    return pack, list(zip(edges[:-1], edges[1:]))


def out_norm_kernel(blocks, norm_at, index_ref, *refs):
    count = len(blocks.pieces)
    pieces = refs[:count]
    out_ref, norm_ref, wide_ref, columns_ref, sems = refs[count:]
    span = out_ref.shape[1]
    copies = blocks.load(index_ref, pieces, 0, 4 * span - 256, wide_ref, sems)
    copies += blocks.load(index_ref, pieces, 0, norm_at, columns_ref, sems.at[pl.ds(count, count)])
    for copy in copies:
        copy.wait()
    out_ref[...] = wide_ref[:, 256 - span :]
    norm_ref[...] = columns_ref[...].astype(jnp.float32).T[:8]


def out_and_norms(blocks, span, norm_at):
    count = len(blocks.pieces)
    return pl.pallas_call(
        functools.partial(out_norm_kernel, blocks, norm_at),
        out_shape=(
            jax.ShapeDtypeStruct((blocks.rows(0), span), LOW),
            jax.ShapeDtypeStruct((8, blocks.rows(0)), jnp.float32),
        ),
        in_specs=full_spec(1, pltpu.SMEM) + blocks.specs(),
        out_specs=full_spec(2),
        scratch_shapes=[
            pltpu.VMEM((blocks.rows(0), 256), LOW),
            pltpu.VMEM((blocks.rows(0), 128), LOW),
            pltpu.SemaphoreType.DMA((2 * count,)),
        ],
        compiler_params=pltpu.CompilerParams(vmem_limit_bytes=VMEM_LIMIT),
        cost_estimate=cost(2.7),
    )(blocks.indices, *blocks.pieces)


def join_kernel(blocks, index_ref, *refs):
    count = len(blocks.pieces)
    join_ref, sems = refs[-2:]
    copies = []
    for section in range(4):
        target = join_ref.at[pl.ds(section * 128, 128)]
        copies += blocks.load(
            index_ref, refs[:count], section, 0, target, sems.at[pl.ds(section * count, count)]
        )
    for copy in copies:
        copy.wait()


def join_decoder(blocks, groups, part, after):
    columns = blocks.pieces[0].shape[1]
    count = len(blocks.pieces)
    if count == 1:
        full = blocks.pieces[0]
        parts = [full[low:high] for low, high in blocks.sections]
        folded = []
        for rows in parts[2:]:
            rows = rows.reshape(groups, -1)[:, : part * 256].reshape(-1, 256)
            folded += [fold_tconv(rows[at * 96 : (at + 1) * 96], columns) for at in range(8)]
        return jnp.concatenate(parts[:2] + folded)
    return pl.pallas_call(
        functools.partial(join_kernel, blocks),
        out_shape=jax.ShapeDtypeStruct((512, columns), LOW),
        in_specs=full_spec(1, pltpu.SMEM) + blocks.specs() + full_spec(1, pl.ANY),
        out_specs=pl.BlockSpec(memory_space=pltpu.VMEM),
        scratch_shapes=[pltpu.SemaphoreType.DMA((4 * count,))],
        compiler_params=pltpu.CompilerParams(vmem_limit_bytes=VMEM_LIMIT),
        cost_estimate=cost(3.8),
    )(blocks.indices, *blocks.pieces, after)


def pass_kernel(value_ref, *refs):
    refs[-1][...] = value_ref[...]


def passed(value, after):
    return pl.pallas_call(
        pass_kernel,
        out_shape=jax.ShapeDtypeStruct(value.shape, value.dtype),
        in_specs=full_spec(1) + full_spec(len(after), pl.ANY),
        out_specs=pl.BlockSpec(memory_space=pltpu.VMEM),
        cost_estimate=cost(1),
    )(value, *after)


def half_sum_kernel(mine_ref, near_ref, *refs):
    refs[-1][...] = (mine_ref[...] + near_ref[...].astype(jnp.float32)).astype(LOW)


def half_sum(mine, near, after):
    return pl.pallas_call(
        half_sum_kernel,
        out_shape=jax.ShapeDtypeStruct(mine.shape, LOW),
        in_specs=full_spec(2) + full_spec(len(after), pl.ANY),
        out_specs=pl.BlockSpec(memory_space=pltpu.VMEM),
        cost_estimate=cost(2),
    )(mine, near, *after)


def rows_sum_kernel(chip_ref, mid_ref, summed_ref, far_ref, after_ref, own_ref, low_ref, total_ref):
    for block in range(2):
        total = summed_ref[block].astype(jnp.float32) + far_ref[block].astype(jnp.float32)
        total_ref[block] = mid_ref[block] + total
        low_ref[block] = total_ref[block].astype(LOW)
    own_ref[...] = total_ref[chip_ref[0]]


def rows_sum(chip, mid, summed, far, after):
    return pl.pallas_call(
        rows_sum_kernel,
        out_shape=(
            jax.ShapeDtypeStruct(mid.shape[1:], jnp.float32),
            jax.ShapeDtypeStruct(mid.shape, LOW),
        ),
        in_specs=full_spec(1, pltpu.SMEM) + full_spec(3) + full_spec(1, pl.ANY),
        out_specs=full_spec(2),
        scratch_shapes=[pltpu.VMEM(mid.shape, jnp.float32)],
        cost_estimate=cost(2),
    )(chip, mid, summed, far, after)


def make_taps(joined, place, which_taps, conv_ref, back_ref):
    chans = 128
    none = jnp.zeros((chans, chans), LOW)
    for plane in range(9):
        conv_ref[plane, 3 * chans :, :chans] = none
        conv_ref[plane, :chans, chans:] = none
        back_ref[plane, :chans, 3 * chans :] = none
        back_ref[plane, chans:, :chans] = none
    for block in range(7):
        lanes = slice((7 * which_taps + block) * chans, (7 * which_taps + block + 1) * chans)
        wide = [joined[t % 2 * 512 + t // 2 * chans : t % 2 * 512 + (t // 2 + 1) * chans, lanes] for t in range(4)]
        made = dot(jnp.concatenate(wide, axis=1), place).astype(LOW)
        for part in range(4):
            tap = 4 * block + part
            if tap == 27:
                continue
            plane, deep = tap // 3, tap % 3
            turned = 2 - deep
            taps = made[:, part * chans : (part + 1) * chans]
            conv_ref[plane, deep * chans : (deep + 1) * chans, :chans] = taps
            conv_ref[plane, (deep + 1) * chans : (deep + 2) * chans, chans:] = taps
            back_ref[8 - plane, :chans, turned * chans : (turned + 1) * chans] = taps
            back_ref[8 - plane, chans:, (turned + 1) * chans : (turned + 2) * chans] = taps


def make_tconv(joined, place, tconv_ref):
    chans = 128
    for half in range(2):
        wide = []
        for t in range(4):
            rows = []
            for group in range(8):
                start = t % 2 * 512 + 256 + t // 2 * chans + group * 16
                for block in range(6):
                    at = block * 256 + half * chans
                    rows.append(joined[start : start + 16, at : at + chans])
            wide.append(jnp.concatenate(rows, axis=0))
        made = dot(jnp.concatenate(wide, axis=1), place)
        tconv_ref[:, half * 512 : (half + 1) * 512] = made.astype(LOW)


def normalise(rows):
    middle = jnp.mean(rows, axis=-1, keepdims=True)
    centred = rows - middle
    spread = jnp.mean(centred * centred, axis=-1, keepdims=True)
    scale = lax.rsqrt(spread + 1e-06)
    return centred * scale, scale


def attention_kernel(blocks, index_ref, depth_ref, me_ref, own_hbm, near_hbm, far_hbm, last_hbm, norm_ref, *refs):
    count = len(blocks.pieces)
    pieces = refs[:count]
    (
        out_ref, rows_hbm, h_hbm, qkv_hbm, probs_hbm,
        rows_ref, h_ref, qkv_ref, probs_ref, weight_ref, sems, load_sems, token_sems,
    ) = refs[-13:]
    patches = rows_ref.shape[0]
    heads = probs_ref.shape[0]
    span = heads * HD
    quarter = patches // 4
    tokens = []
    for flip, packed in enumerate((own_hbm, near_hbm, far_hbm, last_hbm)):
        start = pl.multiple_of(jnp.bitwise_xor(me_ref[0], flip) * quarter, quarter)
        for block in range(6):
            source = packed.at[pl.ds(block * 128, 128)]
            tokens.append((source, rows_ref.at[pl.ds(start, quarter), pl.ds(block * 128, 128)]))
    tokens = fetch(tokens, token_sems)
    loads = blocks.load(index_ref, pieces, 0, 0, weight_ref, load_sems)
    for copy in tokens:
        copy.wait()
    copies = fetch([(rows_ref, rows_hbm)], sems.at[pl.ds(1, 1)])
    norms = norm_ref[...]
    normed, _ = normalise(rows_ref[...].astype(jnp.float32))
    low_rows = (normed * norms[0:1] + norms[1:2]).astype(LOW)
    h_ref[...] = low_rows
    copies += fetch([(h_ref, h_hbm)], sems.at[pl.ds(2, 1)])
    for load in loads:
        load.wait()
    qkv_ref[...] = dot(low_rows, weight_ref[:, : 3 * span]).astype(LOW)
    copies += fetch([(qkv_ref, qkv_hbm)], sems.at[pl.ds(3, 1)])
    key_at = lax.broadcasted_iota(jnp.int32, (1, patches), 1)
    live = key_at < depth_ref[0] * (GRID * GRID)
    outs = []
    for head in range(heads):
        query = qkv_ref[:, head * HD : (head + 1) * HD]
        keys = qkv_ref[:, span + head * HD : span + (head + 1) * HD]
        values = qkv_ref[:, 2 * span + head * HD : 2 * span + (head + 1) * HD]
        scores = jnp.where(live, dot_last(query, keys) * HD ** (-0.5), -1000000000.0)
        expo = jnp.exp(scores - jnp.max(scores, axis=-1, keepdims=True))
        probs = (expo * (1.0 / jnp.sum(expo, axis=-1, keepdims=True))).astype(LOW)
        probs_ref[head] = probs
        copies += fetch([(probs_ref.at[head], probs_hbm.at[head])], sems.at[pl.ds(4 + head, 1)])
        outs.append(dot(probs, values))
    out_ref[...] = jnp.concatenate(outs, axis=1).astype(LOW)
    for copy in copies:
        copy.wait()


def attention(depth, me, rows, blocks, norms, heads, after):
    patches, width = 512, TOKEN_ROWS
    shapes = ((patches, width), (patches, width), (patches, 3 * heads * HD), (heads, patches, patches))
    count = len(blocks.pieces)
    return pl.pallas_call(
        functools.partial(attention_kernel, blocks),
        out_shape=tuple(
            jax.ShapeDtypeStruct(shape, LOW) for shape in ((patches, heads * HD),) + shapes
        ),
        in_specs=full_spec(3, pltpu.SMEM)
        + full_spec(4, pl.ANY)
        + full_spec(1)
        + blocks.specs()
        + full_spec(len(after), pl.ANY),
        out_specs=full_spec(1) + full_spec(4, pltpu.HBM),
        scratch_shapes=[pltpu.VMEM(shape, LOW) for shape in shapes]
        + [
            pltpu.VMEM((width, 4 * heads * HD), LOW),
            pltpu.SemaphoreType.DMA((4 + heads,)),
            pltpu.SemaphoreType.DMA((count,)),
            pltpu.SemaphoreType.DMA((24,)),
        ],
        compiler_params=pltpu.CompilerParams(vmem_limit_bytes=VMEM_LIMIT),
        cost_estimate=cost(7),
    )(blocks.indices, depth, me, *rows, norms, *blocks.pieces, *after)


def mlp_kernel(
    blocks, index_ref, core_ref, rows_hbm, out0, out1, out2, out3, w0, w1, w2, w3, norm_ref, *refs
):
    count = len(blocks.pieces)
    pieces = refs[:count]
    (
        mine_hbm, other_hbm, mid_hbm, mid_half_hbm, h_hbm, hidden_hbm, slope_hbm,
        partial_ref, rows_ref, weight_ref, mid_ref, h_ref, hidden_ref, slope_ref, other_ref,
        outs_ref, out_weights_ref, sems, load_sems, in_sems,
    ) = refs[-20:]
    hidden_here = hidden_ref.shape[1]
    core = core_ref[0]
    norms = norm_ref[...]
    loads = fetch([(rows_hbm, rows_ref)], sems)
    ins = fetch(
        [(out, outs_ref.at[at]) for at, out in enumerate((out0, out1, out2, out3))]
        + [(w, out_weights_ref.at[at]) for at, w in enumerate((w0, w1, w2, w3))],
        in_sems,
    )
    loads += blocks.load(index_ref, pieces, 0, 0, weight_ref, load_sems)
    loads[0].wait()
    for load in ins:
        load.wait()
    copies = []
    for block in range(2):
        at = slice(block * 256, (block + 1) * 256)
        mid = rows_ref[at].astype(jnp.float32)
        attended = jnp.concatenate([outs_ref[t, at] for t in range(4)], axis=1)
        weights = jnp.concatenate([out_weights_ref[t] for t in range(4)], axis=1)
        mid = mid + dot_last(attended, weights)
        mid_ref[at] = mid
        normed, _ = normalise(mid)
        low_rows = (normed * norms[2:3] + norms[3:4]).astype(LOW)
        h_ref[at] = low_rows
        if block == 0:
            for load in loads[1:]:
                load.wait()
        value, slope = gelu_and_slope(dot(low_rows, weight_ref[:, :hidden_here]))
        hidden = value.astype(LOW)
        hidden_ref[at] = hidden
        slope_ref[at] = slope.astype(LOW)
        partial_ref[at] = dot_last(hidden, weight_ref[:, hidden_here : 2 * hidden_here])
        own = pl.ds(pl.multiple_of(block * 256 + core * 128, 128), 128)
        their = pl.ds(pl.multiple_of(block * 256 + (1 - core) * 128, 128), 128)
        other_ref[block] = partial_ref[their].astype(LOW)
        rows = pl.ds(block * 256, 256)
        copies += fetch(
            [
                (other_ref.at[block], other_hbm.at[block]),
                (partial_ref.at[own], mine_hbm.at[block]),
                (mid_ref.at[own], mid_half_hbm.at[block]),
                (mid_ref.at[rows], mid_hbm.at[rows]),
                (h_ref.at[rows], h_hbm.at[rows]),
                (hidden_ref.at[rows], hidden_hbm.at[rows]),
                (slope_ref.at[rows], slope_hbm.at[rows]),
            ],
            sems.at[pl.ds(1 + 7 * block, 7)],
        )
    for copy in copies:
        copy.wait()


def mlp(core, rows, outs, out_weights, norms, blocks, hidden_here, after):
    patches, width = rows.shape
    f32 = jnp.float32
    half = (2, patches // 4, width)
    return pl.pallas_call(
        functools.partial(mlp_kernel, blocks),
        out_shape=(
            jax.ShapeDtypeStruct(half, f32),
            jax.ShapeDtypeStruct(half, LOW),
            jax.ShapeDtypeStruct((patches, width), f32),
            jax.ShapeDtypeStruct(half, f32),
            jax.ShapeDtypeStruct((patches, width), LOW),
            jax.ShapeDtypeStruct((patches, hidden_here), LOW),
            jax.ShapeDtypeStruct((patches, hidden_here), LOW),
        ),
        in_specs=full_spec(2, pltpu.SMEM)
        + full_spec(9, pltpu.HBM)
        + full_spec(1)
        + blocks.specs()
        + full_spec(len(after), pl.ANY),
        out_specs=full_spec(7, pltpu.HBM),
        scratch_shapes=[
            pltpu.VMEM((patches, width), f32),
            pltpu.VMEM((patches, width), LOW),
            pltpu.VMEM((width, 2 * hidden_here), LOW),
            pltpu.VMEM((patches, width), f32),
            pltpu.VMEM((patches, width), LOW),
            pltpu.VMEM((patches, hidden_here), LOW),
            pltpu.VMEM((patches, hidden_here), LOW),
            pltpu.VMEM(half, LOW),
            pltpu.VMEM((4,) + outs[0].shape, LOW),
            pltpu.VMEM((4,) + out_weights[0].shape, LOW),
            pltpu.SemaphoreType.DMA((15,)),
            pltpu.SemaphoreType.DMA((len(blocks.pieces),)),
            pltpu.SemaphoreType.DMA((8,)),
        ],
        compiler_params=pltpu.CompilerParams(vmem_limit_bytes=VMEM_LIMIT),
        cost_estimate=cost(9.3),
    )(blocks.indices, core, rows, *outs, *out_weights, norms, *blocks.pieces, *after)


def split_row(rows):
    return rows // 2 if rows % 16 else rows // 32 * 16


def put_chunks(index_ref, source, parts, targets, sems):
    target = targets[0]
    groups = target.shape[0]
    cut = split_row(target.shape[1])
    pairs, start, first = [], 0, 0
    for height in parts:
        rows = height // groups
        for at in range(groups):
            row = first if groups == 1 else pl.multiple_of(first + index_ref[at] * rows, 16)
            pairs.append((source.at[pl.ds(row, rows)], target.at[at, pl.ds(start, rows)]))
            if groups > 1 and at == groups - 1:
                for far, low, high in ((targets[1], 0, cut), (targets[2], cut, target.shape[1])):
                    begin, end = max(low, start), min(high, start + rows)
                    if begin < end:
                        taken = source.at[pl.ds(row + begin - start, end - begin)]
                        pairs.append((taken, far.at[pl.ds(begin - low, end - begin)]))
        start += rows
        first += height
    return fetch(pairs, sems)


def chunk_shapes(groups, rows, columns):
    cut = split_row(rows)
    shapes = [(groups, rows, columns)]
    if groups > 1:
        shapes += [(cut, columns), (rows - cut, columns)]
    return [jax.ShapeDtypeStruct(shape, LOW) for shape in shapes]


def in_ring_order(call, indices, parts):
    groups = indices.shape[0]
    if groups % 2 == 0 and all(rows // groups % 16 == 0 for rows in parts):
        return call(indices, groups)
    flat = call(jnp.zeros((1,), jnp.int32), 1)[0][0]
    blocks, start = [], 0
    for rows in parts:
        blocks.append(flat[start : start + rows].reshape(groups, rows // groups, -1)[indices])
        start += rows
    terms = jnp.concatenate(blocks, axis=1)
    cut = split_row(terms.shape[1])
    return terms, terms[-1, :cut], terms[-1, cut:]


def ring_add_kernel(above, below, cut, one_ref, two_ref, terms_hbm, *refs):
    ahead_ref, behind_ref, sems = refs[-3:]
    rows = ahead_ref.shape[0]
    for copy in fetch([(terms_hbm.at[above], ahead_ref), (terms_hbm.at[below], behind_ref)], sems):
        copy.wait()
    ahead = slice(0, cut) if one_ref.shape[0] < rows else slice(0, rows)
    behind = slice(cut, rows) if one_ref.shape[0] < rows else slice(0, rows)
    for target, at, came in ((ahead_ref, ahead, one_ref), (behind_ref, behind, two_ref)):
        target[at] = (target[at].astype(jnp.float32) + came[...].astype(jnp.float32)).astype(LOW)


def ring_add(one, two, terms, above, below, after, own_kernel):
    rows, columns = terms.shape[1:]
    cut = split_row(rows)
    if rows % 16 or not own_kernel:
        if after:
            one, two, _ = lax.optimization_barrier((one, two, after))
        above, below = terms[above], terms[below]
        if one.shape[0] == rows:
            return above + one, below + two
        return (
            jnp.concatenate([above[:cut] + one, above[cut:]]),
            jnp.concatenate([below[:cut], below[cut:] + two]),
        )
    return pl.pallas_call(
        functools.partial(ring_add_kernel, above, below, cut),
        out_shape=(jax.ShapeDtypeStruct((rows, columns), LOW),) * 2,
        in_specs=full_spec(2) + full_spec(1 + len(after), pl.ANY),
        out_specs=full_spec(2),
        scratch_shapes=[pltpu.SemaphoreType.DMA((2,))],
        compiler_params=pltpu.CompilerParams(vmem_limit_bytes=VMEM_LIMIT),
        cost_estimate=cost(2),
    )(one, two, terms, *after)


def mlp_sum_kernel(ahead_ref, behind_ref, own_ref, turn_ref, *refs):
    up_ref, down_ref, tconv_ref, conv1_ref, conv2_ref = refs[-5:]
    part, hidden = up_ref.shape
    total = (
        own_ref[0].astype(jnp.float32)
        + ahead_ref[...].astype(jnp.float32)
        + behind_ref[...].astype(jnp.float32)
    )
    up_ref[...] = total[:part, :hidden]
    down_ref[...] = total[:part, hidden : 2 * hidden]
    tconv_ref[...] = dot(total[:part, 2 * hidden :].astype(LOW), turn_ref[...])
    for which, conv_ref in enumerate((conv1_ref, conv2_ref)):
        for tap in range(27):
            at = which * 896 + tap * 32
            conv_ref[tap] = total[part:, at : at + 32]


def mlp_sum(ahead, behind, terms, part, hidden, after):
    rows, columns = ahead.shape
    conv_part = rows - part
    f32 = jnp.float32
    if part % 16 or conv_part % 16:
        total = terms[0].astype(f32) + ahead.astype(f32) + behind.astype(f32)
        tconv = total[:part, 2 * hidden :].reshape(part, 8, -1).transpose(0, 2, 1).reshape(part, -1)
        conv = total[part:].reshape(conv_part, 2, 28, 32)[:, :, :27].transpose(1, 2, 0, 3)
        return total[:part, :hidden], total[:part, hidden : 2 * hidden], tconv, conv[0], conv[1]
    return pl.pallas_call(
        mlp_sum_kernel,
        out_shape=(
            jax.ShapeDtypeStruct((part, hidden), f32),
            jax.ShapeDtypeStruct((part, hidden), f32),
            jax.ShapeDtypeStruct((part, 256), f32),
            jax.ShapeDtypeStruct((27, conv_part, 32), f32),
            jax.ShapeDtypeStruct((27, conv_part, 32), f32),
        ),
        in_specs=full_spec(2)
        + [pl.BlockSpec((1,) + terms.shape[1:], lambda at: (0, 0, 0))]
        + full_spec(1)
        + full_spec(len(after), pl.ANY),
        out_specs=full_spec(5),
        grid=(1,),
        compiler_params=pltpu.CompilerParams(vmem_limit_bytes=VMEM_LIMIT),
        cost_estimate=cost(2.4),
    )(ahead, behind, terms, jnp.asarray(turn_matrix().T), *after)


def norm_back_kernel(chip_ref, sum_ref, far_ref, grad_hbm, rows_hbm, norm_ref, *refs):
    own_ref, low_ref, grad_ref, rows_ref, sems = refs[-5:]
    for copy in fetch([(grad_hbm, grad_ref), (rows_hbm, rows_ref)], sems):
        copy.wait()
    gain = norm_ref[2:3]
    for block in range(2):
        summed = sum_ref[block].astype(jnp.float32) + far_ref[block].astype(jnp.float32)
        normed, scale = normalise(rows_ref[block])
        grad = grad_ref[block] + layer_norm_back(summed * gain, normed, scale)
        grad_ref[block] = grad
        low_ref[block] = grad.astype(LOW)
    own_ref[...] = grad_ref[chip_ref[0]]


def norm_back(chip, summed, far, grad, rows, norms, after):
    return pl.pallas_call(
        norm_back_kernel,
        out_shape=(
            jax.ShapeDtypeStruct(grad.shape[1:], jnp.float32),
            jax.ShapeDtypeStruct(grad.shape, LOW),
        ),
        in_specs=full_spec(1, pltpu.SMEM)
        + full_spec(2)
        + full_spec(2, pltpu.HBM)
        + full_spec(1)
        + full_spec(len(after), pl.ANY),
        out_specs=full_spec(2),
        scratch_shapes=[
            pltpu.VMEM(grad.shape, jnp.float32),
            pltpu.VMEM(rows.shape, jnp.float32),
            pltpu.SemaphoreType.DMA((2,)),
        ],
        compiler_params=pltpu.CompilerParams(vmem_limit_bytes=VMEM_LIMIT),
        cost_estimate=cost(4),
    )(chip, summed, far, grad, rows, norms, *after)


def attention_back_kernel(
    blocks, index_ref, core_ref, own_hbm, near_hbm, qkv_hbm, probs_hbm, rows_hbm, *refs
):
    count = len(blocks.pieces)
    pieces = refs[:count]
    (
        mine_hbm, other_hbm, grad_qkv_hbm, grad_hbm, sums_ref, grad_qkv_ref, grad_ref, partial_ref, other_ref,
        out_weight_ref, weight_ref, qkv_ref, probs_ref, rows_ref, sems, out_sems, load_sems,
    ) = refs[-17:]
    heads = probs_ref.shape[0]
    span = heads * HD
    core = core_ref[0]
    halves = []
    for block in range(2):
        own = pl.ds(pl.multiple_of(block * 256 + core * 128, 128), 128)
        their = pl.ds(pl.multiple_of(block * 256 + (1 - core) * 128, 128), 128)
        halves += [(own_hbm.at[block], grad_ref.at[own]), (near_hbm.at[block], grad_ref.at[their])]
    halves = fetch(halves, sems)
    outs = blocks.load(index_ref, pieces, 0, 4 * span - 256, out_weight_ref, load_sems)
    copies = fetch(
        [(qkv_hbm, qkv_ref)]
        + [(probs_hbm.at[head], probs_ref.at[head]) for head in range(heads)]
        + [(rows_hbm, rows_ref)],
        sems.at[pl.ds(4, 2 + heads)],
    )
    loads = blocks.load(index_ref, pieces, 0, 0, weight_ref, load_sems.at[pl.ds(count, count)])
    for copy in halves + outs:
        copy.wait()
    sent = fetch([(grad_ref, grad_hbm)], out_sems)
    grad_out = dot(grad_ref[...], out_weight_ref[:, 256 - span :]).astype(LOW)
    copies[0].wait()
    grad_query, grad_keys, grad_values = [], [], []
    for head in range(heads):
        query = qkv_ref[:, head * HD : (head + 1) * HD]
        keys = qkv_ref[:, span + head * HD : span + (head + 1) * HD]
        values = qkv_ref[:, 2 * span + head * HD : 2 * span + (head + 1) * HD]
        grad_head = grad_out[:, head * HD : (head + 1) * HD]
        copies[1 + head].wait()
        probs = probs_ref[head]
        grad_values.append(contract_first(probs, grad_head))
        probs = probs.astype(jnp.float32)
        grad_probs = dot_last(grad_head, values)
        inner = jnp.sum(probs * grad_probs, axis=-1, keepdims=True)
        grad_scores = (probs * (grad_probs - inner)).astype(LOW)
        grad_query.append(dot(grad_scores, keys) * HD ** (-0.5))
        grad_keys.append(contract_first(grad_scores, query) * HD ** (-0.5))
    grad_qkv = jnp.concatenate(grad_query + grad_keys + grad_values, axis=1).astype(LOW)
    grad_qkv_ref[...] = grad_qkv
    sent += fetch([(grad_qkv_ref, grad_qkv_hbm)], out_sems.at[pl.ds(1, 1)])
    for load in loads:
        load.wait()
    partial_ref[...] = dot_last(grad_qkv, weight_ref[:, : 3 * span])
    pairs = []
    for block in range(2):
        own = pl.ds(pl.multiple_of(block * 256 + core * 128, 128), 128)
        their = pl.ds(pl.multiple_of(block * 256 + (1 - core) * 128, 128), 128)
        other_ref[block] = partial_ref[their].astype(LOW)
        pairs += [(partial_ref.at[own], mine_hbm.at[block]), (other_ref.at[block], other_hbm.at[block])]
    sent += fetch(pairs, out_sems.at[pl.ds(2, 4)])
    copies[1 + heads].wait()
    gain = shift = 0.0
    for block in range(2):
        at = slice(block * 256, (block + 1) * 256)
        normed, _ = normalise(rows_ref[at].astype(jnp.float32))
        gain += jnp.sum(partial_ref[at] * normed, axis=0, keepdims=True)
        shift += jnp.sum(partial_ref[at], axis=0, keepdims=True)
    sums_ref[...] = jnp.concatenate([gain, shift], axis=0)
    for copy in sent:
        copy.wait()


def attention_back(core, own, near, blocks, qkv, probs, rows, after):
    patches, width = rows.shape
    f32 = jnp.float32
    half = (2, patches // 4, width)
    return pl.pallas_call(
        functools.partial(attention_back_kernel, blocks),
        out_shape=(
            jax.ShapeDtypeStruct(half, f32),
            jax.ShapeDtypeStruct(half, LOW),
            jax.ShapeDtypeStruct(qkv.shape, LOW),
            jax.ShapeDtypeStruct((patches, width), LOW),
            jax.ShapeDtypeStruct((2, width), f32),
        ),
        in_specs=full_spec(2, pltpu.SMEM)
        + full_spec(5, pltpu.HBM)
        + blocks.specs()
        + full_spec(len(after), pl.ANY),
        out_specs=full_spec(4, pltpu.HBM) + full_spec(1),
        scratch_shapes=[
            pltpu.VMEM(qkv.shape, LOW),
            pltpu.VMEM((patches, width), LOW),
            pltpu.VMEM((patches, width), f32),
            pltpu.VMEM(half, LOW),
            pltpu.VMEM((width, 256), LOW),
            pltpu.VMEM((width, 4 * qkv.shape[1] // 3), LOW),
            pltpu.VMEM(qkv.shape, LOW),
            pltpu.VMEM(probs.shape, LOW),
            pltpu.VMEM(rows.shape, LOW),
            pltpu.SemaphoreType.DMA((6 + probs.shape[0],)),
            pltpu.SemaphoreType.DMA((6,)),
            pltpu.SemaphoreType.DMA((2 * len(blocks.pieces),)),
        ],
        compiler_params=pltpu.CompilerParams(vmem_limit_bytes=VMEM_LIMIT),
        cost_estimate=cost(9),
    )(blocks.indices, core, own, near, qkv, probs, rows, *blocks.pieces, *after)


def attention_weights_kernel(targets, order_ref, h_ref, out_ref, grad_qkv_ref, grad_ref, first_ref, second_ref, *refs):
    pack_ref, out_sems = refs[-2:]
    span = out_ref.shape[1]
    none = jnp.zeros((124, h_ref.shape[1]), jnp.float32)
    stacked = jnp.concatenate([first_ref[...], second_ref[...], none], axis=0)
    pack_ref[:, 4 * span :] = stacked.T.astype(LOW)
    pack_ref[:, : 3 * span] = contract_first(h_ref[...], grad_qkv_ref[...]).astype(LOW)
    pack_ref[:, 3 * span : 4 * span] = contract_first(grad_ref[...], out_ref[...]).astype(LOW)
    for copy in put_chunks(order_ref, pack_ref, (pack_ref.shape[0],), refs[len(refs) - 2 - targets : -2], out_sems):
        copy.wait()


def attention_weights(order, h_rows, out, grad_qkv, grad, first, second, after):
    width = h_rows.shape[1]
    columns = 4 * out.shape[1] + 128

    def call(order, groups):
        shapes = chunk_shapes(groups, width // groups, columns)
        return pl.pallas_call(
            functools.partial(attention_weights_kernel, len(shapes)),
            out_shape=tuple(shapes),
            in_specs=full_spec(1, pltpu.SMEM) + full_spec(6) + full_spec(len(after), pl.ANY),
            out_specs=full_spec(len(shapes), pltpu.HBM),
            scratch_shapes=[pltpu.VMEM((width, columns), LOW), pltpu.SemaphoreType.DMA((groups + 2,))],
            compiler_params=pltpu.CompilerParams(vmem_limit_bytes=VMEM_LIMIT),
            cost_estimate=cost(4),
        )(order, h_rows, out, grad_qkv, grad, first, second, *after)

    return in_ring_order(call, order, (width,))


def attention_sum_kernel(ahead_ref, behind_ref, own_ref, after_ref, query_ref, key_ref, value_ref, out_ref):
    span = query_ref.shape[1]
    total = (
        own_ref[0].astype(jnp.float32)
        + ahead_ref[...].astype(jnp.float32)
        + behind_ref[...].astype(jnp.float32)
    )
    query_ref[...] = total[:, :span]
    key_ref[...] = total[:, span : 2 * span]
    value_ref[...] = total[:, 2 * span : 3 * span]
    out_ref[...] = total[:, 3 * span : 4 * span].T


def attention_sum(ahead, behind, terms, span, after):
    part = ahead.shape[0]
    f32 = jnp.float32
    if part % 16:
        total = terms[0].astype(f32) + ahead.astype(f32) + behind.astype(f32)
        parts = [total[:, at * span : (at + 1) * span] for at in range(4)]
        return parts[0], parts[1], parts[2], parts[3].T
    return pl.pallas_call(
        attention_sum_kernel,
        out_shape=(jax.ShapeDtypeStruct((part, span), f32),) * 3
        + (jax.ShapeDtypeStruct((span, part), f32),),
        in_specs=full_spec(2)
        + [pl.BlockSpec((1,) + terms.shape[1:], lambda at: (0, 0, 0))]
        + full_spec(1, pl.ANY),
        out_specs=full_spec(4),
        grid=(1,),
        cost_estimate=cost(2),
    )(ahead, behind, terms, after)


class Ring:
    def __init__(self, size):
        self.size = size
        order = ring_order(size)
        self.ahead = [(order[i], order[(i + 1) % size]) for i in range(size)]
        self.behind = [(b, a) for a, b in self.ahead]
        reach = (size - 1) // 2
        self.distances = [0]
        for step in range(1, reach + 1):
            self.distances += [-step, step]
        if size % 2 == 0:
            self.distances.append(size // 2)
        table = np.array(
            [
                [order[(order.index(me) + distance) % size] for distance in self.distances]
                for me in range(size)
            ],
            np.int32,
        )
        self.indices = jnp.asarray(table)[lax.axis_index("dp")]

    def send(self, value, forward):
        return lax.ppermute(value, "dp", self.ahead if forward else self.behind)

    def gather(self, array):
        return Gather(self, array)

    def scatter(self, blocks):
        return Scatter(self, *blocks)


class Scatter:
    def __init__(self, ring, terms, far_one, far_two):
        self.ring = ring
        self.terms = terms
        self.far = far_one, far_two
        self.place = {distance: at for at, distance in enumerate(ring.distances)}
        self.reach = (ring.size - 1) // 2
        self.one = self.two = None
        self.left = self.reach + 1 if ring.size % 2 == 0 else self.reach

    def add(self, *after, own_kernel=False):
        distance = self.left
        if distance > self.reach:
            self.one, self.two = self.far
        elif self.one is None:
            self.one, self.two = self.terms[self.place[distance]], self.terms[self.place[-distance]]
        else:
            self.one, self.two = ring_add(
                self.one, self.two, self.terms, self.place[distance], self.place[-distance], after, own_kernel
            )
        return self.one, self.two

    def send(self, *after):
        one, two = self.one, self.two
        if after:
            one, two, _ = lax.optimization_barrier((one, two, after))
        self.one, self.two = self.ring.send(one, True), self.ring.send(two, False)
        self.left -= 1

    def result(self):
        while self.left > 0:
            self.add()
            self.send()
        if self.one is None:
            return jnp.zeros_like(self.terms[0]), jnp.zeros_like(self.terms[0])
        if self.one.shape[0] < self.terms.shape[1]:
            return jnp.concatenate([self.one, self.two]), jnp.zeros_like(self.terms[0])
        return self.one, self.two


class Gather:
    def __init__(self, ring, array):
        self.ring = ring
        self.array = array
        self.one = self.two = array
        self.starts = [0]
        self.pieces = [array]
        self.done = 0
        self.last = ()

    def step(self, *after):
        size = self.ring.size
        self.done += 1
        if after:
            self.one, self.two, _ = lax.optimization_barrier((self.one, self.two, after))
        if self.done <= (size - 1) // 2:
            self.one = self.ring.send(self.one, True)
            self.two = self.ring.send(self.two, False)
            self.starts += [0, 0]
        else:
            rows = self.array.shape[0]
            half = rows // 2 if rows % 16 else rows // 32 * 16
            self.last = self.one[:half], self.two[half:]
            self.one = self.ring.send(self.last[0], True)
            self.two = self.ring.send(self.last[1], False)
            self.starts += [0, half]
        self.pieces += [self.one, self.two]

    def steps_left(self):
        return self.ring.size // 2 - self.done

    def blocks(self, sections, base=0):
        indices = self.ring.indices
        if self.ring.size % 2 == 0:
            indices = jnp.concatenate([indices, indices[-1:]])
        return Blocks(indices, self.starts, self.pieces, self.ring.size, sections, base)


class Quad:
    def __init__(self):
        self.me = lax.axis_index("tensor")
        self.core = self.me % 2
        self.chip = self.me // 2

    def over_core(self, value):
        return lax.ppermute(value, "tensor", [(i, i ^ 1) for i in range(4)])

    def over_chip(self, value):
        return lax.ppermute(value, "tensor", [(i, i ^ 2) for i in range(4)])

    def spread(self, block):
        far = self.over_chip(block)
        return block, self.over_core(block), far, self.over_core(far)

    def spread_direct(self, block):
        last = lax.ppermute(block, "tensor", [(i, i ^ 3) for i in range(4)])
        return block, self.over_core(block), self.over_chip(block), last

    def pick(self, half):
        return jnp.where(self.chip == 0, half[0], half[1])


def selections(chans, chans_here):
    own = np.zeros((4, 2, chans_here, 2, chans), np.float32)
    spread = np.zeros((2, 4, 2, 2, chans_here, 2, chans), np.float32)
    place = np.zeros((4, 4, chans_here, 4, 4, chans_here), np.float32)
    for t in range(4):
        for c in range(chans_here):
            for e in range(2):
                own[t, e, c, e, t * chans_here + c] = 1.0
                for a in range(2):
                    spread[a, t, a, e, c, e, t * chans_here + c] = 1.0
            for group in range(4):
                place[t, group, c, group, t, c] = 1.0
    own = own.reshape(4, 2, chans_here, 2 * chans).astype(LOW)
    spread = spread.reshape(2, 16 * chans_here, 2 * chans).astype(LOW)
    place = place.reshape(16 * chans_here, 16 * chans_here).astype(LOW)
    return jnp.asarray(own), jnp.asarray(spread), jnp.asarray(place)


def shards(
    tokens,
    crop_depth,
    w_query,
    w_key,
    w_value,
    w_out,
    w_up,
    w_down,
    w_tconv,
    w_conv1,
    w_conv2,
    ln1_gain,
    ln1_bias,
    ln2_gain,
    ln2_bias,
    cot_out,
    cot_dec,
    groups,
):
    ring = Ring(groups)
    quad = Quad()
    grid = GRID
    vox = 2 * grid
    patches = grid**3
    width = w_query.shape[0] * groups
    part = w_query.shape[0]
    heads_here = w_query.shape[1] // HD
    span = heads_here * HD
    chans = w_conv1.shape[0] * groups
    chans_here = w_conv1.shape[2]

    low = lambda value: value.astype(LOW)
    hidden_here = w_up.shape[1]
    norm_rows = jnp.stack([ln1_gain, ln1_bias, ln2_gain, ln2_bias])
    norm_rows = jnp.pad(norm_rows, ((0, 124), (0, 0)))
    encoder_pack = pack_encoder(w_query, w_key, w_value, w_out, norm_rows, w_up, w_down.T)
    first = ring.gather(encoder_pack)
    first.step()
    own_pack = pack_own(w_tconv, w_conv1, w_conv2, encoder_pack)
    local_blocks = quad.spread(pack_local(tokens, cot_out, cot_dec[0], own_pack))
    while first.steps_left():
        first.step()
    blocks = first.blocks([(0, part)])
    mlp_blocks = first.blocks([(0, part)], 4 * span + 128)
    out_weight, norms = out_and_norms(blocks, span, 4 * span)
    pair_pack, sections = pack_pair(
        quad.chip[None], local_blocks[0], local_blocks[2], part, w_conv1.shape[0], encoder_pack
    )
    third = ring.gather(pair_pack)
    third.step(out_weight)
    arrived = third.one, third.two
    select, spread, place = selections(chans, chans_here)
    core = quad.core[None]
    me = quad.me[None]

    attended, rows_low, h_one, qkv, probs = attention(
        crop_depth, me, local_blocks, blocks, norms, heads_here, ()
    )
    attended = passed(attended, arrived)
    attended_blocks = quad.spread(attended)
    arrived = ()
    if third.steps_left():
        third.step(attended)
        arrived = third.one, third.two
    mine, other, mid, mid_half, h_two, hidden, slope = mlp(
        core,
        rows_low,
        attended_blocks,
        quad.spread(out_weight),
        norms,
        mlp_blocks,
        hidden_here,
        arrived,
    )
    arrived = ()
    if third.steps_left():
        third.step()
        arrived = third.one, third.two
    summed = half_sum(mine, quad.over_core(passed(other, arrived)), ())
    far = quad.over_chip(summed)
    while third.steps_left():
        third.step()
    decoder_own = join_decoder(third.blocks(sections), groups, part, summed)
    after, low_half = rows_sum(quad.chip[None], mid_half, summed, far, decoder_own)
    decoder_near, low_half = lax.optimization_barrier((decoder_own, low_half))
    decoder_near = quad.over_core(decoder_near)
    dec_out, grad_half, mlp_terms, mine, other, sums_two = decoder(
        ring.indices,
        crop_depth,
        me,
        low_half,
        quad.over_core(low_half),
        decoder_own,
        decoder_near,
        select,
        spread,
        place,
        local_blocks,
        slope,
        mid,
        h_two,
        hidden,
        mlp_blocks,
    )
    mlp_ring = ring.scatter(mlp_terms)
    mlp_ring.add()
    mlp_ring.send()
    summed = half_sum(mine, quad.over_core(other), ())
    far = quad.over_chip(summed)
    ready = mlp_ring.add(summed, own_kernel=True) if mlp_ring.left > 0 else ()
    grad_mid_own, low_mid_half = norm_back(
        quad.chip[None], summed, far, grad_half, mid_half, norms, ready
    )
    if mlp_ring.left > 0:
        mlp_ring.send(low_mid_half)
    mine, other, grad_qkv, grad_branch, sums_one = attention_back(
        core, low_mid_half, quad.over_core(low_mid_half), blocks, qkv, probs, rows_low, ()
    )
    ready = ()
    if mlp_ring.left > 0:
        ready = mlp_ring.add(sums_one)
        mlp_ring.send()
    attention_terms = attention_weights(
        ring.indices, h_one, attended, grad_qkv, grad_branch, sums_one, sums_two, ready
    )
    attention_ring = ring.scatter(attention_terms)
    attention_ring.add()
    attention_ring.send()
    last = ()
    while mlp_ring.left > 0 or attention_ring.left > 0:
        if attention_ring.left > 0:
            last = attention_ring.add(mlp_ring.one, mlp_ring.two)
            attention_ring.send()
        if mlp_ring.left > 0:
            mlp_ring.add()
            mlp_ring.send()
    mlp_ahead, mlp_behind = mlp_ring.result()
    ahead, behind = attention_ring.result()
    columns = slice(4 * span, 4 * span + 8)
    norm_grads = attention_terms[0][0, :, columns].astype(jnp.float32)
    norm_grads = norm_grads + ahead[:, columns].astype(jnp.float32)
    norm_grads = norm_grads + behind[:, columns].astype(jnp.float32)
    grad_query, grad_key, grad_value, grad_out = attention_sum(
        ahead, behind, attention_terms[0], span, norm_grads
    )
    norm_grads = sum(quad.spread_direct(norm_grads))
    summed = mine + quad.over_core(other).astype(jnp.float32)
    norm_own = quad.pick(summed) + quad.over_chip(low(quad.pick(summed[::-1]))).astype(jnp.float32)
    normed_own, scale_own = normalise(tokens.astype(jnp.float32))
    grad_tokens = grad_mid_own + layer_norm_back(norm_own * norms[0:1], normed_own, scale_own)
    grad_up, grad_down, grad_tconv, grad_conv1, grad_conv2 = mlp_sum(
        mlp_ahead, mlp_behind, mlp_terms[0], part, hidden_here, last
    )
    return (
        after,
        dec_out[None],
        grad_tokens,
        grad_query,
        grad_key,
        grad_value,
        grad_out,
        grad_up,
        grad_down.T,
        grad_tconv,
        grad_conv1.transpose(1, 0, 2),
        grad_conv2.transpose(1, 0, 2),
        norm_grads[:, 0],
        norm_grads[:, 1],
        norm_grads[:, 2],
        norm_grads[:, 3],
    )


def solution(mesh):
    in_specs = (
        P(("dp", "tensor"), None),
        P("dp"),
        P("dp", "tensor"),
        P("dp", "tensor"),
        P("dp", "tensor"),
        P("tensor", "dp"),
        P("dp", "tensor"),
        P("tensor", "dp"),
        P("dp", "tensor"),
        P("dp", None, "tensor"),
        P("dp", None, "tensor"),
        P("dp"),
        P("dp"),
        P("dp"),
        P("dp"),
        P(("dp", "tensor"), None),
        P("dp", None, None, None, "tensor"),
    )
    out_specs = (
        P(("dp", "tensor"), None),
        P("dp", None, None, None, "tensor"),
        P(("dp", "tensor"), None),
        P("dp", "tensor"),
        P("dp", "tensor"),
        P("dp", "tensor"),
        P("tensor", "dp"),
        P("dp", "tensor"),
        P("tensor", "dp"),
        P("dp", "tensor"),
        P("dp", None, "tensor"),
        P("dp", None, "tensor"),
        P("dp"),
        P("dp"),
        P("dp"),
        P("dp"),
    )
    groups = mesh.shape["dp"]

    def run(*arrays):
        return shards(*arrays, groups)

    return jax.shard_map(run, mesh=mesh, in_specs=in_specs, out_specs=out_specs, check_vma=False)
```

```python
import functools

import jax
import jax.numpy as jnp
import numpy as np
from jax import lax
from jax.experimental import pallas as pl
from jax.experimental.pallas import tpu as pltpu
from jax.sharding import PartitionSpec as P

HD = 64
GRID = 8
LOW = jnp.bfloat16


def ring_order(size):
    if size % 2:
        return list(range(size))
    return list(range(0, size, 2)) + list(range(size - 1, 0, -2))


def layer_norm_back(grad_normed, normed, scale):
    mean_grad = jnp.mean(grad_normed, axis=-1, keepdims=True)
    mean_dot = jnp.mean(grad_normed * normed, axis=-1, keepdims=True)
    return scale * (grad_normed - mean_grad - normed * mean_dot)


def contract_first(left, right):
    return lax.dot_general(
        left, right, (((0,), (0,)), ((), ())), preferred_element_type=jnp.float32
    )


MIB = 2**20
VMEM_LIMIT = 60 * MIB


def cost(microseconds):
    return pl.CostEstimate(flops=0, bytes_accessed=int(microseconds * 3.5e6), transcendentals=0)


def gelu_and_slope(x):
    bell = jnp.exp(-0.5 * x * x)
    frac = 1.0 / (1.0 + 0.3275911 * 0.7071067811865476 * jnp.abs(x))
    poly = frac * (
        0.254829592
        + frac * (-0.284496736 + frac * (1.421413741 + frac * (-1.453152027 + frac * 1.061405429)))
    )
    tail = 0.5 * poly * bell
    phi = jnp.where(x >= 0.0, 1.0 - tail, tail)
    return x * phi, phi + x * bell * 0.3989422804014327


def dot(left, right):
    return jnp.dot(left, right, preferred_element_type=jnp.float32)


def dot_last(left, right):
    return lax.dot_general(
        left, right, (((1,), (1,)), ((), ())), preferred_element_type=jnp.float32
    )


BATCH = 4


DECODER_REFS = 40


def decoder_kernel(
    blocks,
    index_ref,
    order_ref,
    depth_ref,
    me_ref,
    own_ref,
    near_ref,
    joined_hbm,
    joined_near_hbm,
    select_ref,
    spread_ref,
    place_ref,
    cot0_hbm,
    cot1_hbm,
    cot2_hbm,
    cot3_hbm,
    slope_hbm,
    mid_hbm,
    h_hbm,
    hidden_hbm,
    *refs,
):
    decoder_steps(
        blocks,
        refs[: len(blocks.pieces)],
        index_ref,
        order_ref,
        depth_ref,
        me_ref,
        own_ref,
        near_ref,
        joined_hbm,
        joined_near_hbm,
        select_ref,
        spread_ref,
        place_ref,
        (cot0_hbm, cot1_hbm, cot2_hbm, cot3_hbm),
        slope_hbm,
        mid_hbm,
        h_hbm,
        hidden_hbm,
        refs[len(blocks.pieces) : -DECODER_REFS],
        *refs[-DECODER_REFS:],
    )


def decoder_steps(
    blocks,
    pieces,
    index_ref,
    order_ref,
    depth_ref,
    me_ref,
    own_ref,
    near_ref,
    joined_hbm,
    joined_near_hbm,
    select_ref,
    spread_ref,
    place_ref,
    cots_hbm,
    slope_hbm,
    mid_hbm,
    h_hbm,
    hidden_hbm,
    terms_hbm,
    dec_hbm,
    grad_half_hbm,
    mine_hbm,
    other_hbm,
    sums_ref,
    other_ref,
    grad_low_ref,
    dec_ref,
    rows_ref,
    grad_tconv_ref,
    terms_ref,
    upper_ref,
    grad_rows_ref,
    wgrad_ref,
    first_even,
    first_odd,
    act_even,
    act_odd,
    grad_even,
    grad_odd,
    conv_ref,
    normed_ref,
    slope_ref,
    held_ref,
    carry_ref,
    low_grad_ref,
    columns_ref,
    tconv_ref,
    conv_w,
    back_w,
    cot_ref,
    up_ref,
    down_ref,
    gate_ref,
    mid_ref,
    h_ref,
    hidden_ref,
    sems,
    load_sems,
    out_sems,
):
    grid = 8
    vox = 16
    chans = 128
    depth = depth_ref[0]
    count = (depth * (2 * vox * vox)).astype(jnp.float32)

    core = lax.rem(me_ref[0], 2)
    loads = fetch(
        [
            (joined_hbm, terms_ref.at[pl.ds(pl.multiple_of(core * 512, 512), 512)]),
            (joined_near_hbm, terms_ref.at[pl.ds(pl.multiple_of((1 - core) * 512, 512), 512)]),
            (cots_hbm[0].at[pl.ds(TOKEN_ROWS, FIELD_ROWS)], cot_ref.at[me_ref[0]]),
            (cots_hbm[1].at[pl.ds(TOKEN_ROWS, FIELD_ROWS)], cot_ref.at[jnp.bitwise_xor(me_ref[0], 1)]),
            (cots_hbm[2].at[pl.ds(TOKEN_ROWS, FIELD_ROWS)], cot_ref.at[jnp.bitwise_xor(me_ref[0], 2)]),
            (cots_hbm[3].at[pl.ds(TOKEN_ROWS, FIELD_ROWS)], cot_ref.at[jnp.bitwise_xor(me_ref[0], 3)]),
            (slope_hbm, gate_ref),
            (mid_hbm, mid_ref),
            (h_hbm, h_ref),
            (hidden_hbm, hidden_ref),
        ],
        sems.at[pl.ds(3, 10)],
    )
    hidden = up_ref.shape[1]
    loads += blocks.load(index_ref, pieces, 0, hidden, down_ref, load_sems)
    loads += blocks.load(index_ref, pieces, 0, 0, up_ref, load_sems.at[pl.ds(len(pieces), len(pieces))])
    dec_copy = pltpu.make_async_copy(dec_ref, dec_hbm, sems.at[0])

    for even in (first_even, act_even, grad_even):
        even[:, 0] = jnp.zeros((grid, vox, 4 * chans), LOW)
        even[:, vox + 1] = jnp.zeros((grid, vox, 4 * chans), LOW)
    for odd in (first_odd, act_odd, grad_odd):
        odd[:, 0] = jnp.zeros((grid + 1, vox, 4 * chans), LOW)
        odd[:, vox + 1] = jnp.zeros((grid + 1, vox, 4 * chans), LOW)
    wgrad_ref[:, 864:] = jnp.zeros((2, 32, chans), jnp.float32)
    low_grad_ref[:, 0] = jnp.zeros((grid, vox, 2 * chans), LOW)
    low_grad_ref[:, vox + 1] = jnp.zeros((grid, vox, 2 * chans), LOW)

    spot = lax.broadcasted_iota(jnp.int32, (1, 1, 8, 1), 2)

    def put_field(even, odd, at, value):
        left = value[..., :chans]
        right = value[..., chans:]
        flat = (2 * vox, 8, chans)
        before = pltpu.roll(right.reshape(flat), 1, 1).reshape(right.shape)
        after = pltpu.roll(left.reshape(flat), 7, 1).reshape(left.shape)
        before = jnp.where(spot == 0, 0.0, before)
        after = jnp.where(spot == 7, 0.0, after)
        window = jnp.concatenate([before, value, after], axis=3)
        even[at, 1 : vox + 1] = window.reshape(vox, 16, 4 * chans).astype(LOW)
        early = jnp.concatenate([carry_ref[...][:, None], window[:, :1]], axis=1)
        odd[at, 1 : vox + 1] = early.reshape(vox, 16, 4 * chans).astype(LOW)
        carry_ref[...] = window[:, 1]

    def open_field():
        carry_ref[...] = jnp.zeros(carry_ref.shape, jnp.float32)

    def close_field(odd):
        late = jnp.concatenate([carry_ref[...], jnp.zeros(carry_ref.shape, jnp.float32)], axis=1)
        odd[grid, 1 : vox + 1] = late.astype(LOW)

    def live_at(at):
        return (at < depth).astype(jnp.float32)

    def convolve(even, odd, weights, target, turned):
        def step(block, total):
            at = block * BATCH
            summed = None
            for deep in range(3):
                field = even if deep == 1 else odd
                start = at + 1 if deep == 2 else at
                for tall in range(3):
                    left = field[pl.ds(start, BATCH), tall : tall + vox]
                    left = left.reshape(BATCH * vox * 16, 4 * chans)
                    right = weights[deep * 3 + tall]
                    term = dot_last(left, right) if turned else dot(left, right)
                    summed = term if summed is None else summed + term
            target[pl.ds(at, BATCH)] = summed.reshape(BATCH, vox, 16, 2 * chans)
            return total

        lax.fori_loop(0, grid // BATCH, step, 0)

    def both(total):
        row = jnp.sum(total, axis=0, keepdims=True)
        half = (row[:, :chans] + row[:, chans:]) / count
        return jnp.concatenate([half, half], axis=1)

    def zero():
        return jnp.zeros((8, 2 * chans), jnp.float32)

    def fold(value):
        return jnp.sum(value.reshape(2 * vox, 8, 2 * chans), axis=0)

    def statistics(source):
        def first(at, total):
            return total + live_at(at) * fold(source[at])

        middle = both(lax.fori_loop(0, grid, first, zero()))

        def second(at, total):
            away = source[at] - middle
            return total + live_at(at) * fold(away * away)

        spread = both(lax.fori_loop(0, grid, second, zero()))
        return middle, lax.rsqrt(spread + 1e-05)

    for block in range(2):
        rows_ref[pl.ds(pl.multiple_of(block * 256 + core * 128, 128), 128)] = own_ref[block]
        rows_ref[pl.ds(pl.multiple_of(block * 256 + (1 - core) * 128, 128), 128)] = near_ref[block]
    loads[0].wait()
    loads[1].wait()
    make_tconv(terms_ref, place_ref[...], tconv_ref)
    for part in range(4):
        wide = dot(rows_ref[...], tconv_ref[:, part * 256 : (part + 1) * 256])
        held_ref[:, part * 4 : (part + 1) * 4] = wide.reshape(grid, 4, 16, 2 * chans)
    open_field()

    def place_first(at, state):
        tokens = held_ref[at] * live_at(at)
        offsets = [
            [tokens[8 * a + 4 * b : 8 * a + 4 * b + 4].reshape(8, 1, 1, 8, 256) for a in range(2)]
            for b in range(2)
        ]
        value = jnp.concatenate(
            [jnp.concatenate(offsets[b], axis=2) for b in range(2)], axis=1
        ).reshape(vox, 2, 8, 256)
        put_field(first_even, first_odd, at, value)
        return state

    lax.fori_loop(0, grid, place_first, 0)
    close_field(first_odd)

    for which in range(2):
        make_taps(terms_ref, place_ref[...], which, conv_w.at[which], back_w.at[which])
    convolve(first_even, first_odd, conv_w.at[0], normed_ref, False)
    middle, scale_one = statistics(normed_ref)
    open_field()

    def act_first(at, state):
        normed = (normed_ref[at] - middle) * scale_one
        normed_ref[at] = normed
        value, slope = gelu_and_slope(normed)
        live = live_at(at)
        slope_ref[at] = slope * live
        put_field(act_even, act_odd, at, (value * live).reshape(vox, 2, 8, 2 * chans))
        return state

    lax.fori_loop(0, grid, act_first, 0)
    close_field(act_odd)

    convolve(act_even, act_odd, conv_w.at[1], conv_ref, False)
    middle, scale_two = statistics(conv_ref)
    for load in loads[2:6]:
        load.wait()

    def act_second(at, totals):
        normed = (conv_ref[at] - middle) * scale_two
        conv_ref[at] = normed
        value, slope = gelu_and_slope(normed)
        live = live_at(at)
        low_value = (value * live).astype(LOW).reshape(vox * 16, 2 * chans)
        for e in range(2):
            shown = dot_last(low_value, select_ref[me_ref[0], e]).reshape(vox, 2, 8, 32)
            for a in range(2):
                dec_ref[2 * at + a, :, pl.ds(e, 8, stride=2), :] = shown[:, a]
        parts = [cot_ref[t, pl.ds(768 + at * vox * 8, vox * 8)] for t in range(4)]
        packed = jnp.concatenate(parts, axis=1)
        cot = jnp.concatenate(
            [dot(packed, spread_ref[a]).reshape(vox, 1, 8, 2 * chans) for a in range(2)], axis=1
        ).reshape(vox, 16, 2 * chans)
        grad = cot * slope * live
        held_ref[at] = grad
        return totals[0] + fold(grad), totals[1] + fold(grad * normed)

    totals = lax.fori_loop(0, grid, act_second, (zero(), zero()))
    dec_copy.start()

    def norm_back(source, normed_source, scale, sums):
        mean_grad = both(sums[0])
        mean_dot = both(sums[1])
        open_field()

        def step(at, state):
            grad = source[at] - live_at(at) * (mean_grad + normed_source[at] * mean_dot)
            grad = scale * grad
            low_grad_ref[at, 1 : vox + 1] = grad.astype(LOW)
            put_field(grad_even, grad_odd, at, grad.reshape(vox, 2, 8, 2 * chans))
            return state

        lax.fori_loop(0, grid, step, 0)
        close_field(grad_odd)

    def weight_grad(even, odd, which):
        own = select_ref[me_ref[0]].reshape(64, 2 * chans)
        for at in range(grid):
            shifts = [
                dot_last(own, low_grad_ref[at, 2 - tall : 18 - tall].reshape(vox * 16, 2 * chans))
                for tall in range(3)
            ]
            columns_ref[:, at * 256 : (at + 1) * 256] = jnp.concatenate(shifts, axis=0).astype(LOW)
        for deep in range(3):
            field = even if deep == 1 else odd
            start = 1 if deep == 2 else 0
            right = field[start : start + grid, 1 : vox + 1].reshape(grid * vox * 16, 4 * chans)
            sums = dot(columns_ref[...], right)
            for tall in range(3):
                for wide in range(3):
                    top = sums[tall * 64 : tall * 64 + 32, wide * chans : (wide + 1) * chans]
                    low = sums[tall * 64 + 32 : tall * 64 + 64, (wide + 1) * chans : (wide + 2) * chans]
                    tap = deep * 9 + tall * 3 + wide
                    wgrad_ref[which, tap * 32 : (tap + 1) * 32] = top + low

    norm_back(held_ref, conv_ref, scale_two, totals)
    weight_grad(act_even, act_odd, 1)
    convolve(grad_even, grad_odd, back_w.at[1], conv_ref, True)

    def slope_first(at, totals):
        grad = conv_ref[at] * slope_ref[at]
        conv_ref[at] = grad
        return totals[0] + fold(grad), totals[1] + fold(grad * normed_ref[at])

    totals = lax.fori_loop(0, grid, slope_first, (zero(), zero()))
    norm_back(conv_ref, normed_ref, scale_one, totals)
    weight_grad(first_even, first_odd, 0)
    convolve(grad_even, grad_odd, back_w.at[0], conv_ref, True)

    def rows_back(at, state):
        grad = (conv_ref[at] * live_at(at)).reshape(8, 2, 2, 8, 2 * chans)
        for a in range(2):
            for b in range(2):
                block = grad[:, b, a].reshape(64, 2 * chans).astype(LOW)
                column = (2 * a + b) * 256
                grad_tconv_ref[pl.ds(at * 64, 64), column : column + 256] = block
        return state

    lax.fori_loop(0, grid, rows_back, 0)
    for which in range(2):
        for block in range(7):
            at = (7 * which + block) * 128
            taps = wgrad_ref[which, block * 128 : (block + 1) * 128].T.astype(LOW)
            terms_ref[768:896, at : at + 128] = taps
    own = select_ref[me_ref[0]].reshape(64, 2 * chans)
    spans = [dot_last(grad_tconv_ref[:, at * 256 : (at + 1) * 256], own) for at in range(4)]
    mine = jnp.concatenate(spans, axis=1).astype(LOW)
    terms_ref[:768, 2 * hidden :] = contract_first(rows_ref[...], mine).astype(LOW)
    for t in range(4):
        at = slice(t * 128, (t + 1) * 128)
        tiles = [cot_ref[t, block * 128 : (block + 1) * 128] for block in range(6)]
        cot_rows = jnp.concatenate(tiles, axis=1).astype(jnp.float32)
        grad_rows_ref[at] = cot_rows + dot_last(grad_tconv_ref[at], tconv_ref[...])
    grad_low_ref[...] = grad_rows_ref[...].astype(LOW)
    halves = []
    for block in range(2):
        own = pl.ds(pl.multiple_of(block * 256 + core * 128, 128), 128)
        halves.append((grad_rows_ref.at[own], grad_half_hbm.at[block]))
    half_copies = fetch(halves, sems.at[pl.ds(1, 2)])
    for load in loads[6:]:
        load.wait()
    for copy in half_copies:
        copy.wait()
    sent = []
    gain = shift = 0.0
    for block in range(2):
        at = slice(block * 256, (block + 1) * 256)
        grad = dot(grad_low_ref[at], down_ref[...])
        upper = (grad * gate_ref[at].astype(jnp.float32)).astype(LOW)
        upper_ref[at] = upper
        grad_normed = dot_last(upper, up_ref[...])
        normed, _ = normalise(mid_ref[at])
        gain += jnp.sum(grad_normed * normed, axis=0, keepdims=True)
        shift += jnp.sum(grad_normed, axis=0, keepdims=True)
        grad_rows_ref[at] = grad_normed
        own = pl.ds(pl.multiple_of(block * 256 + core * 128, 128), 128)
        their = pl.ds(pl.multiple_of(block * 256 + (1 - core) * 128, 128), 128)
        other_ref[block] = grad_rows_ref[their].astype(LOW)
        sent += fetch(
            [(grad_rows_ref.at[own], mine_hbm.at[block]), (other_ref.at[block], other_hbm.at[block])],
            sems.at[pl.ds(3 + 2 * block, 2)],
        )
    sums_ref[...] = jnp.concatenate([gain, shift], axis=0)
    terms_ref[:768, :hidden] = contract_first(h_ref[...], upper_ref[...]).astype(LOW)
    terms_ref[:768, hidden : 2 * hidden] = contract_first(grad_low_ref[...], hidden_ref[...]).astype(LOW)
    for copy in sent + put_chunks(order_ref, terms_ref, (768, 128), terms_hbm, out_sems):
        copy.wait()
    dec_copy.wait()


def decoder(
    order, depth, me, own, near, joined, joined_near, select, spread, place, cots, slope, mid, h_rows, hidden, blocks
):
    f32 = jnp.float32
    vmem = pl.BlockSpec(memory_space=pltpu.VMEM)
    hbm = pl.BlockSpec(memory_space=pltpu.HBM)
    here = slope.shape[1]
    columns = 2 * here + 256
    window = lambda planes: pltpu.VMEM((planes, 18, 16, 512), LOW)
    field = lambda kind: pltpu.VMEM((8, 16, 16, 256), kind)
    kept = []

    def call(order, groups):
        shapes = chunk_shapes(groups, 896 // groups, columns)
        outs = pl.pallas_call(
            functools.partial(decoder_kernel, blocks),
            out_shape=(
                *shapes,
                jax.ShapeDtypeStruct((16, 16, 16, 32), f32),
                jax.ShapeDtypeStruct((2, 128, 768), f32),
                jax.ShapeDtypeStruct((2, 128, 768), f32),
                jax.ShapeDtypeStruct((2, 128, 768), LOW),
                jax.ShapeDtypeStruct((2, 768), f32),
            ),
            in_specs=[pl.BlockSpec(memory_space=pltpu.SMEM)] * 4
            + [vmem] * 2
            + [hbm] * 2
            + [vmem] * 3
            + [hbm] * 8
            + blocks.specs(),
            out_specs=[hbm] * (len(shapes) + 4) + [vmem],
            scratch_shapes=[
                pltpu.VMEM((2, 128, 768), LOW),
                pltpu.VMEM((512, 768), LOW),
                pltpu.VMEM((16, 16, 16, 32), f32),
                pltpu.VMEM((512, 768), LOW),
                pltpu.VMEM((512, 1024), LOW),
                pltpu.VMEM((1024, columns), LOW),
                pltpu.VMEM(slope.shape, LOW),
                pltpu.VMEM((512, 768), f32),
                pltpu.VMEM((2, 896, 128), f32),
                window(8),
                window(9),
                window(8),
                window(9),
                window(8),
                window(9),
                field(f32),
                field(f32),
                field(f32),
                field(f32),
                pltpu.VMEM((16, 8, 512), f32),
                pltpu.VMEM((8, 18, 16, 256), LOW),
                pltpu.VMEM((192, 2048), LOW),
                pltpu.VMEM((768, 1024), LOW),
                pltpu.VMEM((2, 9, 512, 256), LOW),
                pltpu.VMEM((2, 9, 256, 512), LOW),
                pltpu.VMEM((4, 1792, 128), LOW),
                pltpu.VMEM((768, here), LOW),
                pltpu.VMEM((768, here), LOW),
                pltpu.VMEM(slope.shape, LOW),
                pltpu.VMEM(mid.shape, f32),
                pltpu.VMEM(h_rows.shape, LOW),
                pltpu.VMEM(hidden.shape, LOW),
                pltpu.SemaphoreType.DMA((13,)),
                pltpu.SemaphoreType.DMA((2 * len(blocks.pieces),)),
                pltpu.SemaphoreType.DMA((2 * groups + 4,)),
            ],
            compiler_params=pltpu.CompilerParams(vmem_limit_bytes=VMEM_LIMIT),
            cost_estimate=cost(52),
        )(
            blocks.indices,
            order,
            depth,
            me,
            own,
            near,
            joined,
            joined_near,
            select,
            spread,
            place,
            *cots,
            slope,
            mid,
            h_rows,
            hidden,
            *blocks.pieces,
        )
        kept.extend(outs[len(shapes) :])
        return outs[: len(shapes)]

    terms = in_ring_order(call, order, (768, 128))
    dec, half, mine, other, sums = kept
    return dec, half, terms, mine, other, sums


def full_spec(count, space=pltpu.VMEM):
    return [pl.BlockSpec(memory_space=space)] * count


def fetch(pairs, sems):
    copies = [
        pltpu.make_async_copy(source, target, sems.at[at]) for at, (source, target) in enumerate(pairs)
    ]
    for copy in copies:
        copy.start()
    return copies


class Blocks:
    def __init__(self, indices, starts, pieces, size, sections, base=0):
        self.base = base
        block, columns = pieces[0].shape
        edges = [end for section in sections for end in section]
        if any(edge % 16 for edge in edges + list(starts)):
            full = jnp.zeros((size * block, columns), pieces[0].dtype)
            for at, (start, piece) in enumerate(zip(starts, pieces)):
                full = lax.dynamic_update_slice(full, piece, (indices[at] * block + start, 0))
            full = full.reshape(size, block, columns)
            parts = [full[:, low:high].reshape(-1, columns) for low, high in sections]
            pieces, starts, indices = [jnp.concatenate(parts)], [0], jnp.zeros((1,), jnp.int32)
            sections = [(size * low, size * high) for low, high in sections]
            size = 1
        self.indices = indices
        self.starts = tuple(starts)
        self.pieces = tuple(pieces)
        self.size = size
        self.sections = tuple(sections)

    def specs(self):
        return full_spec(len(self.pieces), pl.ANY)

    def rows(self, section):
        low, high = self.sections[section]
        return self.size * (high - low)

    def load(self, index_ref, refs, section, column, target, sems):
        low, high = self.sections[section]
        copies = []
        for at, (piece, start) in enumerate(zip(refs, self.starts)):
            first, last = max(low, start), min(high, start + piece.shape[0])
            if first >= last:
                continue
            row = index_ref[at] * (high - low) + first - low
            if len(self.pieces) > 1:
                row = pl.multiple_of(row, 16)
            columns = pl.ds(self.base + column, target.shape[1])
            source = piece.at[pl.ds(first - start, last - first), columns]
            copies += fetch([(source, target.at[pl.ds(row, last - first)])], sems.at[pl.ds(at, 1)])
        return copies


def pack_kernel(
    query_ref, key_ref, value_ref, out_ref, gain1_ref, bias1_ref, gain2_ref, bias2_ref, up_ref, down_ref, pack_ref
):
    at = 0
    none = jnp.zeros((124, gain1_ref.shape[1]), jnp.float32)
    norms = [gain1_ref[...], bias1_ref[...], gain2_ref[...], bias2_ref[...], none]
    norms = jnp.concatenate(norms, axis=0).T
    for value in (
        query_ref[...], key_ref[...], value_ref[...], out_ref[...].T, norms, up_ref[...], down_ref[...],
    ):
        pack_ref[:, at : at + value.shape[1]] = value.astype(LOW)
        at += value.shape[1]


def pack_encoder(query, key, value, out, norms, up, down):
    part = query.shape[0]
    if part % 16:
        columns = jnp.pad(jnp.concatenate(norms), ((0, 124), (0, 0))).T
        parts = (query, key, value, out.T, columns, up, down)
        return jnp.concatenate([array.astype(LOW) for array in parts], axis=1)
    return pl.pallas_call(
        pack_kernel,
        out_shape=jax.ShapeDtypeStruct((part, 4 * query.shape[1] + 128 + 2 * up.shape[1]), LOW),
        in_specs=full_spec(10),
        out_specs=pl.BlockSpec(memory_space=pltpu.VMEM),
        cost_estimate=cost(2),
    )(query, key, value, out, *norms, up, down)


def pack_own_kernel(tconv_ref, conv1_ref, conv2_ref, turn_ref, after_ref, pack_ref):
    part = tconv_ref.shape[0]
    conv_part = conv1_ref.shape[1]
    pack_ref[:part] = dot(tconv_ref[...].astype(LOW), turn_ref[...]).astype(LOW)
    taps = []
    for conv_ref in (conv1_ref, conv2_ref):
        taps += [conv_ref[tap] for tap in range(27)] + [jnp.zeros(conv_ref.shape[1:], jnp.float32)]
    for tile in range(14):
        made = jnp.concatenate(taps[4 * tile : 4 * tile + 4], axis=1).astype(LOW)
        at = part + tile // 2 * conv_part
        pack_ref[at : at + conv_part, tile % 2 * 128 : (tile % 2 + 1) * 128] = made


def turn_matrix():
    turn = np.zeros((32, 8, 8, 32), np.float32)
    for group in range(8):
        for chan in range(32):
            turn[chan, group, group, chan] = 1.0
    return turn.reshape(256, 256).astype(LOW)


def pack_own(tconv, conv1, conv2, after):
    part, conv_part = tconv.shape[0], conv1.shape[0]
    if part % 16 or conv_part % 16:
        conv = jnp.stack([conv1.astype(LOW), conv2.astype(LOW)], axis=1)
        conv = jnp.pad(conv, ((0, 0), (0, 0), (0, 1), (0, 0)))
        conv = conv.reshape(conv_part, 7, 256).transpose(1, 0, 2)
        turned = tconv.astype(LOW).reshape(part, 32, 8).transpose(0, 2, 1).reshape(part, -1)
        return jnp.concatenate([turned, conv.reshape(-1, 256)])
    return pl.pallas_call(
        pack_own_kernel,
        out_shape=jax.ShapeDtypeStruct((part + 7 * conv_part, 256), LOW),
        in_specs=full_spec(4) + full_spec(1, pl.ANY),
        out_specs=pl.BlockSpec(memory_space=pltpu.VMEM),
        cost_estimate=cost(2),
    )(tconv, conv1.transpose(1, 0, 2), conv2.transpose(1, 0, 2), jnp.asarray(turn_matrix()), after)


def fold_tconv(rows, columns):
    count = rows.shape[0]
    if count % 16:
        flat = rows.reshape(-1)
        flat = jnp.pad(flat, (0, -flat.shape[0] % columns))
        return flat.reshape(-1, columns)
    folded = rows.reshape(count // 16, 16, 256).transpose(1, 0, 2).reshape(16, -1)
    return jnp.pad(folded, ((0, 0), (0, columns - folded.shape[1])))


TOKEN_ROWS = 768
FIELD_ROWS = 1792
PACK_AT = TOKEN_ROWS + FIELD_ROWS


def pack_local_kernel(tokens_ref, cot_ref, field_ref, own_ref, pack_ref):
    for block in range(6):
        lanes = slice(block * 128, (block + 1) * 128)
        pack_ref[block * 128 : (block + 1) * 128] = tokens_ref[:, lanes]
        at = TOKEN_ROWS + block * 128
        pack_ref[at : at + 128] = cot_ref[:, lanes].astype(LOW)
    for pair in range(8):
        parts = [
            field_ref[2 * pair + a, :, pl.ds(e, 8, stride=2), :].reshape(128, 32)
            for a in range(2)
            for e in range(2)
        ]
        at = 2 * TOKEN_ROWS + pair * 128
        pack_ref[at : at + 128] = jnp.concatenate(parts, axis=1).astype(LOW)
    count = own_ref.shape[0]
    if count % 16 == 0:
        for half in range(2):
            at = PACK_AT + half * count
            pack_ref[at : at + count] = own_ref[:, half * 128 : (half + 1) * 128]


def pack_local(tokens, cot, field, own):
    aligned = own.shape[0] % 16 == 0
    total = PACK_AT + (2 * own.shape[0] if aligned else 0)
    pack = pl.pallas_call(
        pack_local_kernel,
        out_shape=jax.ShapeDtypeStruct((total, 128), LOW),
        in_specs=full_spec(4),
        out_specs=pl.BlockSpec(memory_space=pltpu.VMEM),
        compiler_params=pltpu.CompilerParams(vmem_limit_bytes=VMEM_LIMIT),
        cost_estimate=cost(3),
    )(tokens, cot, field, own)
    if aligned:
        return pack
    halves = own.reshape(-1, 2, 128).transpose(1, 0, 2).reshape(-1, 128)
    return jnp.concatenate([pack, halves])


def pack_pair_kernel(part, conv_part, chip_ref, own_hbm, far_hbm, after_ref, pack_ref, held_ref, sems):
    columns = pack_ref.shape[1]
    count = part + 7 * conv_part
    source = pl.ds(PACK_AT, 2 * count)
    for copy in fetch(
        [
            (own_hbm.at[source], held_ref.at[chip_ref[0]]),
            (far_hbm.at[source], held_ref.at[1 - chip_ref[0]]),
        ],
        sems,
    ):
        copy.wait()
    for which in range(2):
        for half in range(2):
            first = half * count
            at = which * conv_part
            for block in range(7):
                start = first + part + block * conv_part
                lanes = slice(block * 256 + half * 128, block * 256 + (half + 1) * 128)
                pack_ref[at : at + conv_part, lanes] = held_ref[which, start : start + conv_part]
            at = 2 * conv_part + which * 16
            for block in range(part // 16):
                start = first + block * 16
                lanes = slice(block * 256 + half * 128, block * 256 + (half + 1) * 128)
                pack_ref[at : at + 16, lanes] = held_ref[which, start : start + 16]
        at = 2 * conv_part + which * 16
        pack_ref[at : at + 16, part * 16 :] = jnp.zeros((16, columns - part * 16), LOW)


def pack_pair(chip, own, far, part, conv_part, after):
    columns = 7 * 256
    count = part + 7 * conv_part
    if part % 16 or conv_part % 16:
        own, far = [
            packed[PACK_AT:].reshape(2, count, 128).transpose(1, 0, 2).reshape(count, 256)
            for packed in (own, far)
        ]
        first = jnp.where(chip[0] > 0, far, own)
        second = jnp.where(chip[0] > 0, own, far)
        convs = [
            packed[part:].reshape(7, conv_part, 256).transpose(1, 0, 2).reshape(conv_part, columns)
            for packed in (first, second)
        ]
        pack = jnp.concatenate(convs + [fold_tconv(packed[:part], columns) for packed in (first, second)])
    else:
        pack = pl.pallas_call(
            functools.partial(pack_pair_kernel, part, conv_part),
            out_shape=jax.ShapeDtypeStruct((2 * conv_part + 32, columns), LOW),
            in_specs=full_spec(1, pltpu.SMEM) + full_spec(3, pl.ANY),
            out_specs=pl.BlockSpec(memory_space=pltpu.VMEM),
            scratch_shapes=[pltpu.VMEM((2, 2 * count, 128), LOW), pltpu.SemaphoreType.DMA((2,))],
            cost_estimate=cost(1.7),
        )(chip, own, far, after)
    fold = (pack.shape[0] - 2 * conv_part) // 2
    edges = [0, conv_part, 2 * conv_part, 2 * conv_part + fold, pack.shape[0]]
    return pack, list(zip(edges[:-1], edges[1:]))


def out_norm_kernel(blocks, norm_at, index_ref, *refs):
    count = len(blocks.pieces)
    pieces = refs[:count]
    out_ref, norm_ref, wide_ref, columns_ref, sems = refs[count:]
    span = out_ref.shape[1]
    copies = blocks.load(index_ref, pieces, 0, 4 * span - 256, wide_ref, sems)
    copies += blocks.load(index_ref, pieces, 0, norm_at, columns_ref, sems.at[pl.ds(count, count)])
    for copy in copies:
        copy.wait()
    out_ref[...] = wide_ref[:, 256 - span :]
    norm_ref[...] = columns_ref[...].astype(jnp.float32).T[:8]


def out_and_norms(blocks, span, norm_at):
    count = len(blocks.pieces)
    return pl.pallas_call(
        functools.partial(out_norm_kernel, blocks, norm_at),
        out_shape=(
            jax.ShapeDtypeStruct((blocks.rows(0), span), LOW),
            jax.ShapeDtypeStruct((8, blocks.rows(0)), jnp.float32),
        ),
        in_specs=full_spec(1, pltpu.SMEM) + blocks.specs(),
        out_specs=full_spec(2),
        scratch_shapes=[
            pltpu.VMEM((blocks.rows(0), 256), LOW),
            pltpu.VMEM((blocks.rows(0), 128), LOW),
            pltpu.SemaphoreType.DMA((2 * count,)),
        ],
        compiler_params=pltpu.CompilerParams(vmem_limit_bytes=12 * MIB),
        cost_estimate=cost(2.7),
    )(blocks.indices, *blocks.pieces)


def join_kernel(blocks, index_ref, *refs):
    count = len(blocks.pieces)
    join_ref, sems = refs[-2:]
    copies = []
    for section in range(4):
        target = join_ref.at[pl.ds(section * 128, 128)]
        copies += blocks.load(
            index_ref, refs[:count], section, 0, target, sems.at[pl.ds(section * count, count)]
        )
    for copy in copies:
        copy.wait()


def join_decoder(blocks, groups, part, after):
    columns = blocks.pieces[0].shape[1]
    count = len(blocks.pieces)
    if count == 1:
        full = blocks.pieces[0]
        parts = [full[low:high] for low, high in blocks.sections]
        folded = []
        for rows in parts[2:]:
            rows = rows.reshape(groups, -1)[:, : part * 256].reshape(-1, 256)
            folded += [fold_tconv(rows[at * 96 : (at + 1) * 96], columns) for at in range(8)]
        return jnp.concatenate(parts[:2] + folded)
    return pl.pallas_call(
        functools.partial(join_kernel, blocks),
        out_shape=jax.ShapeDtypeStruct((512, columns), LOW),
        in_specs=full_spec(1, pltpu.SMEM) + blocks.specs() + full_spec(1, pl.ANY),
        out_specs=pl.BlockSpec(memory_space=pltpu.VMEM),
        scratch_shapes=[pltpu.SemaphoreType.DMA((4 * count,))],
        compiler_params=pltpu.CompilerParams(vmem_limit_bytes=12 * MIB),
        cost_estimate=cost(3.8),
    )(blocks.indices, *blocks.pieces, after)


def pass_kernel(value_ref, *refs):
    refs[-1][...] = value_ref[...]


def passed(value, after):
    return pl.pallas_call(
        pass_kernel,
        out_shape=jax.ShapeDtypeStruct(value.shape, value.dtype),
        in_specs=full_spec(1) + full_spec(len(after), pl.ANY),
        out_specs=pl.BlockSpec(memory_space=pltpu.VMEM),
        compiler_params=pltpu.CompilerParams(vmem_limit_bytes=8 * MIB),
        cost_estimate=cost(1),
    )(value, *after)


def half_sum_kernel(mine_ref, near_ref, *refs):
    refs[-1][...] = (mine_ref[...] + near_ref[...].astype(jnp.float32)).astype(LOW)


def half_sum(mine, near, after):
    return pl.pallas_call(
        half_sum_kernel,
        out_shape=jax.ShapeDtypeStruct(mine.shape, LOW),
        in_specs=full_spec(2) + full_spec(len(after), pl.ANY),
        out_specs=pl.BlockSpec(memory_space=pltpu.VMEM),
        compiler_params=pltpu.CompilerParams(vmem_limit_bytes=8 * MIB),
        cost_estimate=cost(2),
    )(mine, near, *after)


def rows_sum_kernel(chip_ref, mid_ref, summed_ref, far_ref, after_ref, own_ref, low_ref, total_ref):
    for block in range(2):
        total = summed_ref[block].astype(jnp.float32) + far_ref[block].astype(jnp.float32)
        total_ref[block] = mid_ref[block] + total
        low_ref[block] = total_ref[block].astype(LOW)
    own_ref[...] = total_ref[chip_ref[0]]


def rows_sum(chip, mid, summed, far, after):
    return pl.pallas_call(
        rows_sum_kernel,
        out_shape=(
            jax.ShapeDtypeStruct(mid.shape[1:], jnp.float32),
            jax.ShapeDtypeStruct(mid.shape, LOW),
        ),
        in_specs=full_spec(1, pltpu.SMEM) + full_spec(3) + full_spec(1, pl.ANY),
        out_specs=full_spec(2),
        scratch_shapes=[pltpu.VMEM(mid.shape, jnp.float32)],
        compiler_params=pltpu.CompilerParams(vmem_limit_bytes=12 * MIB),
        cost_estimate=cost(2),
    )(chip, mid, summed, far, after)


def make_taps(joined, place, which_taps, conv_ref, back_ref):
    chans = 128
    none = jnp.zeros((chans, chans), LOW)
    for plane in range(9):
        conv_ref[plane, 3 * chans :, :chans] = none
        conv_ref[plane, :chans, chans:] = none
        back_ref[plane, :chans, 3 * chans :] = none
        back_ref[plane, chans:, :chans] = none
    for block in range(7):
        lanes = slice((7 * which_taps + block) * chans, (7 * which_taps + block + 1) * chans)
        wide = [joined[t % 2 * 512 + t // 2 * chans : t % 2 * 512 + (t // 2 + 1) * chans, lanes] for t in range(4)]
        made = dot(jnp.concatenate(wide, axis=1), place).astype(LOW)
        for part in range(4):
            tap = 4 * block + part
            if tap == 27:
                continue
            plane, deep = tap // 3, tap % 3
            turned = 2 - deep
            taps = made[:, part * chans : (part + 1) * chans]
            conv_ref[plane, deep * chans : (deep + 1) * chans, :chans] = taps
            conv_ref[plane, (deep + 1) * chans : (deep + 2) * chans, chans:] = taps
            back_ref[8 - plane, :chans, turned * chans : (turned + 1) * chans] = taps
            back_ref[8 - plane, chans:, (turned + 1) * chans : (turned + 2) * chans] = taps


def make_tconv(joined, place, tconv_ref):
    chans = 128
    for half in range(2):
        wide = []
        for t in range(4):
            rows = []
            for group in range(8):
                start = t % 2 * 512 + 256 + t // 2 * chans + group * 16
                for block in range(6):
                    at = block * 256 + half * chans
                    rows.append(joined[start : start + 16, at : at + chans])
            wide.append(jnp.concatenate(rows, axis=0))
        made = dot(jnp.concatenate(wide, axis=1), place)
        tconv_ref[:, half * 512 : (half + 1) * 512] = made.astype(LOW)


def normalise(rows):
    middle = jnp.mean(rows, axis=-1, keepdims=True)
    centred = rows - middle
    spread = jnp.mean(centred * centred, axis=-1, keepdims=True)
    scale = lax.rsqrt(spread + 1e-06)
    return centred * scale, scale


def attention_kernel(blocks, index_ref, depth_ref, me_ref, own_hbm, near_hbm, far_hbm, last_hbm, norm_ref, *refs):
    count = len(blocks.pieces)
    pieces = refs[:count]
    (
        out_ref, rows_hbm, h_hbm, qkv_hbm, probs_hbm,
        rows_ref, h_ref, qkv_ref, probs_ref, weight_ref, sems, load_sems, token_sems,
    ) = refs[-13:]
    patches = rows_ref.shape[0]
    heads = probs_ref.shape[0]
    span = heads * HD
    quarter = patches // 4
    tokens = []
    for flip, packed in enumerate((own_hbm, near_hbm, far_hbm, last_hbm)):
        start = pl.multiple_of(jnp.bitwise_xor(me_ref[0], flip) * quarter, quarter)
        for block in range(6):
            source = packed.at[pl.ds(block * 128, 128)]
            tokens.append((source, rows_ref.at[pl.ds(start, quarter), pl.ds(block * 128, 128)]))
    tokens = fetch(tokens, token_sems)
    loads = blocks.load(index_ref, pieces, 0, 0, weight_ref, load_sems)
    for copy in tokens:
        copy.wait()
    copies = fetch([(rows_ref, rows_hbm)], sems.at[pl.ds(1, 1)])
    norms = norm_ref[...]
    normed, _ = normalise(rows_ref[...].astype(jnp.float32))
    low_rows = (normed * norms[0:1] + norms[1:2]).astype(LOW)
    h_ref[...] = low_rows
    copies += fetch([(h_ref, h_hbm)], sems.at[pl.ds(2, 1)])
    for load in loads:
        load.wait()
    qkv_ref[...] = dot(low_rows, weight_ref[:, : 3 * span]).astype(LOW)
    copies += fetch([(qkv_ref, qkv_hbm)], sems.at[pl.ds(3, 1)])
    key_at = lax.broadcasted_iota(jnp.int32, (patches, 1), 0)
    live = key_at < depth_ref[0] * (GRID * GRID)
    outs = []
    for head in range(heads):
        query = qkv_ref[:, head * HD : (head + 1) * HD]
        keys = qkv_ref[:, span + head * HD : span + (head + 1) * HD]
        values = qkv_ref[:, 2 * span + head * HD : 2 * span + (head + 1) * HD]
        scores = jnp.where(live, dot_last(keys, query) * HD ** (-0.5), -1000000000.0)
        expo = jnp.exp(scores - jnp.max(scores, axis=0, keepdims=True))
        probs = (expo * (1.0 / jnp.sum(expo, axis=0, keepdims=True))).astype(LOW)
        probs_ref[head] = probs
        copies += fetch([(probs_ref.at[head], probs_hbm.at[head])], sems.at[pl.ds(4 + head, 1)])
        outs.append(contract_first(probs, values))
    out_ref[...] = jnp.concatenate(outs, axis=1).astype(LOW)
    for copy in copies:
        copy.wait()


def attention(depth, me, rows, blocks, norms, heads, after):
    patches, width = 512, TOKEN_ROWS
    shapes = ((patches, width), (patches, width), (patches, 3 * heads * HD), (heads, patches, patches))
    count = len(blocks.pieces)
    return pl.pallas_call(
        functools.partial(attention_kernel, blocks),
        out_shape=tuple(
            jax.ShapeDtypeStruct(shape, LOW) for shape in ((patches, heads * HD),) + shapes
        ),
        in_specs=full_spec(3, pltpu.SMEM)
        + full_spec(4, pl.ANY)
        + full_spec(1)
        + blocks.specs()
        + full_spec(len(after), pl.ANY),
        out_specs=full_spec(1) + full_spec(4, pltpu.HBM),
        scratch_shapes=[pltpu.VMEM(shape, LOW) for shape in shapes]
        + [
            pltpu.VMEM((width, 4 * heads * HD), LOW),
            pltpu.SemaphoreType.DMA((4 + heads,)),
            pltpu.SemaphoreType.DMA((count,)),
            pltpu.SemaphoreType.DMA((24,)),
        ],
        compiler_params=pltpu.CompilerParams(vmem_limit_bytes=VMEM_LIMIT),
        cost_estimate=cost(7),
    )(blocks.indices, depth, me, *rows, norms, *blocks.pieces, *after)


def mlp_kernel(
    blocks, index_ref, core_ref, rows_hbm, out0, out1, out2, out3, w0, w1, w2, w3, norm_ref, *refs
):
    count = len(blocks.pieces)
    pieces = refs[:count]
    (
        mine_hbm, other_hbm, mid_hbm, mid_half_hbm, h_hbm, hidden_hbm, slope_hbm,
        partial_ref, rows_ref, weight_ref, mid_ref, h_ref, hidden_ref, slope_ref, other_ref,
        outs_ref, out_weights_ref, sems, load_sems, in_sems,
    ) = refs[-20:]
    hidden_here = hidden_ref.shape[1]
    core = core_ref[0]
    norms = norm_ref[...]
    loads = fetch([(rows_hbm, rows_ref)], sems)
    ins = fetch(
        [(out, outs_ref.at[at]) for at, out in enumerate((out0, out1, out2, out3))]
        + [(w, out_weights_ref.at[at]) for at, w in enumerate((w0, w1, w2, w3))],
        in_sems,
    )
    loads += blocks.load(index_ref, pieces, 0, 0, weight_ref, load_sems)
    loads[0].wait()
    for load in ins:
        load.wait()
    copies = []
    for block in range(2):
        at = slice(block * 256, (block + 1) * 256)
        mid = rows_ref[at].astype(jnp.float32)
        attended = jnp.concatenate([outs_ref[t, at] for t in range(4)], axis=1)
        weights = jnp.concatenate([out_weights_ref[t] for t in range(4)], axis=1)
        mid = mid + dot_last(attended, weights)
        mid_ref[at] = mid
        normed, _ = normalise(mid)
        low_rows = (normed * norms[2:3] + norms[3:4]).astype(LOW)
        h_ref[at] = low_rows
        if block == 0:
            for load in loads[1:]:
                load.wait()
        value, slope = gelu_and_slope(dot(low_rows, weight_ref[:, :hidden_here]))
        hidden = value.astype(LOW)
        hidden_ref[at] = hidden
        slope_ref[at] = slope.astype(LOW)
        partial_ref[at] = dot_last(hidden, weight_ref[:, hidden_here : 2 * hidden_here])
        own = pl.ds(pl.multiple_of(block * 256 + core * 128, 128), 128)
        their = pl.ds(pl.multiple_of(block * 256 + (1 - core) * 128, 128), 128)
        other_ref[block] = partial_ref[their].astype(LOW)
        rows = pl.ds(block * 256, 256)
        copies += fetch(
            [
                (other_ref.at[block], other_hbm.at[block]),
                (partial_ref.at[own], mine_hbm.at[block]),
                (mid_ref.at[own], mid_half_hbm.at[block]),
                (mid_ref.at[rows], mid_hbm.at[rows]),
                (h_ref.at[rows], h_hbm.at[rows]),
                (hidden_ref.at[rows], hidden_hbm.at[rows]),
                (slope_ref.at[rows], slope_hbm.at[rows]),
            ],
            sems.at[pl.ds(1 + 7 * block, 7)],
        )
    for copy in copies:
        copy.wait()


def mlp(core, rows, outs, out_weights, norms, blocks, hidden_here, after):
    patches, width = rows.shape
    f32 = jnp.float32
    half = (2, patches // 4, width)
    return pl.pallas_call(
        functools.partial(mlp_kernel, blocks),
        out_shape=(
            jax.ShapeDtypeStruct(half, f32),
            jax.ShapeDtypeStruct(half, LOW),
            jax.ShapeDtypeStruct((patches, width), f32),
            jax.ShapeDtypeStruct(half, f32),
            jax.ShapeDtypeStruct((patches, width), LOW),
            jax.ShapeDtypeStruct((patches, hidden_here), LOW),
            jax.ShapeDtypeStruct((patches, hidden_here), LOW),
        ),
        in_specs=full_spec(2, pltpu.SMEM)
        + full_spec(9, pltpu.HBM)
        + full_spec(1)
        + blocks.specs()
        + full_spec(len(after), pl.ANY),
        out_specs=full_spec(7, pltpu.HBM),
        scratch_shapes=[
            pltpu.VMEM((patches, width), f32),
            pltpu.VMEM((patches, width), LOW),
            pltpu.VMEM((width, 2 * hidden_here), LOW),
            pltpu.VMEM((patches, width), f32),
            pltpu.VMEM((patches, width), LOW),
            pltpu.VMEM((patches, hidden_here), LOW),
            pltpu.VMEM((patches, hidden_here), LOW),
            pltpu.VMEM(half, LOW),
            pltpu.VMEM((4,) + outs[0].shape, LOW),
            pltpu.VMEM((4,) + out_weights[0].shape, LOW),
            pltpu.SemaphoreType.DMA((15,)),
            pltpu.SemaphoreType.DMA((len(blocks.pieces),)),
            pltpu.SemaphoreType.DMA((8,)),
        ],
        compiler_params=pltpu.CompilerParams(vmem_limit_bytes=VMEM_LIMIT),
        cost_estimate=cost(9.3),
    )(blocks.indices, core, rows, *outs, *out_weights, norms, *blocks.pieces, *after)


def split_row(rows):
    return rows // 2 if rows % 16 else rows // 32 * 16


def put_chunks(index_ref, source, parts, targets, sems):
    target = targets[0]
    groups = target.shape[0]
    cut = split_row(target.shape[1])
    pairs, start, first = [], 0, 0
    for height in parts:
        rows = height // groups
        for at in range(groups):
            row = first if groups == 1 else pl.multiple_of(first + index_ref[at] * rows, 16)
            pairs.append((source.at[pl.ds(row, rows)], target.at[at, pl.ds(start, rows)]))
            if groups > 1 and at == groups - 1:
                for far, low, high in ((targets[1], 0, cut), (targets[2], cut, target.shape[1])):
                    begin, end = max(low, start), min(high, start + rows)
                    if begin < end:
                        taken = source.at[pl.ds(row + begin - start, end - begin)]
                        pairs.append((taken, far.at[pl.ds(begin - low, end - begin)]))
        start += rows
        first += height
    return fetch(pairs, sems)


def chunk_shapes(groups, rows, columns):
    cut = split_row(rows)
    shapes = [(groups, rows, columns)]
    if groups > 1:
        shapes += [(cut, columns), (rows - cut, columns)]
    return [jax.ShapeDtypeStruct(shape, LOW) for shape in shapes]


def in_ring_order(call, indices, parts):
    groups = indices.shape[0]
    if groups % 2 == 0 and all(rows // groups % 16 == 0 for rows in parts):
        return call(indices, groups)
    flat = call(jnp.zeros((1,), jnp.int32), 1)[0][0]
    blocks, start = [], 0
    for rows in parts:
        blocks.append(flat[start : start + rows].reshape(groups, rows // groups, -1)[indices])
        start += rows
    terms = jnp.concatenate(blocks, axis=1)
    cut = split_row(terms.shape[1])
    return terms, terms[-1, :cut], terms[-1, cut:]


def ring_add_kernel(above, below, cut, one_ref, two_ref, terms_hbm, *refs):
    ahead_ref, behind_ref, sems = refs[-3:]
    rows = ahead_ref.shape[0]
    for copy in fetch([(terms_hbm.at[above], ahead_ref), (terms_hbm.at[below], behind_ref)], sems):
        copy.wait()
    ahead = slice(0, cut) if one_ref.shape[0] < rows else slice(0, rows)
    behind = slice(cut, rows) if one_ref.shape[0] < rows else slice(0, rows)
    for target, at, came in ((ahead_ref, ahead, one_ref), (behind_ref, behind, two_ref)):
        target[at] = (target[at].astype(jnp.float32) + came[...].astype(jnp.float32)).astype(LOW)


def ring_add(one, two, terms, above, below, after, own_kernel):
    rows, columns = terms.shape[1:]
    cut = split_row(rows)
    if rows % 16 or not own_kernel:
        if after:
            one, two, _ = lax.optimization_barrier((one, two, after))
        above, below = terms[above], terms[below]
        if one.shape[0] == rows:
            return above + one, below + two
        return (
            jnp.concatenate([above[:cut] + one, above[cut:]]),
            jnp.concatenate([below[:cut], below[cut:] + two]),
        )
    return pl.pallas_call(
        functools.partial(ring_add_kernel, above, below, cut),
        out_shape=(jax.ShapeDtypeStruct((rows, columns), LOW),) * 2,
        in_specs=full_spec(2) + full_spec(1 + len(after), pl.ANY),
        out_specs=full_spec(2),
        scratch_shapes=[pltpu.SemaphoreType.DMA((2,))],
        compiler_params=pltpu.CompilerParams(vmem_limit_bytes=12 * MIB),
        cost_estimate=cost(2),
    )(one, two, terms, *after)


def mlp_sum_kernel(ahead_ref, behind_ref, own_ref, turn_ref, *refs):
    up_ref, down_ref, tconv_ref, conv1_ref, conv2_ref = refs[-5:]
    part, hidden = up_ref.shape
    total = (
        own_ref[0].astype(jnp.float32)
        + ahead_ref[...].astype(jnp.float32)
        + behind_ref[...].astype(jnp.float32)
    )
    up_ref[...] = total[:part, :hidden]
    down_ref[...] = total[:part, hidden : 2 * hidden]
    tconv_ref[...] = dot(total[:part, 2 * hidden :].astype(LOW), turn_ref[...])
    for which, conv_ref in enumerate((conv1_ref, conv2_ref)):
        for tap in range(27):
            at = which * 896 + tap * 32
            conv_ref[tap] = total[part:, at : at + 32]


def mlp_sum(ahead, behind, terms, part, hidden, after):
    rows, columns = ahead.shape
    conv_part = rows - part
    f32 = jnp.float32
    if part % 16 or conv_part % 16:
        total = terms[0].astype(f32) + ahead.astype(f32) + behind.astype(f32)
        tconv = total[:part, 2 * hidden :].reshape(part, 8, -1).transpose(0, 2, 1).reshape(part, -1)
        conv = total[part:].reshape(conv_part, 2, 28, 32)[:, :, :27].transpose(1, 2, 0, 3)
        return total[:part, :hidden], total[:part, hidden : 2 * hidden], tconv, conv[0], conv[1]
    return pl.pallas_call(
        mlp_sum_kernel,
        out_shape=(
            jax.ShapeDtypeStruct((part, hidden), f32),
            jax.ShapeDtypeStruct((part, hidden), f32),
            jax.ShapeDtypeStruct((part, 256), f32),
            jax.ShapeDtypeStruct((27, conv_part, 32), f32),
            jax.ShapeDtypeStruct((27, conv_part, 32), f32),
        ),
        in_specs=full_spec(2)
        + [pl.BlockSpec((1,) + terms.shape[1:], lambda at: (0, 0, 0))]
        + full_spec(1)
        + full_spec(len(after), pl.ANY),
        out_specs=full_spec(5),
        grid=(1,),
        compiler_params=pltpu.CompilerParams(vmem_limit_bytes=16 * MIB),
        cost_estimate=cost(2.4),
    )(ahead, behind, terms, jnp.asarray(turn_matrix().T), *after)


def norm_back_kernel(chip_ref, sum_ref, far_ref, grad_hbm, rows_hbm, norm_ref, *refs):
    own_ref, low_ref, grad_ref, rows_ref, sems = refs[-5:]
    for copy in fetch([(grad_hbm, grad_ref), (rows_hbm, rows_ref)], sems):
        copy.wait()
    gain = norm_ref[2:3]
    for block in range(2):
        summed = sum_ref[block].astype(jnp.float32) + far_ref[block].astype(jnp.float32)
        normed, scale = normalise(rows_ref[block])
        grad = grad_ref[block] + layer_norm_back(summed * gain, normed, scale)
        grad_ref[block] = grad
        low_ref[block] = grad.astype(LOW)
    own_ref[...] = grad_ref[chip_ref[0]]


def norm_back(chip, summed, far, grad, rows, norms, after):
    return pl.pallas_call(
        norm_back_kernel,
        out_shape=(
            jax.ShapeDtypeStruct(grad.shape[1:], jnp.float32),
            jax.ShapeDtypeStruct(grad.shape, LOW),
        ),
        in_specs=full_spec(1, pltpu.SMEM)
        + full_spec(2)
        + full_spec(2, pltpu.HBM)
        + full_spec(1)
        + full_spec(len(after), pl.ANY),
        out_specs=full_spec(2),
        scratch_shapes=[
            pltpu.VMEM(grad.shape, jnp.float32),
            pltpu.VMEM(rows.shape, jnp.float32),
            pltpu.SemaphoreType.DMA((2,)),
        ],
        compiler_params=pltpu.CompilerParams(vmem_limit_bytes=16 * MIB),
        cost_estimate=cost(4),
    )(chip, summed, far, grad, rows, norms, *after)


def attention_back_kernel(
    blocks, index_ref, core_ref, own_hbm, near_hbm, qkv_hbm, probs_hbm, rows_hbm, *refs
):
    count = len(blocks.pieces)
    pieces = refs[:count]
    (
        mine_hbm, other_hbm, grad_qkv_hbm, grad_hbm, sums_ref, grad_qkv_ref, grad_ref, partial_ref, other_ref,
        out_weight_ref, weight_ref, qkv_ref, probs_ref, rows_ref, sems, out_sems, load_sems,
    ) = refs[-17:]
    heads = probs_ref.shape[0]
    span = heads * HD
    core = core_ref[0]
    halves = []
    for block in range(2):
        own = pl.ds(pl.multiple_of(block * 256 + core * 128, 128), 128)
        their = pl.ds(pl.multiple_of(block * 256 + (1 - core) * 128, 128), 128)
        halves += [(own_hbm.at[block], grad_ref.at[own]), (near_hbm.at[block], grad_ref.at[their])]
    halves = fetch(halves, sems)
    outs = blocks.load(index_ref, pieces, 0, 4 * span - 256, out_weight_ref, load_sems)
    copies = fetch(
        [(qkv_hbm, qkv_ref)]
        + [(probs_hbm.at[head], probs_ref.at[head]) for head in range(heads)]
        + [(rows_hbm, rows_ref)],
        sems.at[pl.ds(4, 2 + heads)],
    )
    loads = blocks.load(index_ref, pieces, 0, 0, weight_ref, load_sems.at[pl.ds(count, count)])
    for copy in halves + outs:
        copy.wait()
    sent = fetch([(grad_ref, grad_hbm)], out_sems)
    grad_out = dot(grad_ref[...], out_weight_ref[:, 256 - span :]).astype(LOW)
    copies[0].wait()
    grad_query, grad_keys, grad_values = [], [], []
    for head in range(heads):
        query = qkv_ref[:, head * HD : (head + 1) * HD]
        keys = qkv_ref[:, span + head * HD : span + (head + 1) * HD]
        values = qkv_ref[:, 2 * span + head * HD : 2 * span + (head + 1) * HD]
        grad_head = grad_out[:, head * HD : (head + 1) * HD]
        copies[1 + head].wait()
        probs = probs_ref[head]
        grad_values.append(dot(probs, grad_head))
        probs = probs.astype(jnp.float32)
        grad_probs = dot_last(values, grad_head)
        inner = jnp.sum(probs * grad_probs, axis=0, keepdims=True)
        grad_scores = (probs * (grad_probs - inner)).astype(LOW)
        grad_query.append(contract_first(grad_scores, keys) * HD ** (-0.5))
        grad_keys.append(dot(grad_scores, query) * HD ** (-0.5))
    grad_qkv = jnp.concatenate(grad_query + grad_keys + grad_values, axis=1).astype(LOW)
    grad_qkv_ref[...] = grad_qkv
    sent += fetch([(grad_qkv_ref, grad_qkv_hbm)], out_sems.at[pl.ds(1, 1)])
    for load in loads:
        load.wait()
    partial_ref[...] = dot_last(grad_qkv, weight_ref[:, : 3 * span])
    pairs = []
    for block in range(2):
        own = pl.ds(pl.multiple_of(block * 256 + core * 128, 128), 128)
        their = pl.ds(pl.multiple_of(block * 256 + (1 - core) * 128, 128), 128)
        other_ref[block] = partial_ref[their].astype(LOW)
        pairs += [(partial_ref.at[own], mine_hbm.at[block]), (other_ref.at[block], other_hbm.at[block])]
    sent += fetch(pairs, out_sems.at[pl.ds(2, 4)])
    copies[1 + heads].wait()
    gain = shift = 0.0
    for block in range(2):
        at = slice(block * 256, (block + 1) * 256)
        normed, _ = normalise(rows_ref[at].astype(jnp.float32))
        gain += jnp.sum(partial_ref[at] * normed, axis=0, keepdims=True)
        shift += jnp.sum(partial_ref[at], axis=0, keepdims=True)
    sums_ref[...] = jnp.concatenate([gain, shift], axis=0)
    for copy in sent:
        copy.wait()


def attention_back(core, own, near, blocks, qkv, probs, rows, after):
    patches, width = rows.shape
    f32 = jnp.float32
    half = (2, patches // 4, width)
    return pl.pallas_call(
        functools.partial(attention_back_kernel, blocks),
        out_shape=(
            jax.ShapeDtypeStruct(half, f32),
            jax.ShapeDtypeStruct(half, LOW),
            jax.ShapeDtypeStruct(qkv.shape, LOW),
            jax.ShapeDtypeStruct((patches, width), LOW),
            jax.ShapeDtypeStruct((2, width), f32),
        ),
        in_specs=full_spec(2, pltpu.SMEM)
        + full_spec(5, pltpu.HBM)
        + blocks.specs()
        + full_spec(len(after), pl.ANY),
        out_specs=full_spec(4, pltpu.HBM) + full_spec(1),
        scratch_shapes=[
            pltpu.VMEM(qkv.shape, LOW),
            pltpu.VMEM((patches, width), LOW),
            pltpu.VMEM((patches, width), f32),
            pltpu.VMEM(half, LOW),
            pltpu.VMEM((width, 256), LOW),
            pltpu.VMEM((width, 4 * qkv.shape[1] // 3), LOW),
            pltpu.VMEM(qkv.shape, LOW),
            pltpu.VMEM(probs.shape, LOW),
            pltpu.VMEM(rows.shape, LOW),
            pltpu.SemaphoreType.DMA((6 + probs.shape[0],)),
            pltpu.SemaphoreType.DMA((6,)),
            pltpu.SemaphoreType.DMA((2 * len(blocks.pieces),)),
        ],
        compiler_params=pltpu.CompilerParams(vmem_limit_bytes=VMEM_LIMIT),
        cost_estimate=cost(9),
    )(blocks.indices, core, own, near, qkv, probs, rows, *blocks.pieces, *after)


def attention_weights_kernel(targets, order_ref, h_ref, out_ref, grad_qkv_ref, grad_ref, first_ref, second_ref, *refs):
    pack_ref, out_sems = refs[-2:]
    span = out_ref.shape[1]
    none = jnp.zeros((124, h_ref.shape[1]), jnp.float32)
    stacked = jnp.concatenate([first_ref[...], second_ref[...], none], axis=0)
    pack_ref[:, 4 * span :] = stacked.T.astype(LOW)
    pack_ref[:, : 3 * span] = contract_first(h_ref[...], grad_qkv_ref[...]).astype(LOW)
    pack_ref[:, 3 * span : 4 * span] = contract_first(grad_ref[...], out_ref[...]).astype(LOW)
    for copy in put_chunks(order_ref, pack_ref, (pack_ref.shape[0],), refs[len(refs) - 2 - targets : -2], out_sems):
        copy.wait()


def attention_weights(order, h_rows, out, grad_qkv, grad, first, second, after):
    width = h_rows.shape[1]
    columns = 4 * out.shape[1] + 128

    def call(order, groups):
        shapes = chunk_shapes(groups, width // groups, columns)
        return pl.pallas_call(
            functools.partial(attention_weights_kernel, len(shapes)),
            out_shape=tuple(shapes),
            in_specs=full_spec(1, pltpu.SMEM) + full_spec(6) + full_spec(len(after), pl.ANY),
            out_specs=full_spec(len(shapes), pltpu.HBM),
            scratch_shapes=[pltpu.VMEM((width, columns), LOW), pltpu.SemaphoreType.DMA((groups + 2,))],
            compiler_params=pltpu.CompilerParams(vmem_limit_bytes=16 * MIB),
            cost_estimate=cost(4),
        )(order, h_rows, out, grad_qkv, grad, first, second, *after)

    return in_ring_order(call, order, (width,))


def attention_sum_kernel(ahead_ref, behind_ref, own_ref, after_ref, query_ref, key_ref, value_ref, out_ref):
    span = query_ref.shape[1]
    total = (
        own_ref[0].astype(jnp.float32)
        + ahead_ref[...].astype(jnp.float32)
        + behind_ref[...].astype(jnp.float32)
    )
    query_ref[...] = total[:, :span]
    key_ref[...] = total[:, span : 2 * span]
    value_ref[...] = total[:, 2 * span : 3 * span]
    out_ref[...] = total[:, 3 * span : 4 * span].T


def attention_sum(ahead, behind, terms, span, after):
    part = ahead.shape[0]
    f32 = jnp.float32
    if part % 16:
        total = terms[0].astype(f32) + ahead.astype(f32) + behind.astype(f32)
        parts = [total[:, at * span : (at + 1) * span] for at in range(4)]
        return parts[0], parts[1], parts[2], parts[3].T
    return pl.pallas_call(
        attention_sum_kernel,
        out_shape=(jax.ShapeDtypeStruct((part, span), f32),) * 3
        + (jax.ShapeDtypeStruct((span, part), f32),),
        in_specs=full_spec(2)
        + [pl.BlockSpec((1,) + terms.shape[1:], lambda at: (0, 0, 0))]
        + full_spec(1, pl.ANY),
        out_specs=full_spec(4),
        grid=(1,),
        compiler_params=pltpu.CompilerParams(vmem_limit_bytes=12 * MIB),
        cost_estimate=cost(2),
    )(ahead, behind, terms, after)


class Ring:
    def __init__(self, size):
        self.size = size
        order = ring_order(size)
        self.ahead = [(order[i], order[(i + 1) % size]) for i in range(size)]
        self.behind = [(b, a) for a, b in self.ahead]
        reach = (size - 1) // 2
        self.distances = [0]
        for step in range(1, reach + 1):
            self.distances += [-step, step]
        if size % 2 == 0:
            self.distances.append(size // 2)
        table = np.array(
            [
                [order[(order.index(me) + distance) % size] for distance in self.distances]
                for me in range(size)
            ],
            np.int32,
        )
        self.indices = jnp.asarray(table)[lax.axis_index("dp")]

    def send(self, value, forward):
        return lax.ppermute(value, "dp", self.ahead if forward else self.behind)

    def gather(self, array):
        return Gather(self, array)

    def scatter(self, blocks):
        return Scatter(self, *blocks)


class Scatter:
    def __init__(self, ring, terms, far_one, far_two):
        self.ring = ring
        self.terms = terms
        self.far = far_one, far_two
        self.place = {distance: at for at, distance in enumerate(ring.distances)}
        self.reach = (ring.size - 1) // 2
        self.one = self.two = None
        self.left = self.reach + 1 if ring.size % 2 == 0 else self.reach

    def add(self, *after, own_kernel=False):
        distance = self.left
        if distance > self.reach:
            self.one, self.two = self.far
        elif self.one is None:
            self.one, self.two = self.terms[self.place[distance]], self.terms[self.place[-distance]]
        else:
            self.one, self.two = ring_add(
                self.one, self.two, self.terms, self.place[distance], self.place[-distance], after, own_kernel
            )
        return self.one, self.two

    def send(self, *after):
        one, two = self.one, self.two
        if after:
            one, two, _ = lax.optimization_barrier((one, two, after))
        self.one, self.two = self.ring.send(one, True), self.ring.send(two, False)
        self.left -= 1

    def result(self):
        while self.left > 0:
            self.add()
            self.send()
        if self.one is None:
            return jnp.zeros_like(self.terms[0]), jnp.zeros_like(self.terms[0])
        if self.one.shape[0] < self.terms.shape[1]:
            return jnp.concatenate([self.one, self.two]), jnp.zeros_like(self.terms[0])
        return self.one, self.two


class Gather:
    def __init__(self, ring, array):
        self.ring = ring
        self.array = array
        self.one = self.two = array
        self.starts = [0]
        self.pieces = [array]
        self.done = 0
        self.last = ()

    def step(self, *after):
        size = self.ring.size
        self.done += 1
        if after:
            self.one, self.two, _ = lax.optimization_barrier((self.one, self.two, after))
        if self.done <= (size - 1) // 2:
            self.one = self.ring.send(self.one, True)
            self.two = self.ring.send(self.two, False)
            self.starts += [0, 0]
        else:
            rows = self.array.shape[0]
            half = rows // 2 if rows % 16 else rows // 32 * 16
            self.last = self.one[:half], self.two[half:]
            self.one = self.ring.send(self.last[0], True)
            self.two = self.ring.send(self.last[1], False)
            self.starts += [0, half]
        self.pieces += [self.one, self.two]

    def steps_left(self):
        return self.ring.size // 2 - self.done

    def blocks(self, sections, base=0):
        indices = self.ring.indices
        if self.ring.size % 2 == 0:
            indices = jnp.concatenate([indices, indices[-1:]])
        return Blocks(indices, self.starts, self.pieces, self.ring.size, sections, base)


class Quad:
    def __init__(self):
        self.me = lax.axis_index("tensor")
        self.core = self.me % 2
        self.chip = self.me // 2

    def over_core(self, value):
        return lax.ppermute(value, "tensor", [(i, i ^ 1) for i in range(4)])

    def over_chip(self, value):
        return lax.ppermute(value, "tensor", [(i, i ^ 2) for i in range(4)])

    def spread(self, block):
        far = self.over_chip(block)
        return block, self.over_core(block), far, self.over_core(far)

    def spread_direct(self, block):
        last = lax.ppermute(block, "tensor", [(i, i ^ 3) for i in range(4)])
        return block, self.over_core(block), self.over_chip(block), last

    def pick(self, half):
        return jnp.where(self.chip == 0, half[0], half[1])


def selections(chans, chans_here):
    own = np.zeros((4, 2, chans_here, 2, chans), np.float32)
    spread = np.zeros((2, 4, 2, 2, chans_here, 2, chans), np.float32)
    place = np.zeros((4, 4, chans_here, 4, 4, chans_here), np.float32)
    for t in range(4):
        for c in range(chans_here):
            for e in range(2):
                own[t, e, c, e, t * chans_here + c] = 1.0
                for a in range(2):
                    spread[a, t, a, e, c, e, t * chans_here + c] = 1.0
            for group in range(4):
                place[t, group, c, group, t, c] = 1.0
    own = own.reshape(4, 2, chans_here, 2 * chans).astype(LOW)
    spread = spread.reshape(2, 16 * chans_here, 2 * chans).astype(LOW)
    place = place.reshape(16 * chans_here, 16 * chans_here).astype(LOW)
    return jnp.asarray(own), jnp.asarray(spread), jnp.asarray(place)


def shards(
    tokens,
    crop_depth,
    w_query,
    w_key,
    w_value,
    w_out,
    w_up,
    w_down,
    w_tconv,
    w_conv1,
    w_conv2,
    ln1_gain,
    ln1_bias,
    ln2_gain,
    ln2_bias,
    cot_out,
    cot_dec,
    groups,
):
    ring = Ring(groups)
    quad = Quad()
    grid = GRID
    vox = 2 * grid
    patches = grid**3
    width = w_query.shape[0] * groups
    part = w_query.shape[0]
    heads_here = w_query.shape[1] // HD
    span = heads_here * HD
    chans = w_conv1.shape[0] * groups
    chans_here = w_conv1.shape[2]

    low = lambda value: value.astype(LOW)
    hidden_here = w_up.shape[1]
    norm_rows = [row[None] for row in (ln1_gain, ln1_bias, ln2_gain, ln2_bias)]
    encoder_pack = pack_encoder(w_query, w_key, w_value, w_out, norm_rows, w_up, w_down.T)
    first = ring.gather(encoder_pack)
    first.step()
    own_pack = pack_own(w_tconv, w_conv1, w_conv2, encoder_pack)
    local_blocks = quad.spread(pack_local(tokens, cot_out, cot_dec[0], own_pack))
    while first.steps_left():
        first.step()
    blocks = first.blocks([(0, part)])
    mlp_blocks = first.blocks([(0, part)], 4 * span + 128)
    out_weight, norms = out_and_norms(blocks, span, 4 * span)
    pair_pack, sections = pack_pair(
        quad.chip[None], local_blocks[0], local_blocks[2], part, w_conv1.shape[0], encoder_pack
    )
    third = ring.gather(pair_pack)
    third.step(out_weight)
    arrived = third.one, third.two
    select, spread, place = selections(chans, chans_here)
    core = quad.core[None]
    me = quad.me[None]

    attended, rows_low, h_one, qkv, probs = attention(
        crop_depth, me, local_blocks, blocks, norms, heads_here, ()
    )
    attended = passed(attended, arrived)
    attended_blocks = quad.spread(attended)
    arrived = ()
    if third.steps_left():
        third.step(attended)
        arrived = third.one, third.two
    mine, other, mid, mid_half, h_two, hidden, slope = mlp(
        core,
        rows_low,
        attended_blocks,
        quad.spread(out_weight),
        norms,
        mlp_blocks,
        hidden_here,
        arrived,
    )
    arrived = ()
    if third.steps_left():
        third.step()
        arrived = third.one, third.two
    summed = half_sum(mine, quad.over_core(passed(other, arrived)), ())
    far = quad.over_chip(summed)
    while third.steps_left():
        third.step()
    decoder_own = join_decoder(third.blocks(sections), groups, part, summed)
    after, low_half = rows_sum(quad.chip[None], mid_half, summed, far, decoder_own)
    decoder_near, low_half = lax.optimization_barrier((decoder_own, low_half))
    decoder_near = quad.over_core(decoder_near)
    dec_out, grad_half, mlp_terms, mine, other, sums_two = decoder(
        ring.indices,
        crop_depth,
        me,
        low_half,
        quad.over_core(low_half),
        decoder_own,
        decoder_near,
        select,
        spread,
        place,
        local_blocks,
        slope,
        mid,
        h_two,
        hidden,
        mlp_blocks,
    )
    mlp_ring = ring.scatter(mlp_terms)
    mlp_ring.add()
    mlp_ring.send()
    summed = half_sum(mine, quad.over_core(other), ())
    far = quad.over_chip(summed)
    ready = mlp_ring.add(summed, own_kernel=True) if mlp_ring.left > 0 else ()
    grad_mid_own, low_mid_half = norm_back(
        quad.chip[None], summed, far, grad_half, mid_half, norms, ready
    )
    if mlp_ring.left > 0:
        mlp_ring.send(low_mid_half)
    mine, other, grad_qkv, grad_branch, sums_one = attention_back(
        core, low_mid_half, quad.over_core(low_mid_half), blocks, qkv, probs, rows_low, ()
    )
    ready = ()
    if mlp_ring.left > 0:
        ready = mlp_ring.add(sums_one)
        mlp_ring.send()
    attention_terms = attention_weights(
        ring.indices, h_one, attended, grad_qkv, grad_branch, sums_one, sums_two, ready
    )
    attention_ring = ring.scatter(attention_terms)
    attention_ring.add()
    attention_ring.send()
    last = ()
    while mlp_ring.left > 0 or attention_ring.left > 0:
        if attention_ring.left > 0:
            last = attention_ring.add(mlp_ring.one, mlp_ring.two)
            attention_ring.send()
        if mlp_ring.left > 0:
            mlp_ring.add()
            mlp_ring.send()
    mlp_ahead, mlp_behind = mlp_ring.result()
    ahead, behind = attention_ring.result()
    columns = slice(4 * span, 4 * span + 8)
    norm_grads = attention_terms[0][0, :, columns].astype(jnp.float32)
    norm_grads = norm_grads + ahead[:, columns].astype(jnp.float32)
    norm_grads = norm_grads + behind[:, columns].astype(jnp.float32)
    grad_query, grad_key, grad_value, grad_out = attention_sum(
        ahead, behind, attention_terms[0], span, norm_grads
    )
    norm_grads = sum(quad.spread_direct(norm_grads))
    summed = mine + quad.over_core(other).astype(jnp.float32)
    norm_own = quad.pick(summed) + quad.over_chip(low(quad.pick(summed[::-1]))).astype(jnp.float32)
    normed_own, scale_own = normalise(tokens.astype(jnp.float32))
    grad_tokens = grad_mid_own + layer_norm_back(norm_own * norms[0:1], normed_own, scale_own)
    grad_up, grad_down, grad_tconv, grad_conv1, grad_conv2 = mlp_sum(
        mlp_ahead, mlp_behind, mlp_terms[0], part, hidden_here, last
    )
    return (
        after,
        dec_out[None],
        grad_tokens,
        grad_query,
        grad_key,
        grad_value,
        grad_out,
        grad_up,
        grad_down.T,
        grad_tconv,
        grad_conv1.transpose(1, 0, 2),
        grad_conv2.transpose(1, 0, 2),
        norm_grads[:, 0],
        norm_grads[:, 1],
        norm_grads[:, 2],
        norm_grads[:, 3],
    )


def solution(mesh):
    in_specs = (
        P(("dp", "tensor"), None),
        P("dp"),
        P("dp", "tensor"),
        P("dp", "tensor"),
        P("dp", "tensor"),
        P("tensor", "dp"),
        P("dp", "tensor"),
        P("tensor", "dp"),
        P("dp", "tensor"),
        P("dp", None, "tensor"),
        P("dp", None, "tensor"),
        P("dp"),
        P("dp"),
        P("dp"),
        P("dp"),
        P(("dp", "tensor"), None),
        P("dp", None, None, None, "tensor"),
    )
    out_specs = (
        P(("dp", "tensor"), None),
        P("dp", None, None, None, "tensor"),
        P(("dp", "tensor"), None),
        P("dp", "tensor"),
        P("dp", "tensor"),
        P("dp", "tensor"),
        P("tensor", "dp"),
        P("dp", "tensor"),
        P("tensor", "dp"),
        P("dp", "tensor"),
        P("dp", None, "tensor"),
        P("dp", None, "tensor"),
        P("dp"),
        P("dp"),
        P("dp"),
        P("dp"),
    )
    groups = mesh.shape["dp"]

    def run(*arrays):
        return shards(*arrays, groups)

    return jax.shard_map(run, mesh=mesh, in_specs=in_specs, out_specs=out_specs, check_vma=False)
```

```python
import functools

import jax
import jax.numpy as jnp
import numpy as np
from jax import lax
from jax.experimental import pallas as pl
from jax.experimental.pallas import tpu as pltpu
from jax.sharding import PartitionSpec as P

HD = 64
GRID = 8
LOW = jnp.bfloat16


def ring_order(size):
    if size % 2:
        return list(range(size))
    return list(range(0, size, 2)) + list(range(size - 1, 0, -2))


def layer_norm_back(grad_normed, normed, scale):
    mean_grad = jnp.mean(grad_normed, axis=-1, keepdims=True)
    mean_dot = jnp.mean(grad_normed * normed, axis=-1, keepdims=True)
    return scale * (grad_normed - mean_grad - normed * mean_dot)


def contract_first(left, right):
    return lax.dot_general(
        left, right, (((0,), (0,)), ((), ())), preferred_element_type=jnp.float32
    )


MIB = 2**20
VMEM_LIMIT = 60 * MIB


def cost(microseconds):
    return pl.CostEstimate(flops=0, bytes_accessed=int(microseconds * 3.5e6), transcendentals=0)


def gelu_and_slope(x):
    bell = jnp.exp(-0.5 * x * x)
    frac = 1.0 / (1.0 + 0.3275911 * 0.7071067811865476 * jnp.abs(x))
    poly = frac * (
        0.254829592
        + frac * (-0.284496736 + frac * (1.421413741 + frac * (-1.453152027 + frac * 1.061405429)))
    )
    tail = 0.5 * poly * bell
    phi = jnp.where(x >= 0.0, 1.0 - tail, tail)
    return x * phi, phi + x * bell * 0.3989422804014327


def dot(left, right):
    return jnp.dot(left, right, preferred_element_type=jnp.float32)


def dot_last(left, right):
    return lax.dot_general(
        left, right, (((1,), (1,)), ((), ())), preferred_element_type=jnp.float32
    )


BATCH = 4


DECODER_REFS = 40


def decoder_kernel(
    blocks,
    index_ref,
    order_ref,
    depth_ref,
    me_ref,
    own_ref,
    near_ref,
    joined_hbm,
    joined_near_hbm,
    select_ref,
    spread_ref,
    place_ref,
    cot0_hbm,
    cot1_hbm,
    cot2_hbm,
    cot3_hbm,
    slope_hbm,
    mid_hbm,
    h_hbm,
    hidden_hbm,
    *refs,
):
    decoder_steps(
        blocks,
        refs[: len(blocks.pieces)],
        index_ref,
        order_ref,
        depth_ref,
        me_ref,
        own_ref,
        near_ref,
        joined_hbm,
        joined_near_hbm,
        select_ref,
        spread_ref,
        place_ref,
        (cot0_hbm, cot1_hbm, cot2_hbm, cot3_hbm),
        slope_hbm,
        mid_hbm,
        h_hbm,
        hidden_hbm,
        refs[len(blocks.pieces) : -DECODER_REFS],
        *refs[-DECODER_REFS:],
    )


def decoder_steps(
    blocks,
    pieces,
    index_ref,
    order_ref,
    depth_ref,
    me_ref,
    own_ref,
    near_ref,
    joined_hbm,
    joined_near_hbm,
    select_ref,
    spread_ref,
    place_ref,
    cots_hbm,
    slope_hbm,
    mid_hbm,
    h_hbm,
    hidden_hbm,
    terms_hbm,
    dec_hbm,
    grad_half_hbm,
    mine_hbm,
    other_hbm,
    sums_ref,
    other_ref,
    grad_low_ref,
    dec_ref,
    rows_ref,
    grad_tconv_ref,
    terms_ref,
    upper_ref,
    grad_rows_ref,
    wgrad_ref,
    first_even,
    first_odd,
    act_even,
    act_odd,
    grad_even,
    grad_odd,
    conv_ref,
    normed_ref,
    slope_ref,
    held_ref,
    carry_ref,
    low_grad_ref,
    columns_ref,
    tconv_ref,
    conv_w,
    back_w,
    cot_ref,
    up_ref,
    down_ref,
    gate_ref,
    mid_ref,
    h_ref,
    hidden_ref,
    sems,
    load_sems,
    out_sems,
):
    grid = 8
    vox = 16
    chans = 128
    depth = depth_ref[0]
    count = (depth * (2 * vox * vox)).astype(jnp.float32)

    core = lax.rem(me_ref[0], 2)
    loads = fetch(
        [
            (joined_hbm, terms_ref.at[pl.ds(pl.multiple_of(core * 512, 512), 512)]),
            (joined_near_hbm, terms_ref.at[pl.ds(pl.multiple_of((1 - core) * 512, 512), 512)]),
            (cots_hbm[0].at[pl.ds(TOKEN_ROWS, FIELD_ROWS)], cot_ref.at[me_ref[0]]),
            (cots_hbm[1].at[pl.ds(TOKEN_ROWS, FIELD_ROWS)], cot_ref.at[jnp.bitwise_xor(me_ref[0], 1)]),
            (cots_hbm[2].at[pl.ds(TOKEN_ROWS, FIELD_ROWS)], cot_ref.at[jnp.bitwise_xor(me_ref[0], 2)]),
            (cots_hbm[3].at[pl.ds(TOKEN_ROWS, FIELD_ROWS)], cot_ref.at[jnp.bitwise_xor(me_ref[0], 3)]),
            (slope_hbm, gate_ref),
            (mid_hbm, mid_ref),
            (h_hbm, h_ref),
            (hidden_hbm, hidden_ref),
        ],
        sems.at[pl.ds(3, 10)],
    )
    hidden = up_ref.shape[1]
    loads += blocks.load(index_ref, pieces, 0, hidden, down_ref, load_sems)
    loads += blocks.load(index_ref, pieces, 0, 0, up_ref, load_sems.at[pl.ds(len(pieces), len(pieces))])
    dec_copy = pltpu.make_async_copy(dec_ref, dec_hbm, sems.at[0])

    for even in (first_even, act_even, grad_even):
        even[:, 0] = jnp.zeros((grid, vox, 4 * chans), LOW)
        even[:, vox + 1] = jnp.zeros((grid, vox, 4 * chans), LOW)
    for odd in (first_odd, act_odd, grad_odd):
        odd[:, 0] = jnp.zeros((grid + 1, vox, 4 * chans), LOW)
        odd[:, vox + 1] = jnp.zeros((grid + 1, vox, 4 * chans), LOW)
    wgrad_ref[:, 864:] = jnp.zeros((2, 32, chans), jnp.float32)
    low_grad_ref[:, 0] = jnp.zeros((grid, vox, 2 * chans), LOW)
    low_grad_ref[:, vox + 1] = jnp.zeros((grid, vox, 2 * chans), LOW)

    spot = lax.broadcasted_iota(jnp.int32, (1, 1, 8, 1), 2)

    def put_field(even, odd, at, value):
        left = value[..., :chans]
        right = value[..., chans:]
        flat = (2 * vox, 8, chans)
        before = pltpu.roll(right.reshape(flat), 1, 1).reshape(right.shape)
        after = pltpu.roll(left.reshape(flat), 7, 1).reshape(left.shape)
        before = jnp.where(spot == 0, 0.0, before)
        after = jnp.where(spot == 7, 0.0, after)
        window = jnp.concatenate([before, value, after], axis=3)
        even[at, 1 : vox + 1] = window.reshape(vox, 16, 4 * chans).astype(LOW)
        early = jnp.concatenate([carry_ref[...][:, None], window[:, :1]], axis=1)
        odd[at, 1 : vox + 1] = early.reshape(vox, 16, 4 * chans).astype(LOW)
        carry_ref[...] = window[:, 1]

    def open_field():
        carry_ref[...] = jnp.zeros(carry_ref.shape, jnp.float32)

    def close_field(odd):
        late = jnp.concatenate([carry_ref[...], jnp.zeros(carry_ref.shape, jnp.float32)], axis=1)
        odd[grid, 1 : vox + 1] = late.astype(LOW)

    def live_at(at):
        return (at < depth).astype(jnp.float32)

    def convolve(even, odd, weights, target, turned):
        def step(block, total):
            at = block * BATCH
            summed = None
            for deep in range(3):
                field = even if deep == 1 else odd
                start = at + 1 if deep == 2 else at
                for tall in range(3):
                    left = field[pl.ds(start, BATCH), tall : tall + vox]
                    left = left.reshape(BATCH * vox * 16, 4 * chans)
                    right = weights[deep * 3 + tall]
                    term = dot_last(left, right) if turned else dot(left, right)
                    summed = term if summed is None else summed + term
            target[pl.ds(at, BATCH)] = summed.reshape(BATCH, vox, 16, 2 * chans)
            return total

        lax.fori_loop(0, grid // BATCH, step, 0)

    def both(total):
        row = jnp.sum(total, axis=0, keepdims=True)
        half = (row[:, :chans] + row[:, chans:]) / count
        return jnp.concatenate([half, half], axis=1)

    def zero():
        return jnp.zeros((8, 2 * chans), jnp.float32)

    def fold(value):
        return jnp.sum(value.reshape(2 * vox, 8, 2 * chans), axis=0)

    def statistics(source):
        def first(at, total):
            return total + live_at(at) * fold(source[at])

        middle = both(lax.fori_loop(0, grid, first, zero()))

        def second(at, total):
            away = source[at] - middle
            return total + live_at(at) * fold(away * away)

        spread = both(lax.fori_loop(0, grid, second, zero()))
        return middle, lax.rsqrt(spread + 1e-05)

    for block in range(2):
        rows_ref[pl.ds(pl.multiple_of(block * 256 + core * 128, 128), 128)] = own_ref[block]
        rows_ref[pl.ds(pl.multiple_of(block * 256 + (1 - core) * 128, 128), 128)] = near_ref[block]
    loads[0].wait()
    loads[1].wait()
    make_tconv(terms_ref, place_ref[...], tconv_ref)
    for part in range(4):
        wide = dot(rows_ref[...], tconv_ref[:, part * 256 : (part + 1) * 256])
        held_ref[:, part * 4 : (part + 1) * 4] = wide.reshape(grid, 4, 16, 2 * chans)
    open_field()

    def place_first(at, state):
        tokens = held_ref[at] * live_at(at)
        offsets = [
            [tokens[8 * a + 4 * b : 8 * a + 4 * b + 4].reshape(8, 1, 1, 8, 256) for a in range(2)]
            for b in range(2)
        ]
        value = jnp.concatenate(
            [jnp.concatenate(offsets[b], axis=2) for b in range(2)], axis=1
        ).reshape(vox, 2, 8, 256)
        put_field(first_even, first_odd, at, value)
        return state

    lax.fori_loop(0, grid, place_first, 0)
    close_field(first_odd)

    for which in range(2):
        make_taps(terms_ref, place_ref[...], which, conv_w.at[which], back_w.at[which])
    convolve(first_even, first_odd, conv_w.at[0], normed_ref, False)
    middle, scale_one = statistics(normed_ref)
    open_field()

    def act_first(at, state):
        normed = (normed_ref[at] - middle) * scale_one
        normed_ref[at] = normed
        value, slope = gelu_and_slope(normed)
        live = live_at(at)
        slope_ref[at] = slope * live
        put_field(act_even, act_odd, at, (value * live).reshape(vox, 2, 8, 2 * chans))
        return state

    lax.fori_loop(0, grid, act_first, 0)
    close_field(act_odd)

    convolve(act_even, act_odd, conv_w.at[1], conv_ref, False)
    middle, scale_two = statistics(conv_ref)
    for load in loads[2:6]:
        load.wait()

    def act_second(at, totals):
        normed = (conv_ref[at] - middle) * scale_two
        conv_ref[at] = normed
        value, slope = gelu_and_slope(normed)
        live = live_at(at)
        low_value = (value * live).astype(LOW).reshape(vox * 16, 2 * chans)
        for e in range(2):
            shown = dot_last(low_value, select_ref[me_ref[0], e]).reshape(vox, 2, 8, 32)
            for a in range(2):
                dec_ref[2 * at + a, :, pl.ds(e, 8, stride=2), :] = shown[:, a]
        parts = [cot_ref[t, pl.ds(768 + at * vox * 8, vox * 8)] for t in range(4)]
        packed = jnp.concatenate(parts, axis=1)
        cot = jnp.concatenate(
            [dot(packed, spread_ref[a]).reshape(vox, 1, 8, 2 * chans) for a in range(2)], axis=1
        ).reshape(vox, 16, 2 * chans)
        grad = cot * slope * live
        held_ref[at] = grad
        return totals[0] + fold(grad), totals[1] + fold(grad * normed)

    totals = lax.fori_loop(0, grid, act_second, (zero(), zero()))
    dec_copy.start()

    def norm_back(source, normed_source, scale, sums):
        mean_grad = both(sums[0])
        mean_dot = both(sums[1])
        open_field()

        def step(at, state):
            grad = source[at] - live_at(at) * (mean_grad + normed_source[at] * mean_dot)
            grad = scale * grad
            low_grad_ref[at, 1 : vox + 1] = grad.astype(LOW)
            put_field(grad_even, grad_odd, at, grad.reshape(vox, 2, 8, 2 * chans))
            return state

        lax.fori_loop(0, grid, step, 0)
        close_field(grad_odd)

    def weight_grad(even, odd, which):
        own = select_ref[me_ref[0]].reshape(64, 2 * chans)
        for at in range(grid):
            shifts = [
                dot_last(own, low_grad_ref[at, 2 - tall : 18 - tall].reshape(vox * 16, 2 * chans))
                for tall in range(3)
            ]
            columns_ref[:, at * 256 : (at + 1) * 256] = jnp.concatenate(shifts, axis=0).astype(LOW)
        for deep in range(3):
            field = even if deep == 1 else odd
            start = 1 if deep == 2 else 0
            right = field[start : start + grid, 1 : vox + 1].reshape(grid * vox * 16, 4 * chans)
            sums = dot(columns_ref[...], right)
            for tall in range(3):
                for wide in range(3):
                    top = sums[tall * 64 : tall * 64 + 32, wide * chans : (wide + 1) * chans]
                    low = sums[tall * 64 + 32 : tall * 64 + 64, (wide + 1) * chans : (wide + 2) * chans]
                    tap = deep * 9 + tall * 3 + wide
                    wgrad_ref[which, tap * 32 : (tap + 1) * 32] = top + low

    norm_back(held_ref, conv_ref, scale_two, totals)
    weight_grad(act_even, act_odd, 1)
    convolve(grad_even, grad_odd, back_w.at[1], conv_ref, True)

    def slope_first(at, totals):
        grad = conv_ref[at] * slope_ref[at]
        conv_ref[at] = grad
        return totals[0] + fold(grad), totals[1] + fold(grad * normed_ref[at])

    totals = lax.fori_loop(0, grid, slope_first, (zero(), zero()))
    norm_back(conv_ref, normed_ref, scale_one, totals)
    weight_grad(first_even, first_odd, 0)
    convolve(grad_even, grad_odd, back_w.at[0], conv_ref, True)

    def rows_back(at, state):
        grad = (conv_ref[at] * live_at(at)).reshape(8, 2, 2, 8, 2 * chans)
        for a in range(2):
            for b in range(2):
                block = grad[:, b, a].reshape(64, 2 * chans).astype(LOW)
                column = (2 * a + b) * 256
                grad_tconv_ref[pl.ds(at * 64, 64), column : column + 256] = block
        return state

    lax.fori_loop(0, grid, rows_back, 0)
    for which in range(2):
        for block in range(7):
            at = (7 * which + block) * 128
            taps = wgrad_ref[which, block * 128 : (block + 1) * 128].T.astype(LOW)
            terms_ref[768:896, at : at + 128] = taps
    own = select_ref[me_ref[0]].reshape(64, 2 * chans)
    spans = [dot_last(grad_tconv_ref[:, at * 256 : (at + 1) * 256], own) for at in range(4)]
    mine = jnp.concatenate(spans, axis=1).astype(LOW)
    terms_ref[:768, 2 * hidden :] = contract_first(rows_ref[...], mine).astype(LOW)
    for t in range(4):
        at = slice(t * 128, (t + 1) * 128)
        tiles = [cot_ref[t, block * 128 : (block + 1) * 128] for block in range(6)]
        cot_rows = jnp.concatenate(tiles, axis=1).astype(jnp.float32)
        grad_rows_ref[at] = cot_rows + dot_last(grad_tconv_ref[at], tconv_ref[...])
    grad_low_ref[...] = grad_rows_ref[...].astype(LOW)
    halves = []
    for block in range(2):
        own = pl.ds(pl.multiple_of(block * 256 + core * 128, 128), 128)
        halves.append((grad_rows_ref.at[own], grad_half_hbm.at[block]))
    half_copies = fetch(halves, sems.at[pl.ds(1, 2)])
    for load in loads[6:]:
        load.wait()
    for copy in half_copies:
        copy.wait()
    sent = []
    gain = shift = 0.0
    for block in range(2):
        at = slice(block * 256, (block + 1) * 256)
        grad = dot(grad_low_ref[at], down_ref[...])
        upper = (grad * gate_ref[at].astype(jnp.float32)).astype(LOW)
        upper_ref[at] = upper
        grad_normed = dot_last(upper, up_ref[...])
        normed, _ = normalise(mid_ref[at])
        gain += jnp.sum(grad_normed * normed, axis=0, keepdims=True)
        shift += jnp.sum(grad_normed, axis=0, keepdims=True)
        grad_rows_ref[at] = grad_normed
        own = pl.ds(pl.multiple_of(block * 256 + core * 128, 128), 128)
        their = pl.ds(pl.multiple_of(block * 256 + (1 - core) * 128, 128), 128)
        other_ref[block] = grad_rows_ref[their].astype(LOW)
        sent += fetch(
            [(grad_rows_ref.at[own], mine_hbm.at[block]), (other_ref.at[block], other_hbm.at[block])],
            sems.at[pl.ds(3 + 2 * block, 2)],
        )
    sums_ref[...] = jnp.concatenate([gain, shift], axis=0)
    terms_ref[:768, :hidden] = contract_first(h_ref[...], upper_ref[...]).astype(LOW)
    terms_ref[:768, hidden : 2 * hidden] = contract_first(grad_low_ref[...], hidden_ref[...]).astype(LOW)
    for copy in sent + put_chunks(order_ref, terms_ref, (768, 128), terms_hbm, out_sems):
        copy.wait()
    dec_copy.wait()


def decoder(
    order, depth, me, own, near, joined, joined_near, select, spread, place, cots, slope, mid, h_rows, hidden, blocks
):
    f32 = jnp.float32
    vmem = pl.BlockSpec(memory_space=pltpu.VMEM)
    hbm = pl.BlockSpec(memory_space=pltpu.HBM)
    here = slope.shape[1]
    columns = 2 * here + 256
    window = lambda planes: pltpu.VMEM((planes, 18, 16, 512), LOW)
    field = lambda kind: pltpu.VMEM((8, 16, 16, 256), kind)
    kept = []

    def call(order, groups):
        shapes = chunk_shapes(groups, 896 // groups, columns)
        outs = pl.pallas_call(
            functools.partial(decoder_kernel, blocks),
            out_shape=(
                *shapes,
                jax.ShapeDtypeStruct((16, 16, 16, 32), f32),
                jax.ShapeDtypeStruct((2, 128, 768), f32),
                jax.ShapeDtypeStruct((2, 128, 768), f32),
                jax.ShapeDtypeStruct((2, 128, 768), LOW),
                jax.ShapeDtypeStruct((2, 768), f32),
            ),
            in_specs=[pl.BlockSpec(memory_space=pltpu.SMEM)] * 4
            + [vmem] * 2
            + [hbm] * 2
            + [vmem] * 3
            + [hbm] * 8
            + blocks.specs(),
            out_specs=[hbm] * (len(shapes) + 4) + [vmem],
            scratch_shapes=[
                pltpu.VMEM((2, 128, 768), LOW),
                pltpu.VMEM((512, 768), LOW),
                pltpu.VMEM((16, 16, 16, 32), f32),
                pltpu.VMEM((512, 768), LOW),
                pltpu.VMEM((512, 1024), LOW),
                pltpu.VMEM((1024, columns), LOW),
                pltpu.VMEM(slope.shape, LOW),
                pltpu.VMEM((512, 768), f32),
                pltpu.VMEM((2, 896, 128), f32),
                window(8),
                window(9),
                window(8),
                window(9),
                window(8),
                window(9),
                field(f32),
                field(f32),
                field(f32),
                field(f32),
                pltpu.VMEM((16, 8, 512), f32),
                pltpu.VMEM((8, 18, 16, 256), LOW),
                pltpu.VMEM((192, 2048), LOW),
                pltpu.VMEM((768, 1024), LOW),
                pltpu.VMEM((2, 9, 512, 256), LOW),
                pltpu.VMEM((2, 9, 256, 512), LOW),
                pltpu.VMEM((4, 1792, 128), LOW),
                pltpu.VMEM((768, here), LOW),
                pltpu.VMEM((768, here), LOW),
                pltpu.VMEM(slope.shape, LOW),
                pltpu.VMEM(mid.shape, f32),
                pltpu.VMEM(h_rows.shape, LOW),
                pltpu.VMEM(hidden.shape, LOW),
                pltpu.SemaphoreType.DMA((13,)),
                pltpu.SemaphoreType.DMA((2 * len(blocks.pieces),)),
                pltpu.SemaphoreType.DMA((2 * groups + 4,)),
            ],
            compiler_params=pltpu.CompilerParams(vmem_limit_bytes=VMEM_LIMIT),
            cost_estimate=cost(52),
        )(
            blocks.indices,
            order,
            depth,
            me,
            own,
            near,
            joined,
            joined_near,
            select,
            spread,
            place,
            *cots,
            slope,
            mid,
            h_rows,
            hidden,
            *blocks.pieces,
        )
        kept.extend(outs[len(shapes) :])
        return outs[: len(shapes)]

    terms = in_ring_order(call, order, (768, 128))
    dec, half, mine, other, sums = kept
    return dec, half, terms, mine, other, sums


def full_spec(count, space=pltpu.VMEM):
    return [pl.BlockSpec(memory_space=space)] * count


def fetch(pairs, sems):
    copies = [
        pltpu.make_async_copy(source, target, sems.at[at]) for at, (source, target) in enumerate(pairs)
    ]
    for copy in copies:
        copy.start()
    return copies


class Blocks:
    def __init__(self, indices, starts, pieces, size, sections, base=0):
        self.base = base
        block, columns = pieces[0].shape
        edges = [end for section in sections for end in section]
        if any(edge % 16 for edge in edges + list(starts)):
            full = jnp.zeros((size * block, columns), pieces[0].dtype)
            for at, (start, piece) in enumerate(zip(starts, pieces)):
                full = lax.dynamic_update_slice(full, piece, (indices[at] * block + start, 0))
            full = full.reshape(size, block, columns)
            parts = [full[:, low:high].reshape(-1, columns) for low, high in sections]
            pieces, starts, indices = [jnp.concatenate(parts)], [0], jnp.zeros((1,), jnp.int32)
            sections = [(size * low, size * high) for low, high in sections]
            size = 1
        self.indices = indices
        self.starts = tuple(starts)
        self.pieces = tuple(pieces)
        self.size = size
        self.sections = tuple(sections)

    def specs(self):
        return full_spec(len(self.pieces), pl.ANY)

    def rows(self, section):
        low, high = self.sections[section]
        return self.size * (high - low)

    def load(self, index_ref, refs, section, column, target, sems):
        low, high = self.sections[section]
        copies = []
        for at, (piece, start) in enumerate(zip(refs, self.starts)):
            first, last = max(low, start), min(high, start + piece.shape[0])
            if first >= last:
                continue
            row = index_ref[at] * (high - low) + first - low
            if len(self.pieces) > 1:
                row = pl.multiple_of(row, 16)
            columns = pl.ds(self.base + column, target.shape[1])
            source = piece.at[pl.ds(first - start, last - first), columns]
            copies += fetch([(source, target.at[pl.ds(row, last - first)])], sems.at[pl.ds(at, 1)])
        return copies


def pack_kernel(
    query_ref, key_ref, value_ref, out_ref, gain1_ref, bias1_ref, gain2_ref, bias2_ref, up_ref, down_ref, pack_ref
):
    at = 0
    none = jnp.zeros((124, gain1_ref.shape[1]), jnp.float32)
    norms = [gain1_ref[...], bias1_ref[...], gain2_ref[...], bias2_ref[...], none]
    norms = jnp.concatenate(norms, axis=0).T
    for value in (
        query_ref[...], key_ref[...], value_ref[...], out_ref[...].T, norms, up_ref[...], down_ref[...],
    ):
        pack_ref[:, at : at + value.shape[1]] = value.astype(LOW)
        at += value.shape[1]


def pack_encoder(query, key, value, out, norms, up, down):
    part = query.shape[0]
    if part % 16:
        columns = jnp.pad(jnp.concatenate(norms), ((0, 124), (0, 0))).T
        parts = (query, key, value, out.T, columns, up, down)
        return jnp.concatenate([array.astype(LOW) for array in parts], axis=1)
    return pl.pallas_call(
        pack_kernel,
        out_shape=jax.ShapeDtypeStruct((part, 4 * query.shape[1] + 128 + 2 * up.shape[1]), LOW),
        in_specs=full_spec(10),
        out_specs=pl.BlockSpec(memory_space=pltpu.VMEM),
        cost_estimate=cost(2),
    )(query, key, value, out, *norms, up, down)


def pack_own_kernel(tconv_ref, conv1_ref, conv2_ref, turn_ref, after_ref, pack_ref):
    part = tconv_ref.shape[0]
    conv_part = conv1_ref.shape[1]
    pack_ref[:part] = dot(tconv_ref[...].astype(LOW), turn_ref[...]).astype(LOW)
    taps = []
    for conv_ref in (conv1_ref, conv2_ref):
        taps += [conv_ref[tap] for tap in range(27)] + [jnp.zeros(conv_ref.shape[1:], jnp.float32)]
    for tile in range(14):
        made = jnp.concatenate(taps[4 * tile : 4 * tile + 4], axis=1).astype(LOW)
        at = part + tile // 2 * conv_part
        pack_ref[at : at + conv_part, tile % 2 * 128 : (tile % 2 + 1) * 128] = made


def turn_matrix():
    turn = np.zeros((32, 8, 8, 32), np.float32)
    for group in range(8):
        for chan in range(32):
            turn[chan, group, group, chan] = 1.0
    return turn.reshape(256, 256).astype(LOW)


def pack_own(tconv, conv1, conv2, after):
    part, conv_part = tconv.shape[0], conv1.shape[0]
    if part % 16 or conv_part % 16:
        conv = jnp.stack([conv1.astype(LOW), conv2.astype(LOW)], axis=1)
        conv = jnp.pad(conv, ((0, 0), (0, 0), (0, 1), (0, 0)))
        conv = conv.reshape(conv_part, 7, 256).transpose(1, 0, 2)
        turned = tconv.astype(LOW).reshape(part, 32, 8).transpose(0, 2, 1).reshape(part, -1)
        return jnp.concatenate([turned, conv.reshape(-1, 256)])
    return pl.pallas_call(
        pack_own_kernel,
        out_shape=jax.ShapeDtypeStruct((part + 7 * conv_part, 256), LOW),
        in_specs=full_spec(4) + full_spec(1, pl.ANY),
        out_specs=pl.BlockSpec(memory_space=pltpu.VMEM),
        cost_estimate=cost(2),
    )(tconv, conv1.transpose(1, 0, 2), conv2.transpose(1, 0, 2), jnp.asarray(turn_matrix()), after)


def fold_tconv(rows, columns):
    count = rows.shape[0]
    if count % 16:
        flat = rows.reshape(-1)
        flat = jnp.pad(flat, (0, -flat.shape[0] % columns))
        return flat.reshape(-1, columns)
    folded = rows.reshape(count // 16, 16, 256).transpose(1, 0, 2).reshape(16, -1)
    return jnp.pad(folded, ((0, 0), (0, columns - folded.shape[1])))


TOKEN_ROWS = 768
FIELD_ROWS = 1792
PACK_AT = TOKEN_ROWS + FIELD_ROWS


def pack_local_kernel(tokens_ref, cot_ref, field_ref, own_ref, pack_ref):
    for block in range(6):
        lanes = slice(block * 128, (block + 1) * 128)
        pack_ref[block * 128 : (block + 1) * 128] = tokens_ref[:, lanes]
        at = TOKEN_ROWS + block * 128
        pack_ref[at : at + 128] = cot_ref[:, lanes].astype(LOW)
    for pair in range(8):
        parts = [
            field_ref[2 * pair + a, :, pl.ds(e, 8, stride=2), :].reshape(128, 32)
            for a in range(2)
            for e in range(2)
        ]
        at = 2 * TOKEN_ROWS + pair * 128
        pack_ref[at : at + 128] = jnp.concatenate(parts, axis=1).astype(LOW)
    count = own_ref.shape[0]
    if count % 16 == 0:
        for half in range(2):
            at = PACK_AT + half * count
            pack_ref[at : at + count] = own_ref[:, half * 128 : (half + 1) * 128]


def pack_local(tokens, cot, field, own):
    aligned = own.shape[0] % 16 == 0
    total = PACK_AT + (2 * own.shape[0] if aligned else 0)
    pack = pl.pallas_call(
        pack_local_kernel,
        out_shape=jax.ShapeDtypeStruct((total, 128), LOW),
        in_specs=full_spec(4),
        out_specs=pl.BlockSpec(memory_space=pltpu.VMEM),
        compiler_params=pltpu.CompilerParams(vmem_limit_bytes=VMEM_LIMIT),
        cost_estimate=cost(3),
    )(tokens, cot, field, own)
    if aligned:
        return pack
    halves = own.reshape(-1, 2, 128).transpose(1, 0, 2).reshape(-1, 128)
    return jnp.concatenate([pack, halves])


def pack_pair_kernel(part, conv_part, chip_ref, own_hbm, far_hbm, after_ref, pack_ref, held_ref, sems):
    columns = pack_ref.shape[1]
    count = part + 7 * conv_part
    source = pl.ds(PACK_AT, 2 * count)
    for copy in fetch(
        [
            (own_hbm.at[source], held_ref.at[chip_ref[0]]),
            (far_hbm.at[source], held_ref.at[1 - chip_ref[0]]),
        ],
        sems,
    ):
        copy.wait()
    for which in range(2):
        for half in range(2):
            first = half * count
            at = which * conv_part
            for block in range(7):
                start = first + part + block * conv_part
                lanes = slice(block * 256 + half * 128, block * 256 + (half + 1) * 128)
                pack_ref[at : at + conv_part, lanes] = held_ref[which, start : start + conv_part]
            at = 2 * conv_part + which * 16
            for block in range(part // 16):
                start = first + block * 16
                lanes = slice(block * 256 + half * 128, block * 256 + (half + 1) * 128)
                pack_ref[at : at + 16, lanes] = held_ref[which, start : start + 16]
        at = 2 * conv_part + which * 16
        pack_ref[at : at + 16, part * 16 :] = jnp.zeros((16, columns - part * 16), LOW)


def pack_pair(chip, own, far, part, conv_part, after):
    columns = 7 * 256
    count = part + 7 * conv_part
    if part % 16 or conv_part % 16:
        own, far = [
            packed[PACK_AT:].reshape(2, count, 128).transpose(1, 0, 2).reshape(count, 256)
            for packed in (own, far)
        ]
        first = jnp.where(chip[0] > 0, far, own)
        second = jnp.where(chip[0] > 0, own, far)
        convs = [
            packed[part:].reshape(7, conv_part, 256).transpose(1, 0, 2).reshape(conv_part, columns)
            for packed in (first, second)
        ]
        pack = jnp.concatenate(convs + [fold_tconv(packed[:part], columns) for packed in (first, second)])
    else:
        pack = pl.pallas_call(
            functools.partial(pack_pair_kernel, part, conv_part),
            out_shape=jax.ShapeDtypeStruct((2 * conv_part + 32, columns), LOW),
            in_specs=full_spec(1, pltpu.SMEM) + full_spec(3, pl.ANY),
            out_specs=pl.BlockSpec(memory_space=pltpu.VMEM),
            scratch_shapes=[pltpu.VMEM((2, 2 * count, 128), LOW), pltpu.SemaphoreType.DMA((2,))],
            cost_estimate=cost(1.7),
        )(chip, own, far, after)
    fold = (pack.shape[0] - 2 * conv_part) // 2
    edges = [0, conv_part, 2 * conv_part, 2 * conv_part + fold, pack.shape[0]]
    return pack, list(zip(edges[:-1], edges[1:]))


def out_norm_kernel(blocks, norm_at, index_ref, *refs):
    count = len(blocks.pieces)
    pieces = refs[:count]
    out_ref, norm_ref, wide_ref, columns_ref, sems = refs[count:]
    span = out_ref.shape[1]
    copies = blocks.load(index_ref, pieces, 0, 4 * span - 256, wide_ref, sems)
    copies += blocks.load(index_ref, pieces, 0, norm_at, columns_ref, sems.at[pl.ds(count, count)])
    for copy in copies:
        copy.wait()
    out_ref[...] = wide_ref[:, 256 - span :]
    norm_ref[...] = columns_ref[...].astype(jnp.float32).T[:8]


def out_and_norms(blocks, span, norm_at):
    count = len(blocks.pieces)
    return pl.pallas_call(
        functools.partial(out_norm_kernel, blocks, norm_at),
        out_shape=(
            jax.ShapeDtypeStruct((blocks.rows(0), span), LOW),
            jax.ShapeDtypeStruct((8, blocks.rows(0)), jnp.float32),
        ),
        in_specs=full_spec(1, pltpu.SMEM) + blocks.specs(),
        out_specs=full_spec(2),
        scratch_shapes=[
            pltpu.VMEM((blocks.rows(0), 256), LOW),
            pltpu.VMEM((blocks.rows(0), 128), LOW),
            pltpu.SemaphoreType.DMA((2 * count,)),
        ],
        compiler_params=pltpu.CompilerParams(vmem_limit_bytes=12 * MIB),
        cost_estimate=cost(2.7),
    )(blocks.indices, *blocks.pieces)


def join_kernel(blocks, index_ref, *refs):
    count = len(blocks.pieces)
    join_ref, sems = refs[-2:]
    copies = []
    for section in range(4):
        target = join_ref.at[pl.ds(section * 128, 128)]
        copies += blocks.load(
            index_ref, refs[:count], section, 0, target, sems.at[pl.ds(section * count, count)]
        )
    for copy in copies:
        copy.wait()


def join_decoder(blocks, groups, part, after):
    columns = blocks.pieces[0].shape[1]
    count = len(blocks.pieces)
    if count == 1:
        full = blocks.pieces[0]
        parts = [full[low:high] for low, high in blocks.sections]
        folded = []
        for rows in parts[2:]:
            rows = rows.reshape(groups, -1)[:, : part * 256].reshape(-1, 256)
            folded += [fold_tconv(rows[at * 96 : (at + 1) * 96], columns) for at in range(8)]
        return jnp.concatenate(parts[:2] + folded)
    return pl.pallas_call(
        functools.partial(join_kernel, blocks),
        out_shape=jax.ShapeDtypeStruct((512, columns), LOW),
        in_specs=full_spec(1, pltpu.SMEM) + blocks.specs() + full_spec(1, pl.ANY),
        out_specs=pl.BlockSpec(memory_space=pltpu.VMEM),
        scratch_shapes=[pltpu.SemaphoreType.DMA((4 * count,))],
        compiler_params=pltpu.CompilerParams(vmem_limit_bytes=12 * MIB),
        cost_estimate=cost(3.8),
    )(blocks.indices, *blocks.pieces, after)


def pass_kernel(value_ref, *refs):
    refs[-1][...] = value_ref[...]


def passed(value, after):
    return pl.pallas_call(
        pass_kernel,
        out_shape=jax.ShapeDtypeStruct(value.shape, value.dtype),
        in_specs=full_spec(1) + full_spec(len(after), pl.ANY),
        out_specs=pl.BlockSpec(memory_space=pltpu.VMEM),
        compiler_params=pltpu.CompilerParams(vmem_limit_bytes=8 * MIB),
        cost_estimate=cost(1),
    )(value, *after)


def half_sum_kernel(mine_ref, near_ref, *refs):
    refs[-1][...] = (mine_ref[...] + near_ref[...].astype(jnp.float32)).astype(LOW)


def half_sum(mine, near, after):
    return pl.pallas_call(
        half_sum_kernel,
        out_shape=jax.ShapeDtypeStruct(mine.shape, LOW),
        in_specs=full_spec(2) + full_spec(len(after), pl.ANY),
        out_specs=pl.BlockSpec(memory_space=pltpu.VMEM),
        compiler_params=pltpu.CompilerParams(vmem_limit_bytes=8 * MIB),
        cost_estimate=cost(2),
    )(mine, near, *after)


def rows_sum_kernel(chip_ref, mid_ref, summed_ref, far_ref, after_ref, own_ref, low_ref, total_ref):
    for block in range(2):
        total = summed_ref[block].astype(jnp.float32) + far_ref[block].astype(jnp.float32)
        total_ref[block] = mid_ref[block] + total
        low_ref[block] = total_ref[block].astype(LOW)
    own_ref[...] = total_ref[chip_ref[0]]


def rows_sum(chip, mid, summed, far, after):
    return pl.pallas_call(
        rows_sum_kernel,
        out_shape=(
            jax.ShapeDtypeStruct(mid.shape[1:], jnp.float32),
            jax.ShapeDtypeStruct(mid.shape, LOW),
        ),
        in_specs=full_spec(1, pltpu.SMEM) + full_spec(3) + full_spec(1, pl.ANY),
        out_specs=full_spec(2),
        scratch_shapes=[pltpu.VMEM(mid.shape, jnp.float32)],
        compiler_params=pltpu.CompilerParams(vmem_limit_bytes=12 * MIB),
        cost_estimate=cost(2),
    )(chip, mid, summed, far, after)


def make_taps(joined, place, which_taps, conv_ref, back_ref):
    chans = 128
    none = jnp.zeros((chans, chans), LOW)
    for plane in range(9):
        conv_ref[plane, 3 * chans :, :chans] = none
        conv_ref[plane, :chans, chans:] = none
        back_ref[plane, :chans, 3 * chans :] = none
        back_ref[plane, chans:, :chans] = none
    for block in range(7):
        lanes = slice((7 * which_taps + block) * chans, (7 * which_taps + block + 1) * chans)
        wide = [joined[t % 2 * 512 + t // 2 * chans : t % 2 * 512 + (t // 2 + 1) * chans, lanes] for t in range(4)]
        made = dot(jnp.concatenate(wide, axis=1), place).astype(LOW)
        for part in range(4):
            tap = 4 * block + part
            if tap == 27:
                continue
            plane, deep = tap // 3, tap % 3
            turned = 2 - deep
            taps = made[:, part * chans : (part + 1) * chans]
            conv_ref[plane, deep * chans : (deep + 1) * chans, :chans] = taps
            conv_ref[plane, (deep + 1) * chans : (deep + 2) * chans, chans:] = taps
            back_ref[8 - plane, :chans, turned * chans : (turned + 1) * chans] = taps
            back_ref[8 - plane, chans:, (turned + 1) * chans : (turned + 2) * chans] = taps


def make_tconv(joined, place, tconv_ref):
    chans = 128
    for half in range(2):
        wide = []
        for t in range(4):
            rows = []
            for group in range(8):
                start = t % 2 * 512 + 256 + t // 2 * chans + group * 16
                for block in range(6):
                    at = block * 256 + half * chans
                    rows.append(joined[start : start + 16, at : at + chans])
            wide.append(jnp.concatenate(rows, axis=0))
        made = dot(jnp.concatenate(wide, axis=1), place)
        tconv_ref[:, half * 512 : (half + 1) * 512] = made.astype(LOW)


def normalise(rows):
    middle = jnp.mean(rows, axis=-1, keepdims=True)
    centred = rows - middle
    spread = jnp.mean(centred * centred, axis=-1, keepdims=True)
    scale = lax.rsqrt(spread + 1e-06)
    return centred * scale, scale


def attention_kernel(blocks, index_ref, depth_ref, me_ref, own_hbm, near_hbm, far_hbm, last_hbm, norm_ref, *refs):
    count = len(blocks.pieces)
    pieces = refs[:count]
    (
        out_ref, rows_hbm, h_hbm, qkv_hbm, probs_hbm,
        rows_ref, h_ref, qkv_ref, probs_ref, weight_ref, sems, load_sems, token_sems,
    ) = refs[-13:]
    patches = rows_ref.shape[0]
    heads = probs_ref.shape[0]
    span = heads * HD
    quarter = patches // 4
    tokens = []
    for flip, packed in enumerate((own_hbm, near_hbm, far_hbm, last_hbm)):
        start = pl.multiple_of(jnp.bitwise_xor(me_ref[0], flip) * quarter, quarter)
        for block in range(6):
            source = packed.at[pl.ds(block * 128, 128)]
            tokens.append((source, rows_ref.at[pl.ds(start, quarter), pl.ds(block * 128, 128)]))
    tokens = fetch(tokens, token_sems)
    loads = blocks.load(index_ref, pieces, 0, 0, weight_ref, load_sems)
    for copy in tokens:
        copy.wait()
    copies = fetch([(rows_ref, rows_hbm)], sems.at[pl.ds(1, 1)])
    norms = norm_ref[...]
    normed, _ = normalise(rows_ref[...].astype(jnp.float32))
    low_rows = (normed * norms[0:1] + norms[1:2]).astype(LOW)
    h_ref[...] = low_rows
    copies += fetch([(h_ref, h_hbm)], sems.at[pl.ds(2, 1)])
    for load in loads:
        load.wait()
    qkv_ref[...] = dot(low_rows, weight_ref[:, : 3 * span]).astype(LOW)
    copies += fetch([(qkv_ref, qkv_hbm)], sems.at[pl.ds(3, 1)])
    key_at = lax.broadcasted_iota(jnp.int32, (patches, 1), 0)
    live = key_at < depth_ref[0] * (GRID * GRID)
    outs = []
    for head in range(heads):
        query = qkv_ref[:, head * HD : (head + 1) * HD]
        keys = qkv_ref[:, span + head * HD : span + (head + 1) * HD]
        values = qkv_ref[:, 2 * span + head * HD : 2 * span + (head + 1) * HD]
        scores = jnp.where(live, dot_last(keys, query) * HD ** (-0.5), -1000000000.0)
        expo = jnp.exp(scores - jnp.max(scores, axis=0, keepdims=True))
        probs = (expo * (1.0 / jnp.sum(expo, axis=0, keepdims=True))).astype(LOW)
        probs_ref[head] = probs
        copies += fetch([(probs_ref.at[head], probs_hbm.at[head])], sems.at[pl.ds(4 + head, 1)])
        outs.append(contract_first(probs, values))
    out_ref[...] = jnp.concatenate(outs, axis=1).astype(LOW)
    for copy in copies:
        copy.wait()


def attention(depth, me, rows, blocks, norms, heads, after):
    patches, width = 512, TOKEN_ROWS
    shapes = ((patches, width), (patches, width), (patches, 3 * heads * HD), (heads, patches, patches))
    count = len(blocks.pieces)
    return pl.pallas_call(
        functools.partial(attention_kernel, blocks),
        out_shape=tuple(
            jax.ShapeDtypeStruct(shape, LOW) for shape in ((patches, heads * HD),) + shapes
        ),
        in_specs=full_spec(3, pltpu.SMEM)
        + full_spec(4, pl.ANY)
        + full_spec(1)
        + blocks.specs()
        + full_spec(len(after), pl.ANY),
        out_specs=full_spec(1) + full_spec(4, pltpu.HBM),
        scratch_shapes=[pltpu.VMEM(shape, LOW) for shape in shapes]
        + [
            pltpu.VMEM((width, 4 * heads * HD), LOW),
            pltpu.SemaphoreType.DMA((4 + heads,)),
            pltpu.SemaphoreType.DMA((count,)),
            pltpu.SemaphoreType.DMA((24,)),
        ],
        compiler_params=pltpu.CompilerParams(vmem_limit_bytes=54 * MIB),
        cost_estimate=cost(7),
    )(blocks.indices, depth, me, *rows, norms, *blocks.pieces, *after)


def mlp_kernel(
    blocks, index_ref, core_ref, rows_hbm, out0, out1, out2, out3, w0, w1, w2, w3, norm_ref, *refs
):
    count = len(blocks.pieces)
    pieces = refs[:count]
    (
        mine_hbm, other_hbm, mid_hbm, mid_half_hbm, h_hbm, hidden_hbm, slope_hbm,
        partial_ref, rows_ref, weight_ref, mid_ref, h_ref, hidden_ref, slope_ref, other_ref,
        outs_ref, out_weights_ref, sems, load_sems, in_sems,
    ) = refs[-20:]
    hidden_here = hidden_ref.shape[1]
    core = core_ref[0]
    norms = norm_ref[...]
    loads = fetch([(rows_hbm, rows_ref)], sems)
    ins = fetch(
        [(out, outs_ref.at[at]) for at, out in enumerate((out0, out1, out2, out3))]
        + [(w, out_weights_ref.at[at]) for at, w in enumerate((w0, w1, w2, w3))],
        in_sems,
    )
    loads += blocks.load(index_ref, pieces, 0, 0, weight_ref, load_sems)
    loads[0].wait()
    for load in ins:
        load.wait()
    copies = []
    for block in range(2):
        at = slice(block * 256, (block + 1) * 256)
        mid = rows_ref[at].astype(jnp.float32)
        attended = jnp.concatenate([outs_ref[t, at] for t in range(4)], axis=1)
        weights = jnp.concatenate([out_weights_ref[t] for t in range(4)], axis=1)
        mid = mid + dot_last(attended, weights)
        mid_ref[at] = mid
        normed, _ = normalise(mid)
        low_rows = (normed * norms[2:3] + norms[3:4]).astype(LOW)
        h_ref[at] = low_rows
        if block == 0:
            for load in loads[1:]:
                load.wait()
        value, slope = gelu_and_slope(dot(low_rows, weight_ref[:, :hidden_here]))
        hidden = value.astype(LOW)
        hidden_ref[at] = hidden
        slope_ref[at] = slope.astype(LOW)
        partial_ref[at] = dot_last(hidden, weight_ref[:, hidden_here : 2 * hidden_here])
        own = pl.ds(pl.multiple_of(block * 256 + core * 128, 128), 128)
        their = pl.ds(pl.multiple_of(block * 256 + (1 - core) * 128, 128), 128)
        other_ref[block] = partial_ref[their].astype(LOW)
        rows = pl.ds(block * 256, 256)
        copies += fetch(
            [
                (other_ref.at[block], other_hbm.at[block]),
                (partial_ref.at[own], mine_hbm.at[block]),
                (mid_ref.at[own], mid_half_hbm.at[block]),
                (mid_ref.at[rows], mid_hbm.at[rows]),
                (h_ref.at[rows], h_hbm.at[rows]),
                (hidden_ref.at[rows], hidden_hbm.at[rows]),
                (slope_ref.at[rows], slope_hbm.at[rows]),
            ],
            sems.at[pl.ds(1 + 7 * block, 7)],
        )
    for copy in copies:
        copy.wait()


def mlp(core, rows, outs, out_weights, norms, blocks, hidden_here, after):
    patches, width = rows.shape
    f32 = jnp.float32
    half = (2, patches // 4, width)
    return pl.pallas_call(
        functools.partial(mlp_kernel, blocks),
        out_shape=(
            jax.ShapeDtypeStruct(half, f32),
            jax.ShapeDtypeStruct(half, LOW),
            jax.ShapeDtypeStruct((patches, width), f32),
            jax.ShapeDtypeStruct(half, f32),
            jax.ShapeDtypeStruct((patches, width), LOW),
            jax.ShapeDtypeStruct((patches, hidden_here), LOW),
            jax.ShapeDtypeStruct((patches, hidden_here), LOW),
        ),
        in_specs=full_spec(2, pltpu.SMEM)
        + full_spec(9, pltpu.HBM)
        + full_spec(1)
        + blocks.specs()
        + full_spec(len(after), pl.ANY),
        out_specs=full_spec(7, pltpu.HBM),
        scratch_shapes=[
            pltpu.VMEM((patches, width), f32),
            pltpu.VMEM((patches, width), LOW),
            pltpu.VMEM((width, 2 * hidden_here), LOW),
            pltpu.VMEM((patches, width), f32),
            pltpu.VMEM((patches, width), LOW),
            pltpu.VMEM((patches, hidden_here), LOW),
            pltpu.VMEM((patches, hidden_here), LOW),
            pltpu.VMEM(half, LOW),
            pltpu.VMEM((4,) + outs[0].shape, LOW),
            pltpu.VMEM((4,) + out_weights[0].shape, LOW),
            pltpu.SemaphoreType.DMA((15,)),
            pltpu.SemaphoreType.DMA((len(blocks.pieces),)),
            pltpu.SemaphoreType.DMA((8,)),
        ],
        compiler_params=pltpu.CompilerParams(vmem_limit_bytes=54 * MIB),
        cost_estimate=cost(9.3),
    )(blocks.indices, core, rows, *outs, *out_weights, norms, *blocks.pieces, *after)


def split_row(rows):
    return rows // 2 if rows % 16 else rows // 32 * 16


def put_chunks(index_ref, source, parts, targets, sems):
    target = targets[0]
    groups = target.shape[0]
    cut = split_row(target.shape[1])
    pairs, start, first = [], 0, 0
    for height in parts:
        rows = height // groups
        for at in range(groups):
            row = first if groups == 1 else pl.multiple_of(first + index_ref[at] * rows, 16)
            pairs.append((source.at[pl.ds(row, rows)], target.at[at, pl.ds(start, rows)]))
            if groups > 1 and at == groups - 1:
                for far, low, high in ((targets[1], 0, cut), (targets[2], cut, target.shape[1])):
                    begin, end = max(low, start), min(high, start + rows)
                    if begin < end:
                        taken = source.at[pl.ds(row + begin - start, end - begin)]
                        pairs.append((taken, far.at[pl.ds(begin - low, end - begin)]))
        start += rows
        first += height
    return fetch(pairs, sems)


def chunk_shapes(groups, rows, columns):
    cut = split_row(rows)
    shapes = [(groups, rows, columns)]
    if groups > 1:
        shapes += [(cut, columns), (rows - cut, columns)]
    return [jax.ShapeDtypeStruct(shape, LOW) for shape in shapes]


def in_ring_order(call, indices, parts):
    groups = indices.shape[0]
    if groups % 2 == 0 and all(rows // groups % 16 == 0 for rows in parts):
        return call(indices, groups)
    flat = call(jnp.zeros((1,), jnp.int32), 1)[0][0]
    blocks, start = [], 0
    for rows in parts:
        blocks.append(flat[start : start + rows].reshape(groups, rows // groups, -1)[indices])
        start += rows
    terms = jnp.concatenate(blocks, axis=1)
    cut = split_row(terms.shape[1])
    return terms, terms[-1, :cut], terms[-1, cut:]


def ring_add_kernel(above, below, cut, one_ref, two_ref, terms_hbm, *refs):
    ahead_ref, behind_ref, sems = refs[-3:]
    rows = ahead_ref.shape[0]
    for copy in fetch([(terms_hbm.at[above], ahead_ref), (terms_hbm.at[below], behind_ref)], sems):
        copy.wait()
    ahead = slice(0, cut) if one_ref.shape[0] < rows else slice(0, rows)
    behind = slice(cut, rows) if one_ref.shape[0] < rows else slice(0, rows)
    for target, at, came in ((ahead_ref, ahead, one_ref), (behind_ref, behind, two_ref)):
        target[at] = (target[at].astype(jnp.float32) + came[...].astype(jnp.float32)).astype(LOW)


def ring_add(one, two, terms, above, below, after, own_kernel):
    rows, columns = terms.shape[1:]
    cut = split_row(rows)
    if rows % 16 or not own_kernel:
        if after:
            one, two, _ = lax.optimization_barrier((one, two, after))
        above, below = terms[above], terms[below]
        if one.shape[0] == rows:
            return above + one, below + two
        return (
            jnp.concatenate([above[:cut] + one, above[cut:]]),
            jnp.concatenate([below[:cut], below[cut:] + two]),
        )
    return pl.pallas_call(
        functools.partial(ring_add_kernel, above, below, cut),
        out_shape=(jax.ShapeDtypeStruct((rows, columns), LOW),) * 2,
        in_specs=full_spec(2) + full_spec(1 + len(after), pl.ANY),
        out_specs=full_spec(2),
        scratch_shapes=[pltpu.SemaphoreType.DMA((2,))],
        compiler_params=pltpu.CompilerParams(vmem_limit_bytes=12 * MIB),
        cost_estimate=cost(2),
    )(one, two, terms, *after)


def mlp_sum_kernel(ahead_ref, behind_ref, own_ref, turn_ref, *refs):
    up_ref, down_ref, tconv_ref, conv1_ref, conv2_ref = refs[-5:]
    part, hidden = up_ref.shape
    total = (
        own_ref[0].astype(jnp.float32)
        + ahead_ref[...].astype(jnp.float32)
        + behind_ref[...].astype(jnp.float32)
    )
    up_ref[...] = total[:part, :hidden]
    down_ref[...] = total[:part, hidden : 2 * hidden]
    tconv_ref[...] = dot(total[:part, 2 * hidden :].astype(LOW), turn_ref[...])
    for which, conv_ref in enumerate((conv1_ref, conv2_ref)):
        for tap in range(27):
            at = which * 896 + tap * 32
            conv_ref[tap] = total[part:, at : at + 32]


def mlp_sum(ahead, behind, terms, part, hidden, after):
    rows, columns = ahead.shape
    conv_part = rows - part
    f32 = jnp.float32
    if part % 16 or conv_part % 16:
        total = terms[0].astype(f32) + ahead.astype(f32) + behind.astype(f32)
        tconv = total[:part, 2 * hidden :].reshape(part, 8, -1).transpose(0, 2, 1).reshape(part, -1)
        conv = total[part:].reshape(conv_part, 2, 28, 32)[:, :, :27].transpose(1, 2, 0, 3)
        return total[:part, :hidden], total[:part, hidden : 2 * hidden], tconv, conv[0], conv[1]
    return pl.pallas_call(
        mlp_sum_kernel,
        out_shape=(
            jax.ShapeDtypeStruct((part, hidden), f32),
            jax.ShapeDtypeStruct((part, hidden), f32),
            jax.ShapeDtypeStruct((part, 256), f32),
            jax.ShapeDtypeStruct((27, conv_part, 32), f32),
            jax.ShapeDtypeStruct((27, conv_part, 32), f32),
        ),
        in_specs=full_spec(2)
        + [pl.BlockSpec((1,) + terms.shape[1:], lambda at: (0, 0, 0))]
        + full_spec(1)
        + full_spec(len(after), pl.ANY),
        out_specs=full_spec(5),
        grid=(1,),
        compiler_params=pltpu.CompilerParams(vmem_limit_bytes=16 * MIB),
        cost_estimate=cost(2.4),
    )(ahead, behind, terms, jnp.asarray(turn_matrix().T), *after)


def norm_back_kernel(sum_ref, far_ref, grad_hbm, rows_hbm, norm_ref, *refs):
    low_ref, grad_ref, rows_ref, sems = refs[-4:]
    for copy in fetch([(grad_hbm, grad_ref), (rows_hbm, rows_ref)], sems):
        copy.wait()
    gain = norm_ref[2:3]
    for block in range(2):
        summed = sum_ref[block].astype(jnp.float32) + far_ref[block].astype(jnp.float32)
        normed, scale = normalise(rows_ref[block])
        grad = grad_ref[block] + layer_norm_back(summed * gain, normed, scale)
        low_ref[block] = grad.astype(LOW)


def norm_back(summed, far, grad, rows, norms, after):
    return pl.pallas_call(
        norm_back_kernel,
        out_shape=jax.ShapeDtypeStruct(grad.shape, LOW),
        in_specs=full_spec(2)
        + full_spec(2, pltpu.HBM)
        + full_spec(1)
        + full_spec(len(after), pl.ANY),
        out_specs=pl.BlockSpec(memory_space=pltpu.VMEM),
        scratch_shapes=[
            pltpu.VMEM(grad.shape, jnp.float32),
            pltpu.VMEM(rows.shape, jnp.float32),
            pltpu.SemaphoreType.DMA((2,)),
        ],
        compiler_params=pltpu.CompilerParams(vmem_limit_bytes=16 * MIB),
        cost_estimate=cost(4),
    )(summed, far, grad, rows, norms, *after)


def attention_back_kernel(
    blocks, index_ref, core_ref, own_hbm, near_hbm, qkv_hbm, probs_hbm, rows_hbm, *refs
):
    count = len(blocks.pieces)
    pieces = refs[:count]
    (
        mine_hbm, other_hbm, grad_qkv_hbm, grad_hbm, sums_ref, grad_qkv_ref, grad_ref, partial_ref, other_ref,
        out_weight_ref, weight_ref, qkv_ref, probs_ref, rows_ref, sems, out_sems, load_sems,
    ) = refs[-17:]
    heads = probs_ref.shape[0]
    span = heads * HD
    core = core_ref[0]
    halves = []
    for block in range(2):
        own = pl.ds(pl.multiple_of(block * 256 + core * 128, 128), 128)
        their = pl.ds(pl.multiple_of(block * 256 + (1 - core) * 128, 128), 128)
        halves += [(own_hbm.at[block], grad_ref.at[own]), (near_hbm.at[block], grad_ref.at[their])]
    halves = fetch(halves, sems)
    outs = blocks.load(index_ref, pieces, 0, 4 * span - 256, out_weight_ref, load_sems)
    copies = fetch(
        [(qkv_hbm, qkv_ref)]
        + [(probs_hbm.at[head], probs_ref.at[head]) for head in range(heads)]
        + [(rows_hbm, rows_ref)],
        sems.at[pl.ds(4, 2 + heads)],
    )
    loads = blocks.load(index_ref, pieces, 0, 0, weight_ref, load_sems.at[pl.ds(count, count)])
    for copy in halves + outs:
        copy.wait()
    sent = fetch([(grad_ref, grad_hbm)], out_sems)
    grad_out = dot(grad_ref[...], out_weight_ref[:, 256 - span :]).astype(LOW)
    copies[0].wait()
    grad_query, grad_keys, grad_values = [], [], []
    for head in range(heads):
        query = qkv_ref[:, head * HD : (head + 1) * HD]
        keys = qkv_ref[:, span + head * HD : span + (head + 1) * HD]
        values = qkv_ref[:, 2 * span + head * HD : 2 * span + (head + 1) * HD]
        grad_head = grad_out[:, head * HD : (head + 1) * HD]
        copies[1 + head].wait()
        probs = probs_ref[head]
        grad_values.append(dot(probs, grad_head))
        probs = probs.astype(jnp.float32)
        grad_probs = dot_last(values, grad_head)
        inner = jnp.sum(probs * grad_probs, axis=0, keepdims=True)
        grad_scores = (probs * (grad_probs - inner)).astype(LOW)
        grad_query.append(contract_first(grad_scores, keys) * HD ** (-0.5))
        grad_keys.append(dot(grad_scores, query) * HD ** (-0.5))
    grad_qkv = jnp.concatenate(grad_query + grad_keys + grad_values, axis=1).astype(LOW)
    grad_qkv_ref[...] = grad_qkv
    sent += fetch([(grad_qkv_ref, grad_qkv_hbm)], out_sems.at[pl.ds(1, 1)])
    for load in loads:
        load.wait()
    partial_ref[...] = dot_last(grad_qkv, weight_ref[:, : 3 * span])
    pairs = []
    for block in range(2):
        own = pl.ds(pl.multiple_of(block * 256 + core * 128, 128), 128)
        their = pl.ds(pl.multiple_of(block * 256 + (1 - core) * 128, 128), 128)
        other_ref[block] = partial_ref[their].astype(LOW)
        pairs += [(partial_ref.at[own], mine_hbm.at[block]), (other_ref.at[block], other_hbm.at[block])]
    sent += fetch(pairs, out_sems.at[pl.ds(2, 4)])
    copies[1 + heads].wait()
    gain = shift = 0.0
    for block in range(2):
        at = slice(block * 256, (block + 1) * 256)
        normed, _ = normalise(rows_ref[at].astype(jnp.float32))
        gain += jnp.sum(partial_ref[at] * normed, axis=0, keepdims=True)
        shift += jnp.sum(partial_ref[at], axis=0, keepdims=True)
    sums_ref[...] = jnp.concatenate([gain, shift], axis=0)
    for copy in sent:
        copy.wait()


def attention_back(core, own, near, blocks, qkv, probs, rows, after):
    patches, width = rows.shape
    f32 = jnp.float32
    half = (2, patches // 4, width)
    return pl.pallas_call(
        functools.partial(attention_back_kernel, blocks),
        out_shape=(
            jax.ShapeDtypeStruct(half, f32),
            jax.ShapeDtypeStruct(half, LOW),
            jax.ShapeDtypeStruct(qkv.shape, LOW),
            jax.ShapeDtypeStruct((patches, width), LOW),
            jax.ShapeDtypeStruct((2, width), f32),
        ),
        in_specs=full_spec(2, pltpu.SMEM)
        + full_spec(5, pltpu.HBM)
        + blocks.specs()
        + full_spec(len(after), pl.ANY),
        out_specs=full_spec(4, pltpu.HBM) + full_spec(1),
        scratch_shapes=[
            pltpu.VMEM(qkv.shape, LOW),
            pltpu.VMEM((patches, width), LOW),
            pltpu.VMEM((patches, width), f32),
            pltpu.VMEM(half, LOW),
            pltpu.VMEM((width, 256), LOW),
            pltpu.VMEM((width, 4 * qkv.shape[1] // 3), LOW),
            pltpu.VMEM(qkv.shape, LOW),
            pltpu.VMEM(probs.shape, LOW),
            pltpu.VMEM(rows.shape, LOW),
            pltpu.SemaphoreType.DMA((6 + probs.shape[0],)),
            pltpu.SemaphoreType.DMA((6,)),
            pltpu.SemaphoreType.DMA((2 * len(blocks.pieces),)),
        ],
        compiler_params=pltpu.CompilerParams(vmem_limit_bytes=54 * MIB),
        cost_estimate=cost(9),
    )(blocks.indices, core, own, near, qkv, probs, rows, *blocks.pieces, *after)


def attention_weights_kernel(targets, order_ref, h_ref, out_ref, grad_qkv_ref, grad_ref, first_ref, second_ref, *refs):
    pack_ref, out_sems = refs[-2:]
    span = out_ref.shape[1]
    none = jnp.zeros((124, h_ref.shape[1]), jnp.float32)
    stacked = jnp.concatenate([first_ref[...], second_ref[...], none], axis=0)
    pack_ref[:, 4 * span :] = stacked.T.astype(LOW)
    pack_ref[:, : 3 * span] = contract_first(h_ref[...], grad_qkv_ref[...]).astype(LOW)
    pack_ref[:, 3 * span : 4 * span] = contract_first(grad_ref[...], out_ref[...]).astype(LOW)
    for copy in put_chunks(order_ref, pack_ref, (pack_ref.shape[0],), refs[len(refs) - 2 - targets : -2], out_sems):
        copy.wait()


def attention_weights(order, h_rows, out, grad_qkv, grad, first, second, after):
    width = h_rows.shape[1]
    columns = 4 * out.shape[1] + 128

    def call(order, groups):
        shapes = chunk_shapes(groups, width // groups, columns)
        return pl.pallas_call(
            functools.partial(attention_weights_kernel, len(shapes)),
            out_shape=tuple(shapes),
            in_specs=full_spec(1, pltpu.SMEM) + full_spec(6) + full_spec(len(after), pl.ANY),
            out_specs=full_spec(len(shapes), pltpu.HBM),
            scratch_shapes=[pltpu.VMEM((width, columns), LOW), pltpu.SemaphoreType.DMA((groups + 2,))],
            compiler_params=pltpu.CompilerParams(vmem_limit_bytes=16 * MIB),
            cost_estimate=cost(4),
        )(order, h_rows, out, grad_qkv, grad, first, second, *after)

    return in_ring_order(call, order, (width,))


def attention_sum_kernel(ahead_ref, behind_ref, own_ref, after_ref, query_ref, key_ref, value_ref, out_ref):
    span = query_ref.shape[1]
    total = (
        own_ref[0].astype(jnp.float32)
        + ahead_ref[...].astype(jnp.float32)
        + behind_ref[...].astype(jnp.float32)
    )
    query_ref[...] = total[:, :span]
    key_ref[...] = total[:, span : 2 * span]
    value_ref[...] = total[:, 2 * span : 3 * span]
    out_ref[...] = total[:, 3 * span : 4 * span].T


def attention_sum(ahead, behind, terms, span, after):
    part = ahead.shape[0]
    f32 = jnp.float32
    if part % 16:
        total = terms[0].astype(f32) + ahead.astype(f32) + behind.astype(f32)
        parts = [total[:, at * span : (at + 1) * span] for at in range(4)]
        return parts[0], parts[1], parts[2], parts[3].T
    return pl.pallas_call(
        attention_sum_kernel,
        out_shape=(jax.ShapeDtypeStruct((part, span), f32),) * 3
        + (jax.ShapeDtypeStruct((span, part), f32),),
        in_specs=full_spec(2)
        + [pl.BlockSpec((1,) + terms.shape[1:], lambda at: (0, 0, 0))]
        + full_spec(1, pl.ANY),
        out_specs=full_spec(4),
        grid=(1,),
        compiler_params=pltpu.CompilerParams(vmem_limit_bytes=12 * MIB),
        cost_estimate=cost(2),
    )(ahead, behind, terms, after)


class Ring:
    def __init__(self, size):
        self.size = size
        order = ring_order(size)
        self.ahead = [(order[i], order[(i + 1) % size]) for i in range(size)]
        self.behind = [(b, a) for a, b in self.ahead]
        reach = (size - 1) // 2
        self.distances = [0]
        for step in range(1, reach + 1):
            self.distances += [-step, step]
        if size % 2 == 0:
            self.distances.append(size // 2)
        table = np.array(
            [
                [order[(order.index(me) + distance) % size] for distance in self.distances]
                for me in range(size)
            ],
            np.int32,
        )
        self.indices = jnp.asarray(table)[lax.axis_index("dp")]

    def send(self, value, forward):
        return lax.ppermute(value, "dp", self.ahead if forward else self.behind)

    def gather(self, array):
        return Gather(self, array)

    def scatter(self, blocks):
        return Scatter(self, *blocks)


class Scatter:
    def __init__(self, ring, terms, far_one, far_two):
        self.ring = ring
        self.terms = terms
        self.far = far_one, far_two
        self.place = {distance: at for at, distance in enumerate(ring.distances)}
        self.reach = (ring.size - 1) // 2
        self.one = self.two = None
        self.left = self.reach + 1 if ring.size % 2 == 0 else self.reach

    def add(self, *after, own_kernel=False):
        distance = self.left
        if distance > self.reach:
            self.one, self.two = self.far
        elif self.one is None:
            self.one, self.two = self.terms[self.place[distance]], self.terms[self.place[-distance]]
        else:
            self.one, self.two = ring_add(
                self.one, self.two, self.terms, self.place[distance], self.place[-distance], after, own_kernel
            )
        return self.one, self.two

    def send(self, *after):
        one, two = self.one, self.two
        if after:
            one, two, _ = lax.optimization_barrier((one, two, after))
        self.one, self.two = self.ring.send(one, True), self.ring.send(two, False)
        self.left -= 1

    def result(self):
        while self.left > 0:
            self.add()
            self.send()
        if self.one is None:
            return jnp.zeros_like(self.terms[0]), jnp.zeros_like(self.terms[0])
        if self.one.shape[0] < self.terms.shape[1]:
            return jnp.concatenate([self.one, self.two]), jnp.zeros_like(self.terms[0])
        return self.one, self.two


class Gather:
    def __init__(self, ring, array):
        self.ring = ring
        self.array = array
        self.one = self.two = array
        self.starts = [0]
        self.pieces = [array]
        self.done = 0
        self.last = ()

    def step(self, *after):
        size = self.ring.size
        self.done += 1
        if after:
            self.one, self.two, _ = lax.optimization_barrier((self.one, self.two, after))
        if self.done <= (size - 1) // 2:
            self.one = self.ring.send(self.one, True)
            self.two = self.ring.send(self.two, False)
            self.starts += [0, 0]
        else:
            rows = self.array.shape[0]
            half = rows // 2 if rows % 16 else rows // 32 * 16
            self.last = self.one[:half], self.two[half:]
            self.one = self.ring.send(self.last[0], True)
            self.two = self.ring.send(self.last[1], False)
            self.starts += [0, half]
        self.pieces += [self.one, self.two]

    def steps_left(self):
        return self.ring.size // 2 - self.done

    def blocks(self, sections, base=0):
        indices = self.ring.indices
        if self.ring.size % 2 == 0:
            indices = jnp.concatenate([indices, indices[-1:]])
        return Blocks(indices, self.starts, self.pieces, self.ring.size, sections, base)


class Quad:
    def __init__(self):
        self.me = lax.axis_index("tensor")
        self.core = self.me % 2
        self.chip = self.me // 2

    def over_core(self, value):
        return lax.ppermute(value, "tensor", [(i, i ^ 1) for i in range(4)])

    def over_chip(self, value):
        return lax.ppermute(value, "tensor", [(i, i ^ 2) for i in range(4)])

    def spread(self, block):
        far = self.over_chip(block)
        return block, self.over_core(block), far, self.over_core(far)

    def spread_direct(self, block):
        last = lax.ppermute(block, "tensor", [(i, i ^ 3) for i in range(4)])
        return block, self.over_core(block), self.over_chip(block), last

    def pick(self, half):
        return jnp.where(self.chip == 0, half[0], half[1])


def selections(chans, chans_here):
    own = np.zeros((4, 2, chans_here, 2, chans), np.float32)
    spread = np.zeros((2, 4, 2, 2, chans_here, 2, chans), np.float32)
    place = np.zeros((4, 4, chans_here, 4, 4, chans_here), np.float32)
    for t in range(4):
        for c in range(chans_here):
            for e in range(2):
                own[t, e, c, e, t * chans_here + c] = 1.0
                for a in range(2):
                    spread[a, t, a, e, c, e, t * chans_here + c] = 1.0
            for group in range(4):
                place[t, group, c, group, t, c] = 1.0
    own = own.reshape(4, 2, chans_here, 2 * chans).astype(LOW)
    spread = spread.reshape(2, 16 * chans_here, 2 * chans).astype(LOW)
    place = place.reshape(16 * chans_here, 16 * chans_here).astype(LOW)
    return jnp.asarray(own), jnp.asarray(spread), jnp.asarray(place)


def shards(
    tokens,
    crop_depth,
    w_query,
    w_key,
    w_value,
    w_out,
    w_up,
    w_down,
    w_tconv,
    w_conv1,
    w_conv2,
    ln1_gain,
    ln1_bias,
    ln2_gain,
    ln2_bias,
    cot_out,
    cot_dec,
    groups,
):
    ring = Ring(groups)
    quad = Quad()
    grid = GRID
    vox = 2 * grid
    patches = grid**3
    width = w_query.shape[0] * groups
    part = w_query.shape[0]
    heads_here = w_query.shape[1] // HD
    span = heads_here * HD
    chans = w_conv1.shape[0] * groups
    chans_here = w_conv1.shape[2]

    low = lambda value: value.astype(LOW)
    hidden_here = w_up.shape[1]
    norm_rows = [row[None] for row in (ln1_gain, ln1_bias, ln2_gain, ln2_bias)]
    encoder_pack = pack_encoder(w_query, w_key, w_value, w_out, norm_rows, w_up, w_down.T)
    first = ring.gather(encoder_pack)
    first.step()
    own_pack = pack_own(w_tconv, w_conv1, w_conv2, encoder_pack)
    local_blocks = quad.spread(pack_local(tokens, cot_out, cot_dec[0], own_pack))
    while first.steps_left():
        first.step()
    blocks = first.blocks([(0, part)])
    mlp_blocks = first.blocks([(0, part)], 4 * span + 128)
    out_weight, norms = out_and_norms(blocks, span, 4 * span)
    pair_pack, sections = pack_pair(
        quad.chip[None], local_blocks[0], local_blocks[2], part, w_conv1.shape[0], encoder_pack
    )
    third = ring.gather(pair_pack)
    third.step(out_weight)
    arrived = third.one, third.two
    select, spread, place = selections(chans, chans_here)
    core = quad.core[None]
    me = quad.me[None]

    attended, rows_low, h_one, qkv, probs = attention(
        crop_depth, me, local_blocks, blocks, norms, heads_here, ()
    )
    attended = passed(attended, arrived)
    attended_blocks = quad.spread(attended)
    arrived = ()
    if third.steps_left():
        third.step(attended)
        arrived = third.one, third.two
    mine, other, mid, mid_half, h_two, hidden, slope = mlp(
        core,
        rows_low,
        attended_blocks,
        quad.spread(out_weight),
        norms,
        mlp_blocks,
        hidden_here,
        arrived,
    )
    arrived = ()
    if third.steps_left():
        third.step()
        arrived = third.one, third.two
    summed = half_sum(mine, quad.over_core(passed(other, arrived)), ())
    far = quad.over_chip(summed)
    while third.steps_left():
        third.step()
    decoder_own = join_decoder(third.blocks(sections), groups, part, summed)
    after, low_half = rows_sum(quad.chip[None], mid_half, summed, far, decoder_own)
    decoder_near, low_half = lax.optimization_barrier((decoder_own, low_half))
    decoder_near = quad.over_core(decoder_near)
    dec_out, grad_half, mlp_terms, mine, other, sums_two = decoder(
        ring.indices,
        crop_depth,
        me,
        low_half,
        quad.over_core(low_half),
        decoder_own,
        decoder_near,
        select,
        spread,
        place,
        local_blocks,
        slope,
        mid,
        h_two,
        hidden,
        mlp_blocks,
    )
    mlp_ring = ring.scatter(mlp_terms)
    mlp_ring.add()
    mlp_ring.send()
    summed = half_sum(mine, quad.over_core(other), ())
    far = quad.over_chip(summed)
    ready = mlp_ring.add(summed, own_kernel=True) if mlp_ring.left > 0 else ()
    low_mid_half = norm_back(
        summed, far, grad_half, mid_half, norms, ready
    )
    if mlp_ring.left > 0:
        mlp_ring.send(low_mid_half)
    mine, other, grad_qkv, grad_branch, sums_one = attention_back(
        core, low_mid_half, quad.over_core(low_mid_half), blocks, qkv, probs, rows_low, ()
    )
    ready = ()
    if mlp_ring.left > 0:
        ready = mlp_ring.add(sums_one)
        mlp_ring.send()
    attention_terms = attention_weights(
        ring.indices, h_one, attended, grad_qkv, grad_branch, sums_one, sums_two, ready
    )
    attention_ring = ring.scatter(attention_terms)
    attention_ring.add()
    attention_ring.send()
    last = ()
    while mlp_ring.left > 0 or attention_ring.left > 0:
        if attention_ring.left > 0:
            last = attention_ring.add(mlp_ring.one, mlp_ring.two)
            attention_ring.send()
        if mlp_ring.left > 0:
            mlp_ring.add()
            mlp_ring.send()
    mlp_ahead, mlp_behind = mlp_ring.result()
    ahead, behind = attention_ring.result()
    columns = slice(4 * span, 4 * span + 8)
    norm_grads = attention_terms[0][0, :, columns].astype(jnp.float32)
    norm_grads = norm_grads + ahead[:, columns].astype(jnp.float32)
    norm_grads = norm_grads + behind[:, columns].astype(jnp.float32)
    grad_query, grad_key, grad_value, grad_out = attention_sum(
        ahead, behind, attention_terms[0], span, norm_grads
    )
    norm_grads = sum(quad.spread_direct(norm_grads))
    summed = mine + quad.over_core(other).astype(jnp.float32)
    norm_own = quad.pick(summed) + quad.over_chip(low(quad.pick(summed[::-1]))).astype(jnp.float32)
    normed_own, scale_own = normalise(tokens.astype(jnp.float32))
    grad_tokens = quad.pick(low_mid_half).astype(jnp.float32) + layer_norm_back(norm_own * norms[0:1], normed_own, scale_own)
    grad_up, grad_down, grad_tconv, grad_conv1, grad_conv2 = mlp_sum(
        mlp_ahead, mlp_behind, mlp_terms[0], part, hidden_here, last
    )
    return (
        after,
        dec_out[None],
        grad_tokens,
        grad_query,
        grad_key,
        grad_value,
        grad_out,
        grad_up,
        grad_down.T,
        grad_tconv,
        grad_conv1.transpose(1, 0, 2),
        grad_conv2.transpose(1, 0, 2),
        norm_grads[:, 0],
        norm_grads[:, 1],
        norm_grads[:, 2],
        norm_grads[:, 3],
    )


def solution(mesh):
    in_specs = (
        P(("dp", "tensor"), None),
        P("dp"),
        P("dp", "tensor"),
        P("dp", "tensor"),
        P("dp", "tensor"),
        P("tensor", "dp"),
        P("dp", "tensor"),
        P("tensor", "dp"),
        P("dp", "tensor"),
        P("dp", None, "tensor"),
        P("dp", None, "tensor"),
        P("dp"),
        P("dp"),
        P("dp"),
        P("dp"),
        P(("dp", "tensor"), None),
        P("dp", None, None, None, "tensor"),
    )
    out_specs = (
        P(("dp", "tensor"), None),
        P("dp", None, None, None, "tensor"),
        P(("dp", "tensor"), None),
        P("dp", "tensor"),
        P("dp", "tensor"),
        P("dp", "tensor"),
        P("tensor", "dp"),
        P("dp", "tensor"),
        P("tensor", "dp"),
        P("dp", "tensor"),
        P("dp", None, "tensor"),
        P("dp", None, "tensor"),
        P("dp"),
        P("dp"),
        P("dp"),
        P("dp"),
    )
    groups = mesh.shape["dp"]

    def run(*arrays):
        return shards(*arrays, groups)

    return jax.shard_map(run, mesh=mesh, in_specs=in_specs, out_specs=out_specs, check_vma=False)
```

```python
import functools

import jax
import jax.numpy as jnp
import numpy as np
from jax import lax
from jax.experimental import pallas as pl
from jax.experimental.pallas import tpu as pltpu
from jax.sharding import PartitionSpec as P

HD = 64
GRID = 8
LOW = jnp.bfloat16


def ring_order(size):
    if size % 2:
        return list(range(size))
    return list(range(0, size, 2)) + list(range(size - 1, 0, -2))


def layer_norm_back(grad_normed, normed, scale):
    mean_grad = jnp.mean(grad_normed, axis=-1, keepdims=True)
    mean_dot = jnp.mean(grad_normed * normed, axis=-1, keepdims=True)
    return scale * (grad_normed - mean_grad - normed * mean_dot)


def contract_first(left, right):
    return lax.dot_general(
        left, right, (((0,), (0,)), ((), ())), preferred_element_type=jnp.float32
    )


MIB = 2**20
VMEM_LIMIT = 60 * MIB


def cost(microseconds):
    return pl.CostEstimate(flops=0, bytes_accessed=int(microseconds * 3.5e6), transcendentals=0)


def gelu_and_slope(x):
    bell = jnp.exp(-0.5 * x * x)
    frac = 1.0 / (1.0 + 0.3275911 * 0.7071067811865476 * jnp.abs(x))
    poly = frac * (
        0.254829592
        + frac * (-0.284496736 + frac * (1.421413741 + frac * (-1.453152027 + frac * 1.061405429)))
    )
    tail = 0.5 * poly * bell
    phi = jnp.where(x >= 0.0, 1.0 - tail, tail)
    return x * phi, phi + x * bell * 0.3989422804014327


def dot(left, right):
    return jnp.dot(left, right, preferred_element_type=jnp.float32)


def dot_last(left, right):
    return lax.dot_general(
        left, right, (((1,), (1,)), ((), ())), preferred_element_type=jnp.float32
    )


BATCH = 4


DECODER_REFS = 40


def decoder_kernel(
    blocks,
    index_ref,
    order_ref,
    depth_ref,
    me_ref,
    own_ref,
    near_ref,
    joined_hbm,
    joined_near_hbm,
    select_ref,
    spread_ref,
    place_ref,
    cot0_hbm,
    cot1_hbm,
    cot2_hbm,
    cot3_hbm,
    slope_hbm,
    mid_hbm,
    h_hbm,
    hidden_hbm,
    *refs,
):
    decoder_steps(
        blocks,
        refs[: len(blocks.pieces)],
        index_ref,
        order_ref,
        depth_ref,
        me_ref,
        own_ref,
        near_ref,
        joined_hbm,
        joined_near_hbm,
        select_ref,
        spread_ref,
        place_ref,
        (cot0_hbm, cot1_hbm, cot2_hbm, cot3_hbm),
        slope_hbm,
        mid_hbm,
        h_hbm,
        hidden_hbm,
        refs[len(blocks.pieces) : -DECODER_REFS],
        *refs[-DECODER_REFS:],
    )


def decoder_steps(
    blocks,
    pieces,
    index_ref,
    order_ref,
    depth_ref,
    me_ref,
    own_ref,
    near_ref,
    joined_hbm,
    joined_near_hbm,
    select_ref,
    spread_ref,
    place_ref,
    cots_hbm,
    slope_hbm,
    mid_hbm,
    h_hbm,
    hidden_hbm,
    terms_hbm,
    dec_hbm,
    grad_half_hbm,
    mine_hbm,
    other_hbm,
    sums_ref,
    other_ref,
    grad_low_ref,
    dec_ref,
    rows_ref,
    grad_tconv_ref,
    terms_ref,
    upper_ref,
    grad_rows_ref,
    wgrad_ref,
    first_even,
    first_odd,
    act_even,
    act_odd,
    grad_even,
    grad_odd,
    conv_ref,
    normed_ref,
    slope_ref,
    held_ref,
    carry_ref,
    low_grad_ref,
    columns_ref,
    tconv_ref,
    conv_w,
    back_w,
    cot_ref,
    up_ref,
    down_ref,
    gate_ref,
    mid_ref,
    h_ref,
    hidden_ref,
    sems,
    load_sems,
    out_sems,
):
    grid = 8
    vox = 16
    chans = 128
    depth = depth_ref[0]
    count = (depth * (2 * vox * vox)).astype(jnp.float32)

    core = lax.rem(me_ref[0], 2)
    loads = fetch(
        [
            (joined_hbm, terms_ref.at[pl.ds(pl.multiple_of(core * 512, 512), 512)]),
            (joined_near_hbm, terms_ref.at[pl.ds(pl.multiple_of((1 - core) * 512, 512), 512)]),
            (cots_hbm[0].at[pl.ds(TOKEN_ROWS, FIELD_ROWS)], cot_ref.at[me_ref[0]]),
            (cots_hbm[1].at[pl.ds(TOKEN_ROWS, FIELD_ROWS)], cot_ref.at[jnp.bitwise_xor(me_ref[0], 1)]),
            (cots_hbm[2].at[pl.ds(TOKEN_ROWS, FIELD_ROWS)], cot_ref.at[jnp.bitwise_xor(me_ref[0], 2)]),
            (cots_hbm[3].at[pl.ds(TOKEN_ROWS, FIELD_ROWS)], cot_ref.at[jnp.bitwise_xor(me_ref[0], 3)]),
            (slope_hbm, gate_ref),
            (mid_hbm, mid_ref),
            (h_hbm, h_ref),
            (hidden_hbm, hidden_ref),
        ],
        sems.at[pl.ds(3, 10)],
    )
    hidden = up_ref.shape[1]
    loads += blocks.load(index_ref, pieces, 0, hidden, down_ref, load_sems)
    loads += blocks.load(index_ref, pieces, 0, 0, up_ref, load_sems.at[pl.ds(len(pieces), len(pieces))])
    dec_copy = pltpu.make_async_copy(dec_ref, dec_hbm, sems.at[0])

    for even in (first_even, act_even, grad_even):
        even[:, 0] = jnp.zeros((grid, vox, 4 * chans), LOW)
        even[:, vox + 1] = jnp.zeros((grid, vox, 4 * chans), LOW)
    for odd in (first_odd, act_odd, grad_odd):
        odd[:, 0] = jnp.zeros((grid + 1, vox, 4 * chans), LOW)
        odd[:, vox + 1] = jnp.zeros((grid + 1, vox, 4 * chans), LOW)
    wgrad_ref[:, 864:] = jnp.zeros((2, 32, chans), jnp.float32)
    low_grad_ref[:, 0] = jnp.zeros((grid, vox, 2 * chans), LOW)
    low_grad_ref[:, vox + 1] = jnp.zeros((grid, vox, 2 * chans), LOW)

    spot = lax.broadcasted_iota(jnp.int32, (1, 1, 8, 1), 2)

    def put_field(even, odd, at, value):
        left = value[..., :chans]
        right = value[..., chans:]
        flat = (2 * vox, 8, chans)
        before = pltpu.roll(right.reshape(flat), 1, 1).reshape(right.shape)
        after = pltpu.roll(left.reshape(flat), 7, 1).reshape(left.shape)
        before = jnp.where(spot == 0, 0.0, before)
        after = jnp.where(spot == 7, 0.0, after)
        window = jnp.concatenate([before, value, after], axis=3)
        even[at, 1 : vox + 1] = window.reshape(vox, 16, 4 * chans).astype(LOW)
        early = jnp.concatenate([carry_ref[...][:, None], window[:, :1]], axis=1)
        odd[at, 1 : vox + 1] = early.reshape(vox, 16, 4 * chans).astype(LOW)
        carry_ref[...] = window[:, 1]

    def open_field():
        carry_ref[...] = jnp.zeros(carry_ref.shape, jnp.float32)

    def close_field(odd):
        late = jnp.concatenate([carry_ref[...], jnp.zeros(carry_ref.shape, jnp.float32)], axis=1)
        odd[grid, 1 : vox + 1] = late.astype(LOW)

    def live_at(at):
        return (at < depth).astype(jnp.float32)

    def convolve(even, odd, weights, target, turned):
        def step(block, total):
            at = block * BATCH
            summed = None
            for deep in range(3):
                field = even if deep == 1 else odd
                start = at + 1 if deep == 2 else at
                for tall in range(3):
                    left = field[pl.ds(start, BATCH), tall : tall + vox]
                    left = left.reshape(BATCH * vox * 16, 4 * chans)
                    right = weights[deep * 3 + tall]
                    term = dot_last(left, right) if turned else dot(left, right)
                    summed = term if summed is None else summed + term
            target[pl.ds(at, BATCH)] = summed.reshape(BATCH, vox, 16, 2 * chans)
            return total

        lax.fori_loop(0, grid // BATCH, step, 0)

    def both(total):
        row = jnp.sum(total, axis=0, keepdims=True)
        half = (row[:, :chans] + row[:, chans:]) / count
        return jnp.concatenate([half, half], axis=1)

    def zero():
        return jnp.zeros((8, 2 * chans), jnp.float32)

    def fold(value):
        return jnp.sum(value.reshape(2 * vox, 8, 2 * chans), axis=0)

    def statistics(source):
        def first(at, total):
            return total + live_at(at) * fold(source[at])

        middle = both(lax.fori_loop(0, grid, first, zero()))

        def second(at, total):
            away = source[at] - middle
            return total + live_at(at) * fold(away * away)

        spread = both(lax.fori_loop(0, grid, second, zero()))
        return middle, lax.rsqrt(spread + 1e-05)

    for block in range(2):
        rows_ref[pl.ds(pl.multiple_of(block * 256 + core * 128, 128), 128)] = own_ref[block]
        rows_ref[pl.ds(pl.multiple_of(block * 256 + (1 - core) * 128, 128), 128)] = near_ref[block]
    loads[0].wait()
    loads[1].wait()
    make_tconv(terms_ref, place_ref[...], tconv_ref)
    for part in range(4):
        wide = dot(rows_ref[...], tconv_ref[:, part * 256 : (part + 1) * 256])
        held_ref[:, part * 4 : (part + 1) * 4] = wide.reshape(grid, 4, 16, 2 * chans)
    open_field()

    def place_first(at, state):
        tokens = held_ref[at] * live_at(at)
        offsets = [
            [tokens[8 * a + 4 * b : 8 * a + 4 * b + 4].reshape(8, 1, 1, 8, 256) for a in range(2)]
            for b in range(2)
        ]
        value = jnp.concatenate(
            [jnp.concatenate(offsets[b], axis=2) for b in range(2)], axis=1
        ).reshape(vox, 2, 8, 256)
        put_field(first_even, first_odd, at, value)
        return state

    lax.fori_loop(0, grid, place_first, 0)
    close_field(first_odd)

    for which in range(2):
        make_taps(terms_ref, place_ref[...], which, conv_w.at[which], back_w.at[which])
    convolve(first_even, first_odd, conv_w.at[0], normed_ref, False)
    middle, scale_one = statistics(normed_ref)
    open_field()

    def act_first(at, state):
        normed = (normed_ref[at] - middle) * scale_one
        normed_ref[at] = normed
        value, slope = gelu_and_slope(normed)
        live = live_at(at)
        slope_ref[at] = slope * live
        put_field(act_even, act_odd, at, (value * live).reshape(vox, 2, 8, 2 * chans))
        return state

    lax.fori_loop(0, grid, act_first, 0)
    close_field(act_odd)

    convolve(act_even, act_odd, conv_w.at[1], conv_ref, False)
    middle, scale_two = statistics(conv_ref)
    for load in loads[2:6]:
        load.wait()

    def act_second(at, totals):
        normed = (conv_ref[at] - middle) * scale_two
        conv_ref[at] = normed
        value, slope = gelu_and_slope(normed)
        live = live_at(at)
        low_value = (value * live).astype(LOW).reshape(vox * 16, 2 * chans)
        for e in range(2):
            shown = dot_last(low_value, select_ref[me_ref[0], e]).reshape(vox, 2, 8, 32)
            for a in range(2):
                dec_ref[2 * at + a, :, pl.ds(e, 8, stride=2), :] = shown[:, a]
        parts = [cot_ref[t, pl.ds(768 + at * vox * 8, vox * 8)] for t in range(4)]
        packed = jnp.concatenate(parts, axis=1)
        cot = jnp.concatenate(
            [dot(packed, spread_ref[a]).reshape(vox, 1, 8, 2 * chans) for a in range(2)], axis=1
        ).reshape(vox, 16, 2 * chans)
        grad = cot * slope * live
        held_ref[at] = grad
        return totals[0] + fold(grad), totals[1] + fold(grad * normed)

    totals = lax.fori_loop(0, grid, act_second, (zero(), zero()))
    dec_copy.start()

    def norm_back(source, normed_source, scale, sums):
        mean_grad = both(sums[0])
        mean_dot = both(sums[1])
        open_field()

        def step(at, state):
            grad = source[at] - live_at(at) * (mean_grad + normed_source[at] * mean_dot)
            grad = scale * grad
            low_grad_ref[at, 1 : vox + 1] = grad.astype(LOW)
            put_field(grad_even, grad_odd, at, grad.reshape(vox, 2, 8, 2 * chans))
            return state

        lax.fori_loop(0, grid, step, 0)
        close_field(grad_odd)

    def weight_grad(even, odd, which):
        own = select_ref[me_ref[0]].reshape(64, 2 * chans)
        for at in range(grid):
            shifts = [
                dot_last(own, low_grad_ref[at, 2 - tall : 18 - tall].reshape(vox * 16, 2 * chans))
                for tall in range(3)
            ]
            columns_ref[:, at * 256 : (at + 1) * 256] = jnp.concatenate(shifts, axis=0).astype(LOW)
        for deep in range(3):
            field = even if deep == 1 else odd
            start = 1 if deep == 2 else 0
            right = field[start : start + grid, 1 : vox + 1].reshape(grid * vox * 16, 4 * chans)
            sums = dot(columns_ref[...], right)
            for tall in range(3):
                for wide in range(3):
                    top = sums[tall * 64 : tall * 64 + 32, wide * chans : (wide + 1) * chans]
                    low = sums[tall * 64 + 32 : tall * 64 + 64, (wide + 1) * chans : (wide + 2) * chans]
                    tap = deep * 9 + tall * 3 + wide
                    wgrad_ref[which, tap * 32 : (tap + 1) * 32] = top + low

    norm_back(held_ref, conv_ref, scale_two, totals)
    weight_grad(act_even, act_odd, 1)
    convolve(grad_even, grad_odd, back_w.at[1], conv_ref, True)

    def slope_first(at, totals):
        grad = conv_ref[at] * slope_ref[at]
        conv_ref[at] = grad
        return totals[0] + fold(grad), totals[1] + fold(grad * normed_ref[at])

    totals = lax.fori_loop(0, grid, slope_first, (zero(), zero()))
    norm_back(conv_ref, normed_ref, scale_one, totals)
    weight_grad(first_even, first_odd, 0)
    convolve(grad_even, grad_odd, back_w.at[0], conv_ref, True)

    def rows_back(at, state):
        grad = (conv_ref[at] * live_at(at)).reshape(8, 2, 2, 8, 2 * chans)
        for a in range(2):
            for b in range(2):
                block = grad[:, b, a].reshape(64, 2 * chans).astype(LOW)
                column = (2 * a + b) * 256
                grad_tconv_ref[pl.ds(at * 64, 64), column : column + 256] = block
        return state

    lax.fori_loop(0, grid, rows_back, 0)
    for which in range(2):
        for block in range(7):
            at = (7 * which + block) * 128
            taps = wgrad_ref[which, block * 128 : (block + 1) * 128].T.astype(LOW)
            terms_ref[768:896, at : at + 128] = taps
    own = select_ref[me_ref[0]].reshape(64, 2 * chans)
    spans = [dot_last(grad_tconv_ref[:, at * 256 : (at + 1) * 256], own) for at in range(4)]
    mine = jnp.concatenate(spans, axis=1).astype(LOW)
    terms_ref[:768, 2 * hidden :] = contract_first(rows_ref[...], mine).astype(LOW)
    for t in range(4):
        at = slice(t * 128, (t + 1) * 128)
        tiles = [cot_ref[t, block * 128 : (block + 1) * 128] for block in range(6)]
        cot_rows = jnp.concatenate(tiles, axis=1).astype(jnp.float32)
        grad_rows_ref[at] = cot_rows + dot_last(grad_tconv_ref[at], tconv_ref[...])
    grad_low_ref[...] = grad_rows_ref[...].astype(LOW)
    halves = []
    for block in range(2):
        own = pl.ds(pl.multiple_of(block * 256 + core * 128, 128), 128)
        halves.append((grad_rows_ref.at[own], grad_half_hbm.at[block]))
    half_copies = fetch(halves, sems.at[pl.ds(1, 2)])
    for load in loads[6:]:
        load.wait()
    for copy in half_copies:
        copy.wait()
    sent = []
    gain = shift = 0.0
    for block in range(2):
        at = slice(block * 256, (block + 1) * 256)
        grad = dot(grad_low_ref[at], down_ref[...])
        upper = (grad * gate_ref[at].astype(jnp.float32)).astype(LOW)
        upper_ref[at] = upper
        grad_normed = dot_last(upper, up_ref[...])
        normed, _ = normalise(mid_ref[at])
        gain += jnp.sum(grad_normed * normed, axis=0, keepdims=True)
        shift += jnp.sum(grad_normed, axis=0, keepdims=True)
        grad_rows_ref[at] = grad_normed
        own = pl.ds(pl.multiple_of(block * 256 + core * 128, 128), 128)
        their = pl.ds(pl.multiple_of(block * 256 + (1 - core) * 128, 128), 128)
        other_ref[block] = grad_rows_ref[their].astype(LOW)
        sent += fetch(
            [(grad_rows_ref.at[own], mine_hbm.at[block]), (other_ref.at[block], other_hbm.at[block])],
            sems.at[pl.ds(3 + 2 * block, 2)],
        )
    sums_ref[...] = jnp.concatenate([gain, shift], axis=0)
    terms_ref[:768, :hidden] = contract_first(h_ref[...], upper_ref[...]).astype(LOW)
    terms_ref[:768, hidden : 2 * hidden] = contract_first(grad_low_ref[...], hidden_ref[...]).astype(LOW)
    for copy in sent + put_chunks(order_ref, terms_ref, (768, 128), terms_hbm, out_sems):
        copy.wait()
    dec_copy.wait()


def decoder(
    order, depth, me, own, near, joined, joined_near, select, spread, place, cots, slope, mid, h_rows, hidden, blocks
):
    f32 = jnp.float32
    vmem = pl.BlockSpec(memory_space=pltpu.VMEM)
    hbm = pl.BlockSpec(memory_space=pltpu.HBM)
    here = slope.shape[1]
    columns = 2 * here + 256
    window = lambda planes: pltpu.VMEM((planes, 18, 16, 512), LOW)
    field = lambda kind: pltpu.VMEM((8, 16, 16, 256), kind)
    kept = []

    def call(order, groups):
        shapes = chunk_shapes(groups, 896 // groups, columns)
        outs = pl.pallas_call(
            functools.partial(decoder_kernel, blocks),
            out_shape=(
                *shapes,
                jax.ShapeDtypeStruct((16, 16, 16, 32), f32),
                jax.ShapeDtypeStruct((2, 128, 768), f32),
                jax.ShapeDtypeStruct((2, 128, 768), f32),
                jax.ShapeDtypeStruct((2, 128, 768), LOW),
                jax.ShapeDtypeStruct((2, 768), f32),
            ),
            in_specs=[pl.BlockSpec(memory_space=pltpu.SMEM)] * 4
            + [vmem] * 2
            + [hbm] * 2
            + [vmem] * 3
            + [hbm] * 8
            + blocks.specs(),
            out_specs=[hbm] * (len(shapes) + 4) + [vmem],
            scratch_shapes=[
                pltpu.VMEM((2, 128, 768), LOW),
                pltpu.VMEM((512, 768), LOW),
                pltpu.VMEM((16, 16, 16, 32), f32),
                pltpu.VMEM((512, 768), LOW),
                pltpu.VMEM((512, 1024), LOW),
                pltpu.VMEM((1024, columns), LOW),
                pltpu.VMEM(slope.shape, LOW),
                pltpu.VMEM((512, 768), f32),
                pltpu.VMEM((2, 896, 128), f32),
                window(8),
                window(9),
                window(8),
                window(9),
                window(8),
                window(9),
                field(f32),
                field(f32),
                field(f32),
                field(f32),
                pltpu.VMEM((16, 8, 512), f32),
                pltpu.VMEM((8, 18, 16, 256), LOW),
                pltpu.VMEM((192, 2048), LOW),
                pltpu.VMEM((768, 1024), LOW),
                pltpu.VMEM((2, 9, 512, 256), LOW),
                pltpu.VMEM((2, 9, 256, 512), LOW),
                pltpu.VMEM((4, 1792, 128), LOW),
                pltpu.VMEM((768, here), LOW),
                pltpu.VMEM((768, here), LOW),
                pltpu.VMEM(slope.shape, LOW),
                pltpu.VMEM(mid.shape, f32),
                pltpu.VMEM(h_rows.shape, LOW),
                pltpu.VMEM(hidden.shape, LOW),
                pltpu.SemaphoreType.DMA((13,)),
                pltpu.SemaphoreType.DMA((2 * len(blocks.pieces),)),
                pltpu.SemaphoreType.DMA((2 * groups + 4,)),
            ],
            compiler_params=pltpu.CompilerParams(vmem_limit_bytes=VMEM_LIMIT),
            cost_estimate=cost(52),
        )(
            blocks.indices,
            order,
            depth,
            me,
            own,
            near,
            joined,
            joined_near,
            select,
            spread,
            place,
            *cots,
            slope,
            mid,
            h_rows,
            hidden,
            *blocks.pieces,
        )
        kept.extend(outs[len(shapes) :])
        return outs[: len(shapes)]

    terms = in_ring_order(call, order, (768, 128))
    dec, half, mine, other, sums = kept
    return dec, half, terms, mine, other, sums


def full_spec(count, space=pltpu.VMEM):
    return [pl.BlockSpec(memory_space=space)] * count


def fetch(pairs, sems):
    copies = [
        pltpu.make_async_copy(source, target, sems.at[at]) for at, (source, target) in enumerate(pairs)
    ]
    for copy in copies:
        copy.start()
    return copies


class Blocks:
    def __init__(self, indices, starts, pieces, size, sections, base=0):
        self.base = base
        block, columns = pieces[0].shape
        edges = [end for section in sections for end in section]
        if any(edge % 16 for edge in edges + list(starts)):
            full = jnp.zeros((size * block, columns), pieces[0].dtype)
            for at, (start, piece) in enumerate(zip(starts, pieces)):
                full = lax.dynamic_update_slice(full, piece, (indices[at] * block + start, 0))
            full = full.reshape(size, block, columns)
            parts = [full[:, low:high].reshape(-1, columns) for low, high in sections]
            pieces, starts, indices = [jnp.concatenate(parts)], [0], jnp.zeros((1,), jnp.int32)
            sections = [(size * low, size * high) for low, high in sections]
            size = 1
        self.indices = indices
        self.starts = tuple(starts)
        self.pieces = tuple(pieces)
        self.size = size
        self.sections = tuple(sections)

    def specs(self):
        return full_spec(len(self.pieces), pl.ANY)

    def rows(self, section):
        low, high = self.sections[section]
        return self.size * (high - low)

    def load(self, index_ref, refs, section, column, target, sems):
        low, high = self.sections[section]
        copies = []
        for at, (piece, start) in enumerate(zip(refs, self.starts)):
            first, last = max(low, start), min(high, start + piece.shape[0])
            if first >= last:
                continue
            row = index_ref[at] * (high - low) + first - low
            if len(self.pieces) > 1:
                row = pl.multiple_of(row, 16)
            columns = pl.ds(self.base + column, target.shape[1])
            source = piece.at[pl.ds(first - start, last - first), columns]
            copies += fetch([(source, target.at[pl.ds(row, last - first)])], sems.at[pl.ds(at, 1)])
        return copies


def pack_kernel(
    query_ref, key_ref, value_ref, out_ref, gain1_ref, bias1_ref, gain2_ref, bias2_ref, up_ref, down_ref, pack_ref
):
    at = 0
    none = jnp.zeros((124, gain1_ref.shape[1]), jnp.float32)
    norms = [gain1_ref[...], bias1_ref[...], gain2_ref[...], bias2_ref[...], none]
    norms = jnp.concatenate(norms, axis=0).T
    for value in (
        query_ref[...], key_ref[...], value_ref[...], out_ref[...].T, norms, up_ref[...], down_ref[...],
    ):
        pack_ref[:, at : at + value.shape[1]] = value.astype(LOW)
        at += value.shape[1]


def pack_encoder(query, key, value, out, norms, up, down):
    part = query.shape[0]
    if part % 16:
        columns = jnp.pad(jnp.concatenate(norms), ((0, 124), (0, 0))).T
        parts = (query, key, value, out.T, columns, up, down)
        return jnp.concatenate([array.astype(LOW) for array in parts], axis=1)
    return pl.pallas_call(
        pack_kernel,
        out_shape=jax.ShapeDtypeStruct((part, 4 * query.shape[1] + 128 + 2 * up.shape[1]), LOW),
        in_specs=full_spec(10),
        out_specs=pl.BlockSpec(memory_space=pltpu.VMEM),
        cost_estimate=cost(2),
    )(query, key, value, out, *norms, up, down)


def pack_own_kernel(tconv_ref, conv1_ref, conv2_ref, turn_ref, after_ref, pack_ref):
    part = tconv_ref.shape[0]
    conv_part = conv1_ref.shape[1]
    pack_ref[:part] = dot(tconv_ref[...].astype(LOW), turn_ref[...]).astype(LOW)
    taps = []
    for conv_ref in (conv1_ref, conv2_ref):
        taps += [conv_ref[tap] for tap in range(27)] + [jnp.zeros(conv_ref.shape[1:], jnp.float32)]
    for tile in range(14):
        made = jnp.concatenate(taps[4 * tile : 4 * tile + 4], axis=1).astype(LOW)
        at = part + tile // 2 * conv_part
        pack_ref[at : at + conv_part, tile % 2 * 128 : (tile % 2 + 1) * 128] = made


def turn_matrix():
    turn = np.zeros((32, 8, 8, 32), np.float32)
    for group in range(8):
        for chan in range(32):
            turn[chan, group, group, chan] = 1.0
    return turn.reshape(256, 256).astype(LOW)


def pack_own(tconv, conv1, conv2, after):
    part, conv_part = tconv.shape[0], conv1.shape[0]
    if part % 16 or conv_part % 16:
        conv = jnp.stack([conv1.astype(LOW), conv2.astype(LOW)], axis=1)
        conv = jnp.pad(conv, ((0, 0), (0, 0), (0, 1), (0, 0)))
        conv = conv.reshape(conv_part, 7, 256).transpose(1, 0, 2)
        turned = tconv.astype(LOW).reshape(part, 32, 8).transpose(0, 2, 1).reshape(part, -1)
        return jnp.concatenate([turned, conv.reshape(-1, 256)])
    return pl.pallas_call(
        pack_own_kernel,
        out_shape=jax.ShapeDtypeStruct((part + 7 * conv_part, 256), LOW),
        in_specs=full_spec(4) + full_spec(1, pl.ANY),
        out_specs=pl.BlockSpec(memory_space=pltpu.VMEM),
        cost_estimate=cost(2),
    )(tconv, conv1.transpose(1, 0, 2), conv2.transpose(1, 0, 2), jnp.asarray(turn_matrix()), after)


def fold_tconv(rows, columns):
    count = rows.shape[0]
    if count % 16:
        flat = rows.reshape(-1)
        flat = jnp.pad(flat, (0, -flat.shape[0] % columns))
        return flat.reshape(-1, columns)
    folded = rows.reshape(count // 16, 16, 256).transpose(1, 0, 2).reshape(16, -1)
    return jnp.pad(folded, ((0, 0), (0, columns - folded.shape[1])))


TOKEN_ROWS = 768
FIELD_ROWS = 1792
PACK_AT = TOKEN_ROWS + FIELD_ROWS


def pack_local_kernel(tokens_ref, cot_ref, field_ref, own_ref, pack_ref):
    for block in range(6):
        lanes = slice(block * 128, (block + 1) * 128)
        pack_ref[block * 128 : (block + 1) * 128] = tokens_ref[:, lanes]
        at = TOKEN_ROWS + block * 128
        pack_ref[at : at + 128] = cot_ref[:, lanes].astype(LOW)
    for pair in range(8):
        parts = [
            field_ref[2 * pair + a, :, pl.ds(e, 8, stride=2), :].reshape(128, 32)
            for a in range(2)
            for e in range(2)
        ]
        at = 2 * TOKEN_ROWS + pair * 128
        pack_ref[at : at + 128] = jnp.concatenate(parts, axis=1).astype(LOW)
    count = own_ref.shape[0]
    if count % 16 == 0:
        for half in range(2):
            at = PACK_AT + half * count
            pack_ref[at : at + count] = own_ref[:, half * 128 : (half + 1) * 128]


def pack_local(tokens, cot, field, own):
    aligned = own.shape[0] % 16 == 0
    total = PACK_AT + (2 * own.shape[0] if aligned else 0)
    pack = pl.pallas_call(
        pack_local_kernel,
        out_shape=jax.ShapeDtypeStruct((total, 128), LOW),
        in_specs=full_spec(4),
        out_specs=pl.BlockSpec(memory_space=pltpu.VMEM),
        compiler_params=pltpu.CompilerParams(vmem_limit_bytes=VMEM_LIMIT),
        cost_estimate=cost(3),
    )(tokens, cot, field, own)
    if aligned:
        return pack
    halves = own.reshape(-1, 2, 128).transpose(1, 0, 2).reshape(-1, 128)
    return jnp.concatenate([pack, halves])


def pack_pair_kernel(part, conv_part, chip_ref, own_hbm, far_hbm, after_ref, pack_ref, held_ref, sems):
    columns = pack_ref.shape[1]
    count = part + 7 * conv_part
    source = pl.ds(PACK_AT, 2 * count)
    for copy in fetch(
        [
            (own_hbm.at[source], held_ref.at[chip_ref[0]]),
            (far_hbm.at[source], held_ref.at[1 - chip_ref[0]]),
        ],
        sems,
    ):
        copy.wait()
    for which in range(2):
        for half in range(2):
            first = half * count
            at = which * conv_part
            for block in range(7):
                start = first + part + block * conv_part
                lanes = slice(block * 256 + half * 128, block * 256 + (half + 1) * 128)
                pack_ref[at : at + conv_part, lanes] = held_ref[which, start : start + conv_part]
            at = 2 * conv_part + which * 16
            for block in range(part // 16):
                start = first + block * 16
                lanes = slice(block * 256 + half * 128, block * 256 + (half + 1) * 128)
                pack_ref[at : at + 16, lanes] = held_ref[which, start : start + 16]
        at = 2 * conv_part + which * 16
        pack_ref[at : at + 16, part * 16 :] = jnp.zeros((16, columns - part * 16), LOW)


def pack_pair(chip, own, far, part, conv_part, after):
    columns = 7 * 256
    count = part + 7 * conv_part
    if part % 16 or conv_part % 16:
        own, far = [
            packed[PACK_AT:].reshape(2, count, 128).transpose(1, 0, 2).reshape(count, 256)
            for packed in (own, far)
        ]
        first = jnp.where(chip[0] > 0, far, own)
        second = jnp.where(chip[0] > 0, own, far)
        convs = [
            packed[part:].reshape(7, conv_part, 256).transpose(1, 0, 2).reshape(conv_part, columns)
            for packed in (first, second)
        ]
        pack = jnp.concatenate(convs + [fold_tconv(packed[:part], columns) for packed in (first, second)])
    else:
        pack = pl.pallas_call(
            functools.partial(pack_pair_kernel, part, conv_part),
            out_shape=jax.ShapeDtypeStruct((2 * conv_part + 32, columns), LOW),
            in_specs=full_spec(1, pltpu.SMEM) + full_spec(3, pl.ANY),
            out_specs=pl.BlockSpec(memory_space=pltpu.VMEM),
            scratch_shapes=[pltpu.VMEM((2, 2 * count, 128), LOW), pltpu.SemaphoreType.DMA((2,))],
            cost_estimate=cost(1.7),
        )(chip, own, far, after)
    fold = (pack.shape[0] - 2 * conv_part) // 2
    edges = [0, conv_part, 2 * conv_part, 2 * conv_part + fold, pack.shape[0]]
    return pack, list(zip(edges[:-1], edges[1:]))


def out_norm_kernel(blocks, norm_at, index_ref, *refs):
    count = len(blocks.pieces)
    pieces = refs[:count]
    out_ref, norm_ref, wide_ref, columns_ref, sems = refs[count:]
    span = out_ref.shape[1]
    copies = blocks.load(index_ref, pieces, 0, 4 * span - 256, wide_ref, sems)
    copies += blocks.load(index_ref, pieces, 0, norm_at, columns_ref, sems.at[pl.ds(count, count)])
    for copy in copies:
        copy.wait()
    out_ref[...] = wide_ref[:, 256 - span :]
    norm_ref[...] = columns_ref[...].astype(jnp.float32).T[:8]


def out_and_norms(blocks, span, norm_at):
    count = len(blocks.pieces)
    return pl.pallas_call(
        functools.partial(out_norm_kernel, blocks, norm_at),
        out_shape=(
            jax.ShapeDtypeStruct((blocks.rows(0), span), LOW),
            jax.ShapeDtypeStruct((8, blocks.rows(0)), jnp.float32),
        ),
        in_specs=full_spec(1, pltpu.SMEM) + blocks.specs(),
        out_specs=full_spec(2),
        scratch_shapes=[
            pltpu.VMEM((blocks.rows(0), 256), LOW),
            pltpu.VMEM((blocks.rows(0), 128), LOW),
            pltpu.SemaphoreType.DMA((2 * count,)),
        ],
        compiler_params=pltpu.CompilerParams(vmem_limit_bytes=12 * MIB),
        cost_estimate=cost(2.7),
    )(blocks.indices, *blocks.pieces)


def join_kernel(blocks, index_ref, *refs):
    count = len(blocks.pieces)
    join_ref, sems = refs[-2:]
    copies = []
    for section in range(4):
        target = join_ref.at[pl.ds(section * 128, 128)]
        copies += blocks.load(
            index_ref, refs[:count], section, 0, target, sems.at[pl.ds(section * count, count)]
        )
    for copy in copies:
        copy.wait()


def join_decoder(blocks, groups, part, after):
    columns = blocks.pieces[0].shape[1]
    count = len(blocks.pieces)
    if count == 1:
        full = blocks.pieces[0]
        parts = [full[low:high] for low, high in blocks.sections]
        folded = []
        for rows in parts[2:]:
            rows = rows.reshape(groups, -1)[:, : part * 256].reshape(-1, 256)
            folded += [fold_tconv(rows[at * 96 : (at + 1) * 96], columns) for at in range(8)]
        return jnp.concatenate(parts[:2] + folded)
    return pl.pallas_call(
        functools.partial(join_kernel, blocks),
        out_shape=jax.ShapeDtypeStruct((512, columns), LOW),
        in_specs=full_spec(1, pltpu.SMEM) + blocks.specs() + full_spec(1, pl.ANY),
        out_specs=pl.BlockSpec(memory_space=pltpu.VMEM),
        scratch_shapes=[pltpu.SemaphoreType.DMA((4 * count,))],
        compiler_params=pltpu.CompilerParams(vmem_limit_bytes=12 * MIB),
        cost_estimate=cost(3.8),
    )(blocks.indices, *blocks.pieces, after)


def pass_kernel(value_ref, *refs):
    refs[-1][...] = value_ref[...]


def passed(value, after):
    return pl.pallas_call(
        pass_kernel,
        out_shape=jax.ShapeDtypeStruct(value.shape, value.dtype),
        in_specs=full_spec(1) + full_spec(len(after), pl.ANY),
        out_specs=pl.BlockSpec(memory_space=pltpu.VMEM),
        compiler_params=pltpu.CompilerParams(vmem_limit_bytes=8 * MIB),
        cost_estimate=cost(1),
    )(value, *after)


def half_sum_kernel(mine_ref, near_ref, *refs):
    refs[-1][...] = (mine_ref[...] + near_ref[...].astype(jnp.float32)).astype(LOW)


def half_sum(mine, near, after):
    return pl.pallas_call(
        half_sum_kernel,
        out_shape=jax.ShapeDtypeStruct(mine.shape, LOW),
        in_specs=full_spec(2) + full_spec(len(after), pl.ANY),
        out_specs=pl.BlockSpec(memory_space=pltpu.VMEM),
        compiler_params=pltpu.CompilerParams(vmem_limit_bytes=8 * MIB),
        cost_estimate=cost(2),
    )(mine, near, *after)


def rows_sum_kernel(chip_ref, mid_ref, summed_ref, far_ref, after_ref, own_ref, low_ref, total_ref):
    for block in range(2):
        total = summed_ref[block].astype(jnp.float32) + far_ref[block].astype(jnp.float32)
        total_ref[block] = mid_ref[block] + total
        low_ref[block] = total_ref[block].astype(LOW)
    own_ref[...] = total_ref[chip_ref[0]]


def rows_sum(chip, mid, summed, far, after):
    return pl.pallas_call(
        rows_sum_kernel,
        out_shape=(
            jax.ShapeDtypeStruct(mid.shape[1:], jnp.float32),
            jax.ShapeDtypeStruct(mid.shape, LOW),
        ),
        in_specs=full_spec(1, pltpu.SMEM) + full_spec(3) + full_spec(1, pl.ANY),
        out_specs=full_spec(2),
        scratch_shapes=[pltpu.VMEM(mid.shape, jnp.float32)],
        compiler_params=pltpu.CompilerParams(vmem_limit_bytes=12 * MIB),
        cost_estimate=cost(2),
    )(chip, mid, summed, far, after)


def make_taps(joined, place, which_taps, conv_ref, back_ref):
    chans = 128
    none = jnp.zeros((chans, chans), LOW)
    for plane in range(9):
        conv_ref[plane, 3 * chans :, :chans] = none
        conv_ref[plane, :chans, chans:] = none
        back_ref[plane, :chans, 3 * chans :] = none
        back_ref[plane, chans:, :chans] = none
    for block in range(7):
        lanes = slice((7 * which_taps + block) * chans, (7 * which_taps + block + 1) * chans)
        wide = [joined[t % 2 * 512 + t // 2 * chans : t % 2 * 512 + (t // 2 + 1) * chans, lanes] for t in range(4)]
        made = dot(jnp.concatenate(wide, axis=1), place).astype(LOW)
        for part in range(4):
            tap = 4 * block + part
            if tap == 27:
                continue
            plane, deep = tap // 3, tap % 3
            turned = 2 - deep
            taps = made[:, part * chans : (part + 1) * chans]
            conv_ref[plane, deep * chans : (deep + 1) * chans, :chans] = taps
            conv_ref[plane, (deep + 1) * chans : (deep + 2) * chans, chans:] = taps
            back_ref[8 - plane, :chans, turned * chans : (turned + 1) * chans] = taps
            back_ref[8 - plane, chans:, (turned + 1) * chans : (turned + 2) * chans] = taps


def make_tconv(joined, place, tconv_ref):
    chans = 128
    for half in range(2):
        wide = []
        for t in range(4):
            rows = []
            for group in range(8):
                start = t % 2 * 512 + 256 + t // 2 * chans + group * 16
                for block in range(6):
                    at = block * 256 + half * chans
                    rows.append(joined[start : start + 16, at : at + chans])
            wide.append(jnp.concatenate(rows, axis=0))
        made = dot(jnp.concatenate(wide, axis=1), place)
        tconv_ref[:, half * 512 : (half + 1) * 512] = made.astype(LOW)


def normalise(rows):
    middle = jnp.mean(rows, axis=-1, keepdims=True)
    centred = rows - middle
    spread = jnp.mean(centred * centred, axis=-1, keepdims=True)
    scale = lax.rsqrt(spread + 1e-06)
    return centred * scale, scale


def attention_kernel(blocks, index_ref, depth_ref, me_ref, own_hbm, near_hbm, far_hbm, last_hbm, norm_ref, *refs):
    count = len(blocks.pieces)
    pieces = refs[:count]
    (
        out_ref, rows_hbm, h_hbm, qkv_hbm, probs_hbm,
        rows_ref, h_ref, qkv_ref, probs_ref, weight_ref, sems, load_sems, token_sems,
    ) = refs[-13:]
    patches = rows_ref.shape[0]
    heads = probs_ref.shape[0]
    span = heads * HD
    quarter = patches // 4
    tokens = []
    for flip, packed in enumerate((own_hbm, near_hbm, far_hbm, last_hbm)):
        start = pl.multiple_of(jnp.bitwise_xor(me_ref[0], flip) * quarter, quarter)
        for block in range(6):
            source = packed.at[pl.ds(block * 128, 128)]
            tokens.append((source, rows_ref.at[pl.ds(start, quarter), pl.ds(block * 128, 128)]))
    tokens = fetch(tokens, token_sems)
    loads = blocks.load(index_ref, pieces, 0, 0, weight_ref, load_sems)
    for copy in tokens:
        copy.wait()
    copies = fetch([(rows_ref, rows_hbm)], sems.at[pl.ds(1, 1)])
    norms = norm_ref[...]
    normed, _ = normalise(rows_ref[...].astype(jnp.float32))
    low_rows = (normed * norms[0:1] + norms[1:2]).astype(LOW)
    h_ref[...] = low_rows
    copies += fetch([(h_ref, h_hbm)], sems.at[pl.ds(2, 1)])
    for load in loads:
        load.wait()
    qkv_ref[...] = dot(low_rows, weight_ref[:, : 3 * span]).astype(LOW)
    copies += fetch([(qkv_ref, qkv_hbm)], sems.at[pl.ds(3, 1)])
    key_at = lax.broadcasted_iota(jnp.int32, (patches, 1), 0)
    live = key_at < depth_ref[0] * (GRID * GRID)
    outs = []
    for head in range(heads):
        query = qkv_ref[:, head * HD : (head + 1) * HD]
        keys = qkv_ref[:, span + head * HD : span + (head + 1) * HD]
        values = qkv_ref[:, 2 * span + head * HD : 2 * span + (head + 1) * HD]
        scores = jnp.where(live, dot_last(keys, query) * HD ** (-0.5), -1000000000.0)
        expo = jnp.exp(scores - jnp.max(scores, axis=0, keepdims=True))
        probs = (expo * (1.0 / jnp.sum(expo, axis=0, keepdims=True))).astype(LOW)
        probs_ref[head] = probs
        copies += fetch([(probs_ref.at[head], probs_hbm.at[head])], sems.at[pl.ds(4 + head, 1)])
        outs.append(contract_first(probs, values))
    out_ref[...] = jnp.concatenate(outs, axis=1).astype(LOW)
    for copy in copies:
        copy.wait()


def attention(depth, me, rows, blocks, norms, heads, after):
    patches, width = 512, TOKEN_ROWS
    shapes = ((patches, width), (patches, width), (patches, 3 * heads * HD), (heads, patches, patches))
    count = len(blocks.pieces)
    return pl.pallas_call(
        functools.partial(attention_kernel, blocks),
        out_shape=tuple(
            jax.ShapeDtypeStruct(shape, LOW) for shape in ((patches, heads * HD),) + shapes
        ),
        in_specs=full_spec(3, pltpu.SMEM)
        + full_spec(4, pl.ANY)
        + full_spec(1)
        + blocks.specs()
        + full_spec(len(after), pl.ANY),
        out_specs=full_spec(1) + full_spec(4, pltpu.HBM),
        scratch_shapes=[pltpu.VMEM(shape, LOW) for shape in shapes]
        + [
            pltpu.VMEM((width, 4 * heads * HD), LOW),
            pltpu.SemaphoreType.DMA((4 + heads,)),
            pltpu.SemaphoreType.DMA((count,)),
            pltpu.SemaphoreType.DMA((24,)),
        ],
        compiler_params=pltpu.CompilerParams(vmem_limit_bytes=54 * MIB),
        cost_estimate=cost(7),
    )(blocks.indices, depth, me, *rows, norms, *blocks.pieces, *after)


def mlp_kernel(
    blocks, index_ref, core_ref, rows_hbm, out0, out1, out2, out3, w0, w1, w2, w3, norm_ref, *refs
):
    count = len(blocks.pieces)
    pieces = refs[:count]
    (
        mine_hbm, other_hbm, mid_hbm, mid_half_hbm, h_hbm, hidden_hbm, slope_hbm,
        partial_ref, rows_ref, weight_ref, mid_ref, h_ref, hidden_ref, slope_ref, other_ref,
        outs_ref, out_weights_ref, sems, load_sems, in_sems,
    ) = refs[-20:]
    hidden_here = hidden_ref.shape[1]
    core = core_ref[0]
    norms = norm_ref[...]
    loads = fetch([(rows_hbm, rows_ref)], sems)
    ins = fetch(
        [(out, outs_ref.at[at]) for at, out in enumerate((out0, out1, out2, out3))]
        + [(w, out_weights_ref.at[at]) for at, w in enumerate((w0, w1, w2, w3))],
        in_sems,
    )
    loads += blocks.load(index_ref, pieces, 0, 0, weight_ref, load_sems)
    loads[0].wait()
    for load in ins:
        load.wait()
    copies = []
    for block in range(2):
        at = slice(block * 256, (block + 1) * 256)
        mid = rows_ref[at].astype(jnp.float32)
        attended = jnp.concatenate([outs_ref[t, at] for t in range(4)], axis=1)
        weights = jnp.concatenate([out_weights_ref[t] for t in range(4)], axis=1)
        mid = mid + dot_last(attended, weights)
        mid_ref[at] = mid
        normed, _ = normalise(mid)
        low_rows = (normed * norms[2:3] + norms[3:4]).astype(LOW)
        h_ref[at] = low_rows
        if block == 0:
            for load in loads[1:]:
                load.wait()
        value, slope = gelu_and_slope(dot(low_rows, weight_ref[:, :hidden_here]))
        hidden = value.astype(LOW)
        hidden_ref[at] = hidden
        slope_ref[at] = slope.astype(LOW)
        partial_ref[at] = dot_last(hidden, weight_ref[:, hidden_here : 2 * hidden_here])
        own = pl.ds(pl.multiple_of(block * 256 + core * 128, 128), 128)
        their = pl.ds(pl.multiple_of(block * 256 + (1 - core) * 128, 128), 128)
        other_ref[block] = partial_ref[their].astype(LOW)
        rows = pl.ds(block * 256, 256)
        copies += fetch(
            [
                (other_ref.at[block], other_hbm.at[block]),
                (partial_ref.at[own], mine_hbm.at[block]),
                (mid_ref.at[own], mid_half_hbm.at[block]),
                (mid_ref.at[rows], mid_hbm.at[rows]),
                (h_ref.at[rows], h_hbm.at[rows]),
                (hidden_ref.at[rows], hidden_hbm.at[rows]),
                (slope_ref.at[rows], slope_hbm.at[rows]),
            ],
            sems.at[pl.ds(1 + 7 * block, 7)],
        )
    for copy in copies:
        copy.wait()


def mlp(core, rows, outs, out_weights, norms, blocks, hidden_here, after):
    patches, width = rows.shape
    f32 = jnp.float32
    half = (2, patches // 4, width)
    return pl.pallas_call(
        functools.partial(mlp_kernel, blocks),
        out_shape=(
            jax.ShapeDtypeStruct(half, f32),
            jax.ShapeDtypeStruct(half, LOW),
            jax.ShapeDtypeStruct((patches, width), f32),
            jax.ShapeDtypeStruct(half, f32),
            jax.ShapeDtypeStruct((patches, width), LOW),
            jax.ShapeDtypeStruct((patches, hidden_here), LOW),
            jax.ShapeDtypeStruct((patches, hidden_here), LOW),
        ),
        in_specs=full_spec(2, pltpu.SMEM)
        + full_spec(9, pltpu.HBM)
        + full_spec(1)
        + blocks.specs()
        + full_spec(len(after), pl.ANY),
        out_specs=full_spec(7, pltpu.HBM),
        scratch_shapes=[
            pltpu.VMEM((patches, width), f32),
            pltpu.VMEM((patches, width), LOW),
            pltpu.VMEM((width, 2 * hidden_here), LOW),
            pltpu.VMEM((patches, width), f32),
            pltpu.VMEM((patches, width), LOW),
            pltpu.VMEM((patches, hidden_here), LOW),
            pltpu.VMEM((patches, hidden_here), LOW),
            pltpu.VMEM(half, LOW),
            pltpu.VMEM((4,) + outs[0].shape, LOW),
            pltpu.VMEM((4,) + out_weights[0].shape, LOW),
            pltpu.SemaphoreType.DMA((15,)),
            pltpu.SemaphoreType.DMA((len(blocks.pieces),)),
            pltpu.SemaphoreType.DMA((8,)),
        ],
        compiler_params=pltpu.CompilerParams(vmem_limit_bytes=54 * MIB),
        cost_estimate=cost(9.3),
    )(blocks.indices, core, rows, *outs, *out_weights, norms, *blocks.pieces, *after)


def split_row(rows):
    return rows // 2 if rows % 16 else rows // 32 * 16


def put_chunks(index_ref, source, parts, targets, sems):
    target = targets[0]
    groups = target.shape[0]
    cut = split_row(target.shape[1])
    pairs, start, first = [], 0, 0
    for height in parts:
        rows = height // groups
        for at in range(groups):
            row = first if groups == 1 else pl.multiple_of(first + index_ref[at] * rows, 16)
            pairs.append((source.at[pl.ds(row, rows)], target.at[at, pl.ds(start, rows)]))
            if groups > 1 and at == groups - 1:
                for far, low, high in ((targets[1], 0, cut), (targets[2], cut, target.shape[1])):
                    begin, end = max(low, start), min(high, start + rows)
                    if begin < end:
                        taken = source.at[pl.ds(row + begin - start, end - begin)]
                        pairs.append((taken, far.at[pl.ds(begin - low, end - begin)]))
        start += rows
        first += height
    return fetch(pairs, sems)


def chunk_shapes(groups, rows, columns):
    cut = split_row(rows)
    shapes = [(groups, rows, columns)]
    if groups > 1:
        shapes += [(cut, columns), (rows - cut, columns)]
    return [jax.ShapeDtypeStruct(shape, LOW) for shape in shapes]


def in_ring_order(call, indices, parts):
    groups = indices.shape[0]
    if groups % 2 == 0 and all(rows // groups % 16 == 0 for rows in parts):
        return call(indices, groups)
    flat = call(jnp.zeros((1,), jnp.int32), 1)[0][0]
    blocks, start = [], 0
    for rows in parts:
        blocks.append(flat[start : start + rows].reshape(groups, rows // groups, -1)[indices])
        start += rows
    terms = jnp.concatenate(blocks, axis=1)
    cut = split_row(terms.shape[1])
    return terms, terms[-1, :cut], terms[-1, cut:]


def ring_add_kernel(above, below, cut, one_ref, two_ref, terms_hbm, *refs):
    ahead_ref, behind_ref, sems = refs[-3:]
    rows = ahead_ref.shape[0]
    for copy in fetch([(terms_hbm.at[above], ahead_ref), (terms_hbm.at[below], behind_ref)], sems):
        copy.wait()
    ahead = slice(0, cut) if one_ref.shape[0] < rows else slice(0, rows)
    behind = slice(cut, rows) if one_ref.shape[0] < rows else slice(0, rows)
    for target, at, came in ((ahead_ref, ahead, one_ref), (behind_ref, behind, two_ref)):
        target[at] = (target[at].astype(jnp.float32) + came[...].astype(jnp.float32)).astype(LOW)


def ring_add(one, two, terms, above, below, after, own_kernel):
    rows, columns = terms.shape[1:]
    cut = split_row(rows)
    if rows % 16 or not own_kernel:
        if after:
            one, two, _ = lax.optimization_barrier((one, two, after))
        above, below = terms[above], terms[below]
        if one.shape[0] == rows:
            return above + one, below + two
        return (
            jnp.concatenate([above[:cut] + one, above[cut:]]),
            jnp.concatenate([below[:cut], below[cut:] + two]),
        )
    return pl.pallas_call(
        functools.partial(ring_add_kernel, above, below, cut),
        out_shape=(jax.ShapeDtypeStruct((rows, columns), LOW),) * 2,
        in_specs=full_spec(2) + full_spec(1 + len(after), pl.ANY),
        out_specs=full_spec(2),
        scratch_shapes=[pltpu.SemaphoreType.DMA((2,))],
        compiler_params=pltpu.CompilerParams(vmem_limit_bytes=12 * MIB),
        cost_estimate=cost(2),
    )(one, two, terms, *after)


def mlp_sum_kernel(ahead_ref, behind_ref, own_ref, turn_ref, *refs):
    up_ref, down_ref, tconv_ref, conv1_ref, conv2_ref = refs[-5:]
    part, hidden = up_ref.shape
    total = (
        own_ref[0].astype(jnp.float32)
        + ahead_ref[...].astype(jnp.float32)
        + behind_ref[...].astype(jnp.float32)
    )
    up_ref[...] = total[:part, :hidden]
    down_ref[...] = total[:part, hidden : 2 * hidden]
    tconv_ref[...] = dot(total[:part, 2 * hidden :].astype(LOW), turn_ref[...])
    for which, conv_ref in enumerate((conv1_ref, conv2_ref)):
        for tap in range(27):
            at = which * 896 + tap * 32
            conv_ref[tap] = total[part:, at : at + 32]


def mlp_sum(ahead, behind, terms, part, hidden, after):
    rows, columns = ahead.shape
    conv_part = rows - part
    f32 = jnp.float32
    if part % 16 or conv_part % 16:
        total = terms[0].astype(f32) + ahead.astype(f32) + behind.astype(f32)
        tconv = total[:part, 2 * hidden :].reshape(part, 8, -1).transpose(0, 2, 1).reshape(part, -1)
        conv = total[part:].reshape(conv_part, 2, 28, 32)[:, :, :27].transpose(1, 2, 0, 3)
        return total[:part, :hidden], total[:part, hidden : 2 * hidden], tconv, conv[0], conv[1]
    return pl.pallas_call(
        mlp_sum_kernel,
        out_shape=(
            jax.ShapeDtypeStruct((part, hidden), f32),
            jax.ShapeDtypeStruct((part, hidden), f32),
            jax.ShapeDtypeStruct((part, 256), f32),
            jax.ShapeDtypeStruct((27, conv_part, 32), f32),
            jax.ShapeDtypeStruct((27, conv_part, 32), f32),
        ),
        in_specs=full_spec(2)
        + [pl.BlockSpec((1,) + terms.shape[1:], lambda at: (0, 0, 0))]
        + full_spec(1)
        + full_spec(len(after), pl.ANY),
        out_specs=full_spec(5),
        grid=(1,),
        compiler_params=pltpu.CompilerParams(vmem_limit_bytes=16 * MIB),
        cost_estimate=cost(2.4),
    )(ahead, behind, terms, jnp.asarray(turn_matrix().T), *after)


def norm_back_kernel(sum_ref, far_ref, grad_hbm, rows_hbm, norm_ref, *refs):
    low_ref, grad_ref, rows_ref, sems = refs[-4:]
    for copy in fetch([(grad_hbm, grad_ref), (rows_hbm, rows_ref)], sems):
        copy.wait()
    gain = norm_ref[2:3]
    for block in range(2):
        summed = sum_ref[block].astype(jnp.float32) + far_ref[block].astype(jnp.float32)
        normed, scale = normalise(rows_ref[block])
        grad = grad_ref[block] + layer_norm_back(summed * gain, normed, scale)
        low_ref[block] = grad.astype(LOW)


def norm_back(summed, far, grad, rows, norms, after):
    return pl.pallas_call(
        norm_back_kernel,
        out_shape=jax.ShapeDtypeStruct(grad.shape, LOW),
        in_specs=full_spec(2)
        + full_spec(2, pltpu.HBM)
        + full_spec(1)
        + full_spec(len(after), pl.ANY),
        out_specs=pl.BlockSpec(memory_space=pltpu.VMEM),
        scratch_shapes=[
            pltpu.VMEM(grad.shape, jnp.float32),
            pltpu.VMEM(rows.shape, jnp.float32),
            pltpu.SemaphoreType.DMA((2,)),
        ],
        compiler_params=pltpu.CompilerParams(vmem_limit_bytes=16 * MIB),
        cost_estimate=cost(4),
    )(summed, far, grad, rows, norms, *after)


def attention_back_kernel(
    blocks, index_ref, core_ref, own_hbm, near_hbm, qkv_hbm, probs_hbm, rows_hbm, *refs
):
    count = len(blocks.pieces)
    pieces = refs[:count]
    (
        mine_hbm, other_hbm, grad_qkv_hbm, grad_hbm, sums_ref, grad_qkv_ref, grad_ref, partial_ref, other_ref,
        out_weight_ref, weight_ref, qkv_ref, probs_ref, rows_ref, sems, out_sems, load_sems,
    ) = refs[-17:]
    heads = probs_ref.shape[0]
    span = heads * HD
    core = core_ref[0]
    halves = []
    for block in range(2):
        own = pl.ds(pl.multiple_of(block * 256 + core * 128, 128), 128)
        their = pl.ds(pl.multiple_of(block * 256 + (1 - core) * 128, 128), 128)
        halves += [(own_hbm.at[block], grad_ref.at[own]), (near_hbm.at[block], grad_ref.at[their])]
    halves = fetch(halves, sems)
    outs = blocks.load(index_ref, pieces, 0, 4 * span - 256, out_weight_ref, load_sems)
    copies = fetch(
        [(qkv_hbm, qkv_ref)]
        + [(probs_hbm.at[head], probs_ref.at[head]) for head in range(heads)]
        + [(rows_hbm, rows_ref)],
        sems.at[pl.ds(4, 2 + heads)],
    )
    loads = blocks.load(index_ref, pieces, 0, 0, weight_ref, load_sems.at[pl.ds(count, count)])
    for copy in halves + outs:
        copy.wait()
    sent = fetch([(grad_ref, grad_hbm)], out_sems)
    grad_out = dot(grad_ref[...], out_weight_ref[:, 256 - span :]).astype(LOW)
    copies[0].wait()
    grad_query, grad_keys, grad_values = [], [], []
    for head in range(heads):
        query = qkv_ref[:, head * HD : (head + 1) * HD]
        keys = qkv_ref[:, span + head * HD : span + (head + 1) * HD]
        values = qkv_ref[:, 2 * span + head * HD : 2 * span + (head + 1) * HD]
        grad_head = grad_out[:, head * HD : (head + 1) * HD]
        copies[1 + head].wait()
        probs = probs_ref[head]
        grad_values.append(dot(probs, grad_head))
        probs = probs.astype(jnp.float32)
        grad_probs = dot_last(values, grad_head)
        inner = jnp.sum(probs * grad_probs, axis=0, keepdims=True)
        grad_scores = (probs * (grad_probs - inner)).astype(LOW)
        grad_query.append(contract_first(grad_scores, keys) * HD ** (-0.5))
        grad_keys.append(dot(grad_scores, query) * HD ** (-0.5))
    grad_qkv = jnp.concatenate(grad_query + grad_keys + grad_values, axis=1).astype(LOW)
    grad_qkv_ref[...] = grad_qkv
    sent += fetch([(grad_qkv_ref, grad_qkv_hbm)], out_sems.at[pl.ds(1, 1)])
    for load in loads:
        load.wait()
    partial_ref[...] = dot_last(grad_qkv, weight_ref[:, : 3 * span])
    pairs = []
    for block in range(2):
        own = pl.ds(pl.multiple_of(block * 256 + core * 128, 128), 128)
        their = pl.ds(pl.multiple_of(block * 256 + (1 - core) * 128, 128), 128)
        other_ref[block] = partial_ref[their].astype(LOW)
        pairs += [(partial_ref.at[own], mine_hbm.at[block]), (other_ref.at[block], other_hbm.at[block])]
    sent += fetch(pairs, out_sems.at[pl.ds(2, 4)])
    copies[1 + heads].wait()
    gain = shift = 0.0
    for block in range(2):
        at = slice(block * 256, (block + 1) * 256)
        normed, _ = normalise(rows_ref[at].astype(jnp.float32))
        gain += jnp.sum(partial_ref[at] * normed, axis=0, keepdims=True)
        shift += jnp.sum(partial_ref[at], axis=0, keepdims=True)
    sums_ref[...] = jnp.concatenate([gain, shift], axis=0)
    for copy in sent:
        copy.wait()


def attention_back(core, own, near, blocks, qkv, probs, rows, after):
    patches, width = rows.shape
    f32 = jnp.float32
    half = (2, patches // 4, width)
    return pl.pallas_call(
        functools.partial(attention_back_kernel, blocks),
        out_shape=(
            jax.ShapeDtypeStruct(half, f32),
            jax.ShapeDtypeStruct(half, LOW),
            jax.ShapeDtypeStruct(qkv.shape, LOW),
            jax.ShapeDtypeStruct((patches, width), LOW),
            jax.ShapeDtypeStruct((2, width), f32),
        ),
        in_specs=full_spec(2, pltpu.SMEM)
        + full_spec(5, pltpu.HBM)
        + blocks.specs()
        + full_spec(len(after), pl.ANY),
        out_specs=full_spec(4, pltpu.HBM) + full_spec(1),
        scratch_shapes=[
            pltpu.VMEM(qkv.shape, LOW),
            pltpu.VMEM((patches, width), LOW),
            pltpu.VMEM((patches, width), f32),
            pltpu.VMEM(half, LOW),
            pltpu.VMEM((width, 256), LOW),
            pltpu.VMEM((width, 4 * qkv.shape[1] // 3), LOW),
            pltpu.VMEM(qkv.shape, LOW),
            pltpu.VMEM(probs.shape, LOW),
            pltpu.VMEM(rows.shape, LOW),
            pltpu.SemaphoreType.DMA((6 + probs.shape[0],)),
            pltpu.SemaphoreType.DMA((6,)),
            pltpu.SemaphoreType.DMA((2 * len(blocks.pieces),)),
        ],
        compiler_params=pltpu.CompilerParams(vmem_limit_bytes=54 * MIB),
        cost_estimate=cost(9),
    )(blocks.indices, core, own, near, qkv, probs, rows, *blocks.pieces, *after)


def attention_weights_kernel(targets, order_ref, h_ref, out_ref, grad_qkv_ref, grad_ref, first_ref, second_ref, *refs):
    pack_ref, out_sems = refs[-2:]
    span = out_ref.shape[1]
    none = jnp.zeros((124, h_ref.shape[1]), jnp.float32)
    stacked = jnp.concatenate([first_ref[...], second_ref[...], none], axis=0)
    pack_ref[:, 4 * span :] = stacked.T.astype(LOW)
    pack_ref[:, : 3 * span] = contract_first(h_ref[...], grad_qkv_ref[...]).astype(LOW)
    pack_ref[:, 3 * span : 4 * span] = contract_first(grad_ref[...], out_ref[...]).astype(LOW)
    for copy in put_chunks(order_ref, pack_ref, (pack_ref.shape[0],), refs[len(refs) - 2 - targets : -2], out_sems):
        copy.wait()


def attention_weights(order, h_rows, out, grad_qkv, grad, first, second, after):
    width = h_rows.shape[1]
    columns = 4 * out.shape[1] + 128

    def call(order, groups):
        shapes = chunk_shapes(groups, width // groups, columns)
        return pl.pallas_call(
            functools.partial(attention_weights_kernel, len(shapes)),
            out_shape=tuple(shapes),
            in_specs=full_spec(1, pltpu.SMEM) + full_spec(6) + full_spec(len(after), pl.ANY),
            out_specs=full_spec(len(shapes), pltpu.HBM),
            scratch_shapes=[pltpu.VMEM((width, columns), LOW), pltpu.SemaphoreType.DMA((groups + 2,))],
            compiler_params=pltpu.CompilerParams(vmem_limit_bytes=57 * MIB),
            cost_estimate=cost(4),
        )(order, h_rows, out, grad_qkv, grad, first, second, *after)

    return in_ring_order(call, order, (width,))


def attention_sum_kernel(ahead_ref, behind_ref, own_ref, after_ref, query_ref, key_ref, value_ref, out_ref):
    span = query_ref.shape[1]
    total = (
        own_ref[0].astype(jnp.float32)
        + ahead_ref[...].astype(jnp.float32)
        + behind_ref[...].astype(jnp.float32)
    )
    query_ref[...] = total[:, :span]
    key_ref[...] = total[:, span : 2 * span]
    value_ref[...] = total[:, 2 * span : 3 * span]
    out_ref[...] = total[:, 3 * span : 4 * span].T


def attention_sum(ahead, behind, terms, span, after):
    part = ahead.shape[0]
    f32 = jnp.float32
    if part % 16:
        total = terms[0].astype(f32) + ahead.astype(f32) + behind.astype(f32)
        parts = [total[:, at * span : (at + 1) * span] for at in range(4)]
        return parts[0], parts[1], parts[2], parts[3].T
    return pl.pallas_call(
        attention_sum_kernel,
        out_shape=(jax.ShapeDtypeStruct((part, span), f32),) * 3
        + (jax.ShapeDtypeStruct((span, part), f32),),
        in_specs=full_spec(2)
        + [pl.BlockSpec((1,) + terms.shape[1:], lambda at: (0, 0, 0))]
        + full_spec(1, pl.ANY),
        out_specs=full_spec(4),
        grid=(1,),
        compiler_params=pltpu.CompilerParams(vmem_limit_bytes=12 * MIB),
        cost_estimate=cost(2),
    )(ahead, behind, terms, after)


class Ring:
    def __init__(self, size):
        self.size = size
        order = ring_order(size)
        self.ahead = [(order[i], order[(i + 1) % size]) for i in range(size)]
        self.behind = [(b, a) for a, b in self.ahead]
        reach = (size - 1) // 2
        self.distances = [0]
        for step in range(1, reach + 1):
            self.distances += [-step, step]
        if size % 2 == 0:
            self.distances.append(size // 2)
        table = np.array(
            [
                [order[(order.index(me) + distance) % size] for distance in self.distances]
                for me in range(size)
            ],
            np.int32,
        )
        self.indices = jnp.asarray(table)[lax.axis_index("dp")]

    def send(self, value, forward):
        return lax.ppermute(value, "dp", self.ahead if forward else self.behind)

    def gather(self, array):
        return Gather(self, array)

    def scatter(self, blocks):
        return Scatter(self, *blocks)


class Scatter:
    def __init__(self, ring, terms, far_one, far_two):
        self.ring = ring
        self.terms = terms
        self.far = far_one, far_two
        self.place = {distance: at for at, distance in enumerate(ring.distances)}
        self.reach = (ring.size - 1) // 2
        self.one = self.two = None
        self.left = self.reach + 1 if ring.size % 2 == 0 else self.reach

    def add(self, *after, own_kernel=False):
        distance = self.left
        if distance > self.reach:
            self.one, self.two = self.far
        elif self.one is None:
            self.one, self.two = self.terms[self.place[distance]], self.terms[self.place[-distance]]
        else:
            self.one, self.two = ring_add(
                self.one, self.two, self.terms, self.place[distance], self.place[-distance], after, own_kernel
            )
        return self.one, self.two

    def send(self, *after):
        one, two = self.one, self.two
        if after:
            one, two, _ = lax.optimization_barrier((one, two, after))
        self.one, self.two = self.ring.send(one, True), self.ring.send(two, False)
        self.left -= 1

    def result(self):
        while self.left > 0:
            self.add()
            self.send()
        if self.one is None:
            return jnp.zeros_like(self.terms[0]), jnp.zeros_like(self.terms[0])
        if self.one.shape[0] < self.terms.shape[1]:
            return jnp.concatenate([self.one, self.two]), jnp.zeros_like(self.terms[0])
        return self.one, self.two


class Gather:
    def __init__(self, ring, array):
        self.ring = ring
        self.array = array
        self.one = self.two = array
        self.starts = [0]
        self.pieces = [array]
        self.done = 0
        self.last = ()

    def step(self, *after):
        size = self.ring.size
        self.done += 1
        if after:
            self.one, self.two, _ = lax.optimization_barrier((self.one, self.two, after))
        if self.done <= (size - 1) // 2:
            self.one = self.ring.send(self.one, True)
            self.two = self.ring.send(self.two, False)
            self.starts += [0, 0]
        else:
            rows = self.array.shape[0]
            half = rows // 2 if rows % 16 else rows // 32 * 16
            self.last = self.one[:half], self.two[half:]
            self.one = self.ring.send(self.last[0], True)
            self.two = self.ring.send(self.last[1], False)
            self.starts += [0, half]
        self.pieces += [self.one, self.two]

    def steps_left(self):
        return self.ring.size // 2 - self.done

    def blocks(self, sections, base=0):
        indices = self.ring.indices
        if self.ring.size % 2 == 0:
            indices = jnp.concatenate([indices, indices[-1:]])
        return Blocks(indices, self.starts, self.pieces, self.ring.size, sections, base)


class Quad:
    def __init__(self):
        self.me = lax.axis_index("tensor")
        self.core = self.me % 2
        self.chip = self.me // 2

    def over_core(self, value):
        return lax.ppermute(value, "tensor", [(i, i ^ 1) for i in range(4)])

    def over_chip(self, value):
        return lax.ppermute(value, "tensor", [(i, i ^ 2) for i in range(4)])

    def spread(self, block):
        far = self.over_chip(block)
        return block, self.over_core(block), far, self.over_core(far)

    def spread_direct(self, block):
        last = lax.ppermute(block, "tensor", [(i, i ^ 3) for i in range(4)])
        return block, self.over_core(block), self.over_chip(block), last

    def pick(self, half):
        return jnp.where(self.chip == 0, half[0], half[1])


def selections(chans, chans_here):
    own = np.zeros((4, 2, chans_here, 2, chans), np.float32)
    spread = np.zeros((2, 4, 2, 2, chans_here, 2, chans), np.float32)
    place = np.zeros((4, 4, chans_here, 4, 4, chans_here), np.float32)
    for t in range(4):
        for c in range(chans_here):
            for e in range(2):
                own[t, e, c, e, t * chans_here + c] = 1.0
                for a in range(2):
                    spread[a, t, a, e, c, e, t * chans_here + c] = 1.0
            for group in range(4):
                place[t, group, c, group, t, c] = 1.0
    own = own.reshape(4, 2, chans_here, 2 * chans).astype(LOW)
    spread = spread.reshape(2, 16 * chans_here, 2 * chans).astype(LOW)
    place = place.reshape(16 * chans_here, 16 * chans_here).astype(LOW)
    return jnp.asarray(own), jnp.asarray(spread), jnp.asarray(place)


def shards(
    tokens,
    crop_depth,
    w_query,
    w_key,
    w_value,
    w_out,
    w_up,
    w_down,
    w_tconv,
    w_conv1,
    w_conv2,
    ln1_gain,
    ln1_bias,
    ln2_gain,
    ln2_bias,
    cot_out,
    cot_dec,
    groups,
):
    ring = Ring(groups)
    quad = Quad()
    grid = GRID
    vox = 2 * grid
    patches = grid**3
    width = w_query.shape[0] * groups
    part = w_query.shape[0]
    heads_here = w_query.shape[1] // HD
    span = heads_here * HD
    chans = w_conv1.shape[0] * groups
    chans_here = w_conv1.shape[2]

    low = lambda value: value.astype(LOW)
    hidden_here = w_up.shape[1]
    norm_rows = [row[None] for row in (ln1_gain, ln1_bias, ln2_gain, ln2_bias)]
    encoder_pack = pack_encoder(w_query, w_key, w_value, w_out, norm_rows, w_up, w_down.T)
    first = ring.gather(encoder_pack)
    first.step()
    own_pack = pack_own(w_tconv, w_conv1, w_conv2, encoder_pack)
    local_blocks = quad.spread(pack_local(tokens, cot_out, cot_dec[0], own_pack))
    while first.steps_left():
        first.step()
    blocks = first.blocks([(0, part)])
    mlp_blocks = first.blocks([(0, part)], 4 * span + 128)
    out_weight, norms = out_and_norms(blocks, span, 4 * span)
    pair_pack, sections = pack_pair(
        quad.chip[None], local_blocks[0], local_blocks[2], part, w_conv1.shape[0], encoder_pack
    )
    third = ring.gather(pair_pack)
    third.step(out_weight)
    arrived = third.one, third.two
    select, spread, place = selections(chans, chans_here)
    core = quad.core[None]
    me = quad.me[None]

    attended, rows_low, h_one, qkv, probs = attention(
        crop_depth, me, local_blocks, blocks, norms, heads_here, ()
    )
    attended_blocks = quad.spread(attended)
    arrived = ()
    if third.steps_left():
        third.step(attended)
        arrived = third.one, third.two
    mine, other, mid, mid_half, h_two, hidden, slope = mlp(
        core,
        rows_low,
        attended_blocks,
        quad.spread(out_weight),
        norms,
        mlp_blocks,
        hidden_here,
        arrived,
    )
    arrived = ()
    if third.steps_left():
        third.step()
        arrived = third.one, third.two
    summed = half_sum(mine, quad.over_core(passed(other, arrived)), ())
    far = quad.over_chip(summed)
    while third.steps_left():
        third.step()
    decoder_own = join_decoder(third.blocks(sections), groups, part, summed)
    after, low_half = rows_sum(quad.chip[None], mid_half, summed, far, decoder_own)
    decoder_near, low_half = lax.optimization_barrier((decoder_own, low_half))
    decoder_near = quad.over_core(decoder_near)
    dec_out, grad_half, mlp_terms, mine, other, sums_two = decoder(
        ring.indices,
        crop_depth,
        me,
        low_half,
        quad.over_core(low_half),
        decoder_own,
        decoder_near,
        select,
        spread,
        place,
        local_blocks,
        slope,
        mid,
        h_two,
        hidden,
        mlp_blocks,
    )
    mlp_ring = ring.scatter(mlp_terms)
    mlp_ring.add()
    mlp_ring.send()
    summed = half_sum(mine, quad.over_core(other), ())
    far = quad.over_chip(summed)
    ready = mlp_ring.add(summed, own_kernel=True) if mlp_ring.left > 0 else ()
    low_mid_half = norm_back(
        summed, far, grad_half, mid_half, norms, ready
    )
    if mlp_ring.left > 0:
        mlp_ring.send(low_mid_half)
    mine, other, grad_qkv, grad_branch, sums_one = attention_back(
        core, low_mid_half, quad.over_core(low_mid_half), blocks, qkv, probs, rows_low, ()
    )
    ready = ()
    if mlp_ring.left > 0:
        ready = mlp_ring.add(sums_one)
        mlp_ring.send()
    attention_terms = attention_weights(
        ring.indices, h_one, attended, grad_qkv, grad_branch, sums_one, sums_two, ready
    )
    attention_ring = ring.scatter(attention_terms)
    attention_ring.add()
    attention_ring.send()
    last = ()
    while mlp_ring.left > 0 or attention_ring.left > 0:
        if attention_ring.left > 0:
            last = attention_ring.add(mlp_ring.one, mlp_ring.two)
            attention_ring.send()
        if mlp_ring.left > 0:
            mlp_ring.add()
            mlp_ring.send()
    mlp_ahead, mlp_behind = mlp_ring.result()
    ahead, behind = attention_ring.result()
    columns = slice(4 * span, 4 * span + 8)
    norm_grads = attention_terms[0][0, :, columns].astype(jnp.float32)
    norm_grads = norm_grads + ahead[:, columns].astype(jnp.float32)
    norm_grads = norm_grads + behind[:, columns].astype(jnp.float32)
    grad_query, grad_key, grad_value, grad_out = attention_sum(
        ahead, behind, attention_terms[0], span, norm_grads
    )
    norm_grads = sum(quad.spread_direct(norm_grads))
    summed = mine + quad.over_core(other).astype(jnp.float32)
    norm_own = quad.pick(summed) + quad.over_chip(low(quad.pick(summed[::-1]))).astype(jnp.float32)
    normed_own, scale_own = normalise(tokens.astype(jnp.float32))
    grad_tokens = quad.pick(low_mid_half).astype(jnp.float32) + layer_norm_back(norm_own * norms[0:1], normed_own, scale_own)
    grad_up, grad_down, grad_tconv, grad_conv1, grad_conv2 = mlp_sum(
        mlp_ahead, mlp_behind, mlp_terms[0], part, hidden_here, last
    )
    return (
        after,
        dec_out[None],
        grad_tokens,
        grad_query,
        grad_key,
        grad_value,
        grad_out,
        grad_up,
        grad_down.T,
        grad_tconv,
        grad_conv1.transpose(1, 0, 2),
        grad_conv2.transpose(1, 0, 2),
        norm_grads[:, 0],
        norm_grads[:, 1],
        norm_grads[:, 2],
        norm_grads[:, 3],
    )


def solution(mesh):
    in_specs = (
        P(("dp", "tensor"), None),
        P("dp"),
        P("dp", "tensor"),
        P("dp", "tensor"),
        P("dp", "tensor"),
        P("tensor", "dp"),
        P("dp", "tensor"),
        P("tensor", "dp"),
        P("dp", "tensor"),
        P("dp", None, "tensor"),
        P("dp", None, "tensor"),
        P("dp"),
        P("dp"),
        P("dp"),
        P("dp"),
        P(("dp", "tensor"), None),
        P("dp", None, None, None, "tensor"),
    )
    out_specs = (
        P(("dp", "tensor"), None),
        P("dp", None, None, None, "tensor"),
        P(("dp", "tensor"), None),
        P("dp", "tensor"),
        P("dp", "tensor"),
        P("dp", "tensor"),
        P("tensor", "dp"),
        P("dp", "tensor"),
        P("tensor", "dp"),
        P("dp", "tensor"),
        P("dp", None, "tensor"),
        P("dp", None, "tensor"),
        P("dp"),
        P("dp"),
        P("dp"),
        P("dp"),
    )
    groups = mesh.shape["dp"]

    def run(*arrays):
        return shards(*arrays, groups)

    return jax.shard_map(run, mesh=mesh, in_specs=in_specs, out_specs=out_specs, check_vma=False)
```
